32 devices in a mesh: dp: 8 (over z, x), tensor: 4 (over y, core).
Axes of the slice: x: 2, y: 2, z: 4, core: 2. Of those that a mesh axis runs over, the one named last changes fastest.
Arguments:
- text_rows: bfloat16 [256, 40, 768], P(('dp', 'tensor')), may hold values from -6 to 6
- patch_features: bfloat16 [256, 145, 1024], P(('dp', 'tensor')), may hold values from -6 to 6
- lengths: int32 [256], P(('dp', 'tensor')), may hold values from 8 to 40, as said below
- text_cotangent: bfloat16 [256, 40, 768], P(('dp', 'tensor')), may hold values from -6 to 6
- join_cotangent: bfloat16 [256, 40, 768], P(('dp', 'tensor')), may hold values from -6 to 6
- text_project_in: bfloat16 [3, 768, 768], P(None, None, 'tensor'), may hold values from -0.21875 to 0.21875
- text_project_bias: bfloat16 [2, 768], P(None, 'tensor'), may hold values from -3 to 3
- text_project_out: bfloat16 [768, 768], P('tensor'), may hold values from -0.75 to 0.75
- text_expand: bfloat16 [768, 3072], P(None, 'tensor'), may hold values from -0.21875 to 0.21875
- text_expand_bias: bfloat16 [3072], P('tensor'), may hold values from -3 to 3
- text_contract: bfloat16 [3072, 768], P('tensor'), may hold values from -0.109375 to 0.109375
- text_out_bias: bfloat16 [2, 768], replicated, may hold values from -3 to 3
- text_norm_gain: bfloat16 [2, 768], replicated, may hold values from 0.099609375 to 1.8984375
- text_norm_shift: bfloat16 [2, 768], replicated, may hold values from -3 to 3
- join_project_in: bfloat16 [4, 768, 768], P(None, None, 'tensor'), may hold values from -0.21875 to 0.21875
- join_project_bias: bfloat16 [4, 768], P(None, 'tensor'), may hold values from -3 to 3
- join_project_out: bfloat16 [768, 768], P('tensor'), may hold values from -0.75 to 0.75
- cross_project_out: bfloat16 [768, 768], P('tensor'), may hold values from -1.5 to 1.5
- cross_key_value: bfloat16 [2, 1024, 768], P(None, None, 'tensor'), may hold values from -0.1875 to 0.1875
- join_expand: bfloat16 [768, 3072], P(None, 'tensor'), may hold values from -0.21875 to 0.21875
- join_expand_bias: bfloat16 [3072], P('tensor'), may hold values from -3 to 3
- join_contract: bfloat16 [3072, 768], P('tensor'), may hold values from -0.109375 to 0.109375
- join_out_bias: bfloat16 [3, 768], replicated, may hold values from -3 to 3
- join_norm_gain: bfloat16 [3, 768], replicated, may hold values from 0.099609375 to 1.8984375
- join_norm_shift: bfloat16 [3, 768], replicated, may hold values from -3 to 3
Outputs:
- text_out: bfloat16 [256, 40, 768], P(('dp', 'tensor'))
- join_out: bfloat16 [256, 40, 768], P(('dp', 'tensor'))
- grad_text: bfloat16 [256, 40, 768], P(('dp', 'tensor'))
- grad_patches: bfloat16 [256, 145, 1024], P(('dp', 'tensor'))
- grad_text_project_in: float32 [3, 768, 768], P(None, None, 'tensor')
- grad_text_project_bias: float32 [2, 768], P(None, 'tensor')
- grad_text_project_out: float32 [768, 768], P('tensor')
- grad_text_expand: float32 [768, 3072], P(None, 'tensor')
- grad_text_expand_bias: float32 [3072], P('tensor')
- grad_text_contract: float32 [3072, 768], P('tensor')
- grad_text_out_bias: float32 [2, 768], replicated
- grad_text_norm_gain: float32 [2, 768], replicated
- grad_text_norm_shift: float32 [2, 768], replicated
- grad_join_project_in: float32 [4, 768, 768], P(None, None, 'tensor')
- grad_join_project_bias: float32 [4, 768], P(None, 'tensor')
- grad_join_project_out: float32 [768, 768], P('tensor')
- grad_cross_project_out: float32 [768, 768], P('tensor')
- grad_cross_key_value: float32 [2, 1024, 768], P(None, None, 'tensor')
- grad_join_expand: float32 [768, 3072], P(None, 'tensor')
- grad_join_expand_bias: float32 [3072], P('tensor')
- grad_join_contract: float32 [3072, 768], P('tensor')
- grad_join_out_bias: float32 [3, 768], replicated
- grad_join_norm_gain: float32 [3, 768], replicated
- grad_join_norm_shift: float32 [3, 768], replicated
The draws below stay inside these ranges and needn't reach their ends.
Inputs may be any that keep to these rules, and one draw needn't show every extreme that they name: An item's first lengths slots hold its text, the others padding; in every draw some item has all 40 slots real and some item only 8.
All inputs are finite; a program needn't handle non-finite values.
Results may differ from the reference program's by a relative error of at most 0.029.
Values may be sent and summed in bfloat16 or wider, within the bound.
A program may use at most 256 MiB of HBM per device.

```python
import jax
import jax.numpy as jnp
from jax import lax

D = 768
HEAD_DIM = 64
FF = 3072
PW = 1024
PATCHES = 145
SLOTS = 40
MIN_LEN = 8
ITEMS_DEV = 32
ITEMS = 256
N_DP = 8
N_TENSOR = 4


def draw_lengths(key, part):
    key = jax.random.fold_in(key, 11)
    key_base, key_long, key_distance = jax.random.split(key, 3)
    drawn = jax.random.randint(key_base, (ITEMS,), MIN_LEN, SLOTS + 1)
    longest = jax.random.randint(key_long, (), 0, ITEMS)
    distance = jax.random.randint(key_distance, (), 1, ITEMS)
    shortest = (longest + distance) % ITEMS
    drawn = drawn.at[longest].set(SLOTS)
    drawn = drawn.at[shortest].set(MIN_LEN)
    return drawn.astype(jnp.int32)


def block_scale(stream_key, shape, shards, low, high):
    def one(axis_at, shards_of):
        steps = jax.random.uniform(jax.random.fold_in(jax.random.fold_in(stream_key, 6), axis_at), (shards_of,), jnp.float32, low / len(shards), high / len(shards))
        return jnp.repeat(jnp.exp(steps), shape[axis_at] // shards_of).reshape((-1,) + (1,) * (len(shape) - axis_at - 1))

    factor_of = one(*shards[0])
    for cut in shards[1:]:
        factor_of = factor_of * one(*cut)
    return factor_of


def noise(stream_key, extent, scale, most, shards=(), held_as=jnp.bfloat16):
    result = jax.random.normal(stream_key, extent, jnp.float32) * scale
    if len(shards) > 0:
        result = block_scale(stream_key, extent, shards, -0.22, 0.18) * result
    return jnp.clip(result, min=-most, max=most).astype(held_as)


def setup_inputs(seed: int = 0) -> dict:
    keys = jax.random.split(jax.random.key(seed), 26)
    text_rows = noise(keys[0], (ITEMS, SLOTS, D), 1.0, 6.0, ((0, 32),))
    patch_features = noise(keys[1], (ITEMS, PATCHES, PW), 1.0, 6.0, ((0, 32),))
    lengths = draw_lengths(jax.random.fold_in(keys[25], 71), 0)
    text_cotangent = noise(keys[3], (ITEMS, SLOTS, D), 1.0, 6.0, ((0, 32),))
    join_cotangent = noise(keys[4], (ITEMS, SLOTS, D), 1.0, 6.0, ((0, 32),))
    text_project_in = noise(keys[5], (3, D, D), D ** -0.5, 0.21875, ((2, 4),))
    text_project_bias = noise(keys[6], (2, D), 0.5, 3.0, ((1, 4),))
    text_project_out = noise(keys[7], (D, D), (max(D // 12, 8)) ** -0.5, 0.75, ((0, 4),))
    text_expand = noise(keys[8], (D, FF), D ** -0.5, 0.21875, ((1, 4),))
    text_expand_bias = noise(keys[9], (FF,), 0.5, 3.0, ((0, 4),))
    text_contract = noise(keys[10], (FF, D), FF ** -0.5, 0.109375, ((0, 4),))
    text_out_bias = noise(keys[11], (2, D), 0.5, 3.0)
    text_norm_gain = jnp.clip(1.0 + 0.18 * jax.random.normal(keys[12], (2, D), jnp.float32), 0.099609375, 1.8984375).astype(jnp.bfloat16)
    text_norm_shift = noise(keys[13], (2, D), 0.5, 3.0)
    join_project_in = noise(keys[14], (4, D, D), D ** -0.5, 0.21875, ((2, 4),))
    join_project_bias = noise(keys[15], (4, D), 0.5, 3.0, ((1, 4),))
    join_project_out = noise(keys[16], (D, D), (max(D // 12, 8)) ** -0.5, 0.75, ((0, 4),))
    cross_project_out = noise(keys[17], (D, D), (max(D // 48, 8)) ** -0.5, 1.5, ((0, 4),))
    cross_key_value = noise(keys[18], (2, PW, D), PW ** -0.5, 0.1875, ((2, 4),))
    join_expand = noise(keys[19], (D, FF), D ** -0.5, 0.21875, ((1, 4),))
    join_expand_bias = noise(keys[20], (FF,), 0.5, 3.0, ((0, 4),))
    join_contract = noise(keys[21], (FF, D), FF ** -0.5, 0.109375, ((0, 4),))
    join_out_bias = noise(keys[22], (3, D), 0.5, 3.0)
    join_norm_gain = jnp.clip(1.0 + 0.18 * jax.random.normal(keys[23], (3, D), jnp.float32), 0.099609375, 1.8984375).astype(jnp.bfloat16)
    join_norm_shift = noise(keys[24], (3, D), 0.5, 3.0)
    return {"text_rows": text_rows, "patch_features": patch_features, "lengths": lengths, "text_cotangent": text_cotangent, "join_cotangent": join_cotangent, "text_project_in": text_project_in, "text_project_bias": text_project_bias, "text_project_out": text_project_out, "text_expand": text_expand, "text_expand_bias": text_expand_bias, "text_contract": text_contract, "text_out_bias": text_out_bias, "text_norm_gain": text_norm_gain, "text_norm_shift": text_norm_shift, "join_project_in": join_project_in, "join_project_bias": join_project_bias, "join_project_out": join_project_out, "cross_project_out": cross_project_out, "cross_key_value": cross_key_value, "join_expand": join_expand, "join_expand_bias": join_expand_bias, "join_contract": join_contract, "join_out_bias": join_out_bias, "join_norm_gain": join_norm_gain, "join_norm_shift": join_norm_shift}


@jax.custom_vjp
def low(v):
    return lax.optimization_barrier(v.astype(jnp.bfloat16)).astype(jnp.float32)

@jax.custom_vjp
def low_back(v):
    return v

def low_keep(v):
    return (low(v), None)

def low_pass(kept, grad):
    return (grad,)

def back_keep(v):
    return (v, None)

def back_low(kept, grad):
    return (low(grad),)
low.defvjp(low_keep, low_pass)
low_back.defvjp(back_keep, back_low)

def matmul(first_operand, second_operand):
    return jnp.matmul(first_operand, second_operand, precision=lax.Precision.HIGHEST)

def layer_norm(row_block, gain_vec, shift_vec):
    center = row_block - lax.optimization_barrier(jnp.mean(row_block, axis=-1, keepdims=True))
    variance = lax.optimization_barrier(jnp.mean(center * center, axis=-1, keepdims=True))
    return center * lax.rsqrt(variance + 1e-12) * gain_vec + shift_vec

def split_heads(source_array):
    return source_array.reshape(source_array.shape[:-1] + (source_array.shape[-1] // HEAD_DIM, HEAD_DIM))

def attention(query_in, source_in, w_query, b_query, w_key, w_value, b_value, w_out, valid_mask):
    queries = low(low_back(matmul(query_in, w_query) + b_query))
    key_rows = low(low_back(matmul(source_in, w_key)))
    values = low(low_back(matmul(source_in, w_value) + b_value))
    scores = jnp.einsum('iqhe,ikhe->ihqk', split_heads(queries), split_heads(key_rows), precision=lax.Precision.HIGHEST)
    scores = low_back(scores * HEAD_DIM ** (-0.5))
    if valid_mask is not None:
        scores = jnp.where(valid_mask[:, None, None, :], scores, -1e+30)
    probabilities = jax.nn.softmax(scores, axis=-1)
    mixed_heads = jnp.einsum('ihqk,ikhe->iqhe', low(probabilities), split_heads(values), precision=lax.Precision.HIGHEST)
    mixed_heads = low(low_back(mixed_heads.reshape(queries.shape)))
    return matmul(mixed_heads, w_out)

def self_block(row_block, w_in, b_in, w_out, out_bias, gain_vec, shift_vec, valid_mask):
    rounded = low(row_block)
    group_width = row_block.shape[-1] // N_TENSOR
    summed = jnp.zeros(row_block.shape, jnp.float32)
    for member in range(N_TENSOR):
        columns = slice(member * group_width, (member + 1) * group_width)
        summed = summed + attention(rounded, rounded, w_in[0][:, columns], b_in[0][columns], w_in[1][:, columns], w_in[2][:, columns], b_in[1][columns], w_out[columns, :], valid_mask)
    return layer_norm(row_block + low_back(summed) + out_bias, gain_vec, shift_vec)

def cross_block(row_block, patch_block, w_query, b_query, w_keyval, b_value, w_out, out_bias, gain_vec, shift_vec):
    rounded = low(row_block)
    group_width = row_block.shape[-1] // N_TENSOR
    summed = jnp.zeros(row_block.shape, jnp.float32)
    for member in range(N_TENSOR):
        columns = slice(member * group_width, (member + 1) * group_width)
        summed = summed + attention(rounded, patch_block, w_query[:, columns], b_query[columns], w_keyval[0][:, columns], w_keyval[1][:, columns], b_value[columns], w_out[columns, :], None)
    return layer_norm(row_block + low_back(summed) + out_bias, gain_vec, shift_vec)

def feed_block(row_block, w_expand, b_expand, w_contract, out_bias, gain_vec, shift_vec):
    rounded = low(row_block)
    hidden_width = w_expand.shape[1] // N_TENSOR
    summed = jnp.zeros(row_block.shape, jnp.float32)
    for member in range(N_TENSOR):
        columns = slice(member * hidden_width, (member + 1) * hidden_width)
        pre_act = low_back(matmul(rounded, w_expand[:, columns]) + b_expand[columns])
        hidden = low(jax.nn.gelu(pre_act, approximate=False))
        summed = summed + matmul(hidden, w_contract[columns, :])
    return layer_norm(row_block + low_back(summed) + out_bias, gain_vec, shift_vec)

def forward(text_block, patch_block, valid_mask, weight_set):
    text_project_in, text_project_bias, text_project_out, text_expand, text_expand_bias, text_contract, text_out_bias, text_norm_gain, text_norm_shift, join_project_in, join_project_bias, join_project_out, cross_project_out, cross_key_value, join_expand, join_expand_bias, join_contract, join_out_bias, join_norm_gain, join_norm_shift = weight_set
    hidden_one = self_block(text_block, text_project_in, text_project_bias, text_project_out, text_out_bias[0], text_norm_gain[0], text_norm_shift[0], valid_mask)
    text_out = low(feed_block(hidden_one, text_expand, text_expand_bias, text_contract, text_out_bias[1], text_norm_gain[1], text_norm_shift[1]))
    hidden_two = self_block(text_out, join_project_in[0:3], join_project_bias[0:2], join_project_out, join_out_bias[0], join_norm_gain[0], join_norm_shift[0], valid_mask)
    hidden_three = cross_block(hidden_two, patch_block, join_project_in[3], join_project_bias[2], cross_key_value, join_project_bias[3], cross_project_out, join_out_bias[1], join_norm_gain[1], join_norm_shift[1])
    join_out = low(feed_block(hidden_three, join_expand, join_expand_bias, join_contract, join_out_bias[2], join_norm_gain[2], join_norm_shift[2]))
    return (text_out, join_out)

def reference(text_rows, patch_features, lengths, text_cotangent, join_cotangent, text_project_in, text_project_bias, text_project_out, text_expand, text_expand_bias, text_contract, text_out_bias, text_norm_gain, text_norm_shift, join_project_in, join_project_bias, join_project_out, cross_project_out, cross_key_value, join_expand, join_expand_bias, join_contract, join_out_bias, join_norm_gain, join_norm_shift):
    weight_set = tuple((weight.astype(jnp.float32) for weight in (text_project_in, text_project_bias, text_project_out, text_expand, text_expand_bias, text_contract, text_out_bias, text_norm_gain, text_norm_shift, join_project_in, join_project_bias, join_project_out, cross_project_out, cross_key_value, join_expand, join_expand_bias, join_contract, join_out_bias, join_norm_gain, join_norm_shift)))
    slot_index = jnp.arange(SLOTS, dtype=jnp.int32)
    valid_all = (slot_index[None, :] < lengths.astype(jnp.int32)[:, None]).reshape(N_DP, ITEMS_DEV, SLOTS)
    text_blocks = text_rows.astype(jnp.float32).reshape(N_DP, ITEMS_DEV, SLOTS, D)
    patch_blocks = patch_features.astype(jnp.float32).reshape(N_DP, ITEMS_DEV, PATCHES, PW)
    text_cots = text_cotangent.astype(jnp.float32).reshape(N_DP, ITEMS_DEV, SLOTS, D)
    join_cots = join_cotangent.astype(jnp.float32).reshape(N_DP, ITEMS_DEV, SLOTS, D)

    def block_step(running, block_inputs):
        text_block, patch_block, valid_mask, cot_text, cot_join = block_inputs

        def local_forward(text_in, patch_in, weights_in):
            return forward(text_in, patch_in, valid_mask, weights_in)
        outputs, pullback = jax.vjp(local_forward, text_block, patch_block, weight_set)
        grad_in, grad_patch, grad_weights = pullback((cot_text, cot_join))
        running = jax.tree.map(jnp.add, running, grad_weights)
        return (running, (outputs[0], outputs[1], grad_in, grad_patch))
    zeros_set = tuple((jnp.zeros(weight.shape, jnp.float32) for weight in weight_set))
    running, stacked = lax.scan(block_step, zeros_set, (text_blocks, patch_blocks, valid_all, text_cots, join_cots))
    text_out = stacked[0].reshape(ITEMS, SLOTS, D).astype(jnp.bfloat16)
    join_out = stacked[1].reshape(ITEMS, SLOTS, D).astype(jnp.bfloat16)
    grad_text = stacked[2].reshape(ITEMS, SLOTS, D).astype(jnp.bfloat16)
    grad_patches = stacked[3].reshape(ITEMS, PATCHES, PW).astype(jnp.bfloat16)
    return (text_out, join_out, grad_text, grad_patches, running[0], running[1], running[2], running[3], running[4], running[5], running[6], running[7], running[8], running[9], running[10], running[11], running[12], running[13], running[14], running[15], running[16], running[17], running[18], running[19])
```

```python
import functools

import jax
import jax.numpy as jnp
from jax import lax
from jax.experimental import pallas as pl
from jax.experimental.pallas import tpu as pltpu
from jax.sharding import PartitionSpec as P

HEAD_DIM = 64
BF = jnp.bfloat16
F32 = jnp.float32
ANY = pl.ANY
VMEM_LIMIT = 56 * 1024 * 1024


def dot_nn(a, b):
    return lax.dot_general(a, b, (((1,), (0,)), ((), ())), preferred_element_type=F32)


def dot_nt(a, b):
    return lax.dot_general(a, b, (((1,), (1,)), ((), ())), preferred_element_type=F32)


def dot_tn(a, b):
    return lax.dot_general(a, b, (((0,), (0,)), ((), ())), preferred_element_type=F32)


def norm_forward(e, gain, shift):
    center = e - jnp.mean(e, axis=-1, keepdims=True)
    variance = jnp.mean(center * center, axis=-1, keepdims=True)
    return center * lax.rsqrt(variance + 1e-12) * gain + shift


def norm_backward(e, gain, dy):
    center = e - jnp.mean(e, axis=-1, keepdims=True)
    variance = jnp.mean(center * center, axis=-1, keepdims=True)
    rstd = lax.rsqrt(variance + 1e-12)
    normed = center * rstd
    scaled = dy * gain
    de = rstd * (
        scaled
        - jnp.mean(scaled, axis=-1, keepdims=True)
        - normed * jnp.mean(scaled * normed, axis=-1, keepdims=True)
    )
    sums = jnp.concatenate(
        [
            jnp.sum(de, axis=0, keepdims=True),
            jnp.sum(dy * normed, axis=0, keepdims=True),
            jnp.sum(dy, axis=0, keepdims=True),
        ],
        axis=0,
    )
    return de, sums


def head_masks(width):
    lane = lax.broadcasted_iota(jnp.int32, (1, width), 1)
    return [
        ((lane >= h * HEAD_DIM) & (lane < (h + 1) * HEAD_DIM)).astype(F32)
        for h in range(width // HEAD_DIM)
    ]


def stack_heads(rows, masks):
    return jnp.concatenate([rows * mask for mask in masks], axis=0).astype(BF)


def merge_heads(stacked, masks):
    count = stacked.shape[0] // len(masks)
    total = stacked[:count] * masks[0]
    for h in range(1, len(masks)):
        total = total + stacked[h * count : (h + 1) * count] * masks[h]
    return total


def item_forward(q, k, v, masks, length):
    scores = dot_nt(stack_heads(q, masks), k) * HEAD_DIM ** (-0.5)
    column = lax.broadcasted_iota(jnp.int32, scores.shape, 1)
    scores = jnp.where(column < length, scores, -1e30)
    weights = jnp.exp(scores - jnp.max(scores, axis=-1, keepdims=True))
    probs = (weights / jnp.sum(weights, axis=-1, keepdims=True)).astype(BF)
    return probs, merge_heads(dot_nn(probs, v), masks)


def item_backward(q, k, v, da, probs, masks):
    qs = stack_heads(q, masks)
    das = stack_heads(da, masks)
    dv = dot_tn(probs, das)
    dp = dot_nt(das, v)
    p = probs.astype(F32)
    ds = (p * (dp - jnp.sum(p * dp, axis=-1, keepdims=True))).astype(BF)
    scaling = HEAD_DIM ** (-0.5)
    dq = merge_heads(dot_nn(ds, k), masks) * scaling
    dk = dot_tn(ds, qs) * scaling
    return dq, dk, dv


def fetch_start(sources, target, sem):
    for r in range(len(sources)):
        pltpu.make_async_copy(sources[r], target.at[r], sem.at[r]).start()


def fetch_wait(sources, target, sem, r):
    pltpu.make_async_copy(sources[0], target.at[r], sem.at[r]).wait()


def ffn_forward_kernel(u, *refs):
    w1, w2 = refs[0:4], refs[4:8]
    c1, vec, y, e_out, h_out, slope_out, w1_s, w2_s, ub, acc, sem1, sem2 = refs[8:]
    step = pl.program_id(0)

    @pl.when(step == 0)
    def _():
        fetch_start(w1, w1_s, sem1)
        fetch_start(w2, w2_s, sem2)
        ub[...] = u[...].astype(BF)
        acc[...] = u[...] + vec[0:1, :]

    for j in range(2):
        r = 2 * step + j
        fetch_wait(w1, w1_s, sem1, r)
        z = dot_nn(ub[...], w1_s[r]) + c1[r]
        cdf = 0.5 * (1.0 + lax.erf(z * 0.7071067811865476))
        slope = cdf + z * (jnp.exp(-0.5 * z * z) * 0.3989422804014327)
        h = (z * cdf).astype(BF)
        h_out[j] = h
        slope_out[j] = slope.astype(BF)
        fetch_wait(w2, w2_s, sem2, r)
        acc[...] += dot_nn(h, w2_s[r])

    @pl.when(step == 1)
    def _():
        e = acc[...]
        e_out[...] = e
        y[...] = norm_forward(e, vec[1:2, :], vec[2:3, :]).astype(y.dtype)


def ffn_backward_kernel(has_grad, *refs):
    if has_grad:
        grad, refs = refs[0], refs[1:]
    cot, e_in, u = refs[0:3]
    w1, w2 = refs[3:7], refs[7:11]
    h_in, slope_in, vec = refs[11:14]
    du, g1k, g1s, g2k, g2s, dc1, sums = refs[14:21]
    w1_s, w2_s, ub, dob, acc, sem1, sem2 = refs[21:]
    step = pl.program_id(0)

    @pl.when(step == 0)
    def _():
        fetch_start(w2, w2_s, sem2)
        fetch_start(w1, w1_s, sem1)
        dy = cot[...].astype(F32)
        if has_grad:
            dy = dy + grad[...]
        de, partial = norm_backward(e_in[...], vec[1:2, :], dy)
        sums[...] = partial
        dob[...] = de.astype(BF)
        acc[...] = de
        ub[...] = u[...].astype(BF)

    for j in range(2):
        r = 2 * step + j
        fetch_wait(w2, w2_s, sem2, r)
        dh = dot_nt(dob[...], w2_s[r])
        dz = (dh * slope_in[j].astype(F32)).astype(BF)
        (g2k if j == 0 else g2s)[0] = dot_tn(h_in[j], dob[...]).astype(BF)
        (g1k if j == 0 else g1s)[0] = dot_tn(ub[...], dz).astype(BF)
        dc1[0, j : j + 1, :] = jnp.sum(dz.astype(F32), axis=0, keepdims=True)
        fetch_wait(w1, w1_s, sem1, r)
        acc[...] += dot_nt(dz, w1_s[r])

    @pl.when(step == 1)
    def _():
        du[...] = acc[...]


def self_forward_kernel(items, lengths, x, *refs):
    w = refs[0:4]
    bias, vec, y, e_out, q_out, k_out, v_out, p_out, a_out = refs[4:13]
    w_s, acc, q_s, k_s, v_s, a_s, sem = refs[13:]
    step = pl.program_id(0)
    width = q_s.shape[1]
    slots = x.shape[0] // items

    @pl.when(step == 0)
    def _():
        fetch_start(w, w_s, sem)
        acc[...] = x[...].astype(F32) + vec[0:1, :]

    masks = head_masks(width)
    for j in range(2):
        r = 2 * step + j
        fetch_wait(w, w_s, sem, r)
        xb = x[...]
        q = (dot_nt(xb, w_s[r, 0:width]) + bias[r, 0:1]).astype(BF)
        k = dot_nt(xb, w_s[r, width : 2 * width]).astype(BF)
        v = (dot_nt(xb, w_s[r, 2 * width : 3 * width]) + bias[r, 1:2]).astype(BF)
        q_out[j], k_out[j], v_out[j] = q, k, v
        q_s[...], k_s[...], v_s[...] = q.astype(F32), k.astype(F32), v.astype(F32)
        for i in range(items):
            rows = pl.ds(i * slots, slots)
            probs, a = item_forward(
                q_s[rows], k_s[rows].astype(BF), v_s[rows].astype(BF), masks, lengths[i]
            )
            p_out[j, i] = probs
            a_s[rows] = a
        ab = a_s[...].astype(BF)
        a_out[j] = ab
        acc[...] += dot_nn(ab, w_s[r, 3 * width : 4 * width])

    @pl.when(step == 1)
    def _():
        e = acc[...]
        e_out[...] = e
        y[...] = norm_forward(e, vec[1:2, :], vec[2:3, :]).astype(y.dtype)


def self_backward_kernel(items, dy, e_in, x, *refs):
    w = refs[0:4]
    q_in, k_in, v_in, p_in, a_in, vec = refs[4:10]
    du, gk, gs, db, sums = refs[10:15]
    w_s, dob, acc, q_s, k_s, v_s, da_s, dq_s, dk_s, dv_s, sem = refs[15:]
    step = pl.program_id(0)
    width = q_s.shape[1]
    slots = x.shape[0] // items

    @pl.when(step == 0)
    def _():
        fetch_start(w, w_s, sem)
        de, partial = norm_backward(e_in[...], vec[1:2, :], dy[...])
        sums[...] = partial
        dob[...] = de.astype(BF)
        acc[...] = de

    masks = head_masks(width)
    for j in range(2):
        r = 2 * step + j
        g = gk if j == 0 else gs
        fetch_wait(w, w_s, sem, r)
        da_s[...] = dot_nt(dob[...], w_s[r, 3 * width : 4 * width])
        g[0, 3 * width : 4 * width] = dot_tn(a_in[j], dob[...]).astype(BF)
        q_s[...], k_s[...], v_s[...] = (
            q_in[j].astype(F32),
            k_in[j].astype(F32),
            v_in[j].astype(F32),
        )
        for i in range(items):
            rows = pl.ds(i * slots, slots)
            dq, dk, dv = item_backward(
                q_s[rows],
                k_s[rows].astype(BF),
                v_s[rows].astype(BF),
                da_s[rows],
                p_in[j, i],
                masks,
            )
            dq_s[rows], dk_s[rows], dv_s[rows] = dq, dk, dv
        xb = x[...]
        total = acc[...]
        for c, part in enumerate((dq_s, dk_s, dv_s)):
            pb = part[...].astype(BF)
            g[0, c * width : (c + 1) * width] = dot_tn(pb, xb).astype(BF)
            total = total + dot_nn(pb, w_s[r, c * width : (c + 1) * width])
            if c != 1:
                db[0, j, c // 2 : c // 2 + 1, :] = jnp.sum(
                    pb.astype(F32), axis=0, keepdims=True
                )
        acc[...] = total

    @pl.when(step == 1)
    def _():
        du[...] = acc[...].astype(du.dtype)


def key_value_weight(w_s, r, start, width, model):
    low = w_s[r, pl.ds(start, 2 * width)]
    tail = w_s[r, pl.ds(start + 2 * width, 2 * width * (1024 - model) // model)]
    side = 1024 - model
    high = jnp.concatenate(
        [tail[:, c * side : (c + 1) * side] for c in range(model // side)], axis=0
    )
    return low, high


def cross_forward_kernel(items, patches, u, pf, *refs):
    w = refs[0:4]
    bias, vec, y, e_out, q_out, k_out, v_out, p_out, a_out = refs[4:13]
    w_s, ub, acc, q_s, a_s, sem = refs[13:]
    step = pl.program_id(0)
    width = q_s.shape[1]
    model = u.shape[1]
    slots = u.shape[0] // items
    padded = pf.shape[0] // items

    @pl.when(step == 0)
    def _():
        fetch_start(w, w_s, sem)
        ub[...] = u[...].astype(BF)
        acc[...] = u[...] + vec[0:1, :]

    masks = head_masks(width)
    for j in range(2):
        r = 2 * step + j
        fetch_wait(w, w_s, sem, r)
        q_b = (dot_nt(ub[...], w_s[r, 0:width]) + bias[r, 0:1]).astype(BF)
        q_out[j] = q_b
        q_s[...] = q_b.astype(F32)
        low, high = key_value_weight(w_s, r, 2 * width, width, model)
        chunk = 2 * padded
        for m in range(items // 2):
            rows = slice(m * chunk, (m + 1) * chunk)
            left, right = pf[rows, 0:model], pf[rows, model:]
            k_out[j, rows] = (
                dot_nt(left, low[0:width]) + dot_nt(right, high[0:width])
            ).astype(BF)
            v_out[j, rows] = (
                dot_nt(left, low[width:]) + dot_nt(right, high[width:]) + bias[r, 1:2]
            ).astype(BF)
        for i in range(items):
            rows = pl.ds(i * slots, slots)
            keys = pl.ds(i * padded, padded)
            probs, a = item_forward(
                q_s[rows], k_out[j, keys], v_out[j, keys], masks, patches
            )
            p_out[j, i] = probs
            a_s[rows] = a
        ab = a_s[...].astype(BF)
        a_out[j] = ab
        acc[...] += dot_nn(ab, w_s[r, width : 2 * width])

    @pl.when(step == 1)
    def _():
        e = acc[...]
        e_out[...] = e
        y[...] = norm_forward(e, vec[1:2, :], vec[2:3, :]).astype(y.dtype)


def cross_backward_kernel(items, patches, dy, e_in, u, pf, *refs):
    w = refs[0:4]
    q_in, k_in, v_in, p_in, a_in, vec = refs[4:10]
    du, dpf, gk, gs, db, sums = refs[10:16]
    w_s, ub, dob, acc, pacc, q_s, da_s, dq_s, dkv_s, sem = refs[16:]
    step = pl.program_id(0)
    width = q_s.shape[1]
    model = u.shape[1]
    side = pf.shape[1] - model
    slots = u.shape[0] // items
    padded = pf.shape[0] // items

    @pl.when(step == 0)
    def _():
        fetch_start(w, w_s, sem)
        de, partial = norm_backward(e_in[...], vec[1:2, :], dy[...])
        sums[...] = partial
        dob[...] = de.astype(BF)
        acc[...] = de
        ub[...] = u[...].astype(BF)
        pacc[...] = jnp.zeros_like(pacc)

    masks = head_masks(width)
    for j in range(2):
        r = 2 * step + j
        g = gk if j == 0 else gs
        fetch_wait(w, w_s, sem, r)
        da_s[...] = dot_nt(dob[...], w_s[r, width : 2 * width])
        g[0, width : 2 * width] = dot_tn(a_in[j], dob[...]).astype(BF)
        q_s[...] = q_in[j].astype(F32)
        vsum = jnp.zeros((1, width), F32)
        for i in range(items):
            rows = pl.ds(i * slots, slots)
            keys = pl.ds(i * padded, padded)
            dq, dk, dv = item_backward(
                q_s[rows], k_in[j, keys], v_in[j, keys], da_s[rows], p_in[j, i], masks
            )
            dq_s[rows] = dq
            dkv_s[0, keys] = dk.astype(BF)
            dvb = dv.astype(BF)
            dkv_s[1, keys] = dvb
            vsum = vsum + jnp.sum(dvb.astype(F32), axis=0, keepdims=True)
        dqb = dq_s[...].astype(BF)
        g[0, 0:width] = dot_tn(dqb, ub[...]).astype(BF)
        acc[...] += dot_nn(dqb, w_s[r, 0:width])
        db[0, j, 0:1, :] = jnp.sum(dqb.astype(F32), axis=0, keepdims=True)
        db[0, j, 1:2, :] = vsum
        low, high = key_value_weight(w_s, r, 2 * width, width, model)
        tails = []
        for c in range(2):
            part = dkv_s[c]
            g[0, (2 + c) * width : (3 + c) * width] = dot_tn(part, pf[:, 0:model]).astype(BF)
            tails.append(dot_tn(part, pf[:, model:]).astype(BF))
            pacc[:, 0:model] += dot_nn(part, low[c * width : (c + 1) * width])
            pacc[:, model:] += dot_nn(part, high[c * width : (c + 1) * width])
        tail = jnp.concatenate(tails, axis=0)
        count = tail.shape[0] // (model // side)
        for c in range(model // side):
            g[0, 4 * width : 4 * width + count, c * side : (c + 1) * side] = tail[
                c * count : (c + 1) * count
            ]

    @pl.when(step == 1)
    def _():
        du[...] = acc[...]
        for i in range(items):
            dpf[i] = pacc[i * padded : i * padded + patches, :].astype(BF)


def whole(shape):
    zeros = (0,) * len(shape)
    return pl.BlockSpec(shape, lambda p: zeros)


def halves(shape):
    zeros = (0,) * (len(shape) - 1)
    return pl.BlockSpec((shape[0] // 2,) + tuple(shape[1:]), lambda p: (p,) + zeros)


def call(kernel, name, operands, outputs, scratch, flops, transcendentals=0):
    kinds = {
        "whole": lambda s: whole(s),
        "half": lambda s: halves(s),
        "any": lambda s: pl.BlockSpec(memory_space=ANY),
        "smem": lambda s: pl.BlockSpec(memory_space=pltpu.SMEM),
    }
    size = sum(a.size * a.dtype.itemsize for a, _ in operands)
    for shape, dtype, _ in outputs:
        count = jnp.dtype(dtype).itemsize
        for extent in shape:
            count *= extent
        size += count
    return pl.pallas_call(
        kernel,
        grid=(2,),
        in_specs=[kinds[kind](a.shape) for a, kind in operands],
        out_specs=[kinds[kind](shape) for shape, _, kind in outputs],
        out_shape=[jax.ShapeDtypeStruct(shape, dtype) for shape, dtype, _ in outputs],
        scratch_shapes=scratch,
        compiler_params=pltpu.CompilerParams(
            dimension_semantics=("arbitrary",), vmem_limit_bytes=VMEM_LIMIT
        ),
        cost_estimate=pl.CostEstimate(
            flops=flops, bytes_accessed=size, transcendentals=transcendentals
        ),
        name=name,
    )(*[a for a, _ in operands])


def feed_forward(u, w1, w2, c1, vec, name):
    rows, model = u.shape
    hidden = w1[0].shape[1]
    outs = call(
        ffn_forward_kernel,
        name,
        [(u, "whole")]
        + [(a, "any") for a in w1]
        + [(a, "any") for a in w2]
        + [(c1, "whole"), (vec, "whole")],
        [
            ((rows, model), BF, "whole"),
            ((rows, model), F32, "whole"),
            ((4, rows, hidden), BF, "half"),
            ((4, rows, hidden), BF, "half"),
        ],
        [
            pltpu.VMEM((4, model, hidden), BF),
            pltpu.VMEM((4, hidden, model), BF),
            pltpu.VMEM((rows, model), BF),
            pltpu.VMEM((rows, model), F32),
            pltpu.SemaphoreType.DMA((4,)),
            pltpu.SemaphoreType.DMA((4,)),
        ],
        16 * rows * model * hidden,
        8 * rows * hidden,
    )
    return outs[0], (u, outs[1], outs[2], outs[3])


def feed_backward(grad, cot, saved, w1, w2, vec, name):
    u, e, h, slope = saved
    rows, model = u.shape
    hidden = w1[0].shape[1]
    has_grad = grad is not None
    g = ((2, model, hidden), BF, "half")
    g2 = ((2, hidden, model), BF, "half")
    return call(
        functools.partial(ffn_backward_kernel, has_grad),
        name,
        ([(grad, "whole")] if has_grad else [])
        + [(cot, "whole"), (e, "whole"), (u, "whole")]
        + [(a, "any") for a in w1]
        + [(a, "any") for a in w2]
        + [(h, "half"), (slope, "half"), (vec, "whole")],
        [
            ((rows, model), F32, "whole"),
            g,
            g,
            g2,
            g2,
            ((2, 2, hidden), F32, "half"),
            ((3, model), F32, "whole"),
        ],
        [
            pltpu.VMEM((4, model, hidden), BF),
            pltpu.VMEM((4, hidden, model), BF),
            pltpu.VMEM((rows, model), BF),
            pltpu.VMEM((rows, model), BF),
            pltpu.VMEM((rows, model), F32),
            pltpu.SemaphoreType.DMA((4,)),
            pltpu.SemaphoreType.DMA((4,)),
        ],
        32 * rows * model * hidden,
    )


def self_forward(lengths, x, w, bias, vec, name):
    items = lengths.shape[0]
    rows, model = x.shape
    slots = rows // items
    width = w[0].shape[0] // 4
    heads = width // HEAD_DIM
    mid = ((4, rows, width), BF, "half")
    outs = call(
        functools.partial(self_forward_kernel, items),
        name,
        [(lengths, "smem"), (x, "whole")]
        + [(a, "any") for a in w]
        + [(bias, "whole"), (vec, "whole")],
        [
            ((rows, model), F32, "whole"),
            ((rows, model), F32, "whole"),
            mid,
            mid,
            mid,
            ((4, items, heads * slots, slots), BF, "half"),
            mid,
        ],
        [
            pltpu.VMEM((4,) + w[0].shape, BF),
            pltpu.VMEM((rows, model), F32),
            pltpu.VMEM((rows, width), F32),
            pltpu.VMEM((rows, width), F32),
            pltpu.VMEM((rows, width), F32),
            pltpu.VMEM((rows, width), F32),
            pltpu.SemaphoreType.DMA((4,)),
        ],
        32 * rows * model * width,
    )
    return outs[0], (x, outs[1], outs[2], outs[3], outs[4], outs[5], outs[6])


def self_backward(dy, saved, items, w, vec, dtype, name):
    x, e, q, k, v, p, a = saved
    rows, model = x.shape
    width = q.shape[2]
    g = ((2,) + w[0].shape, BF, "half")
    return call(
        functools.partial(self_backward_kernel, items),
        name,
        [(dy, "whole"), (e, "whole"), (x, "whole")]
        + [(m, "any") for m in w]
        + [(q, "half"), (k, "half"), (v, "half"), (p, "half"), (a, "half"), (vec, "whole")],
        [
            ((rows, model), dtype, "whole"),
            g,
            g,
            ((2, 2, 2, width), F32, "half"),
            ((3, model), F32, "whole"),
        ],
        [
            pltpu.VMEM((4,) + w[0].shape, BF),
            pltpu.VMEM((rows, model), BF),
            pltpu.VMEM((rows, model), F32),
        ]
        + [pltpu.VMEM((rows, width), F32)] * 7
        + [pltpu.SemaphoreType.DMA((4,))],
        64 * rows * model * width,
    )


def cross_forward(u, pf, patches, items, w, bias, vec, name):
    rows, model = u.shape
    slots, padded = rows // items, pf.shape[0] // items
    width = bias.shape[2]
    heads = width // HEAD_DIM
    mid = ((4, rows, width), BF, "half")
    key = ((4, pf.shape[0], width), BF, "half")
    outs = call(
        functools.partial(cross_forward_kernel, items, patches),
        name,
        [(u, "whole"), (pf, "whole")]
        + [(a, "any") for a in w]
        + [(bias, "whole"), (vec, "whole")],
        [
            ((rows, model), F32, "whole"),
            ((rows, model), F32, "whole"),
            mid,
            key,
            key,
            ((4, items, heads * slots, padded), BF, "half"),
            mid,
        ],
        [
            pltpu.VMEM((4,) + w[0].shape, BF),
            pltpu.VMEM((rows, model), BF),
            pltpu.VMEM((rows, model), F32),
            pltpu.VMEM((rows, width), F32),
            pltpu.VMEM((rows, width), F32),
            pltpu.SemaphoreType.DMA((4,)),
        ],
        16 * rows * model * width + 16 * pf.size * width,
    )
    return outs[0], (u, outs[1], outs[2], outs[3], outs[4], outs[5], outs[6])


def cross_backward(dy, saved, pf, patches, items, w, vec, name):
    u, e, q, k, v, p, a = saved
    rows, model = u.shape
    width = q.shape[2]
    g = ((2,) + w[0].shape, BF, "half")
    return call(
        functools.partial(cross_backward_kernel, items, patches),
        name,
        [(dy, "whole"), (e, "whole"), (u, "whole"), (pf, "whole")]
        + [(m, "any") for m in w]
        + [(q, "half"), (k, "half"), (v, "half"), (p, "half"), (a, "half"), (vec, "whole")],
        [
            ((rows, model), F32, "whole"),
            ((items, patches, pf.shape[1]), BF, "whole"),
            g,
            g,
            ((2, 2, 2, width), F32, "half"),
            ((3, model), F32, "whole"),
        ],
        [
            pltpu.VMEM((4,) + w[0].shape, BF),
            pltpu.VMEM((rows, model), BF),
            pltpu.VMEM((rows, model), BF),
            pltpu.VMEM((rows, model), F32),
            pltpu.VMEM(pf.shape, F32),
            pltpu.VMEM((rows, width), F32),
            pltpu.VMEM((rows, width), F32),
            pltpu.VMEM((rows, width), F32),
            pltpu.VMEM((2, pf.shape[0], width), BF),
            pltpu.SemaphoreType.DMA((4,)),
        ],
        32 * rows * model * width + 32 * pf.size * width,
    )


def swap(array, axis, size, distance):
    return lax.ppermute(array, axis, [(i, i ^ distance) for i in range(size)])


class Links:
    def __init__(self, mesh):
        self.tensor = mesh.shape["tensor"]
        self.dp = mesh.shape["dp"]
        self.bits = self.dp.bit_length() - 1

    def core(self, array):
        return swap(array, "tensor", self.tensor, 1)

    def far(self, array):
        return swap(array, "tensor", self.tensor, 2)

    def gather(self, own):
        across = self.far(own)
        return own, self.core(own), across, self.core(across)

    def reduce(self, keep, send):
        got = self.core(send)
        other = (keep[1].astype(F32) + got[1].astype(F32)).astype(BF)
        got_far = self.far(other)
        total = keep[0].astype(F32) + got[0].astype(F32) + got_far.astype(F32)
        total = total.astype(BF)
        me = lax.axis_index("dp")
        for b in range(self.bits):
            bit = (me >> b) & 1
            half = total.shape[0] // 2
            mine = lax.dynamic_slice_in_dim(total, bit * half, half, 0)
            gone = lax.dynamic_slice_in_dim(total, (1 - bit) * half, half, 0)
            got = swap(gone, "dp", self.dp, 1 << b)
            total = (mine.astype(F32) + got.astype(F32)).astype(BF)
        for b in reversed(range(self.bits)):
            bit = (me >> b) & 1
            got = swap(total, "dp", self.dp, 1 << b)
            total = jnp.where(
                bit == 0,
                jnp.concatenate([total, got], axis=0),
                jnp.concatenate([got, total], axis=0),
            )
        return total.astype(F32)


def flat(array):
    return array.reshape(-1)


def self_pack(w_in, w_out):
    turned = jnp.swapaxes(w_in, 1, 2)
    return jnp.concatenate([turned.reshape(-1, w_in.shape[1]), w_out], axis=0)


def self_unpack(total, width):
    model = total.shape[1]
    first = jnp.swapaxes(total[: 3 * width].reshape(3, width, model), 1, 2)
    return first, total[3 * width :]


def cross_pack(w_query, w_out, w_keyval):
    model = w_query.shape[0]
    keyval = jnp.swapaxes(w_keyval, 1, 2).reshape(-1, w_keyval.shape[1])
    side = w_keyval.shape[1] - model
    parts = model // side
    count = keyval.shape[0] // parts
    tail = keyval[:, model:].reshape(parts, count, side)
    tail = jnp.swapaxes(tail, 0, 1).reshape(count, model)
    return jnp.concatenate([w_query.T, w_out, keyval[:, :model], tail], axis=0)


def cross_unpack(total, width, patch_width):
    model = total.shape[1]
    side = patch_width - model
    parts = model // side
    tail = total[4 * width :]
    tail = jnp.swapaxes(tail.reshape(-1, parts, side), 0, 1).reshape(2 * width, side)
    keyval = jnp.concatenate([total[2 * width : 4 * width], tail], axis=1)
    keyval = jnp.swapaxes(keyval.reshape(2, width, patch_width), 1, 2)
    return total[:width].T, total[width : 2 * width], keyval


def per_device(
    links,
    text_rows,
    patch_features,
    lengths,
    text_cotangent,
    join_cotangent,
    text_project_in,
    text_project_bias,
    text_project_out,
    text_expand,
    text_expand_bias,
    text_contract,
    text_out_bias,
    text_norm_gain,
    text_norm_shift,
    join_project_in,
    join_project_bias,
    join_project_out,
    cross_project_out,
    cross_key_value,
    join_expand,
    join_expand_bias,
    join_contract,
    join_out_bias,
    join_norm_gain,
    join_norm_shift,
):
    items, slots, model = text_rows.shape
    patches, patch_width = patch_features.shape[1:]
    width = text_project_in.shape[2]
    hidden = text_expand.shape[1]

    biases = jnp.concatenate(
        [
            flat(text_project_bias),
            flat(join_project_bias),
            text_expand_bias,
            join_expand_bias,
        ]
    )[None]
    weights_one = links.gather(self_pack(text_project_in, text_project_out))
    biases = jnp.concatenate(links.gather(biases), axis=0).astype(F32)
    expand_one = links.gather(text_expand)
    contract_one = links.gather(text_contract)
    weights_two = links.gather(self_pack(join_project_in[0:3], join_project_out))
    weights_cross = links.gather(
        cross_pack(join_project_in[3], cross_project_out, cross_key_value)
    )
    expand_two = links.gather(join_expand)
    contract_two = links.gather(join_contract)

    bias_one = biases[:, : 2 * width].reshape(4, 2, width)
    bias_two = biases[:, 2 * width : 4 * width].reshape(4, 2, width)
    bias_cross = biases[:, 4 * width : 6 * width].reshape(4, 2, width)
    hidden_one = biases[:, 6 * width : 6 * width + hidden].reshape(4, 1, hidden)
    hidden_two = biases[:, 6 * width + hidden :].reshape(4, 1, hidden)

    def vec(bias, gain, shift, n):
        return jnp.stack([bias[n], gain[n], shift[n]]).astype(F32)

    text_vecs = [vec(text_out_bias, text_norm_gain, text_norm_shift, n) for n in range(2)]
    join_vecs = [vec(join_out_bias, join_norm_gain, join_norm_shift, n) for n in range(3)]

    padded = -(-patches // 16) * 16
    pf = jnp.pad(patch_features, ((0, 0), (0, padded - patches), (0, 0)))
    pf = pf.reshape(items * padded, patch_width)
    x = text_rows.reshape(items * slots, model)
    text_cot = text_cotangent.reshape(items * slots, model)
    join_cot = join_cotangent.reshape(items * slots, model)

    h1, saved_one = self_forward(lengths, x, weights_one, bias_one, text_vecs[0], "text_self_forward")
    text_out, saved_two = feed_forward(
        h1, expand_one, contract_one, hidden_one, text_vecs[1], "text_feed_forward"
    )
    h2, saved_three = self_forward(
        lengths, text_out, weights_two, bias_two, join_vecs[0], "join_self_forward"
    )
    h3, saved_four = cross_forward(
        h2, pf, patches, items, weights_cross, bias_cross, join_vecs[1], "cross_forward"
    )
    join_out, saved_five = feed_forward(
        h3, expand_two, contract_two, hidden_two, join_vecs[2], "join_feed_forward"
    )

    du, g1k, g1s, g2k, g2s, dc_two, sums_five = feed_backward(
        None, join_cot, saved_five, expand_two, contract_two, join_vecs[2], "join_feed_backward"
    )
    grad_join_contract = links.reduce(g2k, g2s)
    grad_join_expand = links.reduce(g1k, g1s)
    du, grad_patches, gk, gs, db_cross, sums_four = cross_backward(
        du, saved_four, pf, patches, items, weights_cross, join_vecs[1], "cross_backward"
    )
    grad_query, grad_cross_out, grad_keyval = cross_unpack(
        links.reduce(gk, gs), width, patch_width
    )
    du, gk, gs, db_two, sums_three = self_backward(
        du, saved_three, items, weights_two, join_vecs[0], F32, "join_self_backward"
    )
    grad_join_in, grad_join_out = self_unpack(links.reduce(gk, gs), width)
    du, g1k, g1s, g2k, g2s, dc_one, sums_two = feed_backward(
        du, text_cot, saved_two, expand_one, contract_one, text_vecs[1], "text_feed_backward"
    )
    grad_text_contract = links.reduce(g2k, g2s)
    grad_text_expand = links.reduce(g1k, g1s)
    grad_text, gk, gs, db_one, sums_one = self_backward(
        du, saved_one, items, weights_one, text_vecs[0], BF, "text_self_backward"
    )
    grad_text_in, grad_text_out = self_unpack(links.reduce(gk, gs), width)

    blocks = jnp.concatenate(
        [
            db_one.reshape(4, -1),
            db_two.reshape(4, -1),
            db_cross.reshape(4, -1),
            dc_one.reshape(4, -1),
            dc_two.reshape(4, -1),
        ],
        axis=1,
    )
    shared = jnp.stack([sums_one, sums_two, sums_three, sums_four, sums_five])
    units = blocks.shape[1]
    count = shared.size
    got = links.core(jnp.concatenate([blocks[1], blocks[3], flat(shared)]))
    own = blocks[0] + got[:units]
    other = blocks[2] + got[units : 2 * units]
    shared = flat(shared) + got[2 * units :]
    got = links.far(jnp.concatenate([other, shared]))
    small = jnp.concatenate([own, shared]) + got
    for b in range(links.bits):
        small = small + swap(small, "dp", links.dp, 1 << b)
    shared = small[units:].reshape(5, 3, model)
    attend = small[: 6 * width].reshape(6, width)
    text_shared, join_shared = shared[0:2], shared[2:5]

    return (
        text_out.reshape(text_rows.shape),
        join_out.reshape(text_rows.shape),
        grad_text.reshape(text_rows.shape),
        grad_patches,
        grad_text_in,
        attend[0:2],
        grad_text_out,
        grad_text_expand,
        small[6 * width : 6 * width + hidden],
        grad_text_contract,
        text_shared[:, 0],
        text_shared[:, 1],
        text_shared[:, 2],
        jnp.concatenate([grad_join_in, grad_query[None]], axis=0),
        attend[2:6],
        grad_join_out,
        grad_cross_out,
        grad_keyval,
        grad_join_expand,
        small[6 * width + hidden : 6 * width + 2 * hidden],
        grad_join_contract,
        join_shared[:, 0],
        join_shared[:, 1],
        join_shared[:, 2],
    )


def solution(mesh):
    rows = P(("dp", "tensor"), None, None)
    last = P(None, None, "tensor")
    second = P(None, "tensor")
    first = P("tensor", None)
    line = P("tensor")
    full = P()
    in_specs = (
        (rows, rows, P(("dp", "tensor")), rows, rows)
        + (last, second, first, second, line, first, full, full, full)
        + (last, second, first, first, last, second, line, first, full, full, full)
    )
    out_specs = (
        (rows, rows, rows, rows)
        + (last, second, first, second, line, first, full, full, full)
        + (last, second, first, first, last, second, line, first, full, full, full)
    )
    return jax.shard_map(
        functools.partial(per_device, Links(mesh)),
        mesh=mesh,
        in_specs=in_specs,
        out_specs=out_specs,
        check_vma=False,
    )
```

```python
import functools

import jax
import jax.numpy as jnp
from jax import lax
from jax.experimental import pallas as pl
from jax.experimental.pallas import tpu as pltpu
from jax.sharding import PartitionSpec as P

HEAD_DIM = 64
BF = jnp.bfloat16
F32 = jnp.float32
ANY = pl.ANY
VMEM_LIMIT = 56 * 1024 * 1024


def dot_nn(a, b):
    return lax.dot_general(a, b, (((1,), (0,)), ((), ())), preferred_element_type=F32)


def dot_nt(a, b):
    return lax.dot_general(a, b, (((1,), (1,)), ((), ())), preferred_element_type=F32)


def dot_tn(a, b):
    return lax.dot_general(a, b, (((0,), (0,)), ((), ())), preferred_element_type=F32)


def norm_forward(e, gain, shift):
    center = e - jnp.mean(e, axis=-1, keepdims=True)
    variance = jnp.mean(center * center, axis=-1, keepdims=True)
    return center * lax.rsqrt(variance + 1e-12) * gain + shift


def norm_backward(e, gain, dy):
    center = e - jnp.mean(e, axis=-1, keepdims=True)
    variance = jnp.mean(center * center, axis=-1, keepdims=True)
    rstd = lax.rsqrt(variance + 1e-12)
    normed = center * rstd
    scaled = dy * gain
    de = rstd * (
        scaled
        - jnp.mean(scaled, axis=-1, keepdims=True)
        - normed * jnp.mean(scaled * normed, axis=-1, keepdims=True)
    )
    sums = jnp.concatenate(
        [
            jnp.sum(de, axis=0, keepdims=True),
            jnp.sum(dy * normed, axis=0, keepdims=True),
            jnp.sum(dy, axis=0, keepdims=True),
        ],
        axis=0,
    )
    return de, sums


def head_masks(width):
    lane = lax.broadcasted_iota(jnp.int32, (1, width), 1)
    return [
        ((lane >= h * HEAD_DIM) & (lane < (h + 1) * HEAD_DIM)).astype(F32)
        for h in range(width // HEAD_DIM)
    ]


def stack_heads(rows, masks):
    return jnp.concatenate([rows * mask for mask in masks], axis=0).astype(BF)


def merge_heads(stacked, masks):
    count = stacked.shape[0] // len(masks)
    total = stacked[:count] * masks[0]
    for h in range(1, len(masks)):
        total = total + stacked[h * count : (h + 1) * count] * masks[h]
    return total


def item_forward(q, k, v, masks, length):
    scores = dot_nt(stack_heads(q, masks), k) * HEAD_DIM ** (-0.5)
    column = lax.broadcasted_iota(jnp.int32, scores.shape, 1)
    scores = jnp.where(column < length, scores, -1e30)
    weights = jnp.exp(scores - jnp.max(scores, axis=-1, keepdims=True))
    probs = (weights / jnp.sum(weights, axis=-1, keepdims=True)).astype(BF)
    return probs, merge_heads(dot_nn(probs, v), masks)


def item_backward(q, k, v, da, probs, masks):
    qs = stack_heads(q, masks)
    das = stack_heads(da, masks)
    dv = dot_tn(probs, das)
    dp = dot_nt(das, v)
    p = probs.astype(F32)
    ds = (p * (dp - jnp.sum(p * dp, axis=-1, keepdims=True))).astype(BF)
    scaling = HEAD_DIM ** (-0.5)
    dq = merge_heads(dot_nn(ds, k), masks) * scaling
    dk = dot_tn(ds, qs) * scaling
    return dq, dk, dv


def fetch_start(sources, target, sem):
    for r in range(len(sources)):
        pltpu.make_async_copy(sources[r], target.at[r], sem.at[r]).start()


def fetch_wait(sources, target, sem, r):
    pltpu.make_async_copy(sources[0], target.at[r], sem.at[r]).wait()


def ffn_forward_kernel(u, *refs):
    w1, w2 = refs[0:4], refs[4:8]
    c1, vec, y, e_out, h_out, slope_out, w1_s, w2_s, ub, acc, sem1, sem2 = refs[8:]
    step = pl.program_id(0)

    @pl.when(step == 0)
    def _():
        fetch_start(w1, w1_s, sem1)
        fetch_start(w2, w2_s, sem2)
        ub[...] = u[...].astype(BF)
        acc[...] = u[...] + vec[0:1, :]

    for j in range(2):
        r = 2 * step + j
        fetch_wait(w1, w1_s, sem1, r)
        z = dot_nn(ub[...], w1_s[r]) + c1[r]
        cdf = 0.5 * (1.0 + lax.erf(z * 0.7071067811865476))
        slope = cdf + z * (jnp.exp(-0.5 * z * z) * 0.3989422804014327)
        h = (z * cdf).astype(BF)
        h_out[j] = h
        slope_out[j] = slope.astype(BF)
        fetch_wait(w2, w2_s, sem2, r)
        acc[...] += dot_nn(h, w2_s[r])

    @pl.when(step == 1)
    def _():
        e = acc[...]
        e_out[...] = e
        y[...] = norm_forward(e, vec[1:2, :], vec[2:3, :]).astype(y.dtype)


def ffn_backward_kernel(has_grad, *refs):
    if has_grad:
        grad, refs = refs[0], refs[1:]
    cot, e_in, u = refs[0:3]
    w1, w2 = refs[3:7], refs[7:11]
    h_in, slope_in, vec = refs[11:14]
    du, g1k, g1s, g2k, g2s, dc1, sums = refs[14:21]
    w1_s, w2_s, ub, dob, acc, sem1, sem2 = refs[21:]
    step = pl.program_id(0)

    @pl.when(step == 0)
    def _():
        fetch_start(w2, w2_s, sem2)
        fetch_start(w1, w1_s, sem1)
        dy = cot[...].astype(F32)
        if has_grad:
            dy = dy + grad[...]
        de, partial = norm_backward(e_in[...], vec[1:2, :], dy)
        sums[...] = partial
        dob[...] = de.astype(BF)
        acc[...] = de
        ub[...] = u[...].astype(BF)

    for j in range(2):
        r = 2 * step + j
        fetch_wait(w2, w2_s, sem2, r)
        dh = dot_nt(dob[...], w2_s[r])
        dz = (dh * slope_in[j].astype(F32)).astype(BF)
        hidden, model = w2_s.shape[1:]
        (g2k if j == 0 else g2s)[0, 0:hidden] = dot_tn(h_in[j], dob[...]).astype(BF)
        (g1k if j == 0 else g1s)[0, 0:model] = dot_tn(ub[...], dz).astype(BF)
        dc1[0, j : j + 1, :] = jnp.sum(dz.astype(F32), axis=0, keepdims=True)
        fetch_wait(w1, w1_s, sem1, r)
        acc[...] += dot_nt(dz, w1_s[r])

    @pl.when(step == 1)
    def _():
        du[...] = acc[...]


def self_forward_kernel(items, lengths, x, *refs):
    w = refs[0:4]
    bias, vec, y, e_out, q_out, k_out, v_out, p_out, a_out = refs[4:13]
    w_s, acc, q_s, k_s, v_s, a_s, sem = refs[13:]
    step = pl.program_id(0)
    width = q_s.shape[1]
    slots = x.shape[0] // items

    @pl.when(step == 0)
    def _():
        fetch_start(w, w_s, sem)
        acc[...] = x[...].astype(F32) + vec[0:1, :]

    masks = head_masks(width)
    for j in range(2):
        r = 2 * step + j
        fetch_wait(w, w_s, sem, r)
        xb = x[...]
        q = (dot_nt(xb, w_s[r, 0:width]) + bias[r, 0:1]).astype(BF)
        k = dot_nt(xb, w_s[r, width : 2 * width]).astype(BF)
        v = (dot_nt(xb, w_s[r, 2 * width : 3 * width]) + bias[r, 1:2]).astype(BF)
        q_out[j], k_out[j], v_out[j] = q, k, v
        q_s[...], k_s[...], v_s[...] = q.astype(F32), k.astype(F32), v.astype(F32)
        for i in range(items):
            rows = pl.ds(i * slots, slots)
            probs, a = item_forward(
                q_s[rows], k_s[rows].astype(BF), v_s[rows].astype(BF), masks, lengths[i]
            )
            p_out[j, i] = probs
            a_s[rows] = a
        ab = a_s[...].astype(BF)
        a_out[j] = ab
        acc[...] += dot_nn(ab, w_s[r, 3 * width : 4 * width])

    @pl.when(step == 1)
    def _():
        e = acc[...]
        e_out[...] = e
        y[...] = norm_forward(e, vec[1:2, :], vec[2:3, :]).astype(y.dtype)


def self_backward_kernel(items, dy, e_in, x, *refs):
    w = refs[0:4]
    q_in, k_in, v_in, p_in, a_in, vec = refs[4:10]
    du, gk, gs, db, sums = refs[10:15]
    w_s, dob, acc, q_s, k_s, v_s, da_s, dq_s, dk_s, dv_s, sem = refs[15:]
    step = pl.program_id(0)
    width = q_s.shape[1]
    slots = x.shape[0] // items

    @pl.when(step == 0)
    def _():
        fetch_start(w, w_s, sem)
        de, partial = norm_backward(e_in[...], vec[1:2, :], dy[...])
        sums[...] = partial
        dob[...] = de.astype(BF)
        acc[...] = de

    masks = head_masks(width)
    for j in range(2):
        r = 2 * step + j
        g = gk if j == 0 else gs
        fetch_wait(w, w_s, sem, r)
        da_s[...] = dot_nt(dob[...], w_s[r, 3 * width : 4 * width])
        g[0, 3 * width : 4 * width] = dot_tn(a_in[j], dob[...]).astype(BF)
        q_s[...], k_s[...], v_s[...] = (
            q_in[j].astype(F32),
            k_in[j].astype(F32),
            v_in[j].astype(F32),
        )
        for i in range(items):
            rows = pl.ds(i * slots, slots)
            dq, dk, dv = item_backward(
                q_s[rows],
                k_s[rows].astype(BF),
                v_s[rows].astype(BF),
                da_s[rows],
                p_in[j, i],
                masks,
            )
            dq_s[rows], dk_s[rows], dv_s[rows] = dq, dk, dv
        xb = x[...]
        total = acc[...]
        for c, part in enumerate((dq_s, dk_s, dv_s)):
            pb = part[...].astype(BF)
            g[0, c * width : (c + 1) * width] = dot_tn(pb, xb).astype(BF)
            total = total + dot_nn(pb, w_s[r, c * width : (c + 1) * width])
            if c != 1:
                db[0, j, c // 2 : c // 2 + 1, :] = jnp.sum(
                    pb.astype(F32), axis=0, keepdims=True
                )
        acc[...] = total

    @pl.when(step == 1)
    def _():
        du[...] = acc[...].astype(du.dtype)


def key_value_weight(w_s, r, start, width, model):
    low = w_s[r, pl.ds(start, 2 * width)]
    tail = w_s[r, pl.ds(start + 2 * width, 2 * width * (1024 - model) // model)]
    side = 1024 - model
    high = jnp.concatenate(
        [tail[:, c * side : (c + 1) * side] for c in range(model // side)], axis=0
    )
    return low, high


def cross_forward_kernel(items, patches, u, pf, *refs):
    w = refs[0:4]
    bias, vec, y, e_out, q_out, k_out, v_out, p_out, a_out = refs[4:13]
    w_s, ub, acc, q_s, a_s, sem = refs[13:]
    step = pl.program_id(0)
    width = q_s.shape[1]
    model = u.shape[1]
    slots = u.shape[0] // items
    padded = pf.shape[0] // items

    @pl.when(step == 0)
    def _():
        fetch_start(w, w_s, sem)
        ub[...] = u[...].astype(BF)
        acc[...] = u[...] + vec[0:1, :]

    masks = head_masks(width)
    for j in range(2):
        r = 2 * step + j
        fetch_wait(w, w_s, sem, r)
        q_b = (dot_nt(ub[...], w_s[r, 0:width]) + bias[r, 0:1]).astype(BF)
        q_out[j] = q_b
        q_s[...] = q_b.astype(F32)
        low, high = key_value_weight(w_s, r, 2 * width, width, model)
        chunk = 2 * padded
        for m in range(items // 2):
            rows = slice(m * chunk, (m + 1) * chunk)
            left, right = pf[rows, 0:model], pf[rows, model:]
            k_out[j, rows] = (
                dot_nt(left, low[0:width]) + dot_nt(right, high[0:width])
            ).astype(BF)
            v_out[j, rows] = (
                dot_nt(left, low[width:]) + dot_nt(right, high[width:]) + bias[r, 1:2]
            ).astype(BF)
        for i in range(items):
            rows = pl.ds(i * slots, slots)
            keys = pl.ds(i * padded, padded)
            probs, a = item_forward(
                q_s[rows], k_out[j, keys], v_out[j, keys], masks, patches
            )
            p_out[j, i] = probs
            a_s[rows] = a
        ab = a_s[...].astype(BF)
        a_out[j] = ab
        acc[...] += dot_nn(ab, w_s[r, width : 2 * width])

    @pl.when(step == 1)
    def _():
        e = acc[...]
        e_out[...] = e
        y[...] = norm_forward(e, vec[1:2, :], vec[2:3, :]).astype(y.dtype)


def cross_backward_kernel(items, patches, dy, e_in, u, pf, *refs):
    w = refs[0:4]
    q_in, k_in, v_in, p_in, a_in, vec = refs[4:10]
    du, dpf, gk, gs, db, sums = refs[10:16]
    w_s, ub, dob, acc, pacc, q_s, da_s, dq_s, dkv_s, sem = refs[16:]
    step = pl.program_id(0)
    width = q_s.shape[1]
    model = u.shape[1]
    side = pf.shape[1] - model
    slots = u.shape[0] // items
    padded = pf.shape[0] // items

    @pl.when(step == 0)
    def _():
        fetch_start(w, w_s, sem)
        de, partial = norm_backward(e_in[...], vec[1:2, :], dy[...])
        sums[...] = partial
        dob[...] = de.astype(BF)
        acc[...] = de
        ub[...] = u[...].astype(BF)
        pacc[...] = jnp.zeros_like(pacc)

    masks = head_masks(width)
    for j in range(2):
        r = 2 * step + j
        g = gk if j == 0 else gs
        fetch_wait(w, w_s, sem, r)
        da_s[...] = dot_nt(dob[...], w_s[r, width : 2 * width])
        g[0, width : 2 * width] = dot_tn(a_in[j], dob[...]).astype(BF)
        q_s[...] = q_in[j].astype(F32)
        vsum = jnp.zeros((1, width), F32)
        for i in range(items):
            rows = pl.ds(i * slots, slots)
            keys = pl.ds(i * padded, padded)
            dq, dk, dv = item_backward(
                q_s[rows], k_in[j, keys], v_in[j, keys], da_s[rows], p_in[j, i], masks
            )
            dq_s[rows] = dq
            dkv_s[0, keys] = dk.astype(BF)
            dvb = dv.astype(BF)
            dkv_s[1, keys] = dvb
            vsum = vsum + jnp.sum(dvb.astype(F32), axis=0, keepdims=True)
        dqb = dq_s[...].astype(BF)
        g[0, 0:width] = dot_tn(dqb, ub[...]).astype(BF)
        acc[...] += dot_nn(dqb, w_s[r, 0:width])
        db[0, j, 0:1, :] = jnp.sum(dqb.astype(F32), axis=0, keepdims=True)
        db[0, j, 1:2, :] = vsum
        low, high = key_value_weight(w_s, r, 2 * width, width, model)
        tails = []
        for c in range(2):
            part = dkv_s[c]
            g[0, (2 + c) * width : (3 + c) * width] = dot_tn(part, pf[:, 0:model]).astype(BF)
            tails.append(dot_tn(part, pf[:, model:]).astype(BF))
            pacc[:, 0:model] += dot_nn(part, low[c * width : (c + 1) * width])
            pacc[:, model:] += dot_nn(part, high[c * width : (c + 1) * width])
        tail = jnp.concatenate(tails, axis=0)
        count = tail.shape[0] // (model // side)
        for c in range(model // side):
            g[0, 4 * width : 4 * width + count, c * side : (c + 1) * side] = tail[
                c * count : (c + 1) * count
            ]

    @pl.when(step == 1)
    def _():
        du[...] = acc[...]
        for i in range(items):
            dpf[i] = pacc[i * padded : i * padded + patches, :].astype(BF)


def whole(shape):
    zeros = (0,) * len(shape)
    return pl.BlockSpec(shape, lambda p: zeros)


def halves(shape):
    zeros = (0,) * (len(shape) - 1)
    return pl.BlockSpec((shape[0] // 2,) + tuple(shape[1:]), lambda p: (p,) + zeros)


def call(kernel, name, operands, outputs, scratch, flops, transcendentals=0):
    kinds = {
        "whole": lambda s: whole(s),
        "half": lambda s: halves(s),
        "any": lambda s: pl.BlockSpec(memory_space=ANY),
        "smem": lambda s: pl.BlockSpec(memory_space=pltpu.SMEM),
    }
    size = sum(a.size * a.dtype.itemsize for a, _ in operands)
    for shape, dtype, _ in outputs:
        count = jnp.dtype(dtype).itemsize
        for extent in shape:
            count *= extent
        size += count
    return pl.pallas_call(
        kernel,
        grid=(2,),
        in_specs=[kinds[kind](a.shape) for a, kind in operands],
        out_specs=[kinds[kind](shape) for shape, _, kind in outputs],
        out_shape=[jax.ShapeDtypeStruct(shape, dtype) for shape, dtype, _ in outputs],
        scratch_shapes=scratch,
        compiler_params=pltpu.CompilerParams(
            dimension_semantics=("arbitrary",), vmem_limit_bytes=VMEM_LIMIT
        ),
        cost_estimate=pl.CostEstimate(
            flops=flops, bytes_accessed=size, transcendentals=transcendentals
        ),
        name=name,
    )(*[a for a, _ in operands])


def feed_forward(u, w1, w2, c1, vec, name):
    rows, model = u.shape
    hidden = w1[0].shape[1]
    outs = call(
        ffn_forward_kernel,
        name,
        [(u, "whole")]
        + [(a, "any") for a in w1]
        + [(a, "any") for a in w2]
        + [(c1, "whole"), (vec, "whole")],
        [
            ((rows, model), BF, "whole"),
            ((rows, model), F32, "whole"),
            ((4, rows, hidden), BF, "half"),
            ((4, rows, hidden), BF, "half"),
        ],
        [
            pltpu.VMEM((4, model, hidden), BF),
            pltpu.VMEM((4, hidden, model), BF),
            pltpu.VMEM((rows, model), BF),
            pltpu.VMEM((rows, model), F32),
            pltpu.SemaphoreType.DMA((4,)),
            pltpu.SemaphoreType.DMA((4,)),
        ],
        16 * rows * model * hidden,
        8 * rows * hidden,
    )
    return outs[0], (u, outs[1], outs[2], outs[3])


def feed_backward(links, grad, cot, saved, w1, w2, vec, name):
    u, e, h, slope = saved
    rows, model = u.shape
    hidden = w1[0].shape[1]
    has_grad = grad is not None
    g = ((2, links.padded(model), hidden), BF, "half")
    g2 = ((2, links.padded(hidden), model), BF, "half")
    return call(
        functools.partial(ffn_backward_kernel, has_grad),
        name,
        ([(grad, "whole")] if has_grad else [])
        + [(cot, "whole"), (e, "whole"), (u, "whole")]
        + [(a, "any") for a in w1]
        + [(a, "any") for a in w2]
        + [(h, "half"), (slope, "half"), (vec, "whole")],
        [
            ((rows, model), F32, "whole"),
            g,
            g,
            g2,
            g2,
            ((2, 2, hidden), F32, "half"),
            ((3, model), F32, "whole"),
        ],
        [
            pltpu.VMEM((4, model, hidden), BF),
            pltpu.VMEM((4, hidden, model), BF),
            pltpu.VMEM((rows, model), BF),
            pltpu.VMEM((rows, model), BF),
            pltpu.VMEM((rows, model), F32),
            pltpu.SemaphoreType.DMA((4,)),
            pltpu.SemaphoreType.DMA((4,)),
        ],
        32 * rows * model * hidden,
    )


def self_forward(lengths, x, w, bias, vec, name):
    items = lengths.shape[0]
    rows, model = x.shape
    slots = rows // items
    width = w[0].shape[0] // 4
    heads = width // HEAD_DIM
    mid = ((4, rows, width), BF, "half")
    outs = call(
        functools.partial(self_forward_kernel, items),
        name,
        [(lengths, "smem"), (x, "whole")]
        + [(a, "any") for a in w]
        + [(bias, "whole"), (vec, "whole")],
        [
            ((rows, model), F32, "whole"),
            ((rows, model), F32, "whole"),
            mid,
            mid,
            mid,
            ((4, items, heads * slots, slots), BF, "half"),
            mid,
        ],
        [
            pltpu.VMEM((4,) + w[0].shape, BF),
            pltpu.VMEM((rows, model), F32),
            pltpu.VMEM((rows, width), F32),
            pltpu.VMEM((rows, width), F32),
            pltpu.VMEM((rows, width), F32),
            pltpu.VMEM((rows, width), F32),
            pltpu.SemaphoreType.DMA((4,)),
        ],
        32 * rows * model * width,
    )
    return outs[0], (x, outs[1], outs[2], outs[3], outs[4], outs[5], outs[6])


def self_backward(links, dy, saved, items, w, vec, dtype, name):
    x, e, q, k, v, p, a = saved
    rows, model = x.shape
    width = q.shape[2]
    g = ((2, links.padded(w[0].shape[0]), model), BF, "half")
    return call(
        functools.partial(self_backward_kernel, items),
        name,
        [(dy, "whole"), (e, "whole"), (x, "whole")]
        + [(m, "any") for m in w]
        + [(q, "half"), (k, "half"), (v, "half"), (p, "half"), (a, "half"), (vec, "whole")],
        [
            ((rows, model), dtype, "whole"),
            g,
            g,
            ((2, 2, 2, width), F32, "half"),
            ((3, model), F32, "whole"),
        ],
        [
            pltpu.VMEM((4,) + w[0].shape, BF),
            pltpu.VMEM((rows, model), BF),
            pltpu.VMEM((rows, model), F32),
        ]
        + [pltpu.VMEM((rows, width), F32)] * 7
        + [pltpu.SemaphoreType.DMA((4,))],
        64 * rows * model * width,
    )


def cross_forward(u, pf, patches, items, w, bias, vec, name):
    rows, model = u.shape
    slots, padded = rows // items, pf.shape[0] // items
    width = bias.shape[2]
    heads = width // HEAD_DIM
    mid = ((4, rows, width), BF, "half")
    key = ((4, pf.shape[0], width), BF, "half")
    outs = call(
        functools.partial(cross_forward_kernel, items, patches),
        name,
        [(u, "whole"), (pf, "whole")]
        + [(a, "any") for a in w]
        + [(bias, "whole"), (vec, "whole")],
        [
            ((rows, model), F32, "whole"),
            ((rows, model), F32, "whole"),
            mid,
            key,
            key,
            ((4, items, heads * slots, padded), BF, "half"),
            mid,
        ],
        [
            pltpu.VMEM((4,) + w[0].shape, BF),
            pltpu.VMEM((rows, model), BF),
            pltpu.VMEM((rows, model), F32),
            pltpu.VMEM((rows, width), F32),
            pltpu.VMEM((rows, width), F32),
            pltpu.SemaphoreType.DMA((4,)),
        ],
        16 * rows * model * width + 16 * pf.size * width,
    )
    return outs[0], (u, outs[1], outs[2], outs[3], outs[4], outs[5], outs[6])


def cross_backward(links, dy, saved, pf, patches, items, w, vec, name):
    u, e, q, k, v, p, a = saved
    rows, model = u.shape
    width = q.shape[2]
    g = ((2, links.padded(w[0].shape[0]), model), BF, "half")
    return call(
        functools.partial(cross_backward_kernel, items, patches),
        name,
        [(dy, "whole"), (e, "whole"), (u, "whole"), (pf, "whole")]
        + [(m, "any") for m in w]
        + [(q, "half"), (k, "half"), (v, "half"), (p, "half"), (a, "half"), (vec, "whole")],
        [
            ((rows, model), F32, "whole"),
            ((items, patches, pf.shape[1]), BF, "whole"),
            g,
            g,
            ((2, 2, 2, width), F32, "half"),
            ((3, model), F32, "whole"),
        ],
        [
            pltpu.VMEM((4,) + w[0].shape, BF),
            pltpu.VMEM((rows, model), BF),
            pltpu.VMEM((rows, model), BF),
            pltpu.VMEM((rows, model), F32),
            pltpu.VMEM(pf.shape, F32),
            pltpu.VMEM((rows, width), F32),
            pltpu.VMEM((rows, width), F32),
            pltpu.VMEM((rows, width), F32),
            pltpu.VMEM((2, pf.shape[0], width), BF),
            pltpu.SemaphoreType.DMA((4,)),
        ],
        32 * rows * model * width + 32 * pf.size * width,
    )


def pair(index, width):
    return index + width - 2 * width * ((index // width) % 2)


def add_rounded(a, b):
    return (a.astype(F32) + b.astype(F32)).astype(BF)


def reduce_kernel(n_tensor, n_dp, counts, chunk, *refs):
    arrays = len(counts)
    bits = n_dp.bit_length() - 1
    sends, keeps = refs[:arrays], refs[arrays : 2 * arrays]
    small_send, small_keep = refs[2 * arrays : 2 * arrays + 2]
    outs = refs[2 * arrays + 2 : 3 * arrays + 2]
    small_out = refs[3 * arrays + 2]
    rest = list(refs[3 * arrays + 3 :])
    core_in, kept, far_out, far_in, own, whole_sum = rest[:6]
    parts, halves_in = rest[6 : 6 + bits], rest[6 + bits : 6 + 2 * bits]
    gathered, tiny_sum, tiny_core, tiny_far, tiny_dp = rest[6 + 2 * bits : 11 + 2 * bits]
    send_sem, recv_sem, kept_sem, out_sem, tiny_send, tiny_recv = rest[11 + 2 * bits :]

    t, d = lax.axis_index("tensor"), lax.axis_index("dp")
    core_peer = {"tensor": pair(t, 1)}
    far_peer = {"tensor": lax.rem(t + 2, n_tensor)}
    dp_peers = [{"dp": pair(d, 1 << b)} for b in range(bits)]
    dp_bits = [(d // (1 << b)) % 2 for b in range(bits)]
    peers = [core_peer, far_peer] + dp_peers

    barrier = pltpu.get_barrier_semaphore()
    for peer in peers:
        pl.semaphore_signal(
            barrier, inc=1, device_id=peer, device_id_type=pl.DeviceIdType.MESH
        )
    pl.semaphore_wait(barrier, len(peers))

    total = sum(counts)
    stages = 2 + 2 * bits
    slots = core_in.shape[0]
    depth = gathered.shape[0]

    def remote(source, target, stage, slot, peer):
        return pltpu.make_async_remote_copy(
            src_ref=source,
            dst_ref=target,
            send_sem=send_sem.at[stage, slot],
            recv_sem=recv_sem.at[stage, slot],
            device_id=peer,
            device_id_type=pl.DeviceIdType.MESH,
        )

    def region(b):
        size = chunk >> (b + 1)
        start = 0
        for i in range(b + 1):
            start = start + dp_bits[i] * (chunk >> (i + 1))
        return pl.ds(pl.multiple_of(start, size), size)

    def copy_of(stage, m):
        slot, ring = lax.rem(m, slots), lax.rem(m, depth)
        if stage == 0:
            return remote(
                sends[0].at[:, pl.ds(0, chunk)], core_in.at[slot], 0, slot, core_peer
            )
        if stage == 1:
            return remote(far_out.at[slot], far_in.at[slot], 1, slot, far_peer)
        if stage < 2 + bits:
            b = stage - 2
            size = chunk >> (b + 1)
            source = whole_sum if b == 0 else parts[b - 1]
            gone = pl.ds(pl.multiple_of((1 - dp_bits[b]) * size, size), size)
            return remote(
                source.at[slot, gone], halves_in[b].at[slot], stage, slot, dp_peers[b]
            )
        b = 2 * bits + 1 - stage
        held = gathered.at[ring, region(b)]
        return remote(held, held, stage, slot, dp_peers[b])

    def kept_copy(a, m, base):
        slot = lax.rem(m, slots)
        rows = pl.ds(pl.multiple_of((m - base) * chunk, chunk), chunk)
        return pltpu.make_async_copy(keeps[a].at[:, rows], kept.at[slot], kept_sem.at[slot])

    def out_copy(a, m, base):
        ring = lax.rem(m, depth)
        rows = pl.ds(pl.multiple_of((m - base) * chunk, chunk), chunk)
        return pltpu.make_async_copy(gathered.at[ring], outs[a].at[rows], out_sem.at[ring])

    def each_array(m, act):
        base = 0
        for a in range(arrays):

            @pl.when((m >= base) & (m < base + counts[a]))
            def _(a=a, base=base):
                act(a, base)

            base += counts[a]

    def process(stage, m):
        slot, ring = lax.rem(m, slots), lax.rem(m, depth)
        if stage == 0:

            def begin(a, base):
                rows = pl.ds(pl.multiple_of((m - base) * chunk, chunk), chunk)
                remote(
                    sends[a].at[:, rows], core_in.at[slot], 0, slot, core_peer
                ).start()
                kept_copy(a, m, base).start()

            each_array(m, begin)
            return
        if stage <= stages:
            copy_of(stage - 1, m).wait()
        if stage == 1:
            kept_copy(0, m, m).wait()
            far_out[slot] = add_rounded(kept[slot, 1], core_in[slot, 1])
            own[slot] = add_rounded(kept[slot, 0], core_in[slot, 0])
        elif stage == 2:
            whole_sum[slot] = add_rounded(own[slot], far_in[slot])
        elif stage <= 2 + bits:
            b = stage - 3
            size = chunk >> (b + 1)
            source = whole_sum if b == 0 else parts[b - 1]
            mine = pl.ds(pl.multiple_of(dp_bits[b] * size, size), size)
            summed = add_rounded(source[slot, mine], halves_in[b][slot])
            if b < bits - 1:
                parts[b][slot] = summed
            else:
                gathered[ring, region(b)] = summed
        elif stage == stages:
            each_array(m, lambda a, base: out_copy(a, m, base).start())
        elif stage == stages + 1:
            out_copy(0, m, m).wait()
        if stage < stages:
            copy_of(stage, m).start()

    units = small_keep.shape[0] - tiny_far.shape[0]

    def tiny(stage):
        if stage == 0:
            source, target = small_send, tiny_core
        elif stage == 1:
            source, target = tiny_sum.at[0, pl.ds(units, tiny_far.shape[0])], tiny_far
        else:
            source = tiny_sum.at[stage - 1, pl.ds(0, tiny_far.shape[0])]
            target = tiny_dp.at[stage - 2]
        return pltpu.make_async_remote_copy(
            src_ref=source,
            dst_ref=target,
            send_sem=tiny_send.at[stage],
            recv_sem=tiny_recv.at[stage],
            device_id=peers[stage],
            device_id_type=pl.DeviceIdType.MESH,
        )

    def tiny_step(stage):
        if stage > 0:
            tiny(stage - 1).wait()
        count = tiny_far.shape[0]
        if stage == 1:
            tiny_sum[0] = small_keep[...] + tiny_core[...]
        elif stage == 2:
            tiny_sum[1, 0:units] = tiny_sum[0, 0:units] + tiny_far[0:units]
            tiny_sum[1, units:count] = tiny_sum[0, 2 * units :] + tiny_far[units:]
        elif stage > 2:
            summed = tiny_sum[stage - 2, 0:count] + tiny_dp[stage - 3]
            if stage == 2 + bits:
                small_out[...] = summed
            else:
                tiny_sum[stage - 1, 0:count] = summed
        if stage < 2 + bits:
            tiny(stage).start()

    def tick(k, carry):
        for stage in range(stages + 2):
            m = k - stage

            @pl.when((m >= 0) & (m < total))
            def _(stage=stage, m=m):
                process(stage, m)

        for stage in range(3 + bits):

            @pl.when(k == stage)
            def _(stage=stage):
                tiny_step(stage)

        return carry

    lax.fori_loop(0, total + stages + 2, tick, 0)


def reduce_all(links, pairs, small_keep, small_send, units):
    chunk = links.chunk
    model = pairs[0][0].shape[2]
    bits = links.bits
    counts = [keep.shape[1] // chunk for keep, _ in pairs]
    sends = [send for _, send in pairs]
    keeps = [keep for keep, _ in pairs]
    slots, depth = 4, 8
    anywhere = pl.BlockSpec(memory_space=ANY)
    vmem = pl.BlockSpec(memory_space=pltpu.VMEM)
    rows = small_keep.shape[0]
    stages = 2 + 2 * bits
    outs = pl.pallas_call(
        functools.partial(reduce_kernel, links.tensor, links.dp, counts, chunk),
        in_specs=[anywhere] * (2 * len(pairs)) + [vmem] * 2,
        out_specs=[anywhere] * len(pairs) + [vmem],
        out_shape=[jax.ShapeDtypeStruct(keep.shape[1:], BF) for keep in keeps]
        + [jax.ShapeDtypeStruct((rows - units, 128), F32)],
        scratch_shapes=[
            pltpu.VMEM((slots, 2, chunk, model), BF),
            pltpu.VMEM((slots, 2, chunk, model), BF),
            pltpu.VMEM((slots, chunk, model), BF),
            pltpu.VMEM((slots, chunk, model), BF),
            pltpu.VMEM((slots, chunk, model), BF),
            pltpu.VMEM((slots, chunk, model), BF),
        ]
        + [pltpu.VMEM((slots, chunk >> (b + 1), model), BF) for b in range(bits)]
        + [pltpu.VMEM((slots, chunk >> (b + 1), model), BF) for b in range(bits)]
        + [
            pltpu.VMEM((depth, chunk, model), BF),
            pltpu.VMEM((1 + bits, rows, 128), F32),
            pltpu.VMEM((rows, 128), F32),
            pltpu.VMEM((rows - units, 128), F32),
            pltpu.VMEM((bits, rows - units, 128), F32),
            pltpu.SemaphoreType.DMA((stages, slots)),
            pltpu.SemaphoreType.DMA((stages, slots)),
            pltpu.SemaphoreType.DMA((slots,)),
            pltpu.SemaphoreType.DMA((depth,)),
            pltpu.SemaphoreType.DMA((2 + bits,)),
            pltpu.SemaphoreType.DMA((2 + bits,)),
        ],
        compiler_params=pltpu.CompilerParams(
            collective_id=0, has_side_effects=True, vmem_limit_bytes=VMEM_LIMIT
        ),
        name="reduce_gradients",
    )(*sends, *keeps, small_send, small_keep)
    return outs[:-1], outs[-1]


def swap(array, axis, size, distance):
    return lax.ppermute(array, axis, [(i, i ^ distance) for i in range(size)])


class Links:
    def __init__(self, mesh):
        self.tensor = mesh.shape["tensor"]
        self.dp = mesh.shape["dp"]
        self.bits = self.dp.bit_length() - 1
        self.chunk = max(256, 16 * self.dp)

    def padded(self, rows):
        return -(-rows // self.chunk) * self.chunk

    def core(self, array):
        return swap(array, "tensor", self.tensor, 1)

    def far(self, array):
        return swap(array, "tensor", self.tensor, 2)

    def gather(self, own):
        across = self.far(own)
        return own, self.core(own), across, self.core(across)


def flat(array):
    return array.reshape(-1)


def lines(array):
    n, values = array.shape
    rows = -(-values // 1024) * 8
    return jnp.pad(array, ((0, 0), (0, rows * 128 - values))).reshape(n, rows, 128)


def self_pack(w_in, w_out):
    turned = jnp.swapaxes(w_in, 1, 2)
    return jnp.concatenate([turned.reshape(-1, w_in.shape[1]), w_out], axis=0)


def self_unpack(total, width):
    model = total.shape[1]
    first = jnp.swapaxes(total[: 3 * width].reshape(3, width, model), 1, 2)
    return first, total[3 * width : 4 * width]


def cross_pack(w_query, w_out, w_keyval):
    model = w_query.shape[0]
    keyval = jnp.swapaxes(w_keyval, 1, 2).reshape(-1, w_keyval.shape[1])
    side = w_keyval.shape[1] - model
    parts = model // side
    count = keyval.shape[0] // parts
    tail = keyval[:, model:].reshape(parts, count, side)
    tail = jnp.swapaxes(tail, 0, 1).reshape(count, model)
    return jnp.concatenate([w_query.T, w_out, keyval[:, :model], tail], axis=0)


def cross_unpack(total, width, patch_width):
    model = total.shape[1]
    side = patch_width - model
    parts = model // side
    tail = total[4 * width : 4 * width + 2 * width // parts]
    tail = jnp.swapaxes(tail.reshape(-1, parts, side), 0, 1).reshape(2 * width, side)
    keyval = jnp.concatenate([total[2 * width : 4 * width], tail], axis=1)
    keyval = jnp.swapaxes(keyval.reshape(2, width, patch_width), 1, 2)
    return total[:width].T, total[width : 2 * width], keyval


def per_device(
    links,
    text_rows,
    patch_features,
    lengths,
    text_cotangent,
    join_cotangent,
    text_project_in,
    text_project_bias,
    text_project_out,
    text_expand,
    text_expand_bias,
    text_contract,
    text_out_bias,
    text_norm_gain,
    text_norm_shift,
    join_project_in,
    join_project_bias,
    join_project_out,
    cross_project_out,
    cross_key_value,
    join_expand,
    join_expand_bias,
    join_contract,
    join_out_bias,
    join_norm_gain,
    join_norm_shift,
):
    items, slots, model = text_rows.shape
    patches, patch_width = patch_features.shape[1:]
    width = text_project_in.shape[2]
    hidden = text_expand.shape[1]

    biases = jnp.concatenate(
        [
            flat(text_project_bias),
            flat(join_project_bias),
            text_expand_bias,
            join_expand_bias,
        ]
    )[None]
    weights_one = links.gather(self_pack(text_project_in, text_project_out))
    biases = jnp.concatenate(links.gather(biases), axis=0).astype(F32)
    expand_one = links.gather(text_expand)
    contract_one = links.gather(text_contract)
    weights_two = links.gather(self_pack(join_project_in[0:3], join_project_out))
    weights_cross = links.gather(
        cross_pack(join_project_in[3], cross_project_out, cross_key_value)
    )
    expand_two = links.gather(join_expand)
    contract_two = links.gather(join_contract)

    bias_one = biases[:, : 2 * width].reshape(4, 2, width)
    bias_two = biases[:, 2 * width : 4 * width].reshape(4, 2, width)
    bias_cross = biases[:, 4 * width : 6 * width].reshape(4, 2, width)
    hidden_one = biases[:, 6 * width : 6 * width + hidden].reshape(4, 1, hidden)
    hidden_two = biases[:, 6 * width + hidden :].reshape(4, 1, hidden)

    def vec(bias, gain, shift, n):
        return jnp.stack([bias[n], gain[n], shift[n]]).astype(F32)

    text_vecs = [vec(text_out_bias, text_norm_gain, text_norm_shift, n) for n in range(2)]
    join_vecs = [vec(join_out_bias, join_norm_gain, join_norm_shift, n) for n in range(3)]

    padded = -(-patches // 16) * 16
    pf = jnp.pad(patch_features, ((0, 0), (0, padded - patches), (0, 0)))
    pf = pf.reshape(items * padded, patch_width)
    x = text_rows.reshape(items * slots, model)
    text_cot = text_cotangent.reshape(items * slots, model)
    join_cot = join_cotangent.reshape(items * slots, model)

    h1, saved_one = self_forward(lengths, x, weights_one, bias_one, text_vecs[0], "text_self_forward")
    text_out, saved_two = feed_forward(
        h1, expand_one, contract_one, hidden_one, text_vecs[1], "text_feed_forward"
    )
    h2, saved_three = self_forward(
        lengths, text_out, weights_two, bias_two, join_vecs[0], "join_self_forward"
    )
    h3, saved_four = cross_forward(
        h2, pf, patches, items, weights_cross, bias_cross, join_vecs[1], "cross_forward"
    )
    join_out, saved_five = feed_forward(
        h3, expand_two, contract_two, hidden_two, join_vecs[2], "join_feed_forward"
    )

    du, e2k, e2s, k2k, k2s, dc_two, sums_five = feed_backward(
        links, None, join_cot, saved_five, expand_two, contract_two, join_vecs[2], "join_feed_backward"
    )
    du, grad_patches, ck, cs, db_cross, sums_four = cross_backward(
        links, du, saved_four, pf, patches, items, weights_cross, join_vecs[1], "cross_backward"
    )
    du, s2k, s2s, db_two, sums_three = self_backward(
        links, du, saved_three, items, weights_two, join_vecs[0], F32, "join_self_backward"
    )
    du, e1k, e1s, k1k, k1s, dc_one, sums_two = feed_backward(
        links, du, text_cot, saved_two, expand_one, contract_one, text_vecs[1], "text_feed_backward"
    )
    grad_text, s1k, s1s, db_one, sums_one = self_backward(
        links, du, saved_one, items, weights_one, text_vecs[0], BF, "text_self_backward"
    )

    blocks = jnp.concatenate(
        [
            db_one.reshape(4, -1),
            db_two.reshape(4, -1),
            db_cross.reshape(4, -1),
            dc_one.reshape(4, -1),
            dc_two.reshape(4, -1),
        ],
        axis=1,
    )
    shared = flat(jnp.stack([sums_one, sums_two, sums_three, sums_four, sums_five]))
    units, count = blocks.shape[1], shared.shape[0]
    blocks = lines(blocks)
    shared = lines(shared[None])[0]
    small_keep = jnp.concatenate([blocks[0], blocks[2], shared], axis=0)
    small_send = jnp.concatenate([blocks[1], blocks[3], shared], axis=0)
    pairs = [(k2k, k2s), (e2k, e2s), (ck, cs), (s2k, s2s), (k1k, k1s), (e1k, e1s), (s1k, s1s)]
    totals, small = reduce_all(links, pairs, small_keep, small_send, blocks.shape[1])
    totals = [total.astype(F32) for total in totals]
    grad_join_contract, grad_join_expand = totals[0][:hidden], totals[1][:model]
    grad_query, grad_cross_out, grad_keyval = cross_unpack(totals[2], width, patch_width)
    grad_join_in, grad_join_out = self_unpack(totals[3], width)
    grad_text_contract, grad_text_expand = totals[4][:hidden], totals[5][:model]
    grad_text_in, grad_text_out = self_unpack(totals[6], width)
    shared = flat(small[blocks.shape[1] :])[:count].reshape(5, 3, model)
    small = flat(small[: blocks.shape[1]])[:units]
    attend = small[: 6 * width].reshape(6, width)
    text_shared, join_shared = shared[0:2], shared[2:5]

    return (
        text_out.reshape(text_rows.shape),
        join_out.reshape(text_rows.shape),
        grad_text.reshape(text_rows.shape),
        grad_patches,
        grad_text_in,
        attend[0:2],
        grad_text_out,
        grad_text_expand,
        small[6 * width : 6 * width + hidden],
        grad_text_contract,
        text_shared[:, 0],
        text_shared[:, 1],
        text_shared[:, 2],
        jnp.concatenate([grad_join_in, grad_query[None]], axis=0),
        attend[2:6],
        grad_join_out,
        grad_cross_out,
        grad_keyval,
        grad_join_expand,
        small[6 * width + hidden : 6 * width + 2 * hidden],
        grad_join_contract,
        join_shared[:, 0],
        join_shared[:, 1],
        join_shared[:, 2],
    )


def solution(mesh):
    rows = P(("dp", "tensor"), None, None)
    last = P(None, None, "tensor")
    second = P(None, "tensor")
    first = P("tensor", None)
    line = P("tensor")
    full = P()
    in_specs = (
        (rows, rows, P(("dp", "tensor")), rows, rows)
        + (last, second, first, second, line, first, full, full, full)
        + (last, second, first, first, last, second, line, first, full, full, full)
    )
    out_specs = (
        (rows, rows, rows, rows)
        + (last, second, first, second, line, first, full, full, full)
        + (last, second, first, first, last, second, line, first, full, full, full)
    )
    return jax.shard_map(
        functools.partial(per_device, Links(mesh)),
        mesh=mesh,
        in_specs=in_specs,
        out_specs=out_specs,
        check_vma=False,
    )
```

```python
import functools

import jax
import jax.numpy as jnp
from jax import lax
from jax.experimental import pallas as pl
from jax.experimental.pallas import tpu as pltpu
from jax.sharding import PartitionSpec as P

HEAD_DIM = 64
BF = jnp.bfloat16
F32 = jnp.float32
ANY = pl.ANY
VMEM_LIMIT = 56 * 1024 * 1024


def dot_nn(a, b):
    return lax.dot_general(a, b, (((1,), (0,)), ((), ())), preferred_element_type=F32)


def dot_nt(a, b):
    return lax.dot_general(a, b, (((1,), (1,)), ((), ())), preferred_element_type=F32)


def dot_tn(a, b):
    return lax.dot_general(a, b, (((0,), (0,)), ((), ())), preferred_element_type=F32)


def norm_forward(e, gain, shift):
    center = e - jnp.mean(e, axis=-1, keepdims=True)
    variance = jnp.mean(center * center, axis=-1, keepdims=True)
    return center * lax.rsqrt(variance + 1e-12) * gain + shift


def norm_backward(e, gain, dy):
    center = e - jnp.mean(e, axis=-1, keepdims=True)
    variance = jnp.mean(center * center, axis=-1, keepdims=True)
    rstd = lax.rsqrt(variance + 1e-12)
    normed = center * rstd
    scaled = dy * gain
    de = rstd * (
        scaled
        - jnp.mean(scaled, axis=-1, keepdims=True)
        - normed * jnp.mean(scaled * normed, axis=-1, keepdims=True)
    )
    sums = jnp.concatenate(
        [
            jnp.sum(de, axis=0, keepdims=True),
            jnp.sum(dy * normed, axis=0, keepdims=True),
            jnp.sum(dy, axis=0, keepdims=True),
        ],
        axis=0,
    )
    return de, sums


def head_masks(width):
    lane = lax.broadcasted_iota(jnp.int32, (1, width), 1)
    return [
        ((lane >= h * HEAD_DIM) & (lane < (h + 1) * HEAD_DIM)).astype(F32)
        for h in range(width // HEAD_DIM)
    ]


def stack_heads(rows, masks):
    return jnp.concatenate([rows * mask for mask in masks], axis=0).astype(BF)


def merge_heads(stacked, masks):
    count = stacked.shape[0] // len(masks)
    total = stacked[:count] * masks[0]
    for h in range(1, len(masks)):
        total = total + stacked[h * count : (h + 1) * count] * masks[h]
    return total


def item_forward(q, k, v, masks, length):
    scores = dot_nt(stack_heads(q, masks), k) * HEAD_DIM ** (-0.5)
    column = lax.broadcasted_iota(jnp.int32, scores.shape, 1)
    scores = jnp.where(column < length, scores, -1e30)
    weights = jnp.exp(scores - jnp.max(scores, axis=-1, keepdims=True))
    probs = (weights / jnp.sum(weights, axis=-1, keepdims=True)).astype(BF)
    return probs, merge_heads(dot_nn(probs, v), masks)


def item_backward(q, k, v, da, probs, masks):
    qs = stack_heads(q, masks)
    das = stack_heads(da, masks)
    dv = dot_tn(probs, das)
    dp = dot_nt(das, v)
    p = probs.astype(F32)
    ds = (p * (dp - jnp.sum(p * dp, axis=-1, keepdims=True))).astype(BF)
    scaling = HEAD_DIM ** (-0.5)
    dq = merge_heads(dot_nn(ds, k), masks) * scaling
    dk = dot_tn(ds, qs) * scaling
    return dq, dk, dv


def fetch_start(sources, target, sem):
    for r in range(len(sources)):
        pltpu.make_async_copy(sources[r], target.at[r], sem.at[r]).start()


def fetch_wait(sources, target, sem, r):
    pltpu.make_async_copy(sources[0], target.at[r], sem.at[r]).wait()


def ffn_forward_kernel(u, *refs):
    w1, w2 = refs[0:4], refs[4:8]
    c1, vec, y, e_out, h_out, slope_out, w1_s, w2_s, ub, acc, sem1, sem2 = refs[8:]
    step = pl.program_id(0)

    @pl.when(step == 0)
    def _():
        fetch_start(w1, w1_s, sem1)
        fetch_start(w2, w2_s, sem2)
        ub[...] = u[...].astype(BF)
        acc[...] = u[...] + vec[0:1, :]

    for j in range(2):
        r = 2 * step + j
        fetch_wait(w1, w1_s, sem1, r)
        z = dot_nn(ub[...], w1_s[r]) + c1[r]
        cdf = 0.5 * (1.0 + lax.erf(z * 0.7071067811865476))
        slope = cdf + z * (jnp.exp(-0.5 * z * z) * 0.3989422804014327)
        h = (z * cdf).astype(BF)
        h_out[j] = h
        slope_out[j] = slope.astype(BF)
        fetch_wait(w2, w2_s, sem2, r)
        acc[...] += dot_nn(h, w2_s[r])

    @pl.when(step == 1)
    def _():
        e = acc[...]
        e_out[...] = e
        y[...] = norm_forward(e, vec[1:2, :], vec[2:3, :]).astype(y.dtype)


def ffn_backward_kernel(has_grad, *refs):
    if has_grad:
        grad, refs = refs[0], refs[1:]
    cot, e_in, u = refs[0:3]
    w1, w2 = refs[3:7], refs[7:11]
    h_in, slope_in, vec = refs[11:14]
    du, g1k, g1s, g2k, g2s, dc1, sums = refs[14:21]
    w1_s, w2_s, ub, dob, acc, sem1, sem2 = refs[21:]
    step = pl.program_id(0)

    @pl.when(step == 0)
    def _():
        fetch_start(w2, w2_s, sem2)
        fetch_start(w1, w1_s, sem1)
        dy = cot[...].astype(F32)
        if has_grad:
            dy = dy + grad[...]
        de, partial = norm_backward(e_in[...], vec[1:2, :], dy)
        sums[...] = partial
        dob[...] = de.astype(BF)
        acc[...] = de
        ub[...] = u[...].astype(BF)

    for j in range(2):
        r = 2 * step + j
        fetch_wait(w2, w2_s, sem2, r)
        dh = dot_nt(dob[...], w2_s[r])
        dz = (dh * slope_in[j].astype(F32)).astype(BF)
        hidden, model = w2_s.shape[1:]
        (g2k if j == 0 else g2s)[0, 0:hidden] = dot_tn(h_in[j], dob[...]).astype(BF)
        (g1k if j == 0 else g1s)[0, 0:model] = dot_tn(ub[...], dz).astype(BF)
        dc1[0, j : j + 1, :] = jnp.sum(dz.astype(F32), axis=0, keepdims=True)
        fetch_wait(w1, w1_s, sem1, r)
        acc[...] += dot_nt(dz, w1_s[r])

    @pl.when(step == 1)
    def _():
        du[...] = acc[...]


def self_forward_kernel(items, lengths, x, *refs):
    w = refs[0:4]
    bias, vec, y, e_out, q_out, k_out, v_out, p_out, a_out = refs[4:13]
    w_s, acc, q_s, k_s, v_s, a_s, sem = refs[13:]
    step = pl.program_id(0)
    width = q_s.shape[1]
    slots = x.shape[0] // items

    @pl.when(step == 0)
    def _():
        fetch_start(w, w_s, sem)
        acc[...] = x[...].astype(F32) + vec[0:1, :]

    masks = head_masks(width)
    for j in range(2):
        r = 2 * step + j
        fetch_wait(w, w_s, sem, r)
        xb = x[...]
        q = (dot_nt(xb, w_s[r, 0:width]) + bias[r, 0:1]).astype(BF)
        k = dot_nt(xb, w_s[r, width : 2 * width]).astype(BF)
        v = (dot_nt(xb, w_s[r, 2 * width : 3 * width]) + bias[r, 1:2]).astype(BF)
        q_out[j], k_out[j], v_out[j] = q, k, v
        q_s[...], k_s[...], v_s[...] = q.astype(F32), k.astype(F32), v.astype(F32)
        for i in range(items):
            rows = pl.ds(i * slots, slots)
            probs, a = item_forward(
                q_s[rows], k_s[rows].astype(BF), v_s[rows].astype(BF), masks, lengths[i]
            )
            p_out[j, i] = probs
            a_s[rows] = a
        ab = a_s[...].astype(BF)
        a_out[j] = ab
        acc[...] += dot_nn(ab, w_s[r, 3 * width : 4 * width])

    @pl.when(step == 1)
    def _():
        e = acc[...]
        e_out[...] = e
        y[...] = norm_forward(e, vec[1:2, :], vec[2:3, :]).astype(y.dtype)


def self_backward_kernel(items, dy, e_in, x, *refs):
    w = refs[0:4]
    q_in, k_in, v_in, p_in, a_in, vec = refs[4:10]
    du, gk, gs, db, sums = refs[10:15]
    w_s, dob, acc, q_s, k_s, v_s, da_s, dq_s, dk_s, dv_s, sem = refs[15:]
    step = pl.program_id(0)
    width = q_s.shape[1]
    slots = x.shape[0] // items

    @pl.when(step == 0)
    def _():
        fetch_start(w, w_s, sem)
        de, partial = norm_backward(e_in[...], vec[1:2, :], dy[...])
        sums[...] = partial
        dob[...] = de.astype(BF)
        acc[...] = de

    masks = head_masks(width)
    for j in range(2):
        r = 2 * step + j
        g = gk if j == 0 else gs
        fetch_wait(w, w_s, sem, r)
        da_s[...] = dot_nt(dob[...], w_s[r, 3 * width : 4 * width])
        g[0, 3 * width : 4 * width] = dot_tn(a_in[j], dob[...]).astype(BF)
        q_s[...], k_s[...], v_s[...] = (
            q_in[j].astype(F32),
            k_in[j].astype(F32),
            v_in[j].astype(F32),
        )
        for i in range(items):
            rows = pl.ds(i * slots, slots)
            dq, dk, dv = item_backward(
                q_s[rows],
                k_s[rows].astype(BF),
                v_s[rows].astype(BF),
                da_s[rows],
                p_in[j, i],
                masks,
            )
            dq_s[rows], dk_s[rows], dv_s[rows] = dq, dk, dv
        xb = x[...]
        total = acc[...]
        for c, part in enumerate((dq_s, dk_s, dv_s)):
            pb = part[...].astype(BF)
            g[0, c * width : (c + 1) * width] = dot_tn(pb, xb).astype(BF)
            total = total + dot_nn(pb, w_s[r, c * width : (c + 1) * width])
            if c != 1:
                db[0, j, c // 2 : c // 2 + 1, :] = jnp.sum(
                    pb.astype(F32), axis=0, keepdims=True
                )
        acc[...] = total

    @pl.when(step == 1)
    def _():
        du[...] = acc[...].astype(du.dtype)


def key_value_weight(w_s, r, start, width, model):
    low = w_s[r, pl.ds(start, 2 * width)]
    tail = w_s[r, pl.ds(start + 2 * width, 2 * width * (1024 - model) // model)]
    side = 1024 - model
    high = jnp.concatenate(
        [tail[:, c * side : (c + 1) * side] for c in range(model // side)], axis=0
    )
    return low, high


def cross_forward_kernel(items, patches, u, pf, *refs):
    w = refs[0:4]
    bias, vec, y, e_out, q_out, k_out, v_out, p_out, a_out = refs[4:13]
    w_s, ub, acc, q_s, a_s, sem = refs[13:]
    step = pl.program_id(0)
    width = q_s.shape[1]
    model = u.shape[1]
    slots = u.shape[0] // items
    padded = pf.shape[0] // items

    @pl.when(step == 0)
    def _():
        fetch_start(w, w_s, sem)
        ub[...] = u[...].astype(BF)
        acc[...] = u[...] + vec[0:1, :]

    masks = head_masks(width)
    for j in range(2):
        r = 2 * step + j
        fetch_wait(w, w_s, sem, r)
        q_b = (dot_nt(ub[...], w_s[r, 0:width]) + bias[r, 0:1]).astype(BF)
        q_out[j] = q_b
        q_s[...] = q_b.astype(F32)
        low, high = key_value_weight(w_s, r, 2 * width, width, model)
        chunk = 2 * padded
        for m in range(items // 2):
            rows = slice(m * chunk, (m + 1) * chunk)
            left, right = pf[rows, 0:model], pf[rows, model:]
            k_out[j, rows] = (
                dot_nt(left, low[0:width]) + dot_nt(right, high[0:width])
            ).astype(BF)
            v_out[j, rows] = (
                dot_nt(left, low[width:]) + dot_nt(right, high[width:]) + bias[r, 1:2]
            ).astype(BF)
        for i in range(items):
            rows = pl.ds(i * slots, slots)
            keys = pl.ds(i * padded, padded)
            probs, a = item_forward(
                q_s[rows], k_out[j, keys], v_out[j, keys], masks, patches
            )
            p_out[j, i] = probs
            a_s[rows] = a
        ab = a_s[...].astype(BF)
        a_out[j] = ab
        acc[...] += dot_nn(ab, w_s[r, width : 2 * width])

    @pl.when(step == 1)
    def _():
        e = acc[...]
        e_out[...] = e
        y[...] = norm_forward(e, vec[1:2, :], vec[2:3, :]).astype(y.dtype)


def cross_backward_kernel(items, patches, dy, e_in, u, pf, *refs):
    w = refs[0:4]
    q_in, k_in, v_in, p_in, a_in, vec = refs[4:10]
    du, dpf, gk, gs, db, sums = refs[10:16]
    w_s, ub, dob, acc, pacc, q_s, da_s, dq_s, dkv_s, sem = refs[16:]
    step = pl.program_id(0)
    width = q_s.shape[1]
    model = u.shape[1]
    side = pf.shape[1] - model
    slots = u.shape[0] // items
    padded = pf.shape[0] // items

    @pl.when(step == 0)
    def _():
        fetch_start(w, w_s, sem)
        de, partial = norm_backward(e_in[...], vec[1:2, :], dy[...])
        sums[...] = partial
        dob[...] = de.astype(BF)
        acc[...] = de
        ub[...] = u[...].astype(BF)
        pacc[...] = jnp.zeros_like(pacc)

    masks = head_masks(width)
    for j in range(2):
        r = 2 * step + j
        g = gk if j == 0 else gs
        fetch_wait(w, w_s, sem, r)
        da_s[...] = dot_nt(dob[...], w_s[r, width : 2 * width])
        g[0, width : 2 * width] = dot_tn(a_in[j], dob[...]).astype(BF)
        q_s[...] = q_in[j].astype(F32)
        vsum = jnp.zeros((1, width), F32)
        for i in range(items):
            rows = pl.ds(i * slots, slots)
            keys = pl.ds(i * padded, padded)
            dq, dk, dv = item_backward(
                q_s[rows], k_in[j, keys], v_in[j, keys], da_s[rows], p_in[j, i], masks
            )
            dq_s[rows] = dq
            dkv_s[0, keys] = dk.astype(BF)
            dvb = dv.astype(BF)
            dkv_s[1, keys] = dvb
            vsum = vsum + jnp.sum(dvb.astype(F32), axis=0, keepdims=True)
        dqb = dq_s[...].astype(BF)
        g[0, 0:width] = dot_tn(dqb, ub[...]).astype(BF)
        acc[...] += dot_nn(dqb, w_s[r, 0:width])
        db[0, j, 0:1, :] = jnp.sum(dqb.astype(F32), axis=0, keepdims=True)
        db[0, j, 1:2, :] = vsum
        low, high = key_value_weight(w_s, r, 2 * width, width, model)
        tails = []
        for c in range(2):
            part = dkv_s[c]
            g[0, (2 + c) * width : (3 + c) * width] = dot_tn(part, pf[:, 0:model]).astype(BF)
            tails.append(dot_tn(part, pf[:, model:]).astype(BF))
            pacc[:, 0:model] += dot_nn(part, low[c * width : (c + 1) * width])
            pacc[:, model:] += dot_nn(part, high[c * width : (c + 1) * width])
        tail = jnp.concatenate(tails, axis=0)
        count = tail.shape[0] // (model // side)
        for c in range(model // side):
            g[0, 4 * width : 4 * width + count, c * side : (c + 1) * side] = tail[
                c * count : (c + 1) * count
            ]

    @pl.when(step == 1)
    def _():
        du[...] = acc[...]
        for i in range(items):
            dpf[i] = pacc[i * padded : i * padded + patches, :].astype(BF)


def whole(shape):
    zeros = (0,) * len(shape)
    return pl.BlockSpec(shape, lambda p: zeros)


def halves(shape):
    zeros = (0,) * (len(shape) - 1)
    return pl.BlockSpec((shape[0] // 2,) + tuple(shape[1:]), lambda p: (p,) + zeros)


def call(kernel, name, operands, outputs, scratch, flops, transcendentals=0):
    kinds = {
        "whole": lambda s: whole(s),
        "half": lambda s: halves(s),
        "any": lambda s: pl.BlockSpec(memory_space=ANY),
        "smem": lambda s: pl.BlockSpec(memory_space=pltpu.SMEM),
    }
    size = sum(a.size * a.dtype.itemsize for a, _ in operands)
    for shape, dtype, _ in outputs:
        count = jnp.dtype(dtype).itemsize
        for extent in shape:
            count *= extent
        size += count
    return pl.pallas_call(
        kernel,
        grid=(2,),
        in_specs=[kinds[kind](a.shape) for a, kind in operands],
        out_specs=[kinds[kind](shape) for shape, _, kind in outputs],
        out_shape=[jax.ShapeDtypeStruct(shape, dtype) for shape, dtype, _ in outputs],
        scratch_shapes=scratch,
        compiler_params=pltpu.CompilerParams(
            dimension_semantics=("arbitrary",), vmem_limit_bytes=VMEM_LIMIT
        ),
        cost_estimate=pl.CostEstimate(
            flops=flops, bytes_accessed=size, transcendentals=transcendentals
        ),
        name=name,
    )(*[a for a, _ in operands])


def feed_forward(u, w1, w2, c1, vec, name):
    rows, model = u.shape
    hidden = w1[0].shape[1]
    outs = call(
        ffn_forward_kernel,
        name,
        [(u, "whole")]
        + [(a, "any") for a in w1]
        + [(a, "any") for a in w2]
        + [(c1, "whole"), (vec, "whole")],
        [
            ((rows, model), BF, "whole"),
            ((rows, model), F32, "whole"),
            ((4, rows, hidden), BF, "half"),
            ((4, rows, hidden), BF, "half"),
        ],
        [
            pltpu.VMEM((4, model, hidden), BF),
            pltpu.VMEM((4, hidden, model), BF),
            pltpu.VMEM((rows, model), BF),
            pltpu.VMEM((rows, model), F32),
            pltpu.SemaphoreType.DMA((4,)),
            pltpu.SemaphoreType.DMA((4,)),
        ],
        16 * rows * model * hidden,
        8 * rows * hidden,
    )
    return outs[0], (u, outs[1], outs[2], outs[3])


def feed_backward(links, grad, cot, saved, w1, w2, vec, name):
    u, e, h, slope = saved
    rows, model = u.shape
    hidden = w1[0].shape[1]
    has_grad = grad is not None
    g = ((2, links.padded(model), hidden), BF, "half")
    g2 = ((2, links.padded(hidden), model), BF, "half")
    return call(
        functools.partial(ffn_backward_kernel, has_grad),
        name,
        ([(grad, "whole")] if has_grad else [])
        + [(cot, "whole"), (e, "whole"), (u, "whole")]
        + [(a, "any") for a in w1]
        + [(a, "any") for a in w2]
        + [(h, "half"), (slope, "half"), (vec, "whole")],
        [
            ((rows, model), F32, "whole"),
            g,
            g,
            g2,
            g2,
            ((2, 2, hidden), F32, "half"),
            ((3, model), F32, "whole"),
        ],
        [
            pltpu.VMEM((4, model, hidden), BF),
            pltpu.VMEM((4, hidden, model), BF),
            pltpu.VMEM((rows, model), BF),
            pltpu.VMEM((rows, model), BF),
            pltpu.VMEM((rows, model), F32),
            pltpu.SemaphoreType.DMA((4,)),
            pltpu.SemaphoreType.DMA((4,)),
        ],
        32 * rows * model * hidden,
    )


def self_forward(lengths, x, w, bias, vec, name):
    items = lengths.shape[0]
    rows, model = x.shape
    slots = rows // items
    width = w[0].shape[0] // 4
    heads = width // HEAD_DIM
    mid = ((4, rows, width), BF, "half")
    outs = call(
        functools.partial(self_forward_kernel, items),
        name,
        [(lengths, "smem"), (x, "whole")]
        + [(a, "any") for a in w]
        + [(bias, "whole"), (vec, "whole")],
        [
            ((rows, model), F32, "whole"),
            ((rows, model), F32, "whole"),
            mid,
            mid,
            mid,
            ((4, items, heads * slots, slots), BF, "half"),
            mid,
        ],
        [
            pltpu.VMEM((4,) + w[0].shape, BF),
            pltpu.VMEM((rows, model), F32),
            pltpu.VMEM((rows, width), F32),
            pltpu.VMEM((rows, width), F32),
            pltpu.VMEM((rows, width), F32),
            pltpu.VMEM((rows, width), F32),
            pltpu.SemaphoreType.DMA((4,)),
        ],
        32 * rows * model * width,
    )
    return outs[0], (x, outs[1], outs[2], outs[3], outs[4], outs[5], outs[6])


def self_backward(links, dy, saved, items, w, vec, dtype, name):
    x, e, q, k, v, p, a = saved
    rows, model = x.shape
    width = q.shape[2]
    g = ((2, links.padded(w[0].shape[0]), model), BF, "half")
    return call(
        functools.partial(self_backward_kernel, items),
        name,
        [(dy, "whole"), (e, "whole"), (x, "whole")]
        + [(m, "any") for m in w]
        + [(q, "half"), (k, "half"), (v, "half"), (p, "half"), (a, "half"), (vec, "whole")],
        [
            ((rows, model), dtype, "whole"),
            g,
            g,
            ((2, 2, 2, width), F32, "half"),
            ((3, model), F32, "whole"),
        ],
        [
            pltpu.VMEM((4,) + w[0].shape, BF),
            pltpu.VMEM((rows, model), BF),
            pltpu.VMEM((rows, model), F32),
        ]
        + [pltpu.VMEM((rows, width), F32)] * 7
        + [pltpu.SemaphoreType.DMA((4,))],
        64 * rows * model * width,
    )


def cross_forward(u, pf, patches, items, w, bias, vec, name):
    rows, model = u.shape
    slots, padded = rows // items, pf.shape[0] // items
    width = bias.shape[2]
    heads = width // HEAD_DIM
    mid = ((4, rows, width), BF, "half")
    key = ((4, pf.shape[0], width), BF, "half")
    outs = call(
        functools.partial(cross_forward_kernel, items, patches),
        name,
        [(u, "whole"), (pf, "whole")]
        + [(a, "any") for a in w]
        + [(bias, "whole"), (vec, "whole")],
        [
            ((rows, model), F32, "whole"),
            ((rows, model), F32, "whole"),
            mid,
            key,
            key,
            ((4, items, heads * slots, padded), BF, "half"),
            mid,
        ],
        [
            pltpu.VMEM((4,) + w[0].shape, BF),
            pltpu.VMEM((rows, model), BF),
            pltpu.VMEM((rows, model), F32),
            pltpu.VMEM((rows, width), F32),
            pltpu.VMEM((rows, width), F32),
            pltpu.SemaphoreType.DMA((4,)),
        ],
        16 * rows * model * width + 16 * pf.size * width,
    )
    return outs[0], (u, outs[1], outs[2], outs[3], outs[4], outs[5], outs[6])


def cross_backward(links, dy, saved, pf, patches, items, w, vec, name):
    u, e, q, k, v, p, a = saved
    rows, model = u.shape
    width = q.shape[2]
    g = ((2, links.padded(w[0].shape[0]), model), BF, "half")
    return call(
        functools.partial(cross_backward_kernel, items, patches),
        name,
        [(dy, "whole"), (e, "whole"), (u, "whole"), (pf, "whole")]
        + [(m, "any") for m in w]
        + [(q, "half"), (k, "half"), (v, "half"), (p, "half"), (a, "half"), (vec, "whole")],
        [
            ((rows, model), F32, "whole"),
            ((items, patches, pf.shape[1]), BF, "whole"),
            g,
            g,
            ((2, 2, 2, width), F32, "half"),
            ((3, model), F32, "whole"),
        ],
        [
            pltpu.VMEM((4,) + w[0].shape, BF),
            pltpu.VMEM((rows, model), BF),
            pltpu.VMEM((rows, model), BF),
            pltpu.VMEM((rows, model), F32),
            pltpu.VMEM(pf.shape, F32),
            pltpu.VMEM((rows, width), F32),
            pltpu.VMEM((rows, width), F32),
            pltpu.VMEM((rows, width), F32),
            pltpu.VMEM((2, pf.shape[0], width), BF),
            pltpu.SemaphoreType.DMA((4,)),
        ],
        32 * rows * model * width + 32 * pf.size * width,
    )


def pair(index, width):
    return index + width - 2 * width * ((index // width) % 2)


def add_rounded(a, b):
    return (a.astype(F32) + b.astype(F32)).astype(BF)


def reduce_kernel(n_tensor, n_dp, counts, chunk, *refs):
    arrays = len(counts)
    bits = n_dp.bit_length() - 1
    sends, keeps = refs[:arrays], refs[arrays : 2 * arrays]
    small_send, small_keep = refs[2 * arrays : 2 * arrays + 2]
    outs = refs[2 * arrays + 2 : 3 * arrays + 2]
    small_out = refs[3 * arrays + 2]
    rest = list(refs[3 * arrays + 3 :])
    core_in, kept, far_out, far_in, own, whole_sum = rest[:6]
    parts, halves_in = rest[6 : 6 + bits], rest[6 + bits : 6 + 2 * bits]
    gathered, tiny_sum, tiny_core, tiny_far, tiny_dp = rest[6 + 2 * bits : 11 + 2 * bits]
    send_sem, recv_sem, kept_sem, out_sem, tiny_send, tiny_recv = rest[11 + 2 * bits :]

    t, d = lax.axis_index("tensor"), lax.axis_index("dp")
    core_peer = {"tensor": pair(t, 1)}
    far_peer = {"tensor": lax.rem(t + 2, n_tensor)}
    dp_peers = [{"dp": pair(d, 1 << b)} for b in range(bits)]
    dp_bits = [(d // (1 << b)) % 2 for b in range(bits)]
    peers = [core_peer, far_peer] + dp_peers

    barrier = pltpu.get_barrier_semaphore()
    for peer in peers:
        pl.semaphore_signal(
            barrier, inc=1, device_id=peer, device_id_type=pl.DeviceIdType.MESH
        )
    pl.semaphore_wait(barrier, len(peers))

    total = sum(counts)
    stages = 2 + 2 * bits
    slots = core_in.shape[0]
    depth = gathered.shape[0]

    def remote(source, target, stage, slot, peer):
        return pltpu.make_async_remote_copy(
            src_ref=source,
            dst_ref=target,
            send_sem=send_sem.at[stage, slot],
            recv_sem=recv_sem.at[stage, slot],
            device_id=peer,
            device_id_type=pl.DeviceIdType.MESH,
        )

    def region(b):
        size = chunk >> (b + 1)
        start = 0
        for i in range(b + 1):
            start = start + dp_bits[i] * (chunk >> (i + 1))
        return pl.ds(pl.multiple_of(start, size), size)

    def copy_of(stage, m):
        slot, ring = lax.rem(m, slots), lax.rem(m, depth)
        if stage == 0:
            return remote(
                sends[0].at[:, pl.ds(0, chunk)], core_in.at[slot], 0, slot, core_peer
            )
        if stage == 1:
            return remote(far_out.at[slot], far_in.at[slot], 1, slot, far_peer)
        if stage < 2 + bits:
            b = stage - 2
            size = chunk >> (b + 1)
            source = whole_sum if b == 0 else parts[b - 1]
            gone = pl.ds(pl.multiple_of((1 - dp_bits[b]) * size, size), size)
            return remote(
                source.at[slot, gone], halves_in[b].at[slot], stage, slot, dp_peers[b]
            )
        b = 2 * bits + 1 - stage
        held = gathered.at[ring, region(b)]
        return remote(held, held, stage, slot, dp_peers[b])

    def kept_copy(a, m, base):
        slot = lax.rem(m, slots)
        rows = pl.ds(pl.multiple_of((m - base) * chunk, chunk), chunk)
        return pltpu.make_async_copy(keeps[a].at[:, rows], kept.at[slot], kept_sem.at[slot])

    def out_copy(a, m, base):
        ring = lax.rem(m, depth)
        rows = pl.ds(pl.multiple_of((m - base) * chunk, chunk), chunk)
        return pltpu.make_async_copy(gathered.at[ring], outs[a].at[rows], out_sem.at[ring])

    def each_array(m, act):
        base = 0
        for a in range(arrays):

            @pl.when((m >= base) & (m < base + counts[a]))
            def _(a=a, base=base):
                act(a, base)

            base += counts[a]

    def process(stage, m):
        slot, ring = lax.rem(m, slots), lax.rem(m, depth)
        if stage == 0:

            def begin(a, base):
                rows = pl.ds(pl.multiple_of((m - base) * chunk, chunk), chunk)
                remote(
                    sends[a].at[:, rows], core_in.at[slot], 0, slot, core_peer
                ).start()
                kept_copy(a, m, base).start()

            each_array(m, begin)
            return
        if stage <= stages:
            copy_of(stage - 1, m).wait()
        if stage == 1:
            kept_copy(0, m, m).wait()
            far_out[slot] = add_rounded(kept[slot, 1], core_in[slot, 1])
            own[slot] = add_rounded(kept[slot, 0], core_in[slot, 0])
        elif stage == 2:
            whole_sum[slot] = add_rounded(own[slot], far_in[slot])
        elif stage <= 2 + bits:
            b = stage - 3
            size = chunk >> (b + 1)
            source = whole_sum if b == 0 else parts[b - 1]
            mine = pl.ds(pl.multiple_of(dp_bits[b] * size, size), size)
            summed = add_rounded(source[slot, mine], halves_in[b][slot])
            if b < bits - 1:
                parts[b][slot] = summed
            else:
                gathered[ring, region(b)] = summed
        elif stage == stages:
            each_array(m, lambda a, base: out_copy(a, m, base).start())
        elif stage == stages + 1:
            out_copy(0, m, m).wait()
        if stage < stages:
            copy_of(stage, m).start()

    units = small_keep.shape[0] - tiny_far.shape[0]

    def tiny(stage):
        if stage == 0:
            source, target = small_send, tiny_core
        elif stage == 1:
            source, target = tiny_sum.at[0, pl.ds(units, tiny_far.shape[0])], tiny_far
        else:
            source = tiny_sum.at[stage - 1, pl.ds(0, tiny_far.shape[0])]
            target = tiny_dp.at[stage - 2]
        return pltpu.make_async_remote_copy(
            src_ref=source,
            dst_ref=target,
            send_sem=tiny_send.at[stage],
            recv_sem=tiny_recv.at[stage],
            device_id=peers[stage],
            device_id_type=pl.DeviceIdType.MESH,
        )

    def tiny_step(stage):
        if stage > 0:
            tiny(stage - 1).wait()
        count = tiny_far.shape[0]
        if stage == 1:
            tiny_sum[0] = small_keep[...] + tiny_core[...]
        elif stage == 2:
            tiny_sum[1, 0:units] = tiny_sum[0, 0:units] + tiny_far[0:units]
            tiny_sum[1, units:count] = tiny_sum[0, 2 * units :] + tiny_far[units:]
        elif stage > 2:
            summed = tiny_sum[stage - 2, 0:count] + tiny_dp[stage - 3]
            if stage == 2 + bits:
                small_out[...] = summed
            else:
                tiny_sum[stage - 1, 0:count] = summed
        if stage < 2 + bits:
            tiny(stage).start()

    def tick(k, carry):
        for stage in range(stages + 2):
            m = k - stage

            @pl.when((m >= 0) & (m < total))
            def _(stage=stage, m=m):
                process(stage, m)

        for stage in range(3 + bits):

            @pl.when(k == stage)
            def _(stage=stage):
                tiny_step(stage)

        return carry

    lax.fori_loop(0, total + stages + 2, tick, 0)


def reduce_all(links, pairs, small_keep, small_send, units):
    chunk = links.chunk
    model = pairs[0][0].shape[2]
    bits = links.bits
    counts = [keep.shape[1] // chunk for keep, _ in pairs]
    sends = [send for _, send in pairs]
    keeps = [keep for keep, _ in pairs]
    slots, depth = 4, 8
    anywhere = pl.BlockSpec(memory_space=ANY)
    vmem = pl.BlockSpec(memory_space=pltpu.VMEM)
    rows = small_keep.shape[0]
    stages = 2 + 2 * bits
    outs = pl.pallas_call(
        functools.partial(reduce_kernel, links.tensor, links.dp, counts, chunk),
        in_specs=[anywhere] * (2 * len(pairs)) + [vmem] * 2,
        out_specs=[anywhere] * len(pairs) + [vmem],
        out_shape=[jax.ShapeDtypeStruct(keep.shape[1:], BF) for keep in keeps]
        + [jax.ShapeDtypeStruct((rows - units, 128), F32)],
        scratch_shapes=[
            pltpu.VMEM((slots, 2, chunk, model), BF),
            pltpu.VMEM((slots, 2, chunk, model), BF),
            pltpu.VMEM((slots, chunk, model), BF),
            pltpu.VMEM((slots, chunk, model), BF),
            pltpu.VMEM((slots, chunk, model), BF),
            pltpu.VMEM((slots, chunk, model), BF),
        ]
        + [pltpu.VMEM((slots, chunk >> (b + 1), model), BF) for b in range(bits)]
        + [pltpu.VMEM((slots, chunk >> (b + 1), model), BF) for b in range(bits)]
        + [
            pltpu.VMEM((depth, chunk, model), BF),
            pltpu.VMEM((1 + bits, rows, 128), F32),
            pltpu.VMEM((rows, 128), F32),
            pltpu.VMEM((rows - units, 128), F32),
            pltpu.VMEM((bits, rows - units, 128), F32),
            pltpu.SemaphoreType.DMA((stages, slots)),
            pltpu.SemaphoreType.DMA((stages, slots)),
            pltpu.SemaphoreType.DMA((slots,)),
            pltpu.SemaphoreType.DMA((depth,)),
            pltpu.SemaphoreType.DMA((2 + bits,)),
            pltpu.SemaphoreType.DMA((2 + bits,)),
        ],
        compiler_params=pltpu.CompilerParams(
            collective_id=0, has_side_effects=True, vmem_limit_bytes=VMEM_LIMIT
        ),
        name="reduce_gradients",
    )(*sends, *keeps, small_send, small_keep)
    return outs[:-1], outs[-1]


class Flow:
    def __init__(self, net, a, lo, hi, spread):
        rows = hi - lo
        own, got = net.own[a], net.got[a]
        here = pl.ds(lo, rows)
        self.copies = []
        self.started = self.waited = 0
        if spread and rows % (16 * net.n_dp) == 0:

            def region(count):
                size, start = rows, lo
                for i in range(count):
                    size //= 2
                    start = start + net.dp_bits[i] * size
                return pl.ds(pl.multiple_of(start, 16), size)

            part = region(net.bits)
            self.add(net, own.at[part], got.at[1, part], net.far_peer)
            for b in reversed(range(net.bits)):
                part = region(b + 1)
                self.add(net, got.at[1, part], got.at[1, part], net.dp_peers[b])
        else:
            self.add(net, own.at[here], got.at[1, here], net.far_peer)
        self.add(net, got.at[1, here], got.at[2, here], net.core_peer)

    def add(self, net, source, target, peer):
        self.copies.append(net.remote(source, target, peer))

    def advance(self):
        if self.started < len(self.copies):
            if self.started > 0:
                self.await_copy(self.started - 1)
            self.copies[self.started].start()
            self.started += 1

    def await_copy(self, n):
        while self.started <= n:
            self.advance()
        while self.waited <= n:
            self.copies[self.waited].wait_recv()
            self.waited += 1

    def need(self, r):
        self.await_copy(len(self.copies) - (2 if r == 2 else 1))

    def close(self):
        self.need(3)
        for copy in self.copies:
            copy.wait_send()


class Direct:
    def __init__(self, copy):
        self.copy, self.state = copy, 0

    def advance(self):
        if self.state == 0:
            self.copy.start()
            self.state = 1

    def need(self):
        self.advance()
        if self.state == 1:
            self.copy.wait_recv()
            self.state = 2

    def close(self):
        self.need()
        self.copy.wait_send()


class Net:
    def __init__(self, n_tensor, n_dp, own, got, send_sem, recv_sem):
        self.n_dp, self.bits = n_dp, n_dp.bit_length() - 1
        self.own, self.got = own, got
        self.send_sem, self.recv_sem = send_sem, recv_sem
        self.count = 0
        t, d = lax.axis_index("tensor"), lax.axis_index("dp")
        self.core_peer = {"tensor": pair(t, 1)}
        self.far_peer = {"tensor": lax.rem(t + 2, n_tensor)}
        self.dp_peers = [{"dp": pair(d, 1 << b)} for b in range(self.bits)]
        self.dp_bits = [(d // (1 << b)) % 2 for b in range(self.bits)]
        peers = [self.core_peer, self.far_peer] + self.dp_peers
        barrier = pltpu.get_barrier_semaphore()
        for peer in peers:
            pl.semaphore_signal(
                barrier, inc=1, device_id=peer, device_id_type=pl.DeviceIdType.MESH
            )
        pl.semaphore_wait(barrier, len(peers))

    def remote(self, source, target, peer):
        n = self.count
        self.count += 1
        return pltpu.make_async_remote_copy(
            src_ref=source,
            dst_ref=target,
            send_sem=self.send_sem.at[n],
            recv_sem=self.recv_sem.at[n],
            device_id=peer,
            device_id_type=pl.DeviceIdType.MESH,
        )


ONE, EXPAND_ONE, CONTRACT_ONE, TWO, CROSS, EXPAND_TWO, CONTRACT_TWO = range(7)


def forward_kernel(sizes, *refs):
    n_tensor, n_dp, items, slots, patches, padded, width = sizes
    refs = list(refs)

    def take(n):
        got, refs[:n] = refs[:n], []
        return got

    own = take(7)
    bias_own, lengths, x, pf, vecs = take(5)
    got = take(7)
    text_out, join_out, e_out = take(3)
    self_out = [take(5), take(5)]
    cross_out = take(5)
    feed_out = [take(2), take(2)]
    ws, wf, wc, acc, u, ub, e_s = take(7)
    q_st, k_st, v_st, a_st, p_st = self_st = take(5)
    cross_st = take(5)
    qc_st, kc_st, vc_st, ac_st, pc_st = cross_st
    h_st, slope_st = feed_st = take(2)
    q_s, k_s, v_s, a_s, bias = take(5)
    send_sem, recv_sem, fetch_sem, store_sem = take(4)
    model = x.shape[1]
    hidden = own[EXPAND_ONE].shape[1]

    net = Net(n_tensor, n_dp, own, got, send_sem, recv_sem)
    middle = 2 * width
    flows = {
        "s1a": Flow(net, ONE, 0, middle, False),
        "s1b": Flow(net, ONE, middle, 2 * middle, True),
        "e1": Flow(net, EXPAND_ONE, 0, model, True),
        "k1": Flow(net, CONTRACT_ONE, 0, hidden, True),
        "s2a": Flow(net, TWO, middle, 2 * middle, False),
        "s2b": Flow(net, TWO, 0, middle, True),
        "ckv": Flow(net, CROSS, middle, own[CROSS].shape[0], False),
        "cqo": Flow(net, CROSS, 0, middle, False),
        "e2": Flow(net, EXPAND_TWO, 0, model, True),
        "k2": Flow(net, CONTRACT_TWO, 0, hidden, True),
    }
    parts = {
        ONE: ("s1a", "s1b"),
        EXPAND_ONE: ("e1",),
        CONTRACT_ONE: ("k1",),
        TWO: ("s2a", "s2b"),
        EXPAND_TWO: ("e2",),
        CONTRACT_TWO: ("k2",),
    }
    near = [Direct(net.remote(own[a], got[a].at[0], net.core_peer)) for a in range(7)]
    bias_near = Direct(net.remote(bias_own, bias.at[1], net.core_peer))
    bias_far = Direct(net.remote(bias_own, bias.at[2], net.far_peer))
    bias_last = Direct(net.remote(bias.at[2], bias.at[3], net.core_peer))

    def move(names):
        for name in names.split():
            flows[name].advance()

    fetches = {}

    def fetch(key, a, r, target, lo=0, hi=None, names=None):
        if key in fetches:
            return
        hi = own[a].shape[0] if hi is None else hi
        if r == 1:
            near[a].need()
        elif r > 1:
            for name in names or parts[a]:
                flows[name].need(r)
        source = own[a] if r == 0 else got[a].at[r - 1]
        copy = pltpu.make_async_copy(
            source.at[pl.ds(lo, hi - lo)], target, fetch_sem.at[len(fetches)]
        )
        copy.start()
        fetches[key] = copy

    stores = []

    def store(source, target):
        copy = pltpu.make_async_copy(source, target, store_sem.at[len(stores)])
        copy.start()
        stores.append(copy)
        return len(stores) - 1

    masks = head_masks(width)
    pending = {"self": [], "feed": []}

    def settle(kind):
        for n in pending[kind]:
            stores[n].wait()
            stores[n] = None
        pending[kind] = []

    def close_layer(n, target=None):
        e = acc[...]
        e_s[n] = e
        store(e_s.at[n], e_out.at[n])
        y = norm_forward(e, vecs[n, 1:2], vecs[n, 2:3])
        if target is not None:
            yb = y.astype(BF)
            target[...] = yb
            ub[...] = yb
            u[...] = yb.astype(F32)
        else:
            u[...] = y
            ub[...] = y.astype(BF)

    def open_layer(n):
        acc[...] = u[...] + vecs[n, 0:1]

    def fetch_self(layer, r):
        a = (ONE, TWO)[layer]
        fetch(("self", layer, r), a, r, ws.at[r])

    def self_unit(layer, r):
        fetch_self(layer, r)
        fetches["self", layer, r].wait()
        xb = ub[...]
        q = (
            dot_nt(xb, ws[r, 0:width]) + bias[r, 2 * layer : 2 * layer + 1, 0:width]
        ).astype(BF)
        k = dot_nt(xb, ws[r, width : 2 * width]).astype(BF)
        v = (
            dot_nt(xb, ws[r, 2 * width : 3 * width])
            + bias[r, 2 * layer + 1 : 2 * layer + 2, 0:width]
        ).astype(BF)
        q_st[r], k_st[r], v_st[r] = q, k, v
        q_s[...], k_s[...], v_s[...] = q.astype(F32), k.astype(F32), v.astype(F32)
        for i in range(items):
            rows = pl.ds(i * slots, slots)
            probs, a = item_forward(
                q_s[rows], k_s[rows].astype(BF), v_s[rows].astype(BF), masks, lengths[i]
            )
            p_st[r, i] = probs
            a_s[rows] = a
        ab = a_s[...].astype(BF)
        a_st[r] = ab
        acc[...] += dot_nn(ab, ws[r, 3 * width : 4 * width])

    def self_close(layer):
        for source, target in zip(self_st, self_out[layer]):
            pending["self"].append(store(source, target))

    def fetch_feed(layer, r):
        a, b = ((EXPAND_ONE, CONTRACT_ONE), (EXPAND_TWO, CONTRACT_TWO))[layer]
        fetch(("expand", layer, r), a, r, wf.at[r, 0])
        fetch(("contract", layer, r), b, r, wf.at[r, 1])

    def feed_unit(layer, r):
        fetch_feed(layer, r)
        fetches["expand", layer, r].wait()
        z = dot_nn(ub[...], wf[r, 0]) + bias[r, 6 + layer : 7 + layer, 0:hidden]
        cdf = 0.5 * (1.0 + lax.erf(z * 0.7071067811865476))
        slope = cdf + z * (jnp.exp(-0.5 * z * z) * 0.3989422804014327)
        h = (z * cdf).astype(BF)
        h_st[r] = h
        slope_st[r] = slope.astype(BF)
        fetches["contract", layer, r].wait()
        acc[...] += dot_nn(h, wf[r, 1])

    def feed_close(layer):
        for source, target in zip(feed_st, feed_out[layer]):
            pending["feed"].append(store(source, target))

    tail = own[CROSS].shape[0] - middle

    def fetch_keys(r):
        fetch(
            ("keys", r), CROSS, r, wc.at[r, pl.ds(middle, tail)], middle, middle + tail, ("ckv",)
        )

    def keys_unit(r):
        fetch_keys(r)
        fetches["keys", r].wait()
        low, high = key_value_weight(wc, r, middle, width, model)
        chunk = 2 * padded
        for m in range(items // 2):
            rows = slice(m * chunk, (m + 1) * chunk)
            left, right = pf[rows, 0:model], pf[rows, model:]
            kc_st[r, rows] = (
                dot_nt(left, low[0:width]) + dot_nt(right, high[0:width])
            ).astype(BF)
            vc_st[r, rows] = (
                dot_nt(left, low[width:]) + dot_nt(right, high[width:]) + bias[r, 5:6, 0:width]
            ).astype(BF)

    def fetch_cross(r):
        fetch(("cross", r), CROSS, r, wc.at[r, pl.ds(0, middle)], 0, middle, ("cqo",))

    def cross_unit(r):
        fetch_cross(r)
        fetches["cross", r].wait()
        q = (dot_nt(ub[...], wc[r, 0:width]) + bias[r, 4:5, 0:width]).astype(BF)
        qc_st[r] = q
        q_s[...] = q.astype(F32)
        for i in range(items):
            rows = pl.ds(i * slots, slots)
            keys = pl.ds(i * padded, padded)
            probs, a = item_forward(q_s[rows], kc_st[r, keys], vc_st[r, keys], masks, patches)
            pc_st[r, i] = probs
            a_s[rows] = a
        ab = a_s[...].astype(BF)
        ac_st[r] = ab
        acc[...] += dot_nn(ab, wc[r, width:middle])

    move("s1b e1 s1a")
    near[ONE].advance()
    bias_near.advance()
    bias_far.advance()
    near[CROSS].advance()
    fetch_self(0, 0)
    fetch_keys(0)
    bias[0] = bias_own[...]
    u[...] = x[...].astype(F32)
    ub[...] = x[...]
    open_layer(0)
    self_unit(0, 0)
    move("s1b e1 k1")
    bias_near.need()
    fetch_self(0, 1)
    self_unit(0, 1)
    move("s1b")
    keys_unit(0)
    move("e1 s1b k1")
    bias_far.need()
    bias_last.advance()
    near[EXPAND_ONE].advance()
    near[CONTRACT_ONE].advance()
    fetch_keys(1)
    keys_unit(1)
    move("s1a ckv e1 k1 s2b")
    bias_last.need()
    move("s1b")
    fetch_self(0, 2)
    fetch_self(0, 3)
    self_unit(0, 2)
    fetch_feed(0, 0)
    self_unit(0, 3)
    self_close(0)
    close_layer(0)
    open_layer(1)
    move("e1 k1 s2b s2a")
    near[TWO].advance()
    move("ckv")
    fetch_feed(0, 1)
    fetch_keys(2)
    fetch_keys(3)
    keys_unit(2)
    move("e2 k2 s2b")
    keys_unit(3)
    for source, target in zip(cross_st[1:3], cross_out[1:3]):
        store(source, target)
    move("k1")
    feed_unit(0, 0)
    fetch_feed(0, 2)
    feed_unit(0, 1)
    move("e2")
    fetch_feed(0, 3)
    feed_unit(0, 2)
    fetch_self(1, 0)
    feed_unit(0, 3)
    feed_close(0)
    close_layer(1, text_out)
    open_layer(2)
    settle("self")
    move("s2b s2a e2 k2 cqo")
    near[EXPAND_TWO].advance()
    near[CONTRACT_TWO].advance()
    fetch_self(1, 1)
    self_unit(1, 0)
    fetch_self(1, 2)
    self_unit(1, 1)
    move("e2 k2")
    fetch_self(1, 3)
    self_unit(1, 2)
    fetch_cross(0)
    self_unit(1, 3)
    self_close(1)
    close_layer(2)
    open_layer(3)
    move("cqo k2")
    fetch_cross(1)
    fetch_feed(1, 0)
    cross_unit(0)
    move("e2")
    fetch_cross(2)
    cross_unit(1)
    fetch_cross(3)
    cross_unit(2)
    move("k2")
    fetch_feed(1, 1)
    cross_unit(3)
    for n in (0, 3, 4):
        store(cross_st[n], cross_out[n])
    close_layer(3)
    open_layer(4)
    settle("feed")
    move("e2 k2")
    fetch_feed(1, 2)
    feed_unit(1, 0)
    feed_unit(1, 1)
    fetch_feed(1, 3)
    feed_unit(1, 2)
    feed_unit(1, 3)
    feed_close(1)
    close_layer(4, join_out)

    for copy in stores:
        if copy is not None:
            copy.wait()
    for flow in flows.values():
        flow.close()
    for direct in near + [bias_near, bias_far, bias_last]:
        direct.close()


def forward_all(links, own, bias, lengths, x, pf, vecs, patches, width):
    items = lengths.shape[0]
    rows, model = x.shape
    slots, padded = rows // items, pf.shape[0] // items
    hidden = own[EXPAND_ONE].shape[1]
    heads = width // HEAD_DIM
    anywhere = pl.BlockSpec(memory_space=ANY)
    vmem = pl.BlockSpec(memory_space=pltpu.VMEM)
    sizes = (links.tensor, links.dp, items, slots, patches, padded, width)
    mid = ((4, rows, width), BF)
    key = ((4, pf.shape[0], width), BF)
    probs = ((4, items, heads * slots, slots), BF)
    cross_probs = ((4, items, heads * slots, padded), BF)
    feed = ((4, rows, hidden), BF)
    self_kept = [mid] * 4 + [probs]
    cross_kept = [mid, key, key, mid, cross_probs]
    kept = self_kept * 2 + cross_kept + [feed] * 4
    outputs = [((3,) + a.shape, BF) for a in own]
    outputs += [((rows, model), BF)] * 2 + [((5, rows, model), F32)] + kept
    remotes = 10 * (2 + links.bits) + 10
    outs = pl.pallas_call(
        functools.partial(forward_kernel, sizes),
        in_specs=[anywhere] * 7
        + [vmem, pl.BlockSpec(memory_space=pltpu.SMEM), vmem, vmem, vmem],
        out_specs=[anywhere] * 7 + [vmem] * 2 + [anywhere] * (1 + len(kept)),
        out_shape=[jax.ShapeDtypeStruct(shape, dtype) for shape, dtype in outputs],
        scratch_shapes=[
            pltpu.VMEM((4, 4 * width, model), BF),
            pltpu.VMEM((4, 2, model, hidden), BF),
            pltpu.VMEM((4,) + own[CROSS].shape, BF),
            pltpu.VMEM((rows, model), F32),
            pltpu.VMEM((rows, model), F32),
            pltpu.VMEM((rows, model), BF),
            pltpu.VMEM((5, rows, model), F32),
        ]
        + [pltpu.VMEM(*item) for item in self_kept + cross_kept + [feed] * 2]
        + [pltpu.VMEM((rows, width), F32)] * 4
        + [
            pltpu.VMEM((4, 8, model), F32),
            pltpu.SemaphoreType.DMA((remotes,)),
            pltpu.SemaphoreType.DMA((remotes,)),
            pltpu.SemaphoreType.DMA((40,)),
            pltpu.SemaphoreType.DMA((32,)),
        ],
        compiler_params=pltpu.CompilerParams(
            collective_id=1, has_side_effects=True, vmem_limit_bytes=60 * 1024 * 1024
        ),
        name="forward_and_gather",
    )(*own, bias, lengths, x, pf, vecs)
    got, (text_out, join_out, e), kept = outs[:7], outs[7:10], outs[10:]
    return got, text_out, join_out, e, kept[0:5], kept[5:10], kept[10:15], kept[15:17], kept[17:19]


def swap(array, axis, size, distance):
    return lax.ppermute(array, axis, [(i, i ^ distance) for i in range(size)])


class Links:
    def __init__(self, mesh):
        self.tensor = mesh.shape["tensor"]
        self.dp = mesh.shape["dp"]
        self.bits = self.dp.bit_length() - 1
        self.chunk = max(256, 16 * self.dp)

    def padded(self, rows):
        return -(-rows // self.chunk) * self.chunk

    def core(self, array):
        return swap(array, "tensor", self.tensor, 1)

    def far(self, array):
        return swap(array, "tensor", self.tensor, 2)

    def gather(self, own):
        across = self.far(own)
        return own, self.core(own), across, self.core(across)


def layer_norm(e, vec):
    return norm_forward(e, vec[1:2], vec[2:3])


def flat(array):
    return array.reshape(-1)


def lines(array):
    n, values = array.shape
    rows = -(-values // 1024) * 8
    return jnp.pad(array, ((0, 0), (0, rows * 128 - values))).reshape(n, rows, 128)


def self_pack(w_in, w_out):
    turned = jnp.swapaxes(w_in, 1, 2)
    return jnp.concatenate([turned.reshape(-1, w_in.shape[1]), w_out], axis=0)


def self_unpack(total, width):
    model = total.shape[1]
    first = jnp.swapaxes(total[: 3 * width].reshape(3, width, model), 1, 2)
    return first, total[3 * width : 4 * width]


def cross_pack(w_query, w_out, w_keyval):
    model = w_query.shape[0]
    keyval = jnp.swapaxes(w_keyval, 1, 2).reshape(-1, w_keyval.shape[1])
    side = w_keyval.shape[1] - model
    parts = model // side
    count = keyval.shape[0] // parts
    tail = keyval[:, model:].reshape(parts, count, side)
    tail = jnp.swapaxes(tail, 0, 1).reshape(count, model)
    return jnp.concatenate([w_query.T, w_out, keyval[:, :model], tail], axis=0)


def cross_unpack(total, width, patch_width):
    model = total.shape[1]
    side = patch_width - model
    parts = model // side
    tail = total[4 * width : 4 * width + 2 * width // parts]
    tail = jnp.swapaxes(tail.reshape(-1, parts, side), 0, 1).reshape(2 * width, side)
    keyval = jnp.concatenate([total[2 * width : 4 * width], tail], axis=1)
    keyval = jnp.swapaxes(keyval.reshape(2, width, patch_width), 1, 2)
    return total[:width].T, total[width : 2 * width], keyval


def per_device(
    links,
    text_rows,
    patch_features,
    lengths,
    text_cotangent,
    join_cotangent,
    text_project_in,
    text_project_bias,
    text_project_out,
    text_expand,
    text_expand_bias,
    text_contract,
    text_out_bias,
    text_norm_gain,
    text_norm_shift,
    join_project_in,
    join_project_bias,
    join_project_out,
    cross_project_out,
    cross_key_value,
    join_expand,
    join_expand_bias,
    join_contract,
    join_out_bias,
    join_norm_gain,
    join_norm_shift,
):
    items, slots, model = text_rows.shape
    patches, patch_width = patch_features.shape[1:]
    width = text_project_in.shape[2]
    hidden = text_expand.shape[1]

    own = [
        self_pack(text_project_in, text_project_out),
        text_expand,
        text_contract,
        self_pack(join_project_in[0:3], join_project_out),
        cross_pack(join_project_in[3], cross_project_out, cross_key_value),
        join_expand,
        join_contract,
    ]
    biases = jnp.concatenate([text_project_bias, join_project_bias], axis=0)
    biases = jnp.concatenate(
        [
            jnp.pad(biases, ((0, 0), (0, hidden - width))),
            text_expand_bias[None],
            join_expand_bias[None],
        ],
        axis=0,
    ).astype(F32)

    def vec(bias, gain, shift, n):
        return jnp.stack([bias[n], gain[n], shift[n]]).astype(F32)

    text_vecs = [vec(text_out_bias, text_norm_gain, text_norm_shift, n) for n in range(2)]
    join_vecs = [vec(join_out_bias, join_norm_gain, join_norm_shift, n) for n in range(3)]

    padded = -(-patches // 16) * 16
    pf = jnp.pad(patch_features, ((0, 0), (0, padded - patches), (0, 0)))
    pf = pf.reshape(items * padded, patch_width)
    x = text_rows.reshape(items * slots, model)
    text_cot = text_cotangent.reshape(items * slots, model)
    join_cot = join_cotangent.reshape(items * slots, model)

    vecs = jnp.stack(text_vecs + join_vecs)
    got, text_out, join_out, e, kept_one, kept_two, kept_cross, feed_one, feed_two = forward_all(
        links, own, biases, lengths, x, pf, vecs, patches, width
    )
    weights = [[own[a]] + [got[a][r] for r in range(3)] for a in range(7)]
    h1 = layer_norm(e[0], text_vecs[0])
    h2 = layer_norm(e[2], join_vecs[0])
    h3 = layer_norm(e[3], join_vecs[1])
    saved_one = (x, e[0], *kept_one[:3], kept_one[4], kept_one[3])
    saved_two = (h1, e[1], *feed_one)
    saved_three = (text_out, e[2], *kept_two[:3], kept_two[4], kept_two[3])
    saved_four = (h2, e[3], *kept_cross[:3], kept_cross[4], kept_cross[3])
    saved_five = (h3, e[4], *feed_two)

    du, e2k, e2s, k2k, k2s, dc_two, sums_five = feed_backward(
        links, None, join_cot, saved_five, weights[EXPAND_TWO], weights[CONTRACT_TWO], join_vecs[2], "join_feed_backward"
    )
    du, grad_patches, ck, cs, db_cross, sums_four = cross_backward(
        links, du, saved_four, pf, patches, items, weights[CROSS], join_vecs[1], "cross_backward"
    )
    du, s2k, s2s, db_two, sums_three = self_backward(
        links, du, saved_three, items, weights[TWO], join_vecs[0], F32, "join_self_backward"
    )
    du, e1k, e1s, k1k, k1s, dc_one, sums_two = feed_backward(
        links, du, text_cot, saved_two, weights[EXPAND_ONE], weights[CONTRACT_ONE], text_vecs[1], "text_feed_backward"
    )
    grad_text, s1k, s1s, db_one, sums_one = self_backward(
        links, du, saved_one, items, weights[ONE], text_vecs[0], BF, "text_self_backward"
    )

    blocks = jnp.concatenate(
        [
            db_one.reshape(4, -1),
            db_two.reshape(4, -1),
            db_cross.reshape(4, -1),
            dc_one.reshape(4, -1),
            dc_two.reshape(4, -1),
        ],
        axis=1,
    )
    shared = flat(jnp.stack([sums_one, sums_two, sums_three, sums_four, sums_five]))
    units, count = blocks.shape[1], shared.shape[0]
    blocks = lines(blocks)
    shared = lines(shared[None])[0]
    small_keep = jnp.concatenate([blocks[0], blocks[2], shared], axis=0)
    small_send = jnp.concatenate([blocks[1], blocks[3], shared], axis=0)
    pairs = [(k2k, k2s), (e2k, e2s), (ck, cs), (s2k, s2s), (k1k, k1s), (e1k, e1s), (s1k, s1s)]
    totals, small = reduce_all(links, pairs, small_keep, small_send, blocks.shape[1])
    totals = [total.astype(F32) for total in totals]
    grad_join_contract, grad_join_expand = totals[0][:hidden], totals[1][:model]
    grad_query, grad_cross_out, grad_keyval = cross_unpack(totals[2], width, patch_width)
    grad_join_in, grad_join_out = self_unpack(totals[3], width)
    grad_text_contract, grad_text_expand = totals[4][:hidden], totals[5][:model]
    grad_text_in, grad_text_out = self_unpack(totals[6], width)
    shared = flat(small[blocks.shape[1] :])[:count].reshape(5, 3, model)
    small = flat(small[: blocks.shape[1]])[:units]
    attend = small[: 6 * width].reshape(6, width)
    text_shared, join_shared = shared[0:2], shared[2:5]

    return (
        text_out.reshape(text_rows.shape),
        join_out.reshape(text_rows.shape),
        grad_text.reshape(text_rows.shape),
        grad_patches,
        grad_text_in,
        attend[0:2],
        grad_text_out,
        grad_text_expand,
        small[6 * width : 6 * width + hidden],
        grad_text_contract,
        text_shared[:, 0],
        text_shared[:, 1],
        text_shared[:, 2],
        jnp.concatenate([grad_join_in, grad_query[None]], axis=0),
        attend[2:6],
        grad_join_out,
        grad_cross_out,
        grad_keyval,
        grad_join_expand,
        small[6 * width + hidden : 6 * width + 2 * hidden],
        grad_join_contract,
        join_shared[:, 0],
        join_shared[:, 1],
        join_shared[:, 2],
    )


def solution(mesh):
    rows = P(("dp", "tensor"), None, None)
    last = P(None, None, "tensor")
    second = P(None, "tensor")
    first = P("tensor", None)
    line = P("tensor")
    full = P()
    in_specs = (
        (rows, rows, P(("dp", "tensor")), rows, rows)
        + (last, second, first, second, line, first, full, full, full)
        + (last, second, first, first, last, second, line, first, full, full, full)
    )
    out_specs = (
        (rows, rows, rows, rows)
        + (last, second, first, second, line, first, full, full, full)
        + (last, second, first, first, last, second, line, first, full, full, full)
    )
    return jax.shard_map(
        functools.partial(per_device, Links(mesh)),
        mesh=mesh,
        in_specs=in_specs,
        out_specs=out_specs,
        check_vma=False,
    )
```

```python
import functools

import jax
import jax.numpy as jnp
from jax import lax
from jax.experimental import pallas as pl
from jax.experimental.pallas import tpu as pltpu
from jax.sharding import PartitionSpec as P

HEAD_DIM = 64
BF = jnp.bfloat16
F32 = jnp.float32
ANY = pl.ANY


def dot_nn(a, b):
    return lax.dot_general(a, b, (((1,), (0,)), ((), ())), preferred_element_type=F32)


def dot_nt(a, b):
    return lax.dot_general(a, b, (((1,), (1,)), ((), ())), preferred_element_type=F32)


def dot_tn(a, b):
    return lax.dot_general(a, b, (((0,), (0,)), ((), ())), preferred_element_type=F32)


def norm_forward(e, gain, shift):
    center = e - jnp.mean(e, axis=-1, keepdims=True)
    variance = jnp.mean(center * center, axis=-1, keepdims=True)
    return center * lax.rsqrt(variance + 1e-12) * gain + shift


def norm_backward(e, gain, dy):
    center = e - jnp.mean(e, axis=-1, keepdims=True)
    variance = jnp.mean(center * center, axis=-1, keepdims=True)
    rstd = lax.rsqrt(variance + 1e-12)
    normed = center * rstd
    scaled = dy * gain
    de = rstd * (
        scaled
        - jnp.mean(scaled, axis=-1, keepdims=True)
        - normed * jnp.mean(scaled * normed, axis=-1, keepdims=True)
    )
    sums = jnp.concatenate(
        [
            jnp.sum(de, axis=0, keepdims=True),
            jnp.sum(dy * normed, axis=0, keepdims=True),
            jnp.sum(dy, axis=0, keepdims=True),
        ],
        axis=0,
    )
    return de, sums


def head_masks(width):
    lane = lax.broadcasted_iota(jnp.int32, (1, width), 1)
    return [
        ((lane >= h * HEAD_DIM) & (lane < (h + 1) * HEAD_DIM)).astype(F32)
        for h in range(width // HEAD_DIM)
    ]


def stack_heads(rows, masks):
    return jnp.concatenate([rows * mask for mask in masks], axis=0).astype(BF)


def merge_heads(stacked, masks):
    count = stacked.shape[0] // len(masks)
    total = stacked[:count] * masks[0]
    for h in range(1, len(masks)):
        total = total + stacked[h * count : (h + 1) * count] * masks[h]
    return total


def item_forward(q, k, v, masks, length):
    scores = dot_nt(stack_heads(q, masks), k) * HEAD_DIM ** (-0.5)
    column = lax.broadcasted_iota(jnp.int32, scores.shape, 1)
    scores = jnp.where(column < length, scores, -1e30)
    weights = jnp.exp(scores - jnp.max(scores, axis=-1, keepdims=True))
    probs = (weights / jnp.sum(weights, axis=-1, keepdims=True)).astype(BF)
    return probs, merge_heads(dot_nn(probs, v), masks)


def item_backward(q, k, v, da, probs, masks):
    qs = stack_heads(q, masks)
    das = stack_heads(da, masks)
    dv = dot_tn(probs, das)
    dp = dot_nt(das, v)
    p = probs.astype(F32)
    ds = (p * (dp - jnp.sum(p * dp, axis=-1, keepdims=True))).astype(BF)
    scaling = HEAD_DIM ** (-0.5)
    dq = merge_heads(dot_nn(ds, k), masks) * scaling
    dk = dot_tn(ds, qs) * scaling
    return dq, dk, dv


def key_value_weight(w_s, r, start, width, model):
    low = w_s[r, pl.ds(start, 2 * width)]
    tail = w_s[r, pl.ds(start + 2 * width, 2 * width * (1024 - model) // model)]
    side = 1024 - model
    high = jnp.concatenate(
        [tail[:, c * side : (c + 1) * side] for c in range(model // side)], axis=0
    )
    return low, high


def pair(index, width):
    return index + width - 2 * width * ((index // width) % 2)


def add_rounded(a, b):
    return (a.astype(F32) + b.astype(F32)).astype(BF)


def rest(m, n):
    return m % n if isinstance(m, int) else lax.rem(m, n)


def when(condition, act):
    if isinstance(condition, bool):
        if condition:
            act()
    else:
        pl.when(condition)(act)


def halvings(n_dp, chunk):
    return min(n_dp, chunk // 16).bit_length() - 1


class Sums:
    def __init__(self, n_tensor, n_dp, counts, chunk, sends, keeps, outs, small, scratch):
        self.n_dp, self.bits = n_dp, n_dp.bit_length() - 1
        self.counts, self.chunk = counts, chunk
        self.cuts = halvings(n_dp, chunk)
        self.sends, self.keeps, self.outs = sends, keeps, outs
        self.small_send, self.small_keep, self.small_out = small
        scratch = list(scratch)
        bits = self.bits
        self.core_in, self.kept, self.far_out, self.far_in, self.own, self.whole = scratch[:6]
        self.parts, self.halves = scratch[6 : 6 + bits], scratch[6 + bits : 6 + 2 * bits]
        self.gathered, self.tiny_sum, self.tiny_core, self.tiny_far, self.tiny_dp = scratch[
            6 + 2 * bits : 11 + 2 * bits
        ]
        self.send_sem, self.recv_sem, self.kept_sem, self.out_sem = scratch[
            11 + 2 * bits : 15 + 2 * bits
        ]
        self.tiny_send, self.tiny_recv = scratch[15 + 2 * bits :]
        t, d = lax.axis_index("tensor"), lax.axis_index("dp")
        self.dp_bits = [(d // (1 << b)) % 2 for b in range(bits)]
        self.peers = [{"tensor": pair(t, 1)}, {"tensor": lax.rem(t + 2, n_tensor)}]
        self.peers += [{"dp": pair(d, 1 << b)} for b in range(bits)]
        self.total = sum(counts)
        self.stages = 2 + bits + self.cuts
        self.slots, self.depth = self.core_in.shape[0], self.gathered.shape[0]

    def greet(self):
        barrier = pltpu.get_barrier_semaphore()
        for peer in self.peers:
            pl.semaphore_signal(
                barrier, inc=1, device_id=peer, device_id_type=pl.DeviceIdType.MESH
            )
        pl.semaphore_wait(barrier, len(self.peers))

    def remote(self, source, target, stage, slot, peer):
        return pltpu.make_async_remote_copy(
            src_ref=source,
            dst_ref=target,
            send_sem=self.send_sem.at[stage, slot],
            recv_sem=self.recv_sem.at[stage, slot],
            device_id=self.peers[peer],
            device_id_type=pl.DeviceIdType.MESH,
        )

    def region(self, b):
        b = min(b, self.cuts - 1)
        size = self.chunk >> (b + 1)
        start = 0
        for i in range(b + 1):
            start = start + self.dp_bits[i] * (self.chunk >> (i + 1))
        return pl.ds(pl.multiple_of(start, size), size)

    def half(self, b, mine):
        if b >= self.cuts:
            return pl.ds(0, self.chunk >> self.cuts)
        size = self.chunk >> (b + 1)
        which = self.dp_bits[b] if mine else 1 - self.dp_bits[b]
        return pl.ds(pl.multiple_of(which * size, size), size)

    def halved(self, b):
        return self.whole if b == 0 else self.parts[b - 1]

    def copy_of(self, stage, m):
        slot, two = rest(m, self.slots), rest(m, 2)
        if stage == 0:
            source = self.sends[0].at[:, pl.ds(0, self.chunk)]
            return self.remote(source, self.core_in.at[slot], 0, slot, 0)
        if stage == 1:
            return self.remote(self.far_out.at[two], self.far_in.at[slot], 1, slot, 1)
        if stage < 2 + self.bits:
            b = stage - 2
            source = self.halved(b).at[two, self.half(b, False)]
            return self.remote(source, self.halves[b].at[slot], stage, slot, 2 + b)
        b = 1 + self.bits + self.cuts - stage
        held = self.gathered.at[rest(m, self.depth), self.region(b)]
        return self.remote(held, held, stage, slot, 2 + b)

    def kept_copy(self, a, start, m):
        two = rest(m, 2)
        source = self.keeps[a].at[:, pl.ds(start, self.chunk)]
        return pltpu.make_async_copy(source, self.kept.at[two], self.kept_sem.at[two])

    def out_copy(self, a, start, m):
        ring = rest(m, self.depth)
        target = self.outs[a].at[pl.ds(start, self.chunk)]
        return pltpu.make_async_copy(self.gathered.at[ring], target, self.out_sem.at[ring])

    def each_array(self, m, act):
        base = 0
        for a, count in enumerate(self.counts):
            if isinstance(m, int):
                start = (m - base) * self.chunk
                inside = base <= m < base + count
            else:
                start = pl.multiple_of((m - base) * self.chunk, self.chunk)
                inside = (m >= base) & (m < base + count)
            when(inside, functools.partial(act, a, start))
            base += count

    def process(self, stage, m):
        slot, two, ring = rest(m, self.slots), rest(m, 2), rest(m, self.depth)
        stages, bits = self.stages, self.bits
        if stage == 0:

            def begin(a, start):
                source = self.sends[a].at[:, pl.ds(start, self.chunk)]
                self.remote(source, self.core_in.at[slot], 0, slot, 0).start()
                self.kept_copy(a, start, m).start()

            self.each_array(m, begin)
            return
        if stage <= stages:
            self.copy_of(stage - 1, m).wait()
        if stage == 1:
            self.kept_copy(0, 0, m).wait()
            self.far_out[two] = add_rounded(self.kept[two, 1], self.core_in[slot, 1])
            self.own[two] = add_rounded(self.kept[two, 0], self.core_in[slot, 0])
        elif stage == 2:
            self.whole[two] = add_rounded(self.own[two], self.far_in[slot])
        elif stage <= 2 + bits:
            b = stage - 3
            summed = add_rounded(
                self.halved(b)[two, self.half(b, True)], self.halves[b][slot]
            )
            if b < bits - 1:
                self.parts[b][two] = summed
            else:
                self.gathered[ring, self.region(b)] = summed
        elif stage == stages:
            self.each_array(m, lambda a, start: self.out_copy(a, start, m).start())
        elif stage == stages + 1:
            self.out_copy(0, 0, m).wait()
        if stage < stages:
            self.copy_of(stage, m).start()

    def tiny(self, stage):
        count = self.tiny_far.shape[0]
        if stage == 0:
            source, target = self.small_send, self.tiny_core
        elif stage == 1:
            first = self.small_keep.shape[0] - count
            source, target = self.tiny_sum.at[0, pl.ds(first, count)], self.tiny_far
        else:
            source = self.tiny_sum.at[stage - 1, pl.ds(0, count)]
            target = self.tiny_dp.at[stage - 2]
        return pltpu.make_async_remote_copy(
            src_ref=source,
            dst_ref=target,
            send_sem=self.tiny_send.at[stage],
            recv_sem=self.tiny_recv.at[stage],
            device_id=self.peers[stage],
            device_id_type=pl.DeviceIdType.MESH,
        )

    def tiny_step(self, stage):
        bits = self.bits
        count = self.tiny_far.shape[0]
        units = self.small_keep.shape[0] - count
        if stage > 0:
            self.tiny(stage - 1).wait()
        if stage == 1:
            self.tiny_sum[0] = self.small_keep[...] + self.tiny_core[...]
        elif stage == 2:
            self.tiny_sum[1, 0:units] = self.tiny_sum[0, 0:units] + self.tiny_far[0:units]
            self.tiny_sum[1, units:count] = (
                self.tiny_sum[0, 2 * units :] + self.tiny_far[units:]
            )
        elif stage > 2:
            summed = self.tiny_sum[stage - 2, 0:count] + self.tiny_dp[stage - 3]
            if stage == 2 + bits:
                self.small_out[...] = summed
            else:
                self.tiny_sum[stage - 1, 0:count] = summed
        if stage < 2 + bits:
            self.tiny(stage).start()

    def tick(self, k):
        for stage in range(self.stages + 2):
            m = k - stage
            inside = (m >= 0) & (m < self.total)
            when(inside, functools.partial(self.process, stage, m))

    def finish(self, first):
        def step(k, carry):
            self.tick(k)
            for stage in range(3 + self.bits):
                when(k == first + stage, functools.partial(self.tiny_step, stage))
            return carry

        lax.fori_loop(first, self.total + self.stages + 2, step, 0)

    @staticmethod
    def scratch(n_dp, chunk, model, small, units):
        bits, cuts = n_dp.bit_length() - 1, halvings(n_dp, chunk)
        slots, depth, stages = 4, 8, 2 + bits + cuts
        sizes = [chunk >> min(b + 1, cuts) for b in range(bits)]
        return (
            [
                pltpu.VMEM((slots, 2, chunk, model), BF),
                pltpu.VMEM((2, 2, chunk, model), BF),
                pltpu.VMEM((2, chunk, model), BF),
                pltpu.VMEM((slots, chunk, model), BF),
                pltpu.VMEM((2, chunk, model), BF),
                pltpu.VMEM((2, chunk, model), BF),
            ]
            + [pltpu.VMEM((2, size, model), BF) for size in sizes]
            + [pltpu.VMEM((slots, size, model), BF) for size in sizes]
            + [
                pltpu.VMEM((depth, chunk, model), BF),
                pltpu.VMEM((1 + bits, small, model), F32),
                pltpu.VMEM((small, model), F32),
                pltpu.VMEM((small - units, model), F32),
                pltpu.VMEM((bits, small - units, model), F32),
                pltpu.SemaphoreType.DMA((stages, slots)),
                pltpu.SemaphoreType.DMA((stages, slots)),
                pltpu.SemaphoreType.DMA((2,)),
                pltpu.SemaphoreType.DMA((depth,)),
                pltpu.SemaphoreType.DMA((2 + bits,)),
                pltpu.SemaphoreType.DMA((2 + bits,)),
            ]
        )


class Flow:
    def __init__(self, net, a, lo, hi, spread):
        rows = hi - lo
        own, got = net.own[a], net.got[a]
        here = pl.ds(lo, rows)
        self.copies = []
        self.started = self.waited = 0
        if spread and rows % (16 * net.n_dp) == 0:

            def region(count):
                size, start = rows, lo
                for i in range(count):
                    size //= 2
                    start = start + net.dp_bits[i] * size
                return pl.ds(pl.multiple_of(start, 16), size)

            part = region(net.bits)
            self.add(net, own.at[part], got.at[1, part], net.far_peer)
            for b in reversed(range(net.bits)):
                part = region(b + 1)
                self.add(net, got.at[1, part], got.at[1, part], net.dp_peers[b])
        else:
            self.add(net, own.at[here], got.at[1, here], net.far_peer)
        self.add(net, got.at[1, here], got.at[2, here], net.core_peer)

    def add(self, net, source, target, peer):
        self.copies.append(net.remote(source, target, peer))

    def advance(self):
        if self.started < len(self.copies):
            if self.started > 0:
                self.await_copy(self.started - 1)
            self.copies[self.started].start()
            self.started += 1

    def await_copy(self, n):
        while self.started <= n:
            self.advance()
        while self.waited <= n:
            self.copies[self.waited].wait_recv()
            self.waited += 1

    def need(self, r):
        self.await_copy(len(self.copies) - (2 if r == 2 else 1))

    def close(self):
        self.need(3)
        for copy in self.copies:
            copy.wait_send()


class Direct:
    def __init__(self, copy):
        self.copy, self.state = copy, 0

    def advance(self):
        if self.state == 0:
            self.copy.start()
            self.state = 1

    def need(self):
        self.advance()
        if self.state == 1:
            self.copy.wait_recv()
            self.state = 2

    def close(self):
        self.need()
        self.copy.wait_send()


class Net:
    def __init__(self, n_tensor, n_dp, own, got, send_sem, recv_sem):
        self.n_dp, self.bits = n_dp, n_dp.bit_length() - 1
        self.own, self.got = own, got
        self.send_sem, self.recv_sem = send_sem, recv_sem
        self.count = 0
        t, d = lax.axis_index("tensor"), lax.axis_index("dp")
        self.core_peer = {"tensor": pair(t, 1)}
        self.far_peer = {"tensor": lax.rem(t + 2, n_tensor)}
        self.dp_peers = [{"dp": pair(d, 1 << b)} for b in range(self.bits)]
        self.dp_bits = [(d // (1 << b)) % 2 for b in range(self.bits)]
        peers = [self.core_peer, self.far_peer] + self.dp_peers
        barrier = pltpu.get_barrier_semaphore()
        for peer in peers:
            pl.semaphore_signal(
                barrier, inc=1, device_id=peer, device_id_type=pl.DeviceIdType.MESH
            )
        pl.semaphore_wait(barrier, len(peers))

    def remote(self, source, target, peer):
        n = self.count
        self.count += 1
        return pltpu.make_async_remote_copy(
            src_ref=source,
            dst_ref=target,
            send_sem=self.send_sem.at[n],
            recv_sem=self.recv_sem.at[n],
            device_id=peer,
            device_id_type=pl.DeviceIdType.MESH,
        )


ONE, EXPAND_ONE, CONTRACT_ONE, TWO, CROSS, EXPAND_TWO, CONTRACT_TWO = range(7)


def forward_kernel(sizes, *refs):
    n_tensor, n_dp, items, slots, patches, padded, width = sizes
    refs = list(refs)

    def take(n):
        got, refs[:n] = refs[:n], []
        return got

    own = take(7)
    bias_own, lengths, x, pf, vecs = take(5)
    got = take(7)
    text_out, join_out, e_out = take(3)
    self_out = [take(5), take(5)]
    cross_out = take(5)
    feed_out = [take(2), take(2)]
    ws, wf, wc, acc, u, ub, e_s = take(7)
    q_st, k_st, v_st, a_st, p_st = self_st = take(5)
    cross_st = take(5)
    qc_st, kc_st, vc_st, ac_st, pc_st = cross_st
    h_st, slope_st = feed_st = take(2)
    q_s, k_s, v_s, a_s, bias = take(5)
    send_sem, recv_sem, fetch_sem, store_sem = take(4)
    model = x.shape[1]
    hidden = own[EXPAND_ONE].shape[1]

    net = Net(n_tensor, n_dp, own, got, send_sem, recv_sem)
    middle = 2 * width
    flows = {
        "s1a": Flow(net, ONE, 0, middle, False),
        "s1b": Flow(net, ONE, middle, 2 * middle, True),
        "e1": Flow(net, EXPAND_ONE, 0, model, True),
        "k1": Flow(net, CONTRACT_ONE, 0, hidden, True),
        "s2a": Flow(net, TWO, middle, 2 * middle, False),
        "s2b": Flow(net, TWO, 0, middle, True),
        "ckv": Flow(net, CROSS, middle, own[CROSS].shape[0], False),
        "cqo": Flow(net, CROSS, 0, middle, False),
        "e2": Flow(net, EXPAND_TWO, 0, model, True),
        "k2": Flow(net, CONTRACT_TWO, 0, hidden, True),
    }
    parts = {
        ONE: ("s1a", "s1b"),
        EXPAND_ONE: ("e1",),
        CONTRACT_ONE: ("k1",),
        TWO: ("s2a", "s2b"),
        EXPAND_TWO: ("e2",),
        CONTRACT_TWO: ("k2",),
    }
    near = [Direct(net.remote(own[a], got[a].at[0], net.core_peer)) for a in range(7)]
    bias_near = Direct(net.remote(bias_own, bias.at[1], net.core_peer))
    bias_far = Direct(net.remote(bias_own, bias.at[2], net.far_peer))
    bias_last = Direct(net.remote(bias.at[2], bias.at[3], net.core_peer))

    def move(names):
        for name in names.split():
            flows[name].advance()

    fetches = {}

    def fetch(key, a, r, target, lo=0, hi=None, names=None):
        if key in fetches:
            return
        hi = own[a].shape[0] if hi is None else hi
        if r == 1:
            near[a].need()
        elif r > 1:
            for name in names or parts[a]:
                flows[name].need(r)
        source = own[a] if r == 0 else got[a].at[r - 1]
        copy = pltpu.make_async_copy(
            source.at[pl.ds(lo, hi - lo)], target, fetch_sem.at[len(fetches)]
        )
        copy.start()
        fetches[key] = copy

    stores = []

    def store(source, target):
        copy = pltpu.make_async_copy(source, target, store_sem.at[len(stores)])
        copy.start()
        stores.append(copy)
        return len(stores) - 1

    masks = head_masks(width)
    pending = {"self": [], "feed": []}

    def settle(kind):
        for n in pending[kind]:
            stores[n].wait()
            stores[n] = None
        pending[kind] = []

    def close_layer(n, target=None):
        e = acc[...]
        e_s[n] = e
        store(e_s.at[n], e_out.at[n])
        y = norm_forward(e, vecs[n, 1:2], vecs[n, 2:3])
        if target is not None:
            yb = y.astype(BF)
            target[...] = yb
            ub[...] = yb
            u[...] = yb.astype(F32)
        else:
            u[...] = y
            ub[...] = y.astype(BF)

    def open_layer(n):
        acc[...] = u[...] + vecs[n, 0:1]

    def fetch_self(layer, r):
        a = (ONE, TWO)[layer]
        fetch(("self", layer, r), a, r, ws.at[r])

    def self_unit(layer, r):
        fetch_self(layer, r)
        fetches["self", layer, r].wait()
        xb = ub[...]
        q = (
            dot_nt(xb, ws[r, 0:width]) + bias[r, 2 * layer : 2 * layer + 1, 0:width]
        ).astype(BF)
        k = dot_nt(xb, ws[r, width : 2 * width]).astype(BF)
        v = (
            dot_nt(xb, ws[r, 2 * width : 3 * width])
            + bias[r, 2 * layer + 1 : 2 * layer + 2, 0:width]
        ).astype(BF)
        q_st[r], k_st[r], v_st[r] = q, k, v
        q_s[...], k_s[...], v_s[...] = q.astype(F32), k.astype(F32), v.astype(F32)
        for i in range(items):
            rows = pl.ds(i * slots, slots)
            probs, a = item_forward(
                q_s[rows], k_s[rows].astype(BF), v_s[rows].astype(BF), masks, lengths[i]
            )
            p_st[r, i] = probs
            a_s[rows] = a
        ab = a_s[...].astype(BF)
        a_st[r] = ab
        acc[...] += dot_nn(ab, ws[r, 3 * width : 4 * width])

    def self_close(layer):
        for source, target in zip(self_st, self_out[layer]):
            pending["self"].append(store(source, target))

    def fetch_feed(layer, r):
        a, b = ((EXPAND_ONE, CONTRACT_ONE), (EXPAND_TWO, CONTRACT_TWO))[layer]
        fetch(("expand", layer, r), a, r, wf.at[r, 0])
        fetch(("contract", layer, r), b, r, wf.at[r, 1])

    def feed_unit(layer, r):
        fetch_feed(layer, r)
        fetches["expand", layer, r].wait()
        z = dot_nn(ub[...], wf[r, 0]) + bias[r, 6 + layer : 7 + layer, 0:hidden]
        cdf = 0.5 * (1.0 + lax.erf(z * 0.7071067811865476))
        slope = cdf + z * (jnp.exp(-0.5 * z * z) * 0.3989422804014327)
        h = (z * cdf).astype(BF)
        h_st[r] = h
        slope_st[r] = slope.astype(BF)
        fetches["contract", layer, r].wait()
        acc[...] += dot_nn(h, wf[r, 1])

    def feed_close(layer):
        for source, target in zip(feed_st, feed_out[layer]):
            pending["feed"].append(store(source, target))

    tail = own[CROSS].shape[0] - middle

    def fetch_keys(r):
        fetch(
            ("keys", r), CROSS, r, wc.at[r, pl.ds(middle, tail)], middle, middle + tail, ("ckv",)
        )

    def keys_unit(r):
        fetch_keys(r)
        fetches["keys", r].wait()
        low, high = key_value_weight(wc, r, middle, width, model)
        chunk = 2 * padded
        for m in range(items // 2):
            rows = slice(m * chunk, (m + 1) * chunk)
            left, right = pf[rows, 0:model], pf[rows, model:]
            kc_st[r, rows] = (
                dot_nt(left, low[0:width]) + dot_nt(right, high[0:width])
            ).astype(BF)
            vc_st[r, rows] = (
                dot_nt(left, low[width:]) + dot_nt(right, high[width:]) + bias[r, 5:6, 0:width]
            ).astype(BF)

    def fetch_cross(r):
        fetch(("cross", r), CROSS, r, wc.at[r, pl.ds(0, middle)], 0, middle, ("cqo",))

    def cross_unit(r):
        fetch_cross(r)
        fetches["cross", r].wait()
        q = (dot_nt(ub[...], wc[r, 0:width]) + bias[r, 4:5, 0:width]).astype(BF)
        qc_st[r] = q
        q_s[...] = q.astype(F32)
        for i in range(items):
            rows = pl.ds(i * slots, slots)
            keys = pl.ds(i * padded, padded)
            probs, a = item_forward(q_s[rows], kc_st[r, keys], vc_st[r, keys], masks, patches)
            pc_st[r, i] = probs
            a_s[rows] = a
        ab = a_s[...].astype(BF)
        ac_st[r] = ab
        acc[...] += dot_nn(ab, wc[r, width:middle])

    move("s1b e1 s1a")
    near[ONE].advance()
    bias_near.advance()
    bias_far.advance()
    near[CROSS].advance()
    fetch_self(0, 0)
    fetch_keys(0)
    bias[0] = bias_own[...]
    u[...] = x[...].astype(F32)
    ub[...] = x[...]
    open_layer(0)
    self_unit(0, 0)
    move("s1b e1 k1")
    bias_near.need()
    fetch_self(0, 1)
    self_unit(0, 1)
    move("s1b")
    keys_unit(0)
    move("e1 s1b k1")
    bias_far.need()
    bias_last.advance()
    near[EXPAND_ONE].advance()
    near[CONTRACT_ONE].advance()
    fetch_keys(1)
    keys_unit(1)
    move("s1a ckv e1 k1 s2b")
    bias_last.need()
    move("s1b")
    fetch_self(0, 2)
    fetch_self(0, 3)
    self_unit(0, 2)
    fetch_feed(0, 0)
    self_unit(0, 3)
    self_close(0)
    close_layer(0)
    open_layer(1)
    move("e1 k1 s2b s2a")
    near[TWO].advance()
    move("ckv")
    fetch_feed(0, 1)
    fetch_keys(2)
    fetch_keys(3)
    keys_unit(2)
    move("e2 k2 s2b")
    keys_unit(3)
    for source, target in zip(cross_st[1:3], cross_out[1:3]):
        store(source, target)
    move("k1")
    feed_unit(0, 0)
    fetch_feed(0, 2)
    feed_unit(0, 1)
    move("e2")
    fetch_feed(0, 3)
    feed_unit(0, 2)
    fetch_self(1, 0)
    feed_unit(0, 3)
    feed_close(0)
    close_layer(1, text_out)
    open_layer(2)
    settle("self")
    move("s2b s2a e2 k2 cqo")
    near[EXPAND_TWO].advance()
    near[CONTRACT_TWO].advance()
    fetch_self(1, 1)
    self_unit(1, 0)
    fetch_self(1, 2)
    self_unit(1, 1)
    move("e2 k2")
    fetch_self(1, 3)
    self_unit(1, 2)
    fetch_cross(0)
    self_unit(1, 3)
    self_close(1)
    close_layer(2)
    open_layer(3)
    move("cqo k2")
    fetch_cross(1)
    fetch_feed(1, 0)
    cross_unit(0)
    move("e2")
    fetch_cross(2)
    cross_unit(1)
    fetch_cross(3)
    cross_unit(2)
    move("k2")
    fetch_feed(1, 1)
    cross_unit(3)
    for n in (0, 3, 4):
        store(cross_st[n], cross_out[n])
    close_layer(3)
    open_layer(4)
    settle("feed")
    move("e2 k2")
    fetch_feed(1, 2)
    feed_unit(1, 0)
    feed_unit(1, 1)
    fetch_feed(1, 3)
    feed_unit(1, 2)
    feed_unit(1, 3)
    feed_close(1)
    close_layer(4, join_out)

    for copy in stores:
        if copy is not None:
            copy.wait()
    for flow in flows.values():
        flow.close()
    for direct in near + [bias_near, bias_far, bias_last]:
        direct.close()


def forward_all(links, own, bias, lengths, x, pf, vecs, patches, width):
    items = lengths.shape[0]
    rows, model = x.shape
    slots, padded = rows // items, pf.shape[0] // items
    hidden = own[EXPAND_ONE].shape[1]
    heads = width // HEAD_DIM
    anywhere = pl.BlockSpec(memory_space=ANY)
    vmem = pl.BlockSpec(memory_space=pltpu.VMEM)
    sizes = (links.tensor, links.dp, items, slots, patches, padded, width)
    mid = ((4, rows, width), BF)
    key = ((4, pf.shape[0], width), BF)
    probs = ((4, items, heads * slots, slots), BF)
    cross_probs = ((4, items, heads * slots, padded), BF)
    feed = ((4, rows, hidden), BF)
    self_kept = [mid] * 4 + [probs]
    cross_kept = [mid, key, key, mid, cross_probs]
    kept = self_kept * 2 + cross_kept + [feed] * 4
    outputs = [((3,) + a.shape, BF) for a in own]
    outputs += [((rows, model), BF)] * 2 + [((5, rows, model), F32)] + kept
    remotes = 10 * (2 + links.bits) + 10
    outs = pl.pallas_call(
        functools.partial(forward_kernel, sizes),
        in_specs=[anywhere] * 7
        + [vmem, pl.BlockSpec(memory_space=pltpu.SMEM), vmem, vmem, vmem],
        out_specs=[anywhere] * 7 + [vmem] * 2 + [anywhere] * (1 + len(kept)),
        out_shape=[jax.ShapeDtypeStruct(shape, dtype) for shape, dtype in outputs],
        scratch_shapes=[
            pltpu.VMEM((4, 4 * width, model), BF),
            pltpu.VMEM((4, 2, model, hidden), BF),
            pltpu.VMEM((4,) + own[CROSS].shape, BF),
            pltpu.VMEM((rows, model), F32),
            pltpu.VMEM((rows, model), F32),
            pltpu.VMEM((rows, model), BF),
            pltpu.VMEM((5, rows, model), F32),
        ]
        + [pltpu.VMEM(*item) for item in self_kept + cross_kept + [feed] * 2]
        + [pltpu.VMEM((rows, width), F32)] * 4
        + [
            pltpu.VMEM((4, 8, model), F32),
            pltpu.SemaphoreType.DMA((remotes,)),
            pltpu.SemaphoreType.DMA((remotes,)),
            pltpu.SemaphoreType.DMA((40,)),
            pltpu.SemaphoreType.DMA((32,)),
        ],
        compiler_params=pltpu.CompilerParams(
            collective_id=1, has_side_effects=True, vmem_limit_bytes=60 * 1024 * 1024
        ),
        name="forward_and_gather",
    )(*own, bias, lengths, x, pf, vecs)
    got, (text_out, join_out, e), kept = outs[:7], outs[7:10], outs[10:]
    return got, text_out, join_out, e, kept[0:5], kept[5:10], kept[10:15], kept[15:17], kept[17:19]


ORDER = (CONTRACT_TWO, EXPAND_TWO, CROSS, TWO, CONTRACT_ONE, EXPAND_ONE, ONE)


def backward_kernel(sizes, *refs):
    n_tensor, n_dp, items, slots, patches, padded, width, chunk, counts = sizes
    refs = list(refs)

    def take(n):
        got, refs[:n] = refs[:n], []
        return got

    own, got = take(7), take(7)
    e_in, x, text_out, text_cot, join_cot, pf, vecs = take(7)
    self_in = [take(5), take(5)]
    cross_in = take(5)
    feed_in = [take(2), take(2)]
    keeps, sends, outs = take(7), take(7), take(7)
    small_out, grad_text, dpf = take(3)
    wbuf, stage_buf, e_s, ub, dob, acc, pacc = take(7)
    q_b, k_b, v_b, a_b, p_b = self_buf = take(5)
    qc_b, kc_b, vc_b, ac_b, pc_b = cross_buf = take(5)
    h_b, slope_b = take(2)
    q_s, k_s, v_s, da_s, dq_s, dk_s, dv_s = take(7)
    dkv_s, small_keep, small_send = take(3)
    fetch_sem, store_sem, e_sem = take(3)
    model = x.shape[1]
    hidden = own[EXPAND_ONE].shape[1]
    side = pf.shape[1] - model

    sums = Sums(
        n_tensor,
        n_dp,
        counts,
        chunk,
        sends,
        keeps,
        outs,
        (small_send, small_keep, small_out),
        refs,
    )

    e_copies = [
        pltpu.make_async_copy(e_in.at[n], e_s.at[n], e_sem.at[n]) for n in range(5)
    ]
    for n in (4, 3, 2, 1, 0):
        e_copies[n].start()

    units = []
    for layer in (1, 0):
        expand, contract = ((EXPAND_ONE, CONTRACT_ONE), (EXPAND_TWO, CONTRACT_TWO))[layer]
        for r in range(4):
            units.append(("contract", layer, r, [(feed_in[layer][0].at[r], h_b)]))
        for r in range(4):
            units.append(
                (
                    "expand",
                    layer,
                    r,
                    [
                        (contract, wbuf, hidden),
                        (expand, wbuf, 0),
                        (feed_in[layer][1].at[r], slope_b),
                    ],
                )
            )
        for r in range(4):
            if layer == 1:
                units.append(
                    (
                        "cross",
                        0,
                        r,
                        [(CROSS, wbuf, 0)]
                        + [(cross_in[n].at[r], cross_buf[n]) for n in (3, 0, 1, 2, 4)],
                    )
                )
        for r in range(4):
            a = (ONE, TWO)[layer]
            units.append(
                (
                    "self",
                    layer,
                    r,
                    [(a, wbuf, 0)]
                    + [(self_in[layer][n].at[r], self_buf[n]) for n in (4, 0, 1, 2, 3)],
                )
            )
    position = {unit[:3]: n for n, unit in enumerate(units)}

    def fetches(n):
        _, _, r, wanted = units[n]
        parity = n % 2
        copies = []
        for i, item in enumerate(wanted):
            if len(item) == 3:
                a, target, row = item
                source = own[a] if r == 0 else got[a].at[r - 1]
                target = target.at[parity, pl.ds(row, own[a].shape[0])]
            else:
                source, target = item
                target = target.at[parity]
            copies.append(pltpu.make_async_copy(source, target, fetch_sem.at[parity, i]))
        return copies

    def begin(n):
        if n + 1 < len(units):
            for copy in fetches(n + 1):
                copy.start()
        for copy in fetches(n):
            copy.wait()
        return n % 2

    stores = {}

    def room(r):
        j = r % 2
        if stores.get(j) is not None:
            stores[j].wait()
            stores[j] = None
        return j

    def put(array, r):
        j = r % 2
        n = ORDER.index(array)
        target = (keeps, sends)[j][n]
        rows = target.shape[1]
        stores[j] = pltpu.make_async_copy(
            stage_buf.at[j, pl.ds(0, rows)], target.at[r // 2], store_sem.at[j]
        )
        stores[j].start()

    def settle():
        for j in (0, 1):
            room(j)

    def small_row(r, row, value):
        target = (small_keep, small_send)[r % 2]
        n = 8 * (r // 2) + row
        target[n : n + 1, 0 : value.shape[1]] = value

    def open_layer(n, dy):
        e_copies[n].wait()
        de, partial = norm_backward(e_s[n], vecs[n, 1:2], dy)
        for target in (small_keep, small_send):
            target[16 + 3 * n : 19 + 3 * n] = partial
        dob[...] = de.astype(BF)
        acc[...] = de

    def input_rows(n):
        ub[...] = norm_forward(e_s[n], vecs[n, 1:2], vecs[n, 2:3]).astype(BF)

    def contract_unit(layer, r):
        b = begin(position["contract", layer, r])
        j = room(r)
        stage_buf[j, 0:hidden] = dot_tn(h_b[b], dob[...]).astype(BF)
        put((CONTRACT_ONE, CONTRACT_TWO)[layer], r)

    def expand_unit(layer, r):
        b = begin(position["expand", layer, r])
        dh = dot_nt(dob[...], wbuf[b, hidden : 2 * hidden])
        dz = (dh * slope_b[b].astype(F32)).astype(BF)
        j = room(r)
        stage_buf[j, 0:model] = dot_tn(ub[...], dz).astype(BF)
        put((EXPAND_ONE, EXPAND_TWO)[layer], r)
        small_row(r, 6 + layer, jnp.sum(dz.astype(F32), axis=0, keepdims=True))
        acc[...] += dot_nt(dz, wbuf[b, 0:model])

    masks = head_masks(width)

    def self_unit(layer, r):
        b = begin(position["self", layer, r])
        da_s[...] = dot_nt(dob[...], wbuf[b, 3 * width : 4 * width])
        j = room(r)
        stage_buf[j, 3 * width : 4 * width] = dot_tn(a_b[b], dob[...]).astype(BF)
        q_s[...], k_s[...], v_s[...] = (
            q_b[b].astype(F32),
            k_b[b].astype(F32),
            v_b[b].astype(F32),
        )
        for i in range(items):
            rows = pl.ds(i * slots, slots)
            dq, dk, dv = item_backward(
                q_s[rows],
                k_s[rows].astype(BF),
                v_s[rows].astype(BF),
                da_s[rows],
                p_b[b, i],
                masks,
            )
            dq_s[rows], dk_s[rows], dv_s[rows] = dq, dk, dv
        xb = ub[...]
        total = acc[...]
        for c, part in enumerate((dq_s, dk_s, dv_s)):
            pb = part[...].astype(BF)
            stage_buf[j, c * width : (c + 1) * width] = dot_tn(pb, xb).astype(BF)
            total = total + dot_nn(pb, wbuf[b, c * width : (c + 1) * width])
            if c != 1:
                small_row(
                    r, 2 * layer + c // 2, jnp.sum(pb.astype(F32), axis=0, keepdims=True)
                )
        acc[...] = total
        put((ONE, TWO)[layer], r)

    def cross_unit(r):
        b = begin(position["cross", 0, r])
        da_s[...] = dot_nt(dob[...], wbuf[b, width : 2 * width])
        j = room(r)
        stage_buf[j, width : 2 * width] = dot_tn(ac_b[b], dob[...]).astype(BF)
        q_s[...] = qc_b[b].astype(F32)
        vsum = jnp.zeros((1, width), F32)
        for i in range(items):
            rows = pl.ds(i * slots, slots)
            keys = pl.ds(i * padded, padded)
            dq, dk, dv = item_backward(
                q_s[rows], kc_b[b, keys], vc_b[b, keys], da_s[rows], pc_b[b, i], masks
            )
            dq_s[rows] = dq
            dkv_s[0, keys] = dk.astype(BF)
            dvb = dv.astype(BF)
            dkv_s[1, keys] = dvb
            vsum = vsum + jnp.sum(dvb.astype(F32), axis=0, keepdims=True)
        dqb = dq_s[...].astype(BF)
        stage_buf[j, 0:width] = dot_tn(dqb, ub[...]).astype(BF)
        acc[...] += dot_nn(dqb, wbuf[b, 0:width])
        small_row(r, 4, jnp.sum(dqb.astype(F32), axis=0, keepdims=True))
        small_row(r, 5, vsum)
        low, high = key_value_weight(wbuf, b, 2 * width, width, model)
        tails = []
        for c in range(2):
            part = dkv_s[c]
            stage_buf[j, (2 + c) * width : (3 + c) * width] = dot_tn(
                part, pf[:, 0:model]
            ).astype(BF)
            tails.append(dot_tn(part, pf[:, model:]).astype(BF))
            one = dot_nn(part, low[c * width : (c + 1) * width])
            two = dot_nn(part, high[c * width : (c + 1) * width])
            if r == 0 and c == 0:
                pacc[:, 0:model], pacc[:, model:] = one, two
            else:
                pacc[:, 0:model] += one
                pacc[:, model:] += two
        tail = jnp.concatenate(tails, axis=0)
        count = tail.shape[0] // (model // side)
        for c in range(model // side):
            stage_buf[j, 4 * width : 4 * width + count, c * side : (c + 1) * side] = tail[
                c * count : (c + 1) * count
            ]
        extra = stage_buf.shape[1] - 4 * width - count
        if extra > 0:
            stage_buf[j, 4 * width + count :] = jnp.zeros((extra, model), BF)
        put(CROSS, r)

    small_keep[...] = jnp.zeros_like(small_keep)
    small_send[...] = jnp.zeros_like(small_send)
    for copy in fetches(0):
        copy.start()
    open_layer(4, join_cot[...].astype(F32))
    sums.greet()
    clock = [0]

    def tick():
        sums.tick(clock[0])
        clock[0] += 1

    for r in range(4):
        contract_unit(1, r)
    settle()
    tick()
    e_copies[3].wait()
    input_rows(3)
    expand_unit(1, 0)
    tick()
    expand_unit(1, 1)
    expand_unit(1, 2)
    tick()
    expand_unit(1, 3)
    settle()
    e_copies[3] = Done()
    open_layer(3, acc[...])
    e_copies[2].wait()
    e_copies[2] = Done()
    input_rows(2)
    for r in range(4):
        cross_unit(r)
        if r == 3:
            settle()
        tick()
    open_layer(2, acc[...])
    ub[...] = text_out[...]
    for r in range(4):
        self_unit(1, r)
        if r == 3:
            settle()
        tick()
    open_layer(1, acc[...] + text_cot[...].astype(F32))
    for r in range(4):
        contract_unit(0, r)
    settle()
    tick()
    e_copies[0].wait()
    e_copies[0] = Done()
    input_rows(0)
    for r in range(4):
        expand_unit(0, r)
        if r == 3:
            settle()
        tick()
    open_layer(0, acc[...])
    ub[...] = x[...]
    for r in range(4):
        self_unit(0, r)
        if r == 3:
            settle()
        tick()
    grad_text[...] = acc[...].astype(BF)
    for i in range(items):
        dpf[i] = pacc[i * padded : i * padded + patches, :].astype(BF)
    sums.finish(clock[0])


class Done:
    def wait(self):
        pass


def backward_all(links, own, got, e, x, text_out, cots, pf, vecs, kept, patches, items, width):
    rows, model = x.shape
    slots, padded = rows // items, pf.shape[0] // items
    hidden = own[EXPAND_ONE].shape[1]
    heads = width // HEAD_DIM
    chunk = links.chunk
    anywhere = pl.BlockSpec(memory_space=ANY)
    vmem = pl.BlockSpec(memory_space=pltpu.VMEM)
    extents = [links.padded(own[a].shape[0]) for a in ORDER]
    counts = tuple(extent // chunk for extent in extents)
    sizes = (links.tensor, links.dp, items, slots, patches, padded, width, chunk, counts)
    pairs = [((2, extent, model), BF) for extent in extents]
    totals = [((extent, model), BF) for extent in extents]
    units, small = 8, 32
    outputs = pairs * 2 + totals
    outputs += [
        ((small - units, model), F32),
        ((rows, model), BF),
        ((items, patches, pf.shape[1]), BF),
    ]
    f32_rows = pltpu.VMEM((rows, width), F32)
    outs = pl.pallas_call(
        functools.partial(backward_kernel, sizes),
        in_specs=[anywhere] * 15 + [vmem] * 6 + [anywhere] * len(kept),
        out_specs=[anywhere] * 21 + [vmem] * 3,
        out_shape=[jax.ShapeDtypeStruct(shape, dtype) for shape, dtype in outputs],
        scratch_shapes=[
            pltpu.VMEM((2, 2 * hidden, model), BF),
            pltpu.VMEM((2, max(extents), model), BF),
            pltpu.VMEM((5, rows, model), F32),
            pltpu.VMEM((rows, model), BF),
            pltpu.VMEM((rows, model), BF),
            pltpu.VMEM((rows, model), F32),
            pltpu.VMEM(pf.shape, F32),
        ]
        + [pltpu.VMEM((2, rows, width), BF)] * 4
        + [pltpu.VMEM((2, items, heads * slots, slots), BF)]
        + [pltpu.VMEM((2, rows, width), BF)]
        + [pltpu.VMEM((2, pf.shape[0], width), BF)] * 2
        + [pltpu.VMEM((2, rows, width), BF)]
        + [pltpu.VMEM((2, items, heads * slots, padded), BF)]
        + [pltpu.VMEM((2, rows, hidden), BF)] * 2
        + [f32_rows] * 7
        + [
            pltpu.VMEM((2, pf.shape[0], width), BF),
            pltpu.VMEM((small, model), F32),
            pltpu.VMEM((small, model), F32),
            pltpu.SemaphoreType.DMA((2, 6)),
            pltpu.SemaphoreType.DMA((2,)),
            pltpu.SemaphoreType.DMA((5,)),
        ]
        + Sums.scratch(links.dp, chunk, model, small, units),
        compiler_params=pltpu.CompilerParams(
            collective_id=0, has_side_effects=True, vmem_limit_bytes=60 * 1024 * 1024
        ),
        name="backward_and_sums",
    )(*own, *got, e, x, text_out, *cots, pf, vecs, *kept)
    return outs[14:21], outs[21], outs[22], outs[23]


class Links:
    def __init__(self, mesh):
        self.tensor = mesh.shape["tensor"]
        self.dp = mesh.shape["dp"]
        self.bits = self.dp.bit_length() - 1
        self.chunk = 256

    def padded(self, rows):
        return -(-rows // self.chunk) * self.chunk


def self_pack(w_in, w_out):
    turned = jnp.swapaxes(w_in, 1, 2)
    return jnp.concatenate([turned.reshape(-1, w_in.shape[1]), w_out], axis=0)


def self_unpack(total, width):
    model = total.shape[1]
    first = jnp.swapaxes(total[: 3 * width].reshape(3, width, model), 1, 2)
    return first, total[3 * width : 4 * width]


def cross_pack(w_query, w_out, w_keyval):
    model = w_query.shape[0]
    keyval = jnp.swapaxes(w_keyval, 1, 2).reshape(-1, w_keyval.shape[1])
    side = w_keyval.shape[1] - model
    parts = model // side
    count = keyval.shape[0] // parts
    tail = keyval[:, model:].reshape(parts, count, side)
    tail = jnp.swapaxes(tail, 0, 1).reshape(count, model)
    return jnp.concatenate([w_query.T, w_out, keyval[:, :model], tail], axis=0)


def cross_unpack(total, width, patch_width):
    model = total.shape[1]
    side = patch_width - model
    parts = model // side
    tail = total[4 * width : 4 * width + 2 * width // parts]
    tail = jnp.swapaxes(tail.reshape(-1, parts, side), 0, 1).reshape(2 * width, side)
    keyval = jnp.concatenate([total[2 * width : 4 * width], tail], axis=1)
    keyval = jnp.swapaxes(keyval.reshape(2, width, patch_width), 1, 2)
    return total[:width].T, total[width : 2 * width], keyval


def per_device(
    links,
    text_rows,
    patch_features,
    lengths,
    text_cotangent,
    join_cotangent,
    text_project_in,
    text_project_bias,
    text_project_out,
    text_expand,
    text_expand_bias,
    text_contract,
    text_out_bias,
    text_norm_gain,
    text_norm_shift,
    join_project_in,
    join_project_bias,
    join_project_out,
    cross_project_out,
    cross_key_value,
    join_expand,
    join_expand_bias,
    join_contract,
    join_out_bias,
    join_norm_gain,
    join_norm_shift,
):
    items, slots, model = text_rows.shape
    patches, patch_width = patch_features.shape[1:]
    width = text_project_in.shape[2]
    hidden = text_expand.shape[1]

    own = [
        self_pack(text_project_in, text_project_out),
        text_expand,
        text_contract,
        self_pack(join_project_in[0:3], join_project_out),
        cross_pack(join_project_in[3], cross_project_out, cross_key_value),
        join_expand,
        join_contract,
    ]
    biases = jnp.concatenate([text_project_bias, join_project_bias], axis=0)
    biases = jnp.concatenate(
        [
            jnp.pad(biases, ((0, 0), (0, hidden - width))),
            text_expand_bias[None],
            join_expand_bias[None],
        ],
        axis=0,
    ).astype(F32)

    def vec(bias, gain, shift, n):
        return jnp.stack([bias[n], gain[n], shift[n]]).astype(F32)

    text_vecs = [vec(text_out_bias, text_norm_gain, text_norm_shift, n) for n in range(2)]
    join_vecs = [vec(join_out_bias, join_norm_gain, join_norm_shift, n) for n in range(3)]

    padded = -(-patches // 16) * 16
    pf = jnp.pad(patch_features, ((0, 0), (0, padded - patches), (0, 0)))
    pf = pf.reshape(items * padded, patch_width)
    x = text_rows.reshape(items * slots, model)
    text_cot = text_cotangent.reshape(items * slots, model)
    join_cot = join_cotangent.reshape(items * slots, model)

    vecs = jnp.stack(text_vecs + join_vecs)
    got, text_out, join_out, e, kept_one, kept_two, kept_cross, feed_one, feed_two = forward_all(
        links, own, biases, lengths, x, pf, vecs, patches, width
    )

    totals, small, grad_text, grad_patches = backward_all(
        links,
        own,
        got,
        e,
        x,
        text_out,
        (text_cot, join_cot),
        pf,
        vecs,
        (*kept_one, *kept_two, *kept_cross, *feed_one, *feed_two),
        patches,
        items,
        width,
    )
    totals = [total.astype(F32) for total in totals]
    grad_join_contract, grad_join_expand = totals[0][:hidden], totals[1][:model]
    grad_query, grad_cross_out, grad_keyval = cross_unpack(totals[2], width, patch_width)
    grad_join_in, grad_join_out = self_unpack(totals[3], width)
    grad_text_contract, grad_text_expand = totals[4][:hidden], totals[5][:model]
    grad_text_in, grad_text_out = self_unpack(totals[6], width)
    attend = small[0:6, 0:width]
    shared = small[8:23].reshape(5, 3, model)
    text_shared, join_shared = shared[0:2], shared[2:5]

    return (
        text_out.reshape(text_rows.shape),
        join_out.reshape(text_rows.shape),
        grad_text.reshape(text_rows.shape),
        grad_patches,
        grad_text_in,
        attend[0:2],
        grad_text_out,
        grad_text_expand,
        small[6, :hidden],
        grad_text_contract,
        text_shared[:, 0],
        text_shared[:, 1],
        text_shared[:, 2],
        jnp.concatenate([grad_join_in, grad_query[None]], axis=0),
        attend[2:6],
        grad_join_out,
        grad_cross_out,
        grad_keyval,
        grad_join_expand,
        small[7, :hidden],
        grad_join_contract,
        join_shared[:, 0],
        join_shared[:, 1],
        join_shared[:, 2],
    )


def solution(mesh):
    rows = P(("dp", "tensor"), None, None)
    last = P(None, None, "tensor")
    second = P(None, "tensor")
    first = P("tensor", None)
    line = P("tensor")
    full = P()
    in_specs = (
        (rows, rows, P(("dp", "tensor")), rows, rows)
        + (last, second, first, second, line, first, full, full, full)
        + (last, second, first, first, last, second, line, first, full, full, full)
    )
    out_specs = (
        (rows, rows, rows, rows)
        + (last, second, first, second, line, first, full, full, full)
        + (last, second, first, first, last, second, line, first, full, full, full)
    )
    return jax.shard_map(
        functools.partial(per_device, Links(mesh)),
        mesh=mesh,
        in_specs=in_specs,
        out_specs=out_specs,
        check_vma=False,
    )
```

```python
import functools

import jax
import jax.numpy as jnp
from jax import lax
from jax.experimental import pallas as pl
from jax.experimental.pallas import tpu as pltpu
from jax.sharding import PartitionSpec as P

HEAD_DIM = 64
BF = jnp.bfloat16
F32 = jnp.float32
ANY = pl.ANY


def dot_nn(a, b):
    return lax.dot_general(a, b, (((1,), (0,)), ((), ())), preferred_element_type=F32)


def dot_nt(a, b):
    return lax.dot_general(a, b, (((1,), (1,)), ((), ())), preferred_element_type=F32)


def dot_tn(a, b):
    return lax.dot_general(a, b, (((0,), (0,)), ((), ())), preferred_element_type=F32)


def norm_forward(e, gain, shift):
    center = e - jnp.mean(e, axis=-1, keepdims=True)
    variance = jnp.mean(center * center, axis=-1, keepdims=True)
    return center * lax.rsqrt(variance + 1e-12) * gain + shift


def norm_backward(e, gain, dy):
    center = e - jnp.mean(e, axis=-1, keepdims=True)
    variance = jnp.mean(center * center, axis=-1, keepdims=True)
    rstd = lax.rsqrt(variance + 1e-12)
    normed = center * rstd
    scaled = dy * gain
    de = rstd * (
        scaled
        - jnp.mean(scaled, axis=-1, keepdims=True)
        - normed * jnp.mean(scaled * normed, axis=-1, keepdims=True)
    )
    sums = jnp.concatenate(
        [
            jnp.sum(de, axis=0, keepdims=True),
            jnp.sum(dy * normed, axis=0, keepdims=True),
            jnp.sum(dy, axis=0, keepdims=True),
        ],
        axis=0,
    )
    return de, sums


def head_masks(width):
    lane = lax.broadcasted_iota(jnp.int32, (1, width), 1)
    return [
        ((lane >= h * HEAD_DIM) & (lane < (h + 1) * HEAD_DIM)).astype(F32)
        for h in range(width // HEAD_DIM)
    ]


def stack_heads(rows, masks):
    return jnp.concatenate([rows * mask for mask in masks], axis=0).astype(BF)


def merge_heads(stacked, masks):
    count = stacked.shape[0] // len(masks)
    total = stacked[:count] * masks[0]
    for h in range(1, len(masks)):
        total = total + stacked[h * count : (h + 1) * count] * masks[h]
    return total


def item_forward(q, k, v, masks, length):
    scores = dot_nt(stack_heads(q, masks), k) * HEAD_DIM ** (-0.5)
    column = lax.broadcasted_iota(jnp.int32, scores.shape, 1)
    scores = jnp.where(column < length, scores, -1e30)
    weights = jnp.exp(scores - jnp.max(scores, axis=-1, keepdims=True))
    probs = (weights / jnp.sum(weights, axis=-1, keepdims=True)).astype(BF)
    return probs, merge_heads(dot_nn(probs, v), masks)


def item_backward(q, k, v, da, probs, masks):
    qs = stack_heads(q, masks)
    das = stack_heads(da, masks)
    dv = dot_tn(probs, das)
    dp = dot_nt(das, v)
    p = probs.astype(F32)
    ds = (p * (dp - jnp.sum(p * dp, axis=-1, keepdims=True))).astype(BF)
    scaling = HEAD_DIM ** (-0.5)
    dq = merge_heads(dot_nn(ds, k), masks) * scaling
    dk = dot_tn(ds, qs) * scaling
    return dq, dk, dv


def pair(index, width):
    return index + width - 2 * width * ((index // width) % 2)


def rest(m, n):
    return m % n if isinstance(m, int) else lax.rem(m, n)


def when(condition, act):
    if isinstance(condition, bool):
        if condition:
            act()
    else:
        pl.when(condition)(act)


def halvings(n_dp, chunk):
    return min(n_dp, chunk // 16).bit_length() - 1


class Sums:
    def __init__(self, n_tensor, n_dp, counts, chunk, sends, keeps, outs, small, scratch):
        self.n_dp, self.bits = n_dp, n_dp.bit_length() - 1
        self.counts, self.chunk = counts, chunk
        self.cuts = halvings(n_dp, chunk)
        self.sends, self.keeps, self.outs = sends, keeps, outs
        self.small_send, self.small_keep, self.small_out = small
        scratch = list(scratch)
        bits = self.bits
        self.core_in, self.kept, self.far_out, self.far_in, self.own, self.whole = scratch[:6]
        self.parts, self.halves = scratch[6 : 6 + bits], scratch[6 + bits : 6 + 2 * bits]
        self.gathered, self.tiny_sum, self.tiny_core, self.tiny_far, self.tiny_dp = scratch[
            6 + 2 * bits : 11 + 2 * bits
        ]
        self.send_sem, self.recv_sem, self.kept_sem, self.out_sem = scratch[
            11 + 2 * bits : 15 + 2 * bits
        ]
        self.tiny_send, self.tiny_recv = scratch[15 + 2 * bits :]
        t, d = lax.axis_index("tensor"), lax.axis_index("dp")
        self.dp_bits = [(d // (1 << b)) % 2 for b in range(bits)]
        self.peers = [{"tensor": pair(t, 1)}, {"tensor": lax.rem(t + 2, n_tensor)}]
        self.peers += [{"dp": pair(d, 1 << b)} for b in range(bits)]
        self.total = sum(counts)
        self.stages = 2 + bits + self.cuts
        self.slots, self.depth = self.core_in.shape[0], self.gathered.shape[0]

    def greet(self):
        barrier = pltpu.get_barrier_semaphore()
        for peer in self.peers:
            pl.semaphore_signal(
                barrier, inc=1, device_id=peer, device_id_type=pl.DeviceIdType.MESH
            )
        pl.semaphore_wait(barrier, len(self.peers))

    def remote(self, source, target, stage, slot, peer):
        return pltpu.make_async_remote_copy(
            src_ref=source,
            dst_ref=target,
            send_sem=self.send_sem.at[stage, slot],
            recv_sem=self.recv_sem.at[stage, slot],
            device_id=self.peers[peer],
            device_id_type=pl.DeviceIdType.MESH,
        )

    def region(self, b):
        b = min(b, self.cuts - 1)
        size = self.chunk >> (b + 1)
        start = 0
        for i in range(b + 1):
            start = start + self.dp_bits[i] * (self.chunk >> (i + 1))
        return pl.ds(pl.multiple_of(start, size), size)

    def half(self, b, mine):
        if b >= self.cuts:
            return pl.ds(0, self.chunk >> self.cuts)
        size = self.chunk >> (b + 1)
        which = self.dp_bits[b] if mine else 1 - self.dp_bits[b]
        return pl.ds(pl.multiple_of(which * size, size), size)

    def halved(self, b):
        return self.whole if b == 0 else self.parts[b - 1]

    def copy_of(self, stage, m):
        slot, two = rest(m, self.slots), rest(m, 2)
        if stage == 0:
            source = self.sends[0].at[:, pl.ds(0, self.chunk)]
            return self.remote(source, self.core_in.at[slot], 0, slot, 0)
        if stage == 1:
            ring = rest(m, self.far_in.shape[0])
            return self.remote(self.far_out.at[slot], self.far_in.at[ring], 1, ring, 1)
        if stage < 2 + self.bits:
            b = stage - 2
            source = self.halved(b).at[two, self.half(b, False)]
            return self.remote(source, self.halves[b].at[slot], stage, slot, 2 + b)
        b = 1 + self.bits + self.cuts - stage
        held = self.gathered.at[rest(m, self.depth), self.region(b)]
        return self.remote(held, held, stage, slot, 2 + b)

    def kept_copy(self, a, start, m):
        two = rest(m, 2)
        source = self.keeps[a].at[:, pl.ds(start, self.chunk)]
        return pltpu.make_async_copy(source, self.kept.at[two], self.kept_sem.at[two])

    def out_copy(self, a, start, m):
        ring = rest(m, self.depth)
        target = self.outs[a].at[pl.ds(start, self.chunk)]
        return pltpu.make_async_copy(self.gathered.at[ring], target, self.out_sem.at[ring])

    def each_array(self, m, act):
        base = 0
        for a, count in enumerate(self.counts):
            if isinstance(m, int):
                start = (m - base) * self.chunk
                inside = base <= m < base + count
            else:
                start = pl.multiple_of((m - base) * self.chunk, self.chunk)
                inside = (m >= base) & (m < base + count)
            when(inside, functools.partial(act, a, start))
            base += count

    def process(self, step, m):
        if step == 2:
            return
        stage = step if step < 2 else step - 1
        slot, two, ring = rest(m, self.slots), rest(m, 2), rest(m, self.depth)
        stages, bits = self.stages, self.bits
        if stage == 0:

            def begin(a, start):
                source = self.sends[a].at[:, pl.ds(start, self.chunk)]
                self.remote(source, self.core_in.at[slot], 0, slot, 0).start()
                self.kept_copy(a, start, m).start()

            self.each_array(m, begin)
            return
        if stage <= stages:
            self.copy_of(stage - 1, m).wait()
        if stage == 1:
            self.kept_copy(0, 0, m).wait()
            self.far_out[slot] = self.kept[two, 1] + self.core_in[slot, 1]
            self.own[slot] = self.kept[two, 0] + self.core_in[slot, 0]
        elif stage == 2:
            self.whole[two] = self.own[slot] + self.far_in[rest(m, self.far_in.shape[0])]
        elif stage <= 2 + bits:
            b = stage - 3
            summed = self.halved(b)[two, self.half(b, True)] + self.halves[b][slot]
            if b < bits - 1:
                self.parts[b][two] = summed
            else:
                self.gathered[ring, self.region(b)] = summed
        elif stage == stages:
            self.each_array(m, lambda a, start: self.out_copy(a, start, m).start())
        elif stage == stages + 1:
            self.out_copy(0, 0, m).wait()
        if stage < stages:
            self.copy_of(stage, m).start()

    def tiny(self, stage):
        count = self.tiny_far.shape[0]
        if stage == 0:
            source, target = self.small_send, self.tiny_core
        elif stage == 1:
            first = self.small_keep.shape[0] - count
            source, target = self.tiny_sum.at[0, pl.ds(first, count)], self.tiny_far
        else:
            source = self.tiny_sum.at[stage - 1, pl.ds(0, count)]
            target = self.tiny_dp.at[stage - 2]
        return pltpu.make_async_remote_copy(
            src_ref=source,
            dst_ref=target,
            send_sem=self.tiny_send.at[stage],
            recv_sem=self.tiny_recv.at[stage],
            device_id=self.peers[stage],
            device_id_type=pl.DeviceIdType.MESH,
        )

    def tiny_step(self, stage):
        bits = self.bits
        count = self.tiny_far.shape[0]
        units = self.small_keep.shape[0] - count
        if stage > 0:
            self.tiny(stage - 1).wait()
        if stage == 1:
            self.tiny_sum[0] = self.small_keep[...] + self.tiny_core[...]
        elif stage == 2:
            self.tiny_sum[1, 0:units] = self.tiny_sum[0, 0:units] + self.tiny_far[0:units]
            self.tiny_sum[1, units:count] = (
                self.tiny_sum[0, 2 * units :] + self.tiny_far[units:]
            )
        elif stage > 2:
            summed = self.tiny_sum[stage - 2, 0:count] + self.tiny_dp[stage - 3]
            if stage == 2 + bits:
                self.small_out[...] = summed
            else:
                self.tiny_sum[stage - 1, 0:count] = summed
        if stage < 2 + bits:
            self.tiny(stage).start()

    def tick(self, k):
        for step in range(self.stages + 3):
            m = k - step
            inside = (m >= 0) & (m < self.total)
            when(inside, functools.partial(self.process, step, m))

    def finish(self, first):
        def step(k, carry):
            self.tick(k)
            for stage in range(3 + self.bits):
                when(k == first + stage, functools.partial(self.tiny_step, stage))
            return carry

        lax.fori_loop(first, self.total + self.stages + 3, step, 0)

    @staticmethod
    def scratch(n_dp, chunk, model, small, units):
        bits, cuts = n_dp.bit_length() - 1, halvings(n_dp, chunk)
        slots, far, depth, stages = 4, 6, 8, 2 + bits + cuts
        sizes = [chunk >> min(b + 1, cuts) for b in range(bits)]
        return (
            [
                pltpu.VMEM((slots, 2, chunk, model), BF),
                pltpu.VMEM((2, 2, chunk, model), BF),
                pltpu.VMEM((slots, chunk, model), BF),
                pltpu.VMEM((far, chunk, model), BF),
                pltpu.VMEM((slots, chunk, model), BF),
                pltpu.VMEM((2, chunk, model), BF),
            ]
            + [pltpu.VMEM((2, size, model), BF) for size in sizes]
            + [pltpu.VMEM((slots, size, model), BF) for size in sizes]
            + [
                pltpu.VMEM((depth, chunk, model), BF),
                pltpu.VMEM((1 + bits, small, model), F32),
                pltpu.VMEM((small, model), F32),
                pltpu.VMEM((small - units, model), F32),
                pltpu.VMEM((bits, small - units, model), F32),
                pltpu.SemaphoreType.DMA((stages, far)),
                pltpu.SemaphoreType.DMA((stages, far)),
                pltpu.SemaphoreType.DMA((2,)),
                pltpu.SemaphoreType.DMA((depth,)),
                pltpu.SemaphoreType.DMA((2 + bits,)),
                pltpu.SemaphoreType.DMA((2 + bits,)),
            ]
        )


class Flow:
    def __init__(self, net, a, lo, hi, spread):
        rows = hi - lo
        own, got = net.own[a], net.got[a]
        here = pl.ds(lo, rows)
        self.copies = []
        self.started = self.waited = 0
        if spread and rows % (16 * net.n_dp) == 0:

            def region(count):
                size, start = rows, lo
                for i in range(count):
                    size //= 2
                    start = start + net.dp_bits[i] * size
                return pl.ds(pl.multiple_of(start, 16), size)

            part = region(net.bits)
            self.add(net, own.at[part], got.at[1, part], net.far_peer)
            for b in reversed(range(net.bits)):
                part = region(b + 1)
                self.add(net, got.at[1, part], got.at[1, part], net.dp_peers[b])
        else:
            self.add(net, own.at[here], got.at[1, here], net.far_peer)
        self.add(net, got.at[1, here], got.at[2, here], net.core_peer)

    def add(self, net, source, target, peer):
        self.copies.append(net.remote(source, target, peer))

    def advance(self):
        if self.started < len(self.copies):
            if self.started > 0:
                self.await_copy(self.started - 1)
            self.copies[self.started].start()
            self.started += 1

    def await_copy(self, n):
        while self.started <= n:
            self.advance()
        while self.waited <= n:
            self.copies[self.waited].wait_recv()
            self.waited += 1

    def need(self, r):
        self.await_copy(len(self.copies) - (2 if r == 2 else 1))

    def close(self):
        self.need(3)
        for copy in self.copies:
            copy.wait_send()


class Direct:
    def __init__(self, copy):
        self.copy, self.state = copy, 0

    def advance(self):
        if self.state == 0:
            self.copy.start()
            self.state = 1

    def need(self):
        self.advance()
        if self.state == 1:
            self.copy.wait_recv()
            self.state = 2

    def close(self):
        self.need()
        self.copy.wait_send()


class Net:
    def __init__(self, n_tensor, n_dp, own, got, send_sem, recv_sem):
        self.n_dp, self.bits = n_dp, n_dp.bit_length() - 1
        self.own, self.got = own, got
        self.send_sem, self.recv_sem = send_sem, recv_sem
        self.count = 0
        t, d = lax.axis_index("tensor"), lax.axis_index("dp")
        self.core_peer = {"tensor": pair(t, 1)}
        self.far_peer = {"tensor": lax.rem(t + 2, n_tensor)}
        self.dp_peers = [{"dp": pair(d, 1 << b)} for b in range(self.bits)]
        self.dp_bits = [(d // (1 << b)) % 2 for b in range(self.bits)]
        peers = [self.core_peer, self.far_peer] + self.dp_peers
        barrier = pltpu.get_barrier_semaphore()
        for peer in peers:
            pl.semaphore_signal(
                barrier, inc=1, device_id=peer, device_id_type=pl.DeviceIdType.MESH
            )
        pl.semaphore_wait(barrier, len(peers))

    def remote(self, source, target, peer):
        n = self.count
        self.count += 1
        return pltpu.make_async_remote_copy(
            src_ref=source,
            dst_ref=target,
            send_sem=self.send_sem.at[n],
            recv_sem=self.recv_sem.at[n],
            device_id=peer,
            device_id_type=pl.DeviceIdType.MESH,
        )


TEXT_IN, TEXT_OUT, EXPAND_ONE, CONTRACT_ONE, JOIN_IN = range(5)
JOIN_OUT, KEY_VALUE, CROSS_OUT, EXPAND_TWO, CONTRACT_TWO = range(5, 10)
ARRAYS = 10


def spread_patches(source, wide, target, items, padded):
    patches = source.shape[0]
    least = patches // 8 * 8
    groups, _, lanes = wide.shape
    for i in range(items):
        rows = pl.ds(i * padded + least, padded - least)
        wide[:, rows] = jnp.zeros((groups, padded - least, lanes), F32)

    def step(n, carry):
        for c in range(groups):
            wide[c, pl.ds(n, items, stride=padded)] = source[
                n, :, c * lanes : (c + 1) * lanes
            ].astype(F32)
        return carry

    lax.fori_loop(0, patches, step, 0)
    for c in range(groups):
        target[:, c * lanes : (c + 1) * lanes] = wide[c].astype(BF)


def norm_rows(vecs, text, join):
    for c in range(3):
        for n in range(2):
            vecs[n, c : c + 1] = text[c][...].astype(F32)[n : n + 1]
        for n in range(3):
            vecs[2 + n, c : c + 1] = join[c][...].astype(F32)[n : n + 1]


def forward_kernel(sizes, *refs):
    n_tensor, n_dp, items, slots, patches, padded, width = sizes
    refs = list(refs)

    def take(n):
        got, refs[:n] = refs[:n], []
        return got

    own = take(ARRAYS)
    bias_in, vecs_in = take(4), take(6)
    lengths, x, pf_in = take(3)
    got = take(ARRAYS)
    text_out, join_out, e_out, pf_out = take(4)
    self_out = [take(5), take(5)]
    cross_out = take(5)
    feed_out = [take(2), take(2)]
    ws, wf, wc, wk, acc, u, ub, e_s = take(8)
    pf_raw, pf_wide, pf, vecs = take(4)
    q_st, k_st, v_st, a_st, p_st = self_st = take(5)
    cross_st = take(5)
    qc_st, kc_st, vc_st, ac_st, pc_st = cross_st
    h_st, slope_st = feed_st = take(2)
    q_s, k_s, v_s, a_s, bias = take(5)
    send_sem, recv_sem, fetch_sem, store_sem, pf_sem = take(5)
    model = x.shape[1]
    hidden = own[EXPAND_ONE].shape[1]

    pf_copy = pltpu.make_async_copy(pf_in, pf_raw, pf_sem)
    pf_copy.start()
    net = Net(n_tensor, n_dp, own, got, send_sem, recv_sem)
    middle = 2 * width
    flows = {
        "s1p": Flow(net, TEXT_IN, 0, middle, True),
        "s1v": Flow(net, TEXT_IN, middle, 3 * width, False),
        "s1o": Flow(net, TEXT_OUT, 0, width, False),
        "e1": Flow(net, EXPAND_ONE, 0, model, True),
        "k1": Flow(net, CONTRACT_ONE, 0, hidden, True),
        "s2p": Flow(net, JOIN_IN, 0, middle, True),
        "s2v": Flow(net, JOIN_IN, middle, 3 * width, False),
        "s2o": Flow(net, JOIN_OUT, 0, width, False),
        "ckv": Flow(net, KEY_VALUE, 0, middle, False),
        "cq": Flow(net, JOIN_IN, 3 * width, 4 * width, False),
        "co": Flow(net, CROSS_OUT, 0, width, False),
        "e2": Flow(net, EXPAND_TWO, 0, model, True),
        "k2": Flow(net, CONTRACT_TWO, 0, hidden, True),
    }
    near = [Direct(net.remote(own[a], got[a].at[0], net.core_peer)) for a in range(ARRAYS)]
    bias_near = Direct(net.remote(bias.at[0], bias.at[1], net.core_peer))
    bias_far = Direct(net.remote(bias.at[0], bias.at[2], net.far_peer))
    bias_last = Direct(net.remote(bias.at[2], bias.at[3], net.core_peer))

    def move(names):
        for name in names.split():
            flows[name].advance()

    fetches = {}

    fetch_count = [0]

    def fetch(key, r, wanted):
        if key in fetches:
            return
        fetches[key] = []
        for a, lo, hi, target, names in wanted:
            if r == 1:
                near[a].need()
            elif r > 1:
                for name in names:
                    flows[name].need(r)
            source = own[a] if r == 0 else got[a].at[r - 1]
            copy = pltpu.make_async_copy(
                source.at[pl.ds(lo, hi - lo)], target, fetch_sem.at[fetch_count[0]]
            )
            fetch_count[0] += 1
            copy.start()
            fetches[key].append(copy)

    def arrive(key):
        for copy in fetches[key]:
            copy.wait()

    stores = []

    def store(source, target):
        copy = pltpu.make_async_copy(source, target, store_sem.at[len(stores)])
        copy.start()
        stores.append(copy)
        return len(stores) - 1

    masks = head_masks(width)
    pending = {"self": [], "feed": []}

    def settle(kind):
        for n in pending[kind]:
            stores[n].wait()
            stores[n] = None
        pending[kind] = []

    def close_layer(n, target=None):
        e = acc[...]
        e_s[n] = e
        store(e_s.at[n], e_out.at[n])
        y = norm_forward(e, vecs[n, 1:2], vecs[n, 2:3])
        if target is not None:
            yb = y.astype(BF)
            target[...] = yb
            ub[...] = yb
            u[...] = yb.astype(F32)
        else:
            u[...] = y
            ub[...] = y.astype(BF)

    def open_layer(n):
        acc[...] = u[...] + vecs[n, 0:1]

    def fetch_self(layer, r):
        first = pl.ds(0, 3 * width)
        last = pl.ds(3 * width, width)
        if layer == 0:
            wanted = [
                (TEXT_IN, 0, 3 * width, ws.at[r, first], ("s1p", "s1v")),
                (TEXT_OUT, 0, width, ws.at[r, last], ("s1o",)),
            ]
        else:
            wanted = [
                (JOIN_IN, 0, 3 * width, ws.at[r, first], ("s2p", "s2v")),
                (JOIN_OUT, 0, width, ws.at[r, last], ("s2o",)),
            ]
        fetch(("self", layer, r), r, wanted)

    def self_unit(layer, r):
        fetch_self(layer, r)
        arrive(("self", layer, r))
        xb = ub[...]
        q = (
            dot_nt(xb, ws[r, 0:width]) + bias[r, 2 * layer : 2 * layer + 1, 0:width]
        ).astype(BF)
        k = dot_nt(xb, ws[r, width : 2 * width]).astype(BF)
        v = (
            dot_nt(xb, ws[r, 2 * width : 3 * width])
            + bias[r, 2 * layer + 1 : 2 * layer + 2, 0:width]
        ).astype(BF)
        q_st[r], k_st[r], v_st[r] = q, k, v
        q_s[...], k_s[...], v_s[...] = q.astype(F32), k.astype(F32), v.astype(F32)
        for i in range(items):
            rows = pl.ds(i * slots, slots)
            probs, a = item_forward(
                q_s[rows], k_s[rows].astype(BF), v_s[rows].astype(BF), masks, lengths[i]
            )
            p_st[r, i] = probs
            a_s[rows] = a
        ab = a_s[...].astype(BF)
        a_st[r] = ab
        acc[...] += dot_nn(ab, ws[r, 3 * width : 4 * width])

    def self_close(layer):
        for source, target in zip(self_st, self_out[layer]):
            pending["self"].append(store(source, target))

    def fetch_feed(layer, r, late=False):
        a = (EXPAND_ONE, EXPAND_TWO)[layer]
        fetch(("expand", layer, r), r, [(a, 0, model, wf.at[r, 0], (("e1", "e2")[layer],))])
        if not late:
            fetch_contract(layer, r)

    def fetch_contract(layer, r):
        b = (CONTRACT_ONE, CONTRACT_TWO)[layer]
        name = ("k1", "k2")[layer]
        fetch(("contract", layer, r), r, [(b, 0, hidden, wf.at[r, 1], (name,))])

    def feed_unit(layer, r):
        fetch_feed(layer, r, True)
        arrive(("expand", layer, r))
        z = dot_nn(ub[...], wf[r, 0]) + bias[r, 6 + layer : 7 + layer, 0:hidden]
        cdf = 0.5 * (1.0 + lax.erf(z * 0.7071067811865476))
        slope = cdf + z * (jnp.exp(-0.5 * z * z) * 0.3989422804014327)
        h = (z * cdf).astype(BF)
        h_st[r] = h
        slope_st[r] = slope.astype(BF)
        fetch_contract(layer, r)
        arrive(("contract", layer, r))
        acc[...] += dot_nn(h, wf[r, 1])

    def feed_close(layer):
        for source, target in zip(feed_st, feed_out[layer]):
            pending["feed"].append(store(source, target))

    def fetch_keys(r):
        fetch(("keys", r), r, [(KEY_VALUE, 0, middle, wk.at[r], ("ckv",))])

    def keys_unit(r):
        fetch_keys(r)
        arrive(("keys", r))
        chunk = 2 * padded
        for m in range(items // 2):
            rows = slice(m * chunk, (m + 1) * chunk)
            kc_st[r, rows] = dot_nt(pf[rows], wk[r, 0:width]).astype(BF)
            vc_st[r, rows] = (
                dot_nt(pf[rows], wk[r, width:middle]) + bias[r, 5:6, 0:width]
            ).astype(BF)

    def fetch_cross(r):
        wanted = [
            (JOIN_IN, 3 * width, 4 * width, wc.at[r, pl.ds(0, width)], ("cq",)),
            (CROSS_OUT, 0, width, wc.at[r, pl.ds(width, width)], ("co",)),
        ]
        fetch(("cross", r), r, wanted)

    def cross_unit(r):
        fetch_cross(r)
        arrive(("cross", r))
        q = (dot_nt(ub[...], wc[r, 0:width]) + bias[r, 4:5, 0:width]).astype(BF)
        qc_st[r] = q
        q_s[...] = q.astype(F32)
        for i in range(items):
            rows = pl.ds(i * slots, slots)
            keys = pl.ds(i * padded, padded)
            probs, a = item_forward(q_s[rows], kc_st[r, keys], vc_st[r, keys], masks, patches)
            pc_st[r, i] = probs
            a_s[rows] = a
        ab = a_s[...].astype(BF)
        ac_st[r] = ab
        acc[...] += dot_nn(ab, wc[r, width:middle])

    def near_start(*arrays):
        for a in arrays:
            near[a].advance()

    move("s1p e1 k1")
    near_start(TEXT_IN, TEXT_OUT)
    bias[0] = jnp.zeros(bias.shape[1:], F32)
    bias[0, 0:2, 0:width] = bias_in[0][...].astype(F32)
    bias[0, 2:6, 0:width] = bias_in[1][...].astype(F32)
    bias[0, 6:7] = bias_in[2][...].astype(F32).reshape(1, hidden)
    bias[0, 7:8] = bias_in[3][...].astype(F32).reshape(1, hidden)
    bias_near.advance()
    bias_far.advance()
    near_start(KEY_VALUE)
    fetch_self(0, 0)
    fetch_keys(0)
    norm_rows(vecs, vecs_in[0:3], vecs_in[3:6])
    u[...] = x[...].astype(F32)
    ub[...] = x[...]
    open_layer(0)
    self_unit(0, 0)
    move("s1p s1v s1o")
    bias_near.need()
    fetch_self(0, 1)
    self_unit(0, 1)
    move("e1 s1p k1")
    bias_far.need()
    bias_last.advance()
    near_start(EXPAND_ONE, CONTRACT_ONE)
    pf_copy.wait()
    spread_patches(pf_raw, pf_wide, pf, items, padded)
    store(pf, pf_out)
    keys_unit(0)
    move("s1p e1")
    fetch_keys(1)
    keys_unit(1)
    move("k1 s2p e1 s1p")
    bias_last.need()
    move("s1v s1o ckv")
    near_start(JOIN_IN, JOIN_OUT)
    fetch_self(0, 2)
    fetch_self(0, 3)
    self_unit(0, 2)
    fetch_feed(0, 0)
    self_unit(0, 3)
    self_close(0)
    close_layer(0)
    open_layer(1)
    move("k1 s2p e2 k2")
    fetch_feed(0, 1)
    feed_unit(0, 0)
    feed_unit(0, 1)
    move("e1 s2p e2 k2")
    fetch_feed(0, 2, True)
    fetch_feed(0, 3, True)
    move("s2p e2 ckv s2v s2o")
    fetch_keys(2)
    fetch_keys(3)
    keys_unit(2)
    keys_unit(3)
    for source, target in zip(cross_st[1:3], cross_out[1:3]):
        store(source, target)
    move("k1 e2")
    near_start(CROSS_OUT, EXPAND_TWO, CONTRACT_TWO)
    fetch_contract(0, 2)
    fetch_contract(0, 3)
    feed_unit(0, 2)
    fetch_self(1, 0)
    feed_unit(0, 3)
    feed_close(0)
    close_layer(1, text_out)
    open_layer(2)
    settle("self")
    move("s2p k2 cq co")
    fetch_self(1, 1)
    self_unit(1, 0)
    self_unit(1, 1)
    move("s2v s2o k2")
    fetch_self(1, 2)
    fetch_self(1, 3)
    self_unit(1, 2)
    fetch_cross(0)
    self_unit(1, 3)
    self_close(1)
    close_layer(2)
    open_layer(3)
    move("e2")
    fetch_cross(1)
    cross_unit(0)
    fetch_feed(1, 0)
    cross_unit(1)
    move("cq co")
    fetch_cross(2)
    fetch_cross(3)
    cross_unit(2)
    fetch_feed(1, 1)
    cross_unit(3)
    for n in (0, 3, 4):
        store(cross_st[n], cross_out[n])
    close_layer(3)
    open_layer(4)
    settle("feed")
    move("k2")
    fetch_feed(1, 2, True)
    fetch_feed(1, 3, True)
    feed_unit(1, 0)
    feed_unit(1, 1)
    feed_unit(1, 2)
    feed_unit(1, 3)
    feed_close(1)
    close_layer(4, join_out)

    for copy in stores:
        if copy is not None:
            copy.wait()
    for flow in flows.values():
        flow.close()
    for direct in near + [bias_near, bias_far, bias_last]:
        direct.close()


def forward_all(links, own, biases, vecs, lengths, x, patch_rows, width):
    patches, items, features = patch_rows.shape
    rows, model = x.shape
    slots, padded = rows // items, -(-patches // 16) * 16
    hidden = own[EXPAND_ONE].shape[1]
    heads = width // HEAD_DIM
    anywhere = pl.BlockSpec(memory_space=ANY)
    vmem = pl.BlockSpec(memory_space=pltpu.VMEM)
    sizes = (links.tensor, links.dp, items, slots, patches, padded, width)
    mid = ((4, rows, width), BF)
    key = ((4, items * padded, width), BF)
    probs = ((4, items, heads * slots, slots), BF)
    cross_probs = ((4, items, heads * slots, padded), BF)
    feed = ((4, rows, hidden), BF)
    pf = ((items * padded, features), BF)
    self_kept = [mid] * 4 + [probs]
    cross_kept = [mid, key, key, mid, cross_probs]
    kept = self_kept * 2 + cross_kept + [feed] * 4
    outputs = [((3,) + a.shape, BF) for a in own]
    outputs += [((rows, model), BF)] * 2 + [((5, rows, model), F32), pf] + kept
    remotes = 13 * (2 + links.bits) + ARRAYS + 3
    outs = pl.pallas_call(
        functools.partial(forward_kernel, sizes),
        in_specs=[anywhere] * ARRAYS
        + [vmem] * 10
        + [pl.BlockSpec(memory_space=pltpu.SMEM), vmem, anywhere],
        out_specs=[anywhere] * ARRAYS + [vmem] * 2 + [anywhere] * (2 + len(kept)),
        out_shape=[jax.ShapeDtypeStruct(shape, dtype) for shape, dtype in outputs],
        scratch_shapes=[
            pltpu.VMEM((4, 4 * width, model), BF),
            pltpu.VMEM((4, 2, model, hidden), BF),
            pltpu.VMEM((4, 2 * width, model), BF),
            pltpu.VMEM((4, 2 * width, features), BF),
            pltpu.VMEM((rows, model), F32),
            pltpu.VMEM((rows, model), F32),
            pltpu.VMEM((rows, model), BF),
            pltpu.VMEM((5, rows, model), F32),
            pltpu.VMEM(patch_rows.shape, BF),
            pltpu.VMEM((features // 128, items * padded, 128), F32),
            pltpu.VMEM(*pf),
            pltpu.VMEM((5, 3, model), F32),
        ]
        + [pltpu.VMEM(*item) for item in self_kept + cross_kept + [feed] * 2]
        + [pltpu.VMEM((rows, width), F32)] * 4
        + [
            pltpu.VMEM((4, 8, model), F32),
            pltpu.SemaphoreType.DMA((remotes,)),
            pltpu.SemaphoreType.DMA((remotes,)),
            pltpu.SemaphoreType.DMA((64,)),
            pltpu.SemaphoreType.DMA((32,)),
            pltpu.SemaphoreType.DMA,
        ],
        compiler_params=pltpu.CompilerParams(
            collective_id=1, has_side_effects=True, vmem_limit_bytes=60 * 1024 * 1024
        ),
        name="forward_and_gather",
    )(*own, *biases, *vecs, lengths, x, patch_rows)
    n = ARRAYS
    got, (text_out, join_out, e, pf), kept = outs[:n], outs[n : n + 4], outs[n + 4 :]
    return got, text_out, join_out, e, pf, kept


(
    GRAD_CONTRACT_TWO,
    GRAD_EXPAND_TWO,
    GRAD_CROSS,
    GRAD_TWO,
    GRAD_CONTRACT_ONE,
    GRAD_EXPAND_ONE,
    GRAD_ONE,
) = range(7)


def backward_kernel(sizes, *refs):
    n_tensor, n_dp, items, slots, patches, padded, width, chunk, counts = sizes
    refs = list(refs)

    def take(n):
        got, refs[:n] = refs[:n], []
        return got

    own, got = take(ARRAYS), take(ARRAYS)
    e_in, pf_in, x, text_out, text_cot, join_cot = take(6)
    vecs_in = take(6)
    self_in = [take(5), take(5)]
    cross_in = take(5)
    feed_in = [take(2), take(2)]
    keeps, sends, outs = take(7), take(7), take(7)
    small_out, grad_text, dpf = take(3)
    wbuf, wk, stage_buf, e_s, ub, dob, acc, pacc, pf, vecs = take(10)
    q_b, k_b, v_b, a_b, p_b = self_buf = take(5)
    qc_b, kc_b, vc_b, ac_b, pc_b = cross_buf = take(5)
    h_b, slope_b = take(2)
    q_s, k_s, v_s, da_s, dq_s, dk_s, dv_s = take(7)
    dkv_s, small_keep, small_send = take(3)
    fetch_sem, store_sem, e_sem, pf_sem = take(4)
    model = x.shape[1]
    hidden = own[EXPAND_ONE].shape[1]
    side = pf.shape[1] - model

    sums = Sums(
        n_tensor,
        n_dp,
        counts,
        chunk,
        sends,
        keeps,
        outs,
        (small_send, small_keep, small_out),
        refs,
    )

    norm_rows(vecs, vecs_in[0:3], vecs_in[3:6])
    pf_copy = pltpu.make_async_copy(pf_in, pf, pf_sem)
    e_copies = [
        pltpu.make_async_copy(e_in.at[n], e_s.at[n], e_sem.at[n]) for n in range(5)
    ]
    for n in (4, 3, 2, 1, 0):
        e_copies[n].start()
    pf_copy.start()

    units = []
    for layer in (1, 0):
        expand, contract = ((EXPAND_ONE, CONTRACT_ONE), (EXPAND_TWO, CONTRACT_TWO))[layer]
        for r in range(4):
            units.append(("contract", layer, r, [(feed_in[layer][0].at[r], h_b)]))
        for r in range(4):
            units.append(
                (
                    "expand",
                    layer,
                    r,
                    [
                        (contract, 0, hidden, wbuf, hidden),
                        (expand, 0, model, wbuf, 0),
                        (feed_in[layer][1].at[r], slope_b),
                    ],
                )
            )
        for r in range(4):
            if layer == 1:
                units.append(
                    (
                        "cross",
                        0,
                        r,
                        [
                            (CROSS_OUT, 0, width, wbuf, width),
                            (JOIN_IN, 3 * width, width, wbuf, 0),
                            (KEY_VALUE, 0, 2 * width, wk, 0),
                        ]
                        + [(cross_in[n].at[r], cross_buf[n]) for n in (3, 0, 1, 2, 4)],
                    )
                )
        for r in range(4):
            first, last = ((TEXT_IN, TEXT_OUT), (JOIN_IN, JOIN_OUT))[layer]
            units.append(
                (
                    "self",
                    layer,
                    r,
                    [(last, 0, width, wbuf, 3 * width), (first, 0, 3 * width, wbuf, 0)]
                    + [(self_in[layer][n].at[r], self_buf[n]) for n in (4, 0, 1, 2, 3)],
                )
            )
    position = {unit[:3]: n for n, unit in enumerate(units)}

    def fetches(n):
        _, _, r, wanted = units[n]
        parity = n % 2
        copies = []
        for i, item in enumerate(wanted):
            if len(item) == 5:
                a, low, count, target, row = item
                source = (own[a] if r == 0 else got[a].at[r - 1]).at[pl.ds(low, count)]
                target = target.at[parity, pl.ds(row, count)]
            else:
                source, target = item
                target = target.at[parity]
            copies.append(pltpu.make_async_copy(source, target, fetch_sem.at[parity, i]))
        return copies

    def begin(n):
        if n + 1 < len(units):
            for copy in fetches(n + 1):
                copy.start()
        for copy in fetches(n):
            copy.wait()
        return n % 2

    stores = {}

    def room(r):
        j = r % 2
        if stores.get(j) is not None:
            stores[j].wait()
            stores[j] = None
        return j

    def put(array, r):
        j = r % 2
        target = (keeps, sends)[j][array]
        rows = target.shape[1]
        stores[j] = pltpu.make_async_copy(
            stage_buf.at[j, pl.ds(0, rows)], target.at[r // 2], store_sem.at[j]
        )
        stores[j].start()

    def settle():
        for j in (0, 1):
            room(j)

    def small_row(r, row, value):
        target = (small_keep, small_send)[r % 2]
        n = 8 * (r // 2) + row
        target[n : n + 1, 0 : value.shape[1]] = value

    def open_layer(n, dy):
        e_copies[n].wait()
        de, partial = norm_backward(e_s[n], vecs[n, 1:2], dy)
        for target in (small_keep, small_send):
            target[16 + 3 * n : 19 + 3 * n] = partial
        dob[...] = de.astype(BF)
        acc[...] = de

    def input_rows(n):
        ub[...] = norm_forward(e_s[n], vecs[n, 1:2], vecs[n, 2:3]).astype(BF)

    def contract_unit(layer, r):
        b = begin(position["contract", layer, r])
        j = room(r)
        stage_buf[j, 0:hidden] = dot_tn(h_b[b], dob[...]).astype(BF)
        put((GRAD_CONTRACT_ONE, GRAD_CONTRACT_TWO)[layer], r)

    def expand_unit(layer, r):
        b = begin(position["expand", layer, r])
        dh = dot_nt(dob[...], wbuf[b, hidden : 2 * hidden])
        dz = (dh * slope_b[b].astype(F32)).astype(BF)
        j = room(r)
        stage_buf[j, 0:model] = dot_tn(ub[...], dz).astype(BF)
        put((GRAD_EXPAND_ONE, GRAD_EXPAND_TWO)[layer], r)
        small_row(r, 6 + layer, jnp.sum(dz.astype(F32), axis=0, keepdims=True))
        acc[...] += dot_nt(dz, wbuf[b, 0:model])

    masks = head_masks(width)

    def self_unit(layer, r):
        b = begin(position["self", layer, r])
        da_s[...] = dot_nt(dob[...], wbuf[b, 3 * width : 4 * width])
        j = room(r)
        stage_buf[j, 3 * width : 4 * width] = dot_tn(a_b[b], dob[...]).astype(BF)
        q_s[...], k_s[...], v_s[...] = (
            q_b[b].astype(F32),
            k_b[b].astype(F32),
            v_b[b].astype(F32),
        )
        for i in range(items):
            rows = pl.ds(i * slots, slots)
            dq, dk, dv = item_backward(
                q_s[rows],
                k_s[rows].astype(BF),
                v_s[rows].astype(BF),
                da_s[rows],
                p_b[b, i],
                masks,
            )
            dq_s[rows], dk_s[rows], dv_s[rows] = dq, dk, dv
        xb = ub[...]
        total = acc[...]
        for c, part in enumerate((dq_s, dk_s, dv_s)):
            pb = part[...].astype(BF)
            stage_buf[j, c * width : (c + 1) * width] = dot_tn(pb, xb).astype(BF)
            total = total + dot_nn(pb, wbuf[b, c * width : (c + 1) * width])
            if c != 1:
                small_row(
                    r, 2 * layer + c // 2, jnp.sum(pb.astype(F32), axis=0, keepdims=True)
                )
        acc[...] = total
        put((GRAD_ONE, GRAD_TWO)[layer], r)

    def cross_unit(r):
        b = begin(position["cross", 0, r])
        da_s[...] = dot_nt(dob[...], wbuf[b, width : 2 * width])
        j = room(r)
        stage_buf[j, width : 2 * width] = dot_tn(ac_b[b], dob[...]).astype(BF)
        q_s[...] = qc_b[b].astype(F32)
        vsum = jnp.zeros((1, width), F32)
        for i in range(items):
            rows = pl.ds(i * slots, slots)
            keys = pl.ds(i * padded, padded)
            dq, dk, dv = item_backward(
                q_s[rows], kc_b[b, keys], vc_b[b, keys], da_s[rows], pc_b[b, i], masks
            )
            dq_s[rows] = dq
            dkv_s[0, keys] = dk.astype(BF)
            dvb = dv.astype(BF)
            dkv_s[1, keys] = dvb
            vsum = vsum + jnp.sum(dvb.astype(F32), axis=0, keepdims=True)
        ticks(1)
        dqb = dq_s[...].astype(BF)
        stage_buf[j, 0:width] = dot_tn(dqb, ub[...]).astype(BF)
        acc[...] += dot_nn(dqb, wbuf[b, 0:width])
        small_row(r, 4, jnp.sum(dqb.astype(F32), axis=0, keepdims=True))
        small_row(r, 5, vsum)
        tails = []
        for c in range(2):
            part = dkv_s[c]
            grad = dot_tn(part, pf[...]).astype(BF)
            stage_buf[j, (2 + c) * width : (3 + c) * width] = grad[:, 0:model]
            tails.append(grad[:, model:])
            back = dot_nn(part, wk[b, c * width : (c + 1) * width])
            for n in range(pacc.shape[0]):
                lanes = back[:, n * 128 : (n + 1) * 128]
                if r == 0 and c == 0:
                    pacc[n] = lanes
                else:
                    pacc[n] += lanes
        tail = jnp.concatenate(tails, axis=0)
        count = tail.shape[0] // (model // side)
        for c in range(model // side):
            stage_buf[j, 4 * width : 4 * width + count, c * side : (c + 1) * side] = tail[
                c * count : (c + 1) * count
            ]
        extra = stage_buf.shape[1] - 4 * width - count
        if extra > 0:
            stage_buf[j, 4 * width + count :] = jnp.zeros((extra, model), BF)
        put(GRAD_CROSS, r)

    small_keep[...] = jnp.zeros_like(small_keep)
    small_send[...] = jnp.zeros_like(small_send)
    for copy in fetches(0):
        copy.start()
    open_layer(4, join_cot[...].astype(F32))
    sums.greet()
    clock = [0]

    def ticks(count):
        for _ in range(count):
            sums.tick(clock[0])
            clock[0] += 1

    def collected(n):
        e_copies[n].wait()
        e_copies[n] = Done()

    for r in range(4):
        contract_unit(1, r)
    settle()
    ticks(1)
    collected(3)
    input_rows(3)
    for r in range(4):
        expand_unit(1, r)
        if r == 3:
            settle()
        ticks(1)
    open_layer(3, acc[...])
    collected(2)
    input_rows(2)
    pf_copy.wait()
    for r in range(4):
        cross_unit(r)
        if r == 3:
            settle()
        ticks(1)
    open_layer(2, acc[...])
    ub[...] = text_out[...]
    for r in range(4):
        self_unit(1, r)
        if r == 3:
            settle()
        ticks((1, 2, 1, 2)[r])
    open_layer(1, acc[...] + text_cot[...].astype(F32))
    for r in range(4):
        contract_unit(0, r)
    settle()
    ticks(1)
    collected(0)
    input_rows(0)
    for r in range(4):
        expand_unit(0, r)
        if r == 3:
            settle()
        ticks(1)
    open_layer(0, acc[...])
    ub[...] = x[...]
    for r in range(4):
        self_unit(0, r)
        if r == 3:
            settle()
        ticks((1, 2, 1, 2)[r])
    grad_text[...] = acc[...].astype(BF)

    def gather_patches(n, carry):
        for c in range(pacc.shape[0]):
            dpf[n, :, c * 128 : (c + 1) * 128] = pacc[
                c, pl.ds(n, items, stride=padded)
            ].astype(BF)
        return carry

    lax.fori_loop(0, patches, gather_patches, 0)
    sums.finish(clock[0])


class Done:
    def wait(self):
        pass


def backward_all(links, own, got, e, pf, x, text_out, cots, vecs, kept, patches, items, width):
    rows, model = x.shape
    slots, padded = rows // items, pf.shape[0] // items
    hidden = own[EXPAND_ONE].shape[1]
    heads = width // HEAD_DIM
    chunk = links.chunk
    anywhere = pl.BlockSpec(memory_space=ANY)
    vmem = pl.BlockSpec(memory_space=pltpu.VMEM)
    cross_rows = 2 * width + 2 * width * pf.shape[1] // model
    extents = [hidden, model, cross_rows, 4 * width, hidden, model, 4 * width]
    extents = [-(-extent // chunk) * chunk for extent in extents]
    counts = tuple(extent // chunk for extent in extents)
    sizes = (links.tensor, links.dp, items, slots, patches, padded, width, chunk, counts)
    pairs = [((2, extent, model), BF) for extent in extents]
    totals = [((extent, model), BF) for extent in extents]
    units, small = 8, 32
    outputs = pairs * 2 + totals
    outputs += [
        ((small - units, model), F32),
        ((rows, model), BF),
        ((patches, items, pf.shape[1]), BF),
    ]
    f32_rows = pltpu.VMEM((rows, width), F32)
    outs = pl.pallas_call(
        functools.partial(backward_kernel, sizes),
        in_specs=[anywhere] * (2 * ARRAYS + 2) + [vmem] * 10 + [anywhere] * len(kept),
        out_specs=[anywhere] * 21 + [vmem] * 3,
        out_shape=[jax.ShapeDtypeStruct(shape, dtype) for shape, dtype in outputs],
        scratch_shapes=[
            pltpu.VMEM((2, 2 * hidden, model), BF),
            pltpu.VMEM((2, 2 * width, pf.shape[1]), BF),
            pltpu.VMEM((2, max(extents), model), BF),
            pltpu.VMEM((5, rows, model), F32),
            pltpu.VMEM((rows, model), BF),
            pltpu.VMEM((rows, model), BF),
            pltpu.VMEM((rows, model), F32),
            pltpu.VMEM((pf.shape[1] // 128, pf.shape[0], 128), F32),
            pltpu.VMEM(pf.shape, BF),
            pltpu.VMEM((5, 3, model), F32),
        ]
        + [pltpu.VMEM((2, rows, width), BF)] * 4
        + [pltpu.VMEM((2, items, heads * slots, slots), BF)]
        + [pltpu.VMEM((2, rows, width), BF)]
        + [pltpu.VMEM((2, pf.shape[0], width), BF)] * 2
        + [pltpu.VMEM((2, rows, width), BF)]
        + [pltpu.VMEM((2, items, heads * slots, padded), BF)]
        + [pltpu.VMEM((2, rows, hidden), BF)] * 2
        + [f32_rows] * 7
        + [
            pltpu.VMEM((2, pf.shape[0], width), BF),
            pltpu.VMEM((small, model), F32),
            pltpu.VMEM((small, model), F32),
            pltpu.SemaphoreType.DMA((2, 8)),
            pltpu.SemaphoreType.DMA((2,)),
            pltpu.SemaphoreType.DMA((5,)),
            pltpu.SemaphoreType.DMA,
        ]
        + Sums.scratch(links.dp, chunk, model, small, units),
        compiler_params=pltpu.CompilerParams(
            collective_id=0, has_side_effects=True, vmem_limit_bytes=60 * 1024 * 1024
        ),
        name="backward_and_sums",
    )(*own, *got, e, pf, x, text_out, *cots, *vecs, *kept)
    return outs[14:21], outs[21], outs[22], outs[23]


def finish_kernel(width, *refs):
    refs = list(refs)

    def take(n):
        got, refs[:n] = refs[:n], []
        return got

    totals, passed, (small,) = take(7), take(4), take(1)
    passed_out = take(4)
    text_in, text_out, expand_one, contract_one, join_in = take(5)
    join_out, cross_out, key_value, expand_two, contract_two = take(5)
    text_bias, join_bias, hidden_one, hidden_two = take(4)
    text_shared, join_shared = take(3), take(3)
    half, full, keys = take(3)
    bounced = take(4)
    load_sem, store_sem = take(2)
    model = full.shape[2]
    side = keys.shape[1] - model
    count = 2 * width * side // model

    loads, stores = [], []
    for n in range(7):
        rows = totals[n].shape[0]
        loads.append(
            pltpu.make_async_copy(totals[n], half.at[n, pl.ds(0, rows)], load_sem.at[n])
        )
        loads[n].start()
    for n in range(4):
        loads.append(pltpu.make_async_copy(passed[n], bounced[n], load_sem.at[7 + n]))
        loads[7 + n].start()

    def store(source, target):
        copy = pltpu.make_async_copy(source, target, store_sem.at[len(stores)])
        copy.start()
        stores.append(copy)

    text_bias[...] = small[0:2, 0:width]
    join_bias[...] = small[2:6, 0:width]
    hidden_one[...] = small[6]
    hidden_two[...] = small[7]
    for n in range(5):
        for c in range(3):
            row = 8 + 3 * n + c
            target, m = (text_shared[c], n) if n < 2 else (join_shared[c], n - 2)
            target[m : m + 1] = small[row : row + 1]

    def widen(n):
        loads[n].wait()
        rows = totals[n].shape[0]
        full[n, 0:rows] = half[n, 0:rows].astype(F32)

    def send(n, lo, rows, target):
        store(full.at[n, pl.ds(lo, rows)], target)

    for n, target in (
        (GRAD_CONTRACT_TWO, contract_two),
        (GRAD_EXPAND_TWO, expand_two),
        (GRAD_CONTRACT_ONE, contract_one),
        (GRAD_EXPAND_ONE, expand_one),
    ):
        widen(n)
        send(n, 0, target.shape[0], target)
    widen(GRAD_CROSS)
    send(GRAD_CROSS, 0, width, join_in.at[pl.ds(3 * width, width)])
    send(GRAD_CROSS, width, width, cross_out)
    keys[:, 0:model] = full[GRAD_CROSS, 2 * width : 4 * width]
    for c in range(model // side):
        keys[c * count : (c + 1) * count, model:] = full[
            GRAD_CROSS, 4 * width : 4 * width + count, c * side : (c + 1) * side
        ]
    store(keys, key_value)
    widen(GRAD_TWO)
    send(GRAD_TWO, 0, 3 * width, join_in.at[pl.ds(0, 3 * width)])
    send(GRAD_TWO, 3 * width, width, join_out)
    widen(GRAD_ONE)
    send(GRAD_ONE, 0, 3 * width, text_in)
    send(GRAD_ONE, 3 * width, width, text_out)
    for n in range(4):
        loads[7 + n].wait()
        store(bounced[n], passed_out[n])
    for copy in stores:
        copy.wait()


def finish_all(totals, passed, small, width, hidden, features):
    model = totals[0].shape[1]
    anywhere = pl.BlockSpec(memory_space=ANY)
    vmem = pl.BlockSpec(memory_space=pltpu.VMEM)
    big = [
        (3 * width, model),
        (width, model),
        (model, hidden),
        (hidden, model),
        (4 * width, model),
        (width, model),
        (width, model),
        (2 * width, features),
        (model, hidden),
        (hidden, model),
    ]
    little = [(2, width), (4, width), (hidden,), (hidden,)]
    little += [(2, model)] * 3 + [(3, model)] * 3
    most = max(total.shape[0] for total in totals)
    return pl.pallas_call(
        functools.partial(finish_kernel, width),
        in_specs=[anywhere] * 11 + [vmem],
        out_specs=[anywhere] * (4 + len(big)) + [vmem] * len(little),
        out_shape=[jax.ShapeDtypeStruct(a.shape, a.dtype) for a in passed]
        + [jax.ShapeDtypeStruct(shape, F32) for shape in big + little],
        scratch_shapes=[
            pltpu.VMEM((7, most, model), BF),
            pltpu.VMEM((7, most, model), F32),
            pltpu.VMEM((2 * width, features), F32),
        ]
        + [pltpu.VMEM(a.shape, a.dtype) for a in passed]
        + [
            pltpu.SemaphoreType.DMA((11,)),
            pltpu.SemaphoreType.DMA((16,)),
        ],
        compiler_params=pltpu.CompilerParams(vmem_limit_bytes=60 * 1024 * 1024),
        name="finish",
    )(*totals, *passed, small)


class Links:
    def __init__(self, mesh):
        self.tensor = mesh.shape["tensor"]
        self.dp = mesh.shape["dp"]
        self.bits = self.dp.bit_length() - 1
        self.chunk = 128


def turned(array):
    array = jnp.swapaxes(array, 1, 2)
    return array.reshape(-1, array.shape[2])


def turned_back(rows, units):
    return jnp.swapaxes(rows.reshape(-1, units, rows.shape[1]), 1, 2)


def per_device(
    links,
    text_rows,
    patch_features,
    lengths,
    text_cotangent,
    join_cotangent,
    text_project_in,
    text_project_bias,
    text_project_out,
    text_expand,
    text_expand_bias,
    text_contract,
    text_out_bias,
    text_norm_gain,
    text_norm_shift,
    join_project_in,
    join_project_bias,
    join_project_out,
    cross_project_out,
    cross_key_value,
    join_expand,
    join_expand_bias,
    join_contract,
    join_out_bias,
    join_norm_gain,
    join_norm_shift,
):
    items, slots, model = text_rows.shape
    patches, patch_width = patch_features.shape[1:]
    width = text_project_in.shape[2]
    hidden = text_expand.shape[1]

    own = [
        turned(text_project_in),
        text_project_out,
        text_expand,
        text_contract,
        turned(join_project_in),
        join_project_out,
        turned(cross_key_value),
        cross_project_out,
        join_expand,
        join_contract,
    ]
    biases = (text_project_bias, join_project_bias, text_expand_bias, join_expand_bias)
    vecs = (text_out_bias, text_norm_gain, text_norm_shift)
    vecs += (join_out_bias, join_norm_gain, join_norm_shift)
    x = text_rows.reshape(items * slots, model)
    text_cot = text_cotangent.reshape(items * slots, model)
    join_cot = join_cotangent.reshape(items * slots, model)
    patch_rows = jnp.swapaxes(patch_features, 0, 1)

    got, text_out, join_out, e, pf, kept = forward_all(
        links, own, biases, vecs, lengths, x, patch_rows, width
    )
    totals, small, grad_text, grad_patches = backward_all(
        links, own, got, e, pf, x, text_out, (text_cot, join_cot), vecs, kept, patches, items, width
    )
    outs = finish_all(
        totals, (text_out, join_out, grad_text, grad_patches), small, width, hidden, patch_width
    )
    text_out, join_out, grad_text, grad_patches = outs[:4]
    text_in, text_project, expand_one, contract_one, join_in = outs[4:9]
    join_project, cross_project, key_value, expand_two, contract_two = outs[9:14]
    text_bias, join_bias, hidden_one, hidden_two = outs[14:18]

    return (
        text_out.reshape(text_rows.shape),
        join_out.reshape(text_rows.shape),
        grad_text.reshape(text_rows.shape),
        jnp.swapaxes(grad_patches, 0, 1),
        turned_back(text_in, width),
        text_bias,
        text_project,
        expand_one,
        hidden_one,
        contract_one,
        *outs[18:21],
        turned_back(join_in, width),
        join_bias,
        join_project,
        cross_project,
        turned_back(key_value, width),
        expand_two,
        hidden_two,
        contract_two,
        *outs[21:24],
    )


def solution(mesh):
    rows = P(("dp", "tensor"), None, None)
    last = P(None, None, "tensor")
    second = P(None, "tensor")
    first = P("tensor", None)
    line = P("tensor")
    full = P()
    in_specs = (
        (rows, rows, P(("dp", "tensor")), rows, rows)
        + (last, second, first, second, line, first, full, full, full)
        + (last, second, first, first, last, second, line, first, full, full, full)
    )
    out_specs = (
        (rows, rows, rows, rows)
        + (last, second, first, second, line, first, full, full, full)
        + (last, second, first, first, last, second, line, first, full, full, full)
    )
    return jax.shard_map(
        functools.partial(per_device, Links(mesh)),
        mesh=mesh,
        in_specs=in_specs,
        out_specs=out_specs,
        check_vma=False,
    )
```

```python
import functools

import jax
import jax.numpy as jnp
from jax import lax
from jax.experimental import pallas as pl
from jax.experimental.pallas import tpu as pltpu
from jax.sharding import PartitionSpec as P

HEAD_DIM = 64
BF = jnp.bfloat16
F32 = jnp.float32
ANY = pl.ANY


def dot_nn(a, b):
    return lax.dot_general(a, b, (((1,), (0,)), ((), ())), preferred_element_type=F32)


def dot_nt(a, b):
    return lax.dot_general(a, b, (((1,), (1,)), ((), ())), preferred_element_type=F32)


def dot_tn(a, b):
    return lax.dot_general(a, b, (((0,), (0,)), ((), ())), preferred_element_type=F32)


def norm_forward(e, gain, shift):
    center = e - jnp.mean(e, axis=-1, keepdims=True)
    variance = jnp.mean(center * center, axis=-1, keepdims=True)
    return center * lax.rsqrt(variance + 1e-12) * gain + shift


def norm_backward(e, gain, dy):
    center = e - jnp.mean(e, axis=-1, keepdims=True)
    variance = jnp.mean(center * center, axis=-1, keepdims=True)
    rstd = lax.rsqrt(variance + 1e-12)
    normed = center * rstd
    scaled = dy * gain
    de = rstd * (
        scaled
        - jnp.mean(scaled, axis=-1, keepdims=True)
        - normed * jnp.mean(scaled * normed, axis=-1, keepdims=True)
    )
    sums = jnp.concatenate(
        [
            jnp.sum(de, axis=0, keepdims=True),
            jnp.sum(dy * normed, axis=0, keepdims=True),
            jnp.sum(dy, axis=0, keepdims=True),
        ],
        axis=0,
    )
    return de, sums


def head_masks(width):
    lane = lax.broadcasted_iota(jnp.int32, (1, width), 1)
    return [
        ((lane >= h * HEAD_DIM) & (lane < (h + 1) * HEAD_DIM)).astype(F32)
        for h in range(width // HEAD_DIM)
    ]


def stack_heads(rows, masks):
    return jnp.concatenate([rows * mask for mask in masks], axis=0).astype(BF)


def merge_heads(stacked, masks):
    count = stacked.shape[0] // len(masks)
    total = stacked[:count] * masks[0]
    for h in range(1, len(masks)):
        total = total + stacked[h * count : (h + 1) * count] * masks[h]
    return total


def item_forward(q, k, v, masks, length):
    scores = dot_nt(k, stack_heads(q, masks)) * HEAD_DIM ** (-0.5)
    row = lax.broadcasted_iota(jnp.int32, scores.shape, 0)
    scores = jnp.where(row < length, scores, -1e30)
    weights = jnp.exp(scores - jnp.max(scores, axis=0, keepdims=True))
    probs = (weights / jnp.sum(weights, axis=0, keepdims=True)).astype(BF)
    return probs, merge_heads(dot_tn(probs, v), masks)


def item_backward(q, k, v, da, probs, masks):
    qs = stack_heads(q, masks)
    das = stack_heads(da, masks)
    dv = dot_nn(probs, das)
    dp = dot_nt(v, das)
    p = probs.astype(F32)
    ds = (p * (dp - jnp.sum(p * dp, axis=0, keepdims=True))).astype(BF)
    scaling = HEAD_DIM ** (-0.5)
    dq = merge_heads(dot_tn(ds, k), masks) * scaling
    dk = dot_nn(ds, qs) * scaling
    return dq, dk, dv


def pair(index, width):
    return index + width - 2 * width * ((index // width) % 2)


def rest(m, n):
    return m % n if isinstance(m, int) else lax.rem(m, n)


def when(condition, act):
    if isinstance(condition, bool):
        if condition:
            act()
    else:
        pl.when(condition)(act)


def halvings(n_dp, chunk):
    return min(n_dp, chunk // 16).bit_length() - 1


class Sums:
    def __init__(self, n_tensor, n_dp, counts, chunk, sends, keeps, outs, small, scratch):
        self.n_dp, self.bits = n_dp, n_dp.bit_length() - 1
        self.counts, self.chunk = counts, chunk
        self.cuts = halvings(n_dp, chunk)
        self.sends, self.keeps, self.outs = sends, keeps, outs
        self.small_send, self.small_keep, self.small_out = small
        scratch = list(scratch)
        bits = self.bits
        self.core_in, self.kept, self.far_out, self.far_in, self.own, self.whole = scratch[:6]
        self.parts, self.halves = scratch[6 : 6 + bits], scratch[6 + bits : 6 + 2 * bits]
        self.gathered, self.tiny_sum, self.tiny_core, self.tiny_far, self.tiny_dp = scratch[
            6 + 2 * bits : 11 + 2 * bits
        ]
        self.send_sem, self.recv_sem, self.kept_sem, self.out_sem = scratch[
            11 + 2 * bits : 15 + 2 * bits
        ]
        self.tiny_send, self.tiny_recv = scratch[15 + 2 * bits :]
        t, d = lax.axis_index("tensor"), lax.axis_index("dp")
        self.dp_bits = [(d // (1 << b)) % 2 for b in range(bits)]
        self.peers = [{"tensor": pair(t, 1)}, {"tensor": lax.rem(t + 2, n_tensor)}]
        self.peers += [{"dp": pair(d, 1 << b)} for b in range(bits)]
        self.total = sum(counts)
        self.stages = 2 + bits + self.cuts
        self.slots, self.depth = self.core_in.shape[0], self.gathered.shape[0]

    def greet(self):
        barrier = pltpu.get_barrier_semaphore()
        for peer in self.peers:
            pl.semaphore_signal(
                barrier, inc=1, device_id=peer, device_id_type=pl.DeviceIdType.MESH
            )
        pl.semaphore_wait(barrier, len(self.peers))

    def remote(self, source, target, stage, slot, peer):
        return pltpu.make_async_remote_copy(
            src_ref=source,
            dst_ref=target,
            send_sem=self.send_sem.at[stage, slot],
            recv_sem=self.recv_sem.at[stage, slot],
            device_id=self.peers[peer],
            device_id_type=pl.DeviceIdType.MESH,
        )

    def region(self, b):
        b = min(b, self.cuts - 1)
        size = self.chunk >> (b + 1)
        start = 0
        for i in range(b + 1):
            start = start + self.dp_bits[i] * (self.chunk >> (i + 1))
        return pl.ds(pl.multiple_of(start, size), size)

    def half(self, b, mine):
        if b >= self.cuts:
            return pl.ds(0, self.chunk >> self.cuts)
        size = self.chunk >> (b + 1)
        which = self.dp_bits[b] if mine else 1 - self.dp_bits[b]
        return pl.ds(pl.multiple_of(which * size, size), size)

    def halved(self, b):
        return self.whole if b == 0 else self.parts[b - 1]

    def copy_of(self, stage, m):
        slot, two = rest(m, self.slots), rest(m, 2)
        if stage == 0:
            source = self.sends[0].at[:, pl.ds(0, self.chunk)]
            return self.remote(source, self.core_in.at[slot], 0, slot, 0)
        if stage == 1:
            ring = rest(m, self.far_in.shape[0])
            return self.remote(self.far_out.at[slot], self.far_in.at[ring], 1, ring, 1)
        if stage < 2 + self.bits:
            b = stage - 2
            source = self.halved(b).at[two, self.half(b, False)]
            return self.remote(source, self.halves[b].at[slot], stage, slot, 2 + b)
        b = 1 + self.bits + self.cuts - stage
        held = self.gathered.at[rest(m, self.depth), self.region(b)]
        return self.remote(held, held, stage, slot, 2 + b)

    def kept_copy(self, a, start, m):
        two = rest(m, 2)
        source = self.keeps[a].at[:, pl.ds(start, self.chunk)]
        return pltpu.make_async_copy(source, self.kept.at[two], self.kept_sem.at[two])

    def out_copy(self, a, start, m):
        ring = rest(m, self.depth)
        target = self.outs[a].at[pl.ds(start, self.chunk)]
        return pltpu.make_async_copy(self.gathered.at[ring], target, self.out_sem.at[ring])

    def each_array(self, m, act):
        base = 0
        for a, count in enumerate(self.counts):
            if isinstance(m, int):
                start = (m - base) * self.chunk
                inside = base <= m < base + count
            else:
                start = pl.multiple_of((m - base) * self.chunk, self.chunk)
                inside = (m >= base) & (m < base + count)
            when(inside, functools.partial(act, a, start))
            base += count

    def process(self, step, m):
        if step == 2:
            return
        stage = step if step < 2 else step - 1
        slot, two, ring = rest(m, self.slots), rest(m, 2), rest(m, self.depth)
        stages, bits = self.stages, self.bits
        if stage == 0:

            def begin(a, start):
                source = self.sends[a].at[:, pl.ds(start, self.chunk)]
                self.remote(source, self.core_in.at[slot], 0, slot, 0).start()
                self.kept_copy(a, start, m).start()

            self.each_array(m, begin)
            return
        if stage <= stages:
            self.copy_of(stage - 1, m).wait()
        if stage == 1:
            self.kept_copy(0, 0, m).wait()
            self.far_out[slot] = self.kept[two, 1] + self.core_in[slot, 1]
            self.own[slot] = self.kept[two, 0] + self.core_in[slot, 0]
        elif stage == 2:
            self.whole[two] = self.own[slot] + self.far_in[rest(m, self.far_in.shape[0])]
        elif stage <= 2 + bits:
            b = stage - 3
            summed = self.halved(b)[two, self.half(b, True)] + self.halves[b][slot]
            if b < bits - 1:
                self.parts[b][two] = summed
            else:
                self.gathered[ring, self.region(b)] = summed
        elif stage == stages:
            self.each_array(m, lambda a, start: self.out_copy(a, start, m).start())
        elif stage == stages + 1:
            self.out_copy(0, 0, m).wait()
        if stage < stages:
            self.copy_of(stage, m).start()

    def tiny(self, stage):
        count = self.tiny_far.shape[0]
        if stage == 0:
            source, target = self.small_send, self.tiny_core
        elif stage == 1:
            first = self.small_keep.shape[0] - count
            source, target = self.tiny_sum.at[0, pl.ds(first, count)], self.tiny_far
        else:
            source = self.tiny_sum.at[stage - 1, pl.ds(0, count)]
            target = self.tiny_dp.at[stage - 2]
        return pltpu.make_async_remote_copy(
            src_ref=source,
            dst_ref=target,
            send_sem=self.tiny_send.at[stage],
            recv_sem=self.tiny_recv.at[stage],
            device_id=self.peers[stage],
            device_id_type=pl.DeviceIdType.MESH,
        )

    def tiny_step(self, stage):
        bits = self.bits
        count = self.tiny_far.shape[0]
        units = self.small_keep.shape[0] - count
        if stage > 0:
            self.tiny(stage - 1).wait()
        if stage == 1:
            self.tiny_sum[0] = self.small_keep[...] + self.tiny_core[...]
        elif stage == 2:
            self.tiny_sum[1, 0:units] = self.tiny_sum[0, 0:units] + self.tiny_far[0:units]
            self.tiny_sum[1, units:count] = (
                self.tiny_sum[0, 2 * units :] + self.tiny_far[units:]
            )
        elif stage > 2:
            summed = self.tiny_sum[stage - 2, 0:count] + self.tiny_dp[stage - 3]
            if stage == 2 + bits:
                self.small_out[...] = summed
            else:
                self.tiny_sum[stage - 1, 0:count] = summed
        if stage < 2 + bits:
            self.tiny(stage).start()

    def tick(self, k):
        for step in range(self.stages + 3):
            m = k - step
            inside = (m >= 0) & (m < self.total)
            when(inside, functools.partial(self.process, step, m))

    def finish(self, first):
        def step(k, carry):
            self.tick(k)
            for stage in range(3 + self.bits):
                when(k == first + stage, functools.partial(self.tiny_step, stage))
            return carry

        lax.fori_loop(first, self.total + self.stages + 3, step, 0)

    @staticmethod
    def scratch(n_dp, chunk, model, small, units):
        bits, cuts = n_dp.bit_length() - 1, halvings(n_dp, chunk)
        slots, far, depth, stages = 4, 6, 8, 2 + bits + cuts
        sizes = [chunk >> min(b + 1, cuts) for b in range(bits)]
        return (
            [
                pltpu.VMEM((slots, 2, chunk, model), BF),
                pltpu.VMEM((2, 2, chunk, model), BF),
                pltpu.VMEM((slots, chunk, model), BF),
                pltpu.VMEM((far, chunk, model), BF),
                pltpu.VMEM((slots, chunk, model), BF),
                pltpu.VMEM((2, chunk, model), BF),
            ]
            + [pltpu.VMEM((2, size, model), BF) for size in sizes]
            + [pltpu.VMEM((slots, size, model), BF) for size in sizes]
            + [
                pltpu.VMEM((depth, chunk, model), BF),
                pltpu.VMEM((1 + bits, small, model), F32),
                pltpu.VMEM((small, model), F32),
                pltpu.VMEM((small - units, model), F32),
                pltpu.VMEM((bits, small - units, model), F32),
                pltpu.SemaphoreType.DMA((stages, far)),
                pltpu.SemaphoreType.DMA((stages, far)),
                pltpu.SemaphoreType.DMA((2,)),
                pltpu.SemaphoreType.DMA((depth,)),
                pltpu.SemaphoreType.DMA((2 + bits,)),
                pltpu.SemaphoreType.DMA((2 + bits,)),
            ]
        )


class Flow:
    def __init__(self, net, a, lo, hi, spread):
        rows = hi - lo
        own, got = net.own[a], net.got[a]
        here = pl.ds(lo, rows)
        self.copies = []
        self.started = self.waited = 0
        if spread and rows % (16 * net.n_dp) == 0:

            def region(count):
                size, start = rows, lo
                for i in range(count):
                    size //= 2
                    start = start + net.dp_bits[i] * size
                return pl.ds(pl.multiple_of(start, 16), size)

            part = region(net.bits)
            self.add(net, own.at[part], got.at[1, part], net.far_peer)
            for b in reversed(range(net.bits)):
                part = region(b + 1)
                self.add(net, got.at[1, part], got.at[1, part], net.dp_peers[b])
        else:
            self.add(net, own.at[here], got.at[1, here], net.far_peer)
        self.add(net, got.at[1, here], got.at[2, here], net.core_peer)

    def add(self, net, source, target, peer):
        self.copies.append(net.remote(source, target, peer))

    def advance(self):
        if self.started < len(self.copies):
            if self.started > 0:
                self.await_copy(self.started - 1)
            self.copies[self.started].start()
            self.started += 1

    def await_copy(self, n):
        while self.started <= n:
            self.advance()
        while self.waited <= n:
            self.copies[self.waited].wait_recv()
            self.waited += 1

    def need(self, r):
        self.await_copy(len(self.copies) - (2 if r == 2 else 1))

    def close(self):
        self.need(3)
        for copy in self.copies:
            copy.wait_send()


class Direct:
    def __init__(self, copy):
        self.copy, self.state = copy, 0

    def advance(self):
        if self.state == 0:
            self.copy.start()
            self.state = 1

    def need(self):
        self.advance()
        if self.state == 1:
            self.copy.wait_recv()
            self.state = 2

    def close(self):
        self.need()
        self.copy.wait_send()


class Net:
    def __init__(self, n_tensor, n_dp, own, got, send_sem, recv_sem):
        self.n_dp, self.bits = n_dp, n_dp.bit_length() - 1
        self.own, self.got = own, got
        self.send_sem, self.recv_sem = send_sem, recv_sem
        self.count = 0
        t, d = lax.axis_index("tensor"), lax.axis_index("dp")
        self.core_peer = {"tensor": pair(t, 1)}
        self.far_peer = {"tensor": lax.rem(t + 2, n_tensor)}
        self.dp_peers = [{"dp": pair(d, 1 << b)} for b in range(self.bits)]
        self.dp_bits = [(d // (1 << b)) % 2 for b in range(self.bits)]
        peers = [self.core_peer, self.far_peer] + self.dp_peers
        barrier = pltpu.get_barrier_semaphore()
        for peer in peers:
            pl.semaphore_signal(
                barrier, inc=1, device_id=peer, device_id_type=pl.DeviceIdType.MESH
            )
        pl.semaphore_wait(barrier, len(peers))

    def remote(self, source, target, peer):
        n = self.count
        self.count += 1
        return pltpu.make_async_remote_copy(
            src_ref=source,
            dst_ref=target,
            send_sem=self.send_sem.at[n],
            recv_sem=self.recv_sem.at[n],
            device_id=peer,
            device_id_type=pl.DeviceIdType.MESH,
        )


TEXT_IN, TEXT_OUT, EXPAND_ONE, CONTRACT_ONE, JOIN_IN = range(5)
JOIN_OUT, KEY_VALUE, CROSS_OUT, EXPAND_TWO, CONTRACT_TWO = range(5, 10)
ARRAYS = 10


def spread_patches(source, wide, target, items, padded):
    patches = source.shape[0]
    least = patches // 8 * 8
    groups, _, lanes = wide.shape
    for i in range(items):
        rows = pl.ds(i * padded + least, padded - least)
        wide[:, rows] = jnp.zeros((groups, padded - least, lanes), F32)

    def step(n, carry):
        for c in range(groups):
            wide[c, pl.ds(n, items, stride=padded)] = source[
                n, :, c * lanes : (c + 1) * lanes
            ].astype(F32)
        return carry

    lax.fori_loop(0, patches, step, 0)
    for c in range(groups):
        target[:, c * lanes : (c + 1) * lanes] = wide[c].astype(BF)


def norm_rows(vecs, text, join):
    for c in range(3):
        for n in range(2):
            vecs[n, c : c + 1] = text[c][...].astype(F32)[n : n + 1]
        for n in range(3):
            vecs[2 + n, c : c + 1] = join[c][...].astype(F32)[n : n + 1]


def forward_kernel(sizes, *refs):
    n_tensor, n_dp, items, slots, patches, padded, width = sizes
    refs = list(refs)

    def take(n):
        got, refs[:n] = refs[:n], []
        return got

    own = take(ARRAYS)
    bias_in, vecs_in = take(4), take(6)
    lengths, x, pf_in = take(3)
    got = take(ARRAYS)
    text_out, join_out, e_out, pf_out = take(4)
    self_out = [take(5), take(5)]
    cross_out = take(5)
    feed_out = [take(2), take(2)]
    ws, wf, wc, wk, acc, u, ub, e_s = take(8)
    pf_raw, pf_wide, pf, vecs = take(4)
    q_st, k_st, v_st, a_st, p_st = self_st = take(5)
    cross_st = take(5)
    qc_st, kc_st, vc_st, ac_st, pc_st = cross_st
    h_st, slope_st = feed_st = take(2)
    q_s, k_s, v_s, a_s, bias = take(5)
    send_sem, recv_sem, fetch_sem, store_sem, pf_sem = take(5)
    model = x.shape[1]
    hidden = own[EXPAND_ONE].shape[1]

    pf_copy = pltpu.make_async_copy(pf_in, pf_raw, pf_sem)
    pf_copy.start()
    net = Net(n_tensor, n_dp, own, got, send_sem, recv_sem)
    middle = 2 * width
    flows = {
        "s1p": Flow(net, TEXT_IN, 0, middle, True),
        "s1v": Flow(net, TEXT_IN, middle, 3 * width, False),
        "s1o": Flow(net, TEXT_OUT, 0, width, False),
        "e1": Flow(net, EXPAND_ONE, 0, model, True),
        "k1": Flow(net, CONTRACT_ONE, 0, hidden, True),
        "s2p": Flow(net, JOIN_IN, 0, middle, True),
        "s2v": Flow(net, JOIN_IN, middle, 3 * width, False),
        "s2o": Flow(net, JOIN_OUT, 0, width, False),
        "ckv": Flow(net, KEY_VALUE, 0, middle, False),
        "cq": Flow(net, JOIN_IN, 3 * width, 4 * width, False),
        "co": Flow(net, CROSS_OUT, 0, width, False),
        "e2": Flow(net, EXPAND_TWO, 0, model, True),
        "k2": Flow(net, CONTRACT_TWO, 0, hidden, True),
    }
    near = [Direct(net.remote(own[a], got[a].at[0], net.core_peer)) for a in range(ARRAYS)]
    bias_near = Direct(net.remote(bias.at[0], bias.at[1], net.core_peer))
    bias_far = Direct(net.remote(bias.at[0], bias.at[2], net.far_peer))
    bias_last = Direct(net.remote(bias.at[2], bias.at[3], net.core_peer))

    def move(names):
        for name in names.split():
            flows[name].advance()

    fetches = {}

    fetch_count = [0]

    def fetch(key, r, wanted):
        if key in fetches:
            return
        fetches[key] = []
        for a, lo, hi, target, names in wanted:
            if r == 1:
                near[a].need()
            elif r > 1:
                for name in names:
                    flows[name].need(r)
            source = own[a] if r == 0 else got[a].at[r - 1]
            copy = pltpu.make_async_copy(
                source.at[pl.ds(lo, hi - lo)], target, fetch_sem.at[fetch_count[0]]
            )
            fetch_count[0] += 1
            copy.start()
            fetches[key].append(copy)

    def arrive(key):
        for copy in fetches[key]:
            copy.wait()

    stores = []

    def store(source, target):
        copy = pltpu.make_async_copy(source, target, store_sem.at[len(stores)])
        copy.start()
        stores.append(copy)
        return len(stores) - 1

    masks = head_masks(width)
    pending = {"self": [], "feed": []}

    def settle(kind):
        for n in pending[kind]:
            stores[n].wait()
            stores[n] = None
        pending[kind] = []

    def close_layer(n, target=None):
        e = acc[...]
        e_s[n] = e
        store(e_s.at[n], e_out.at[n])
        y = norm_forward(e, vecs[n, 1:2], vecs[n, 2:3])
        if target is not None:
            yb = y.astype(BF)
            target[...] = yb
            ub[...] = yb
            u[...] = yb.astype(F32)
        else:
            u[...] = y
            ub[...] = y.astype(BF)

    def open_layer(n):
        acc[...] = u[...] + vecs[n, 0:1]

    def fetch_self(layer, r):
        first = pl.ds(0, 3 * width)
        last = pl.ds(3 * width, width)
        if layer == 0:
            wanted = [
                (TEXT_IN, 0, 3 * width, ws.at[r, first], ("s1p", "s1v")),
                (TEXT_OUT, 0, width, ws.at[r, last], ("s1o",)),
            ]
        else:
            wanted = [
                (JOIN_IN, 0, 3 * width, ws.at[r, first], ("s2p", "s2v")),
                (JOIN_OUT, 0, width, ws.at[r, last], ("s2o",)),
            ]
        fetch(("self", layer, r), r, wanted)

    def self_unit(layer, r):
        fetch_self(layer, r)
        arrive(("self", layer, r))
        xb = ub[...]
        q = (
            dot_nt(xb, ws[r, 0:width]) + bias[r, 2 * layer : 2 * layer + 1, 0:width]
        ).astype(BF)
        k = dot_nt(xb, ws[r, width : 2 * width]).astype(BF)
        v = (
            dot_nt(xb, ws[r, 2 * width : 3 * width])
            + bias[r, 2 * layer + 1 : 2 * layer + 2, 0:width]
        ).astype(BF)
        q_st[r], k_st[r], v_st[r] = q, k, v
        q_s[...], k_s[...], v_s[...] = q.astype(F32), k.astype(F32), v.astype(F32)
        for i in range(items):
            rows = pl.ds(i * slots, slots)
            probs, a = item_forward(
                q_s[rows], k_s[rows].astype(BF), v_s[rows].astype(BF), masks, lengths[i]
            )
            p_st[r, i] = probs
            a_s[rows] = a
        ab = a_s[...].astype(BF)
        a_st[r] = ab
        acc[...] += dot_nn(ab, ws[r, 3 * width : 4 * width])

    def self_close(layer):
        for source, target in zip(self_st, self_out[layer]):
            pending["self"].append(store(source, target))

    def fetch_feed(layer, r, late=False):
        a = (EXPAND_ONE, EXPAND_TWO)[layer]
        fetch(("expand", layer, r), r, [(a, 0, model, wf.at[r, 0], (("e1", "e2")[layer],))])
        if not late:
            fetch_contract(layer, r)

    def fetch_contract(layer, r):
        b = (CONTRACT_ONE, CONTRACT_TWO)[layer]
        name = ("k1", "k2")[layer]
        fetch(("contract", layer, r), r, [(b, 0, hidden, wf.at[r, 1], (name,))])

    def feed_unit(layer, r):
        fetch_feed(layer, r, True)
        arrive(("expand", layer, r))
        z = dot_nn(ub[...], wf[r, 0]) + bias[r, 6 + layer : 7 + layer, 0:hidden]
        cdf = 0.5 * (1.0 + lax.erf(z * 0.7071067811865476))
        slope = cdf + z * (jnp.exp(-0.5 * z * z) * 0.3989422804014327)
        h = (z * cdf).astype(BF)
        h_st[r] = h
        slope_st[r] = slope.astype(BF)
        fetch_contract(layer, r)
        arrive(("contract", layer, r))
        acc[...] += dot_nn(h, wf[r, 1])

    def feed_close(layer):
        for source, target in zip(feed_st, feed_out[layer]):
            pending["feed"].append(store(source, target))

    def fetch_keys(r):
        fetch(("keys", r), r, [(KEY_VALUE, 0, middle, wk.at[r], ("ckv",))])

    def keys_unit(r):
        fetch_keys(r)
        arrive(("keys", r))
        chunk = 2 * padded
        for m in range(items // 2):
            rows = slice(m * chunk, (m + 1) * chunk)
            kc_st[r, rows] = dot_nt(pf[rows], wk[r, 0:width]).astype(BF)
            vc_st[r, rows] = (
                dot_nt(pf[rows], wk[r, width:middle]) + bias[r, 5:6, 0:width]
            ).astype(BF)

    def fetch_cross(r):
        wanted = [
            (JOIN_IN, 3 * width, 4 * width, wc.at[r, pl.ds(0, width)], ("cq",)),
            (CROSS_OUT, 0, width, wc.at[r, pl.ds(width, width)], ("co",)),
        ]
        fetch(("cross", r), r, wanted)

    def cross_unit(r):
        fetch_cross(r)
        arrive(("cross", r))
        q = (dot_nt(ub[...], wc[r, 0:width]) + bias[r, 4:5, 0:width]).astype(BF)
        qc_st[r] = q
        q_s[...] = q.astype(F32)
        for i in range(items):
            rows = pl.ds(i * slots, slots)
            keys = pl.ds(i * padded, padded)
            probs, a = item_forward(q_s[rows], kc_st[r, keys], vc_st[r, keys], masks, patches)
            pc_st[r, i] = probs
            a_s[rows] = a
        ab = a_s[...].astype(BF)
        ac_st[r] = ab
        acc[...] += dot_nn(ab, wc[r, width:middle])

    def near_start(*arrays):
        for a in arrays:
            near[a].advance()

    move("s1p e1 k1")
    near_start(TEXT_IN, TEXT_OUT)
    bias[0] = jnp.zeros(bias.shape[1:], F32)
    bias[0, 0:2, 0:width] = bias_in[0][...].astype(F32)
    bias[0, 2:6, 0:width] = bias_in[1][...].astype(F32)
    bias[0, 6:7] = bias_in[2][...].astype(F32).reshape(1, hidden)
    bias[0, 7:8] = bias_in[3][...].astype(F32).reshape(1, hidden)
    bias_near.advance()
    bias_far.advance()
    near_start(KEY_VALUE)
    fetch_self(0, 0)
    fetch_keys(0)
    norm_rows(vecs, vecs_in[0:3], vecs_in[3:6])
    u[...] = x[...].astype(F32)
    ub[...] = x[...]
    open_layer(0)
    move("s1p s1o e1")
    self_unit(0, 0)
    move("s1p s2p")
    bias_near.need()
    fetch_self(0, 1)
    self_unit(0, 1)
    move("k1 s1p s1v e1 e2")
    bias_far.need()
    bias_last.advance()
    near_start(EXPAND_ONE, CONTRACT_ONE)
    pf_copy.wait()
    spread_patches(pf_raw, pf_wide, pf, items, padded)
    store(pf, pf_out)
    move("s2p ckv")
    keys_unit(0)
    move("k1 k2")
    fetch_keys(1)
    keys_unit(1)
    bias_last.need()
    move("s2o s1o e1")
    near_start(JOIN_IN, JOIN_OUT)
    fetch_self(0, 2)
    self_unit(0, 2)
    move("e2")
    fetch_feed(0, 0)
    fetch_feed(0, 1)
    self_unit(0, 3)
    self_close(0)
    move("s2v k1")
    close_layer(0)
    open_layer(1)
    move("s2p e2")
    feed_unit(0, 0)
    move("e1")
    feed_unit(0, 1)
    move("s2p ckv")
    fetch_keys(2)
    keys_unit(2)
    move("cq co k2")
    fetch_keys(3)
    fetch_feed(0, 2, True)
    fetch_feed(0, 3, True)
    keys_unit(3)
    for source, target in zip(cross_st[1:3], cross_out[1:3]):
        store(source, target)
    move("e2 k1")
    near_start(CROSS_OUT, EXPAND_TWO, CONTRACT_TWO)
    feed_unit(0, 2)
    fetch_contract(0, 3)
    fetch_self(1, 0)
    fetch_self(1, 1)
    feed_unit(0, 3)
    move("k2")
    feed_close(0)
    close_layer(1, text_out)
    open_layer(2)
    settle("self")
    move("s2p s2o")
    self_unit(1, 0)
    move("s2v")
    self_unit(1, 1)
    fetch_self(1, 2)
    fetch_cross(0)
    fetch_cross(1)
    self_unit(1, 2)
    move("k2")
    fetch_self(1, 3)
    self_unit(1, 3)
    self_close(1)
    move("cq")
    close_layer(2)
    open_layer(3)
    cross_unit(0)
    fetch_feed(1, 0)
    fetch_feed(1, 1)
    cross_unit(1)
    move("co")
    fetch_cross(2)
    cross_unit(2)
    fetch_cross(3)
    cross_unit(3)
    for n in (0, 3, 4):
        store(cross_st[n], cross_out[n])
    close_layer(3)
    open_layer(4)
    settle("feed")
    move("e2")
    feed_unit(1, 0)
    fetch_feed(1, 2, True)
    feed_unit(1, 1)
    move("k2")
    fetch_feed(1, 3, True)
    fetch_contract(1, 2)
    feed_unit(1, 2)
    fetch_contract(1, 3)
    feed_unit(1, 3)
    feed_close(1)
    close_layer(4, join_out)

    for copy in stores:
        if copy is not None:
            copy.wait()
    for flow in flows.values():
        flow.close()
    for direct in near + [bias_near, bias_far, bias_last]:
        direct.close()


def forward_all(links, own, biases, vecs, lengths, x, patch_rows, width):
    patches, items, features = patch_rows.shape
    rows, model = x.shape
    slots, padded = rows // items, -(-patches // 16) * 16
    hidden = own[EXPAND_ONE].shape[1]
    heads = width // HEAD_DIM
    anywhere = pl.BlockSpec(memory_space=ANY)
    vmem = pl.BlockSpec(memory_space=pltpu.VMEM)
    sizes = (links.tensor, links.dp, items, slots, patches, padded, width)
    mid = ((4, rows, width), BF)
    key = ((4, items * padded, width), BF)
    probs = ((4, items, slots, heads * slots), BF)
    cross_probs = ((4, items, padded, heads * slots), BF)
    feed = ((4, rows, hidden), BF)
    pf = ((items * padded, features), BF)
    self_kept = [mid] * 4 + [probs]
    cross_kept = [mid, key, key, mid, cross_probs]
    kept = self_kept * 2 + cross_kept + [feed] * 4
    outputs = [((3,) + a.shape, BF) for a in own]
    outputs += [((rows, model), BF)] * 2 + [((5, rows, model), F32), pf] + kept
    remotes = 13 * (2 + links.bits) + ARRAYS + 3
    outs = pl.pallas_call(
        functools.partial(forward_kernel, sizes),
        in_specs=[anywhere] * ARRAYS
        + [vmem] * 10
        + [pl.BlockSpec(memory_space=pltpu.SMEM), vmem, anywhere],
        out_specs=[anywhere] * ARRAYS + [vmem] * 2 + [anywhere] * (2 + len(kept)),
        out_shape=[jax.ShapeDtypeStruct(shape, dtype) for shape, dtype in outputs],
        scratch_shapes=[
            pltpu.VMEM((4, 4 * width, model), BF),
            pltpu.VMEM((4, 2, model, hidden), BF),
            pltpu.VMEM((4, 2 * width, model), BF),
            pltpu.VMEM((4, 2 * width, features), BF),
            pltpu.VMEM((rows, model), F32),
            pltpu.VMEM((rows, model), F32),
            pltpu.VMEM((rows, model), BF),
            pltpu.VMEM((5, rows, model), F32),
            pltpu.VMEM(patch_rows.shape, BF),
            pltpu.VMEM((features // 128, items * padded, 128), F32),
            pltpu.VMEM(*pf),
            pltpu.VMEM((5, 3, model), F32),
        ]
        + [pltpu.VMEM(*item) for item in self_kept + cross_kept + [feed] * 2]
        + [pltpu.VMEM((rows, width), F32)] * 4
        + [
            pltpu.VMEM((4, 8, model), F32),
            pltpu.SemaphoreType.DMA((remotes,)),
            pltpu.SemaphoreType.DMA((remotes,)),
            pltpu.SemaphoreType.DMA((64,)),
            pltpu.SemaphoreType.DMA((32,)),
            pltpu.SemaphoreType.DMA,
        ],
        compiler_params=pltpu.CompilerParams(
            collective_id=1, has_side_effects=True, vmem_limit_bytes=60 * 1024 * 1024
        ),
        name="forward_and_gather",
    )(*own, *biases, *vecs, lengths, x, patch_rows)
    n = ARRAYS
    got, (text_out, join_out, e, pf), kept = outs[:n], outs[n : n + 4], outs[n + 4 :]
    return got, text_out, join_out, e, pf, kept


(
    GRAD_CONTRACT_TWO,
    GRAD_EXPAND_TWO,
    GRAD_CROSS,
    GRAD_TWO,
    GRAD_CONTRACT_ONE,
    GRAD_EXPAND_ONE,
    GRAD_ONE,
) = range(7)


def backward_kernel(sizes, *refs):
    n_tensor, n_dp, items, slots, patches, padded, width, chunk, counts = sizes
    refs = list(refs)

    def take(n):
        got, refs[:n] = refs[:n], []
        return got

    own, got = take(ARRAYS), take(ARRAYS)
    e_in, pf_in, x, text_out, text_cot, join_cot = take(6)
    vecs_in = take(6)
    self_in = [take(5), take(5)]
    cross_in = take(5)
    feed_in = [take(2), take(2)]
    keeps, sends, outs = take(7), take(7), take(7)
    small_out, grad_text, dpf = take(3)
    wbuf, wk, stage_buf, e_s, ub, ub_t, dob, acc, pacc, pf, vecs = take(11)
    q_b, k_b, v_b, a_b, p_b = self_buf = take(5)
    qc_b, kc_b, vc_b, ac_b, pc_b = cross_buf = take(5)
    h_b, slope_b = take(2)
    q_s, k_s, v_s, da_s, dq_s, dk_s, dv_s = take(7)
    dkv_s, small_keep, small_send = take(3)
    fetch_sem, store_sem, e_sem, pf_sem = take(4)
    model = x.shape[1]
    hidden = own[EXPAND_ONE].shape[1]
    side = pf.shape[1] - model

    sums = Sums(
        n_tensor,
        n_dp,
        counts,
        chunk,
        sends,
        keeps,
        outs,
        (small_send, small_keep, small_out),
        refs,
    )

    norm_rows(vecs, vecs_in[0:3], vecs_in[3:6])
    pf_copy = pltpu.make_async_copy(pf_in, pf, pf_sem)
    e_copies = [
        pltpu.make_async_copy(e_in.at[n], e_s.at[n], e_sem.at[n]) for n in range(5)
    ]
    for n in (4, 3, 2, 1, 0):
        e_copies[n].start()
    pf_copy.start()

    units = []
    for layer in (1, 0):
        expand, contract = ((EXPAND_ONE, CONTRACT_ONE), (EXPAND_TWO, CONTRACT_TWO))[layer]
        for r in range(4):
            units.append(("contract", layer, r, [(feed_in[layer][0].at[r], h_b)]))
        for r in range(4):
            units.append(
                (
                    "expand",
                    layer,
                    r,
                    [
                        (contract, 0, hidden, wbuf, hidden),
                        (expand, 0, model, wbuf, 0),
                        (feed_in[layer][1].at[r], slope_b),
                    ],
                )
            )
        for r in range(4):
            if layer == 1:
                units.append(
                    (
                        "cross",
                        0,
                        r,
                        [
                            (CROSS_OUT, 0, width, wbuf, width),
                            (JOIN_IN, 3 * width, width, wbuf, 0),
                            (KEY_VALUE, 0, 2 * width, wk, 0),
                        ]
                        + [(cross_in[n].at[r], cross_buf[n]) for n in (3, 0, 1, 2, 4)],
                    )
                )
        for r in range(4):
            first, last = ((TEXT_IN, TEXT_OUT), (JOIN_IN, JOIN_OUT))[layer]
            units.append(
                (
                    "self",
                    layer,
                    r,
                    [(last, 0, width, wbuf, 3 * width), (first, 0, 3 * width, wbuf, 0)]
                    + [(self_in[layer][n].at[r], self_buf[n]) for n in (4, 0, 1, 2, 3)],
                )
            )
    position = {unit[:3]: n for n, unit in enumerate(units)}

    def fetches(n):
        _, _, r, wanted = units[n]
        parity = n % 2
        copies = []
        for i, item in enumerate(wanted):
            if len(item) == 5:
                a, low, count, target, row = item
                source = (own[a] if r == 0 else got[a].at[r - 1]).at[pl.ds(low, count)]
                target = target.at[parity, pl.ds(row, count)]
            else:
                source, target = item
                target = target.at[parity]
            copies.append(pltpu.make_async_copy(source, target, fetch_sem.at[parity, i]))
        return copies

    def begin(n):
        if n + 1 < len(units):
            for copy in fetches(n + 1):
                copy.start()
        for copy in fetches(n):
            copy.wait()
        return n % 2

    stores = {}

    def room(r):
        j = r % 2
        if stores.get(j) is not None:
            stores[j].wait()
            stores[j] = None
        return j

    def put(array, r):
        j = r % 2
        target = (keeps, sends)[j][array]
        rows = target.shape[1]
        stores[j] = pltpu.make_async_copy(
            stage_buf.at[j, pl.ds(0, rows)], target.at[r // 2], store_sem.at[j]
        )
        stores[j].start()

    def settle():
        for j in (0, 1):
            room(j)

    def small_row(r, row, value):
        target = (small_keep, small_send)[r % 2]
        n = 8 * (r // 2) + row
        target[n : n + 1, 0 : value.shape[1]] = value

    def open_layer(n, dy):
        e_copies[n].wait()
        de, partial = norm_backward(e_s[n], vecs[n, 1:2], dy)
        for target in (small_keep, small_send):
            target[16 + 3 * n : 19 + 3 * n] = partial
        dob[...] = de.astype(BF)
        acc[...] = de

    def input_rows(n):
        rows = norm_forward(e_s[n], vecs[n, 1:2], vecs[n, 2:3])
        ub[...] = rows.astype(BF)
        ub_t[...] = rows.T.astype(BF)

    def contract_unit(layer, r):
        b = begin(position["contract", layer, r])
        j = room(r)
        stage_buf[j, 0:hidden] = dot_tn(h_b[b], dob[...]).astype(BF)
        put((GRAD_CONTRACT_ONE, GRAD_CONTRACT_TWO)[layer], r)

    def expand_unit(layer, r):
        b = begin(position["expand", layer, r])
        dh = dot_nt(dob[...], wbuf[b, hidden : 2 * hidden])
        dz = (dh * slope_b[b].astype(F32)).astype(BF)
        j = room(r)
        stage_buf[j, 0:model] = dot_nn(ub_t[...], dz).astype(BF)
        put((GRAD_EXPAND_ONE, GRAD_EXPAND_TWO)[layer], r)
        small_row(r, 6 + layer, jnp.sum(dz.astype(F32), axis=0, keepdims=True))
        acc[...] += dot_nt(dz, wbuf[b, 0:model])

    masks = head_masks(width)

    def self_unit(layer, r):
        b = begin(position["self", layer, r])
        da_s[...] = dot_nt(dob[...], wbuf[b, 3 * width : 4 * width])
        j = room(r)
        stage_buf[j, 3 * width : 4 * width] = dot_tn(a_b[b], dob[...]).astype(BF)
        q_s[...], k_s[...], v_s[...] = (
            q_b[b].astype(F32),
            k_b[b].astype(F32),
            v_b[b].astype(F32),
        )
        for i in range(items):
            rows = pl.ds(i * slots, slots)
            dq, dk, dv = item_backward(
                q_s[rows],
                k_s[rows].astype(BF),
                v_s[rows].astype(BF),
                da_s[rows],
                p_b[b, i],
                masks,
            )
            dq_s[rows], dk_s[rows], dv_s[rows] = dq, dk, dv
        xb = ub[...]
        total = acc[...]
        for c, part in enumerate((dq_s, dk_s, dv_s)):
            pb = part[...].astype(BF)
            stage_buf[j, c * width : (c + 1) * width] = dot_tn(pb, xb).astype(BF)
            total = total + dot_nn(pb, wbuf[b, c * width : (c + 1) * width])
            if c != 1:
                small_row(
                    r, 2 * layer + c // 2, jnp.sum(pb.astype(F32), axis=0, keepdims=True)
                )
        acc[...] = total
        put((GRAD_ONE, GRAD_TWO)[layer], r)

    def cross_unit(r):
        b = begin(position["cross", 0, r])
        da_s[...] = dot_nt(dob[...], wbuf[b, width : 2 * width])
        j = room(r)
        stage_buf[j, width : 2 * width] = dot_tn(ac_b[b], dob[...]).astype(BF)
        q_s[...] = qc_b[b].astype(F32)
        vsum = jnp.zeros((1, width), F32)
        for i in range(items):
            rows = pl.ds(i * slots, slots)
            keys = pl.ds(i * padded, padded)
            dq, dk, dv = item_backward(
                q_s[rows], kc_b[b, keys], vc_b[b, keys], da_s[rows], pc_b[b, i], masks
            )
            dq_s[rows] = dq
            dkv_s[0, keys] = dk.astype(BF)
            dvb = dv.astype(BF)
            dkv_s[1, keys] = dvb
            vsum = vsum + jnp.sum(dvb.astype(F32), axis=0, keepdims=True)
        ticks(1)
        dqb = dq_s[...].astype(BF)
        stage_buf[j, 0:width] = dot_tn(dqb, ub[...]).astype(BF)
        acc[...] += dot_nn(dqb, wbuf[b, 0:width])
        small_row(r, 4, jnp.sum(dqb.astype(F32), axis=0, keepdims=True))
        small_row(r, 5, vsum)
        tails = []
        for c in range(2):
            grad = dot_tn(dkv_s[c], pf[...]).astype(BF)
            stage_buf[j, (2 + c) * width : (3 + c) * width] = grad[:, 0:model]
            tails.append(grad[:, model:])
        back = dot_nn(dkv_s[0], wk[b, 0:width]) + dot_nn(dkv_s[1], wk[b, width : 2 * width])
        for n in range(pacc.shape[0]):
            lanes = back[:, n * 128 : (n + 1) * 128]
            if r == 0:
                pacc[n] = lanes
            else:
                pacc[n] += lanes
        tail = jnp.concatenate(tails, axis=0)
        count = tail.shape[0] // (model // side)
        for c in range(model // side):
            stage_buf[j, 4 * width : 4 * width + count, c * side : (c + 1) * side] = tail[
                c * count : (c + 1) * count
            ]
        extra = stage_buf.shape[1] - 4 * width - count
        if extra > 0:
            stage_buf[j, 4 * width + count :] = jnp.zeros((extra, model), BF)
        put(GRAD_CROSS, r)

    small_keep[...] = jnp.zeros_like(small_keep)
    small_send[...] = jnp.zeros_like(small_send)
    for copy in fetches(0):
        copy.start()
    open_layer(4, join_cot[...].astype(F32))
    sums.greet()
    clock = [0]

    def ticks(count):
        for _ in range(count):
            sums.tick(clock[0])
            clock[0] += 1

    def collected(n):
        e_copies[n].wait()
        e_copies[n] = Done()

    for r in range(4):
        contract_unit(1, r)
    settle()
    ticks(1)
    collected(3)
    input_rows(3)
    ticks(1)
    for r in range(4):
        expand_unit(1, r)
        if r == 3:
            settle()
        ticks((1, 1, 1, 0)[r])
    open_layer(3, acc[...])
    collected(2)
    input_rows(2)
    pf_copy.wait()
    for r in range(4):
        cross_unit(r)
        if r == 3:
            settle()
        ticks(1)
    open_layer(2, acc[...])
    ub[...] = text_out[...]
    for r in range(4):
        self_unit(1, r)
        if r == 3:
            settle()
        ticks((1, 2, 1, 2)[r])
    open_layer(1, acc[...] + text_cot[...].astype(F32))
    for r in range(4):
        contract_unit(0, r)
    settle()
    ticks(1)
    collected(0)
    input_rows(0)
    for r in range(4):
        expand_unit(0, r)
        if r == 3:
            settle()
        ticks(1)
    open_layer(0, acc[...])
    ub[...] = x[...]
    for r in range(4):
        self_unit(0, r)
        if r == 3:
            settle()
        ticks((1, 2, 1, 2)[r])
    grad_text[...] = acc[...].astype(BF)

    def gather_patches(n, carry):
        for c in range(pacc.shape[0]):
            dpf[n, :, c * 128 : (c + 1) * 128] = pacc[
                c, pl.ds(n, items, stride=padded)
            ].astype(BF)
        return carry

    lax.fori_loop(0, patches, gather_patches, 0)
    sums.finish(clock[0])


class Done:
    def wait(self):
        pass


def backward_all(links, own, got, e, pf, x, text_out, cots, vecs, kept, patches, items, width):
    rows, model = x.shape
    slots, padded = rows // items, pf.shape[0] // items
    hidden = own[EXPAND_ONE].shape[1]
    heads = width // HEAD_DIM
    chunk = links.chunk
    anywhere = pl.BlockSpec(memory_space=ANY)
    vmem = pl.BlockSpec(memory_space=pltpu.VMEM)
    cross_rows = 2 * width + 2 * width * pf.shape[1] // model
    extents = [hidden, model, cross_rows, 4 * width, hidden, model, 4 * width]
    extents = [-(-extent // chunk) * chunk for extent in extents]
    counts = tuple(extent // chunk for extent in extents)
    sizes = (links.tensor, links.dp, items, slots, patches, padded, width, chunk, counts)
    pairs = [((2, extent, model), BF) for extent in extents]
    totals = [((extent, model), BF) for extent in extents]
    units, small = 8, 32
    outputs = pairs * 2 + totals
    outputs += [
        ((small - units, model), F32),
        ((rows, model), BF),
        ((patches, items, pf.shape[1]), BF),
    ]
    f32_rows = pltpu.VMEM((rows, width), F32)
    outs = pl.pallas_call(
        functools.partial(backward_kernel, sizes),
        in_specs=[anywhere] * (2 * ARRAYS + 2) + [vmem] * 10 + [anywhere] * len(kept),
        out_specs=[anywhere] * 21 + [vmem] * 3,
        out_shape=[jax.ShapeDtypeStruct(shape, dtype) for shape, dtype in outputs],
        scratch_shapes=[
            pltpu.VMEM((2, 2 * hidden, model), BF),
            pltpu.VMEM((2, 2 * width, pf.shape[1]), BF),
            pltpu.VMEM((2, max(extents), model), BF),
            pltpu.VMEM((5, rows, model), F32),
            pltpu.VMEM((rows, model), BF),
            pltpu.VMEM((model, rows), BF),
            pltpu.VMEM((rows, model), BF),
            pltpu.VMEM((rows, model), F32),
            pltpu.VMEM((pf.shape[1] // 128, pf.shape[0], 128), F32),
            pltpu.VMEM(pf.shape, BF),
            pltpu.VMEM((5, 3, model), F32),
        ]
        + [pltpu.VMEM((2, rows, width), BF)] * 4
        + [pltpu.VMEM((2, items, slots, heads * slots), BF)]
        + [pltpu.VMEM((2, rows, width), BF)]
        + [pltpu.VMEM((2, pf.shape[0], width), BF)] * 2
        + [pltpu.VMEM((2, rows, width), BF)]
        + [pltpu.VMEM((2, items, padded, heads * slots), BF)]
        + [pltpu.VMEM((2, rows, hidden), BF)] * 2
        + [f32_rows] * 7
        + [
            pltpu.VMEM((2, pf.shape[0], width), BF),
            pltpu.VMEM((small, model), F32),
            pltpu.VMEM((small, model), F32),
            pltpu.SemaphoreType.DMA((2, 8)),
            pltpu.SemaphoreType.DMA((2,)),
            pltpu.SemaphoreType.DMA((5,)),
            pltpu.SemaphoreType.DMA,
        ]
        + Sums.scratch(links.dp, chunk, model, small, units),
        compiler_params=pltpu.CompilerParams(
            collective_id=0, has_side_effects=True, vmem_limit_bytes=60 * 1024 * 1024
        ),
        name="backward_and_sums",
    )(*own, *got, e, pf, x, text_out, *cots, *vecs, *kept)
    return outs[14:21], outs[21], outs[22], outs[23]


def finish_kernel(width, *refs):
    refs = list(refs)

    def take(n):
        got, refs[:n] = refs[:n], []
        return got

    totals, passed, (small,) = take(7), take(4), take(1)
    passed_out = take(4)
    text_in, text_out, expand_one, contract_one, join_in = take(5)
    join_out, cross_out, key_value, expand_two, contract_two = take(5)
    text_bias, join_bias, hidden_one, hidden_two = take(4)
    text_shared, join_shared = take(3), take(3)
    half, full, keys = take(3)
    bounced = take(4)
    load_sem, store_sem = take(2)
    model = full.shape[2]
    side = keys.shape[1] - model
    count = 2 * width * side // model

    loads, stores = [], []
    for n in range(7):
        rows = totals[n].shape[0]
        loads.append(
            pltpu.make_async_copy(totals[n], half.at[n, pl.ds(0, rows)], load_sem.at[n])
        )
        loads[n].start()
    for n in range(4):
        loads.append(pltpu.make_async_copy(passed[n], bounced[n], load_sem.at[7 + n]))
        loads[7 + n].start()

    def store(source, target):
        copy = pltpu.make_async_copy(source, target, store_sem.at[len(stores)])
        copy.start()
        stores.append(copy)

    text_bias[...] = small[0:2, 0:width]
    join_bias[...] = small[2:6, 0:width]
    hidden_one[...] = small[6]
    hidden_two[...] = small[7]
    for n in range(5):
        for c in range(3):
            row = 8 + 3 * n + c
            target, m = (text_shared[c], n) if n < 2 else (join_shared[c], n - 2)
            target[m : m + 1] = small[row : row + 1]

    def widen(n):
        loads[n].wait()
        rows = totals[n].shape[0]
        full[n, 0:rows] = half[n, 0:rows].astype(F32)

    def send(n, lo, rows, target):
        store(full.at[n, pl.ds(lo, rows)], target)

    for n, target in (
        (GRAD_CONTRACT_TWO, contract_two),
        (GRAD_EXPAND_TWO, expand_two),
        (GRAD_CONTRACT_ONE, contract_one),
        (GRAD_EXPAND_ONE, expand_one),
    ):
        widen(n)
        send(n, 0, target.shape[0], target)
    widen(GRAD_CROSS)
    send(GRAD_CROSS, 0, width, join_in.at[pl.ds(3 * width, width)])
    send(GRAD_CROSS, width, width, cross_out)
    keys[:, 0:model] = full[GRAD_CROSS, 2 * width : 4 * width]
    for c in range(model // side):
        keys[c * count : (c + 1) * count, model:] = full[
            GRAD_CROSS, 4 * width : 4 * width + count, c * side : (c + 1) * side
        ]
    store(keys, key_value)
    widen(GRAD_TWO)
    send(GRAD_TWO, 0, 3 * width, join_in.at[pl.ds(0, 3 * width)])
    send(GRAD_TWO, 3 * width, width, join_out)
    widen(GRAD_ONE)
    send(GRAD_ONE, 0, 3 * width, text_in)
    send(GRAD_ONE, 3 * width, width, text_out)
    for n in range(4):
        loads[7 + n].wait()
        store(bounced[n], passed_out[n])
    for copy in stores:
        copy.wait()


def finish_all(totals, passed, small, width, hidden, features):
    model = totals[0].shape[1]
    anywhere = pl.BlockSpec(memory_space=ANY)
    vmem = pl.BlockSpec(memory_space=pltpu.VMEM)
    big = [
        (3 * width, model),
        (width, model),
        (model, hidden),
        (hidden, model),
        (4 * width, model),
        (width, model),
        (width, model),
        (2 * width, features),
        (model, hidden),
        (hidden, model),
    ]
    little = [(2, width), (4, width), (hidden,), (hidden,)]
    little += [(2, model)] * 3 + [(3, model)] * 3
    most = max(total.shape[0] for total in totals)
    return pl.pallas_call(
        functools.partial(finish_kernel, width),
        in_specs=[anywhere] * 11 + [vmem],
        out_specs=[anywhere] * (4 + len(big)) + [vmem] * len(little),
        out_shape=[jax.ShapeDtypeStruct(a.shape, a.dtype) for a in passed]
        + [jax.ShapeDtypeStruct(shape, F32) for shape in big + little],
        scratch_shapes=[
            pltpu.VMEM((7, most, model), BF),
            pltpu.VMEM((7, most, model), F32),
            pltpu.VMEM((2 * width, features), F32),
        ]
        + [pltpu.VMEM(a.shape, a.dtype) for a in passed]
        + [
            pltpu.SemaphoreType.DMA((11,)),
            pltpu.SemaphoreType.DMA((16,)),
        ],
        compiler_params=pltpu.CompilerParams(vmem_limit_bytes=60 * 1024 * 1024),
        name="finish",
    )(*totals, *passed, small)


class Links:
    def __init__(self, mesh):
        self.tensor = mesh.shape["tensor"]
        self.dp = mesh.shape["dp"]
        self.bits = self.dp.bit_length() - 1
        self.chunk = 128


def turned(array):
    array = jnp.swapaxes(array, 1, 2)
    return array.reshape(-1, array.shape[2])


def turned_back(rows, units):
    return jnp.swapaxes(rows.reshape(-1, units, rows.shape[1]), 1, 2)


def per_device(
    links,
    text_rows,
    patch_features,
    lengths,
    text_cotangent,
    join_cotangent,
    text_project_in,
    text_project_bias,
    text_project_out,
    text_expand,
    text_expand_bias,
    text_contract,
    text_out_bias,
    text_norm_gain,
    text_norm_shift,
    join_project_in,
    join_project_bias,
    join_project_out,
    cross_project_out,
    cross_key_value,
    join_expand,
    join_expand_bias,
    join_contract,
    join_out_bias,
    join_norm_gain,
    join_norm_shift,
):
    items, slots, model = text_rows.shape
    patches, patch_width = patch_features.shape[1:]
    width = text_project_in.shape[2]
    hidden = text_expand.shape[1]

    own = [
        turned(text_project_in),
        text_project_out,
        text_expand,
        text_contract,
        turned(join_project_in),
        join_project_out,
        turned(cross_key_value),
        cross_project_out,
        join_expand,
        join_contract,
    ]
    biases = (text_project_bias, join_project_bias, text_expand_bias, join_expand_bias)
    vecs = (text_out_bias, text_norm_gain, text_norm_shift)
    vecs += (join_out_bias, join_norm_gain, join_norm_shift)
    x = text_rows.reshape(items * slots, model)
    text_cot = text_cotangent.reshape(items * slots, model)
    join_cot = join_cotangent.reshape(items * slots, model)
    patch_rows = jnp.swapaxes(patch_features, 0, 1)

    got, text_out, join_out, e, pf, kept = forward_all(
        links, own, biases, vecs, lengths, x, patch_rows, width
    )
    totals, small, grad_text, grad_patches = backward_all(
        links, own, got, e, pf, x, text_out, (text_cot, join_cot), vecs, kept, patches, items, width
    )
    outs = finish_all(
        totals, (text_out, join_out, grad_text, grad_patches), small, width, hidden, patch_width
    )
    text_out, join_out, grad_text, grad_patches = outs[:4]
    text_in, text_project, expand_one, contract_one, join_in = outs[4:9]
    join_project, cross_project, key_value, expand_two, contract_two = outs[9:14]
    text_bias, join_bias, hidden_one, hidden_two = outs[14:18]

    return (
        text_out.reshape(text_rows.shape),
        join_out.reshape(text_rows.shape),
        grad_text.reshape(text_rows.shape),
        jnp.swapaxes(grad_patches, 0, 1),
        turned_back(text_in, width),
        text_bias,
        text_project,
        expand_one,
        hidden_one,
        contract_one,
        *outs[18:21],
        turned_back(join_in, width),
        join_bias,
        join_project,
        cross_project,
        turned_back(key_value, width),
        expand_two,
        hidden_two,
        contract_two,
        *outs[21:24],
    )


def solution(mesh):
    rows = P(("dp", "tensor"), None, None)
    last = P(None, None, "tensor")
    second = P(None, "tensor")
    first = P("tensor", None)
    line = P("tensor")
    full = P()
    in_specs = (
        (rows, rows, P(("dp", "tensor")), rows, rows)
        + (last, second, first, second, line, first, full, full, full)
        + (last, second, first, first, last, second, line, first, full, full, full)
    )
    out_specs = (
        (rows, rows, rows, rows)
        + (last, second, first, second, line, first, full, full, full)
        + (last, second, first, first, last, second, line, first, full, full, full)
    )
    return jax.shard_map(
        functools.partial(per_device, Links(mesh)),
        mesh=mesh,
        in_specs=in_specs,
        out_specs=out_specs,
        check_vma=False,
    )
```

```python
import functools

import jax
import jax.numpy as jnp
from jax import lax
from jax.experimental import pallas as pl
from jax.experimental.pallas import tpu as pltpu
from jax.sharding import PartitionSpec as P

HEAD_DIM = 64
BF = jnp.bfloat16
F32 = jnp.float32
ANY = pl.ANY


def dot_nn(a, b):
    return lax.dot_general(a, b, (((1,), (0,)), ((), ())), preferred_element_type=F32)


def dot_nt(a, b):
    return lax.dot_general(a, b, (((1,), (1,)), ((), ())), preferred_element_type=F32)


def dot_tn(a, b):
    return lax.dot_general(a, b, (((0,), (0,)), ((), ())), preferred_element_type=F32)


def norm_forward(e, gain, shift):
    center = e - jnp.mean(e, axis=-1, keepdims=True)
    variance = jnp.mean(center * center, axis=-1, keepdims=True)
    return center * lax.rsqrt(variance + 1e-12) * gain + shift


def norm_backward(e, gain, dy):
    center = e - jnp.mean(e, axis=-1, keepdims=True)
    variance = jnp.mean(center * center, axis=-1, keepdims=True)
    rstd = lax.rsqrt(variance + 1e-12)
    normed = center * rstd
    scaled = dy * gain
    de = rstd * (
        scaled
        - jnp.mean(scaled, axis=-1, keepdims=True)
        - normed * jnp.mean(scaled * normed, axis=-1, keepdims=True)
    )
    sums = jnp.concatenate(
        [
            jnp.sum(de, axis=0, keepdims=True),
            jnp.sum(dy * normed, axis=0, keepdims=True),
            jnp.sum(dy, axis=0, keepdims=True),
        ],
        axis=0,
    )
    return de, sums


def head_masks(width):
    lane = lax.broadcasted_iota(jnp.int32, (1, width), 1)
    return [
        ((lane >= h * HEAD_DIM) & (lane < (h + 1) * HEAD_DIM)).astype(F32)
        for h in range(width // HEAD_DIM)
    ]


def groups(count, most):
    return [range(i, min(i + most, count)) for i in range(0, count, most)]


def stack_heads(rows, masks):
    return jnp.concatenate([rows * mask for mask in masks], axis=0).astype(BF)


def merge_heads(stacked, masks):
    count = stacked.shape[0] // len(masks)
    total = stacked[:count] * masks[0]
    for h in range(1, len(masks)):
        total = total + stacked[h * count : (h + 1) * count] * masks[h]
    return total


def items_forward(operands, masks):
    stacked = [stack_heads(q, masks) for q, _, _, _ in operands]
    scores = [dot_nt(k, qs) for qs, (_, k, _, _) in zip(stacked, operands)]
    row = lax.broadcasted_iota(jnp.int32, scores[0].shape, 0)
    scores = [
        jnp.where(row < length, s * HEAD_DIM ** (-0.5), -1e30)
        for s, (_, _, _, length) in zip(scores, operands)
    ]
    most = [jnp.max(s, axis=0, keepdims=True) for s in scores]
    weights = [jnp.exp(s - m) for s, m in zip(scores, most)]
    totals = [jnp.sum(w, axis=0, keepdims=True) for w in weights]
    probs = [(w / t).astype(BF) for w, t in zip(weights, totals)]
    mixed = [dot_tn(p, v) for p, (_, _, v, _) in zip(probs, operands)]
    return probs, [merge_heads(m, masks) for m in mixed]


def items_backward(operands, masks):
    qs = [stack_heads(q, masks) for q, _, _, _, _ in operands]
    das = [stack_heads(da, masks) for _, _, _, da, _ in operands]
    dp = [dot_nt(v, g) for g, (_, _, v, _, _) in zip(das, operands)]
    dv = [dot_nn(probs, g) for g, (_, _, _, _, probs) in zip(das, operands)]
    p = [probs.astype(F32) for _, _, _, _, probs in operands]
    inner = [jnp.sum(a * b, axis=0, keepdims=True) for a, b in zip(p, dp)]
    ds = [(a * (b - c)).astype(BF) for a, b, c in zip(p, dp, inner)]
    scaling = HEAD_DIM ** (-0.5)
    dk = [dot_nn(s, g) * scaling for s, g in zip(ds, qs)]
    dq = [dot_tn(s, k) for s, (_, k, _, _, _) in zip(ds, operands)]
    return [merge_heads(part, masks) * scaling for part in dq], dk, dv


def pair(index, width):
    return index + width - 2 * width * ((index // width) % 2)


def rest(m, n):
    return m % n if isinstance(m, int) else lax.rem(m, n)


def when(condition, act):
    if isinstance(condition, bool):
        if condition:
            act()
    else:
        pl.when(condition)(act)


def halvings(n_dp, chunk):
    return min(n_dp, chunk // 16).bit_length() - 1


class Sums:
    def __init__(self, n_tensor, n_dp, counts, chunk, sends, keeps, outs, small, scratch):
        self.n_dp, self.bits = n_dp, n_dp.bit_length() - 1
        self.counts, self.chunk = counts, chunk
        self.cuts = halvings(n_dp, chunk)
        self.sends, self.keeps, self.outs = sends, keeps, outs
        self.small_send, self.small_keep, self.small_out = small
        scratch = list(scratch)
        bits = self.bits
        self.core_in, self.kept, self.far_out, self.far_in, self.own, self.whole = scratch[:6]
        self.parts, self.halves = scratch[6 : 6 + bits], scratch[6 + bits : 6 + 2 * bits]
        self.gathered, self.tiny_sum, self.tiny_core, self.tiny_far, self.tiny_dp = scratch[
            6 + 2 * bits : 11 + 2 * bits
        ]
        self.send_sem, self.recv_sem, self.kept_sem, self.out_sem = scratch[
            11 + 2 * bits : 15 + 2 * bits
        ]
        self.tiny_send, self.tiny_recv = scratch[15 + 2 * bits :]
        t, d = lax.axis_index("tensor"), lax.axis_index("dp")
        self.dp_bits = [(d // (1 << b)) % 2 for b in range(bits)]
        self.peers = [{"tensor": pair(t, 1)}, {"tensor": lax.rem(t + 2, n_tensor)}]
        self.peers += [{"dp": pair(d, 1 << b)} for b in range(bits)]
        self.total = sum(counts)
        self.stages = 2 + bits + self.cuts
        self.slots, self.depth = self.core_in.shape[0], self.gathered.shape[0]

    def greet(self):
        barrier = pltpu.get_barrier_semaphore()
        for peer in self.peers:
            pl.semaphore_signal(
                barrier, inc=1, device_id=peer, device_id_type=pl.DeviceIdType.MESH
            )
        pl.semaphore_wait(barrier, len(self.peers))

    def remote(self, source, target, stage, slot, peer):
        return pltpu.make_async_remote_copy(
            src_ref=source,
            dst_ref=target,
            send_sem=self.send_sem.at[stage, slot],
            recv_sem=self.recv_sem.at[stage, slot],
            device_id=self.peers[peer],
            device_id_type=pl.DeviceIdType.MESH,
        )

    def region(self, b):
        b = min(b, self.cuts - 1)
        size = self.chunk >> (b + 1)
        start = 0
        for i in range(b + 1):
            start = start + self.dp_bits[i] * (self.chunk >> (i + 1))
        return pl.ds(pl.multiple_of(start, size), size)

    def half(self, b, mine):
        if b >= self.cuts:
            return pl.ds(0, self.chunk >> self.cuts)
        size = self.chunk >> (b + 1)
        which = self.dp_bits[b] if mine else 1 - self.dp_bits[b]
        return pl.ds(pl.multiple_of(which * size, size), size)

    def halved(self, b):
        return self.whole if b == 0 else self.parts[b - 1]

    def copy_of(self, stage, m):
        slot, two = rest(m, self.slots), rest(m, 2)
        if stage == 0:
            source = self.sends[0].at[:, pl.ds(0, self.chunk)]
            return self.remote(source, self.core_in.at[slot], 0, slot, 0)
        if stage == 1:
            ring = rest(m, self.far_in.shape[0])
            return self.remote(self.far_out.at[slot], self.far_in.at[ring], 1, ring, 1)
        if stage < 2 + self.bits:
            b = stage - 2
            source = self.halved(b).at[two, self.half(b, False)]
            return self.remote(source, self.halves[b].at[slot], stage, slot, 2 + b)
        b = 1 + self.bits + self.cuts - stage
        held = self.gathered.at[rest(m, self.depth), self.region(b)]
        return self.remote(held, held, stage, slot, 2 + b)

    def kept_copy(self, a, start, m):
        two = rest(m, 2)
        source = self.keeps[a].at[:, pl.ds(start, self.chunk)]
        return pltpu.make_async_copy(source, self.kept.at[two], self.kept_sem.at[two])

    def out_copy(self, a, start, m):
        ring = rest(m, self.depth)
        target = self.outs[a].at[pl.ds(start, self.chunk)]
        return pltpu.make_async_copy(self.gathered.at[ring], target, self.out_sem.at[ring])

    def each_array(self, m, act):
        base = 0
        for a, count in enumerate(self.counts):
            if isinstance(m, int):
                start = (m - base) * self.chunk
                inside = base <= m < base + count
            else:
                start = pl.multiple_of((m - base) * self.chunk, self.chunk)
                inside = (m >= base) & (m < base + count)
            when(inside, functools.partial(act, a, start))
            base += count

    def process(self, step, m):
        if step == 2:
            return
        stage = step if step < 2 else step - 1
        slot, two, ring = rest(m, self.slots), rest(m, 2), rest(m, self.depth)
        stages, bits = self.stages, self.bits
        if stage == 0:

            def begin(a, start):
                source = self.sends[a].at[:, pl.ds(start, self.chunk)]
                self.remote(source, self.core_in.at[slot], 0, slot, 0).start()
                self.kept_copy(a, start, m).start()

            self.each_array(m, begin)
            return
        if stage <= stages:
            self.copy_of(stage - 1, m).wait()
        if stage == 1:
            self.kept_copy(0, 0, m).wait()
            self.far_out[slot] = self.kept[two, 1] + self.core_in[slot, 1]
            self.own[slot] = self.kept[two, 0] + self.core_in[slot, 0]
        elif stage == 2:
            self.whole[two] = self.own[slot] + self.far_in[rest(m, self.far_in.shape[0])]
        elif stage <= 2 + bits:
            b = stage - 3
            summed = self.halved(b)[two, self.half(b, True)] + self.halves[b][slot]
            if b < bits - 1:
                self.parts[b][two] = summed
            else:
                self.gathered[ring, self.region(b)] = summed
        elif stage == stages:
            self.each_array(m, lambda a, start: self.out_copy(a, start, m).start())
        elif stage == stages + 1:
            self.out_copy(0, 0, m).wait()
        if stage < stages:
            self.copy_of(stage, m).start()

    def tiny(self, stage):
        count = self.tiny_far.shape[0]
        if stage == 0:
            source, target = self.small_send, self.tiny_core
        elif stage == 1:
            first = self.small_keep.shape[0] - count
            source, target = self.tiny_sum.at[0, pl.ds(first, count)], self.tiny_far
        else:
            source = self.tiny_sum.at[stage - 1, pl.ds(0, count)]
            target = self.tiny_dp.at[stage - 2]
        return pltpu.make_async_remote_copy(
            src_ref=source,
            dst_ref=target,
            send_sem=self.tiny_send.at[stage],
            recv_sem=self.tiny_recv.at[stage],
            device_id=self.peers[stage],
            device_id_type=pl.DeviceIdType.MESH,
        )

    def tiny_step(self, stage):
        bits = self.bits
        count = self.tiny_far.shape[0]
        units = self.small_keep.shape[0] - count
        if stage > 0:
            self.tiny(stage - 1).wait()
        if stage == 1:
            self.tiny_sum[0] = self.small_keep[...] + self.tiny_core[...]
        elif stage == 2:
            self.tiny_sum[1, 0:units] = self.tiny_sum[0, 0:units] + self.tiny_far[0:units]
            self.tiny_sum[1, units:count] = (
                self.tiny_sum[0, 2 * units :] + self.tiny_far[units:]
            )
        elif stage > 2:
            summed = self.tiny_sum[stage - 2, 0:count] + self.tiny_dp[stage - 3]
            if stage == 2 + bits:
                self.small_out[...] = summed
            else:
                self.tiny_sum[stage - 1, 0:count] = summed
        if stage < 2 + bits:
            self.tiny(stage).start()

    def tick(self, k):
        for step in range(self.stages + 3):
            m = k - step
            inside = (m >= 0) & (m < self.total)
            when(inside, functools.partial(self.process, step, m))

    def finish(self, first):
        def step(k, carry):
            self.tick(k)
            for stage in range(3 + self.bits):
                when(k == first + stage, functools.partial(self.tiny_step, stage))
            return carry

        lax.fori_loop(first, self.total + self.stages + 3, step, 0)

    @staticmethod
    def scratch(n_dp, chunk, model, small, units):
        bits, cuts = n_dp.bit_length() - 1, halvings(n_dp, chunk)
        slots, far, depth, stages = 4, 6, 8, 2 + bits + cuts
        sizes = [chunk >> min(b + 1, cuts) for b in range(bits)]
        return (
            [
                pltpu.VMEM((slots, 2, chunk, model), BF),
                pltpu.VMEM((2, 2, chunk, model), BF),
                pltpu.VMEM((slots, chunk, model), BF),
                pltpu.VMEM((far, chunk, model), BF),
                pltpu.VMEM((slots, chunk, model), BF),
                pltpu.VMEM((2, chunk, model), BF),
            ]
            + [pltpu.VMEM((2, size, model), BF) for size in sizes]
            + [pltpu.VMEM((slots, size, model), BF) for size in sizes]
            + [
                pltpu.VMEM((depth, chunk, model), BF),
                pltpu.VMEM((1 + bits, small, model), F32),
                pltpu.VMEM((small, model), F32),
                pltpu.VMEM((small - units, model), F32),
                pltpu.VMEM((bits, small - units, model), F32),
                pltpu.SemaphoreType.DMA((stages, far)),
                pltpu.SemaphoreType.DMA((stages, far)),
                pltpu.SemaphoreType.DMA((2,)),
                pltpu.SemaphoreType.DMA((depth,)),
                pltpu.SemaphoreType.DMA((2 + bits,)),
                pltpu.SemaphoreType.DMA((2 + bits,)),
            ]
        )


class Flow:
    def __init__(self, net, a, lo, hi, spread):
        rows = hi - lo
        own, got = net.own[a], net.got[a]
        here = pl.ds(lo, rows)
        self.copies = []
        self.started = self.waited = 0
        if spread and rows % (16 * net.n_dp) == 0:

            def region(count):
                size, start = rows, lo
                for i in range(count):
                    size //= 2
                    start = start + net.dp_bits[i] * size
                return pl.ds(pl.multiple_of(start, 16), size)

            part = region(net.bits)
            self.add(net, own.at[part], got.at[1, part], net.far_peer)
            for b in reversed(range(net.bits)):
                part = region(b + 1)
                self.add(net, got.at[1, part], got.at[1, part], net.dp_peers[b])
        else:
            self.add(net, own.at[here], got.at[1, here], net.far_peer)
        self.add(net, got.at[1, here], got.at[2, here], net.core_peer)

    def add(self, net, source, target, peer):
        self.copies.append(net.remote(source, target, peer))

    def advance(self):
        if self.started < len(self.copies):
            if self.started > 0:
                self.await_copy(self.started - 1)
            self.copies[self.started].start()
            self.started += 1

    def await_copy(self, n):
        while self.started <= n:
            self.advance()
        while self.waited <= n:
            self.copies[self.waited].wait_recv()
            self.waited += 1

    def need(self, r):
        self.await_copy(len(self.copies) - (2 if r == 2 else 1))

    def close(self):
        self.need(3)
        for copy in self.copies:
            copy.wait_send()


class Direct:
    def __init__(self, copy):
        self.copy, self.state = copy, 0

    def advance(self):
        if self.state == 0:
            self.copy.start()
            self.state = 1

    def need(self):
        self.advance()
        if self.state == 1:
            self.copy.wait_recv()
            self.state = 2

    def close(self):
        self.need()
        self.copy.wait_send()


class Net:
    def __init__(self, n_tensor, n_dp, own, got, send_sem, recv_sem):
        self.n_dp, self.bits = n_dp, n_dp.bit_length() - 1
        self.own, self.got = own, got
        self.send_sem, self.recv_sem = send_sem, recv_sem
        self.count = 0
        t, d = lax.axis_index("tensor"), lax.axis_index("dp")
        self.core_peer = {"tensor": pair(t, 1)}
        self.far_peer = {"tensor": lax.rem(t + 2, n_tensor)}
        self.dp_peers = [{"dp": pair(d, 1 << b)} for b in range(self.bits)]
        self.dp_bits = [(d // (1 << b)) % 2 for b in range(self.bits)]
        peers = [self.core_peer, self.far_peer] + self.dp_peers
        barrier = pltpu.get_barrier_semaphore()
        for peer in peers:
            pl.semaphore_signal(
                barrier, inc=1, device_id=peer, device_id_type=pl.DeviceIdType.MESH
            )
        pl.semaphore_wait(barrier, len(peers))

    def remote(self, source, target, peer):
        n = self.count
        self.count += 1
        return pltpu.make_async_remote_copy(
            src_ref=source,
            dst_ref=target,
            send_sem=self.send_sem.at[n],
            recv_sem=self.recv_sem.at[n],
            device_id=peer,
            device_id_type=pl.DeviceIdType.MESH,
        )


TEXT_IN, TEXT_OUT, EXPAND_ONE, CONTRACT_ONE, JOIN_IN = range(5)
JOIN_OUT, KEY_VALUE, CROSS_OUT, EXPAND_TWO, CONTRACT_TWO = range(5, 10)
ARRAYS = 10


def spread_patches(source, wide, target, items, padded):
    patches = source.shape[0]
    least = patches // 8 * 8
    groups, _, lanes = wide.shape
    for i in range(items):
        rows = pl.ds(i * padded + least, padded - least)
        wide[:, rows] = jnp.zeros((groups, padded - least, lanes), F32)

    def step(n, carry):
        for c in range(groups):
            wide[c, pl.ds(n, items, stride=padded)] = source[
                n, :, c * lanes : (c + 1) * lanes
            ].astype(F32)
        return carry

    lax.fori_loop(0, patches, step, 0)
    for c in range(groups):
        target[:, c * lanes : (c + 1) * lanes] = wide[c].astype(BF)


def norm_rows(vecs, text, join):
    for c in range(3):
        for n in range(2):
            vecs[n, c : c + 1] = text[c][...].astype(F32)[n : n + 1]
        for n in range(3):
            vecs[2 + n, c : c + 1] = join[c][...].astype(F32)[n : n + 1]


def forward_kernel(sizes, *refs):
    n_tensor, n_dp, items, slots, patches, padded, width = sizes
    refs = list(refs)

    def take(n):
        got, refs[:n] = refs[:n], []
        return got

    own = take(ARRAYS)
    bias_in, vecs_in = take(4), take(6)
    lengths, x, pf_in = take(3)
    got = take(ARRAYS)
    text_out, join_out, e_out, pf_out = take(4)
    self_out = [take(5), take(5)]
    cross_out = take(5)
    feed_out = [take(2), take(2)]
    ws, wf, wc, wk, acc, u, ub, e_s = take(8)
    pf_raw, pf_wide, pf, vecs = take(4)
    q_st, k_st, v_st, a_st, p_st = self_st = take(5)
    cross_st = take(5)
    qc_st, kc_st, vc_st, ac_st, pc_st = cross_st
    h_st, slope_st = feed_st = take(2)
    q_s, k_s, v_s, a_s, bias = take(5)
    send_sem, recv_sem, fetch_sem, store_sem, pf_sem = take(5)
    model = x.shape[1]
    hidden = own[EXPAND_ONE].shape[1]

    pf_copy = pltpu.make_async_copy(pf_in, pf_raw, pf_sem)
    pf_copy.start()
    net = Net(n_tensor, n_dp, own, got, send_sem, recv_sem)
    middle = 2 * width
    flows = {
        "s1p": Flow(net, TEXT_IN, 0, middle, True),
        "s1v": Flow(net, TEXT_IN, middle, 3 * width, False),
        "s1o": Flow(net, TEXT_OUT, 0, width, False),
        "e1": Flow(net, EXPAND_ONE, 0, model, True),
        "k1": Flow(net, CONTRACT_ONE, 0, hidden, True),
        "s2p": Flow(net, JOIN_IN, 0, middle, True),
        "s2v": Flow(net, JOIN_IN, middle, 3 * width, False),
        "s2o": Flow(net, JOIN_OUT, 0, width, False),
        "ckv": Flow(net, KEY_VALUE, 0, middle, False),
        "cq": Flow(net, JOIN_IN, 3 * width, 4 * width, False),
        "co": Flow(net, CROSS_OUT, 0, width, False),
        "e2": Flow(net, EXPAND_TWO, 0, model, True),
        "k2": Flow(net, CONTRACT_TWO, 0, hidden, True),
    }
    near = [Direct(net.remote(own[a], got[a].at[0], net.core_peer)) for a in range(ARRAYS)]
    bias_near = Direct(net.remote(bias.at[0], bias.at[1], net.core_peer))
    bias_far = Direct(net.remote(bias.at[0], bias.at[2], net.far_peer))
    bias_last = Direct(net.remote(bias.at[2], bias.at[3], net.core_peer))

    def move(names):
        for name in names.split():
            flows[name].advance()

    fetches = {}

    fetch_count = [0]

    def fetch(key, r, wanted):
        if key in fetches:
            return
        fetches[key] = []
        for a, lo, hi, target, names in wanted:
            if r == 1:
                near[a].need()
            elif r > 1:
                for name in names:
                    flows[name].need(r)
            source = own[a] if r == 0 else got[a].at[r - 1]
            copy = pltpu.make_async_copy(
                source.at[pl.ds(lo, hi - lo)], target, fetch_sem.at[fetch_count[0]]
            )
            fetch_count[0] += 1
            copy.start()
            fetches[key].append(copy)

    def arrive(key):
        for copy in fetches[key]:
            copy.wait()

    stores = []

    def store(source, target):
        copy = pltpu.make_async_copy(source, target, store_sem.at[len(stores)])
        copy.start()
        stores.append(copy)
        return len(stores) - 1

    masks = head_masks(width)
    pending = {"self": [], "feed": []}

    def settle(kind):
        for n in pending[kind]:
            stores[n].wait()
            stores[n] = None
        pending[kind] = []

    def close_layer(n, target=None):
        e = acc[...]
        e_s[n] = e
        store(e_s.at[n], e_out.at[n])
        y = norm_forward(e, vecs[n, 1:2], vecs[n, 2:3])
        if target is not None:
            yb = y.astype(BF)
            target[...] = yb
            ub[...] = yb
            u[...] = yb.astype(F32)
        else:
            u[...] = y
            ub[...] = y.astype(BF)

    def open_layer(n):
        acc[...] = u[...] + vecs[n, 0:1]

    def fetch_self(layer, r):
        first = pl.ds(0, 3 * width)
        last = pl.ds(3 * width, width)
        if layer == 0:
            wanted = [
                (TEXT_IN, 0, 3 * width, ws.at[r, first], ("s1p", "s1v")),
                (TEXT_OUT, 0, width, ws.at[r, last], ("s1o",)),
            ]
        else:
            wanted = [
                (JOIN_IN, 0, 3 * width, ws.at[r, first], ("s2p", "s2v")),
                (JOIN_OUT, 0, width, ws.at[r, last], ("s2o",)),
            ]
        fetch(("self", layer, r), r, wanted)

    def self_unit(layer, r):
        fetch_self(layer, r)
        arrive(("self", layer, r))
        xb = ub[...]
        q = (
            dot_nt(xb, ws[r, 0:width]) + bias[r, 2 * layer : 2 * layer + 1, 0:width]
        ).astype(BF)
        k = dot_nt(xb, ws[r, width : 2 * width]).astype(BF)
        v = (
            dot_nt(xb, ws[r, 2 * width : 3 * width])
            + bias[r, 2 * layer + 1 : 2 * layer + 2, 0:width]
        ).astype(BF)
        q_st[r], k_st[r], v_st[r] = q, k, v
        q_s[...], k_s[...], v_s[...] = q.astype(F32), k.astype(F32), v.astype(F32)
        for group in groups(items, 8):
            spans = [pl.ds(i * slots, slots) for i in group]
            probs, mixed = items_forward(
                [
                    (q_s[rows], k_s[rows].astype(BF), v_s[rows].astype(BF), lengths[i])
                    for i, rows in zip(group, spans)
                ],
                masks,
            )
            for n, i in enumerate(group):
                p_st[r, i] = probs[n]
                a_s[spans[n]] = mixed[n]
        ab = a_s[...].astype(BF)
        a_st[r] = ab
        acc[...] += dot_nn(ab, ws[r, 3 * width : 4 * width])

    def self_close(layer):
        for source, target in zip(self_st, self_out[layer]):
            pending["self"].append(store(source, target))

    def fetch_feed(layer, r, late=False):
        a = (EXPAND_ONE, EXPAND_TWO)[layer]
        fetch(("expand", layer, r), r, [(a, 0, model, wf.at[r, 0], (("e1", "e2")[layer],))])
        if not late:
            fetch_contract(layer, r)

    def fetch_contract(layer, r):
        b = (CONTRACT_ONE, CONTRACT_TWO)[layer]
        name = ("k1", "k2")[layer]
        fetch(("contract", layer, r), r, [(b, 0, hidden, wf.at[r, 1], (name,))])

    def feed_unit(layer, r):
        fetch_feed(layer, r, True)
        arrive(("expand", layer, r))
        z = dot_nn(ub[...], wf[r, 0]) + bias[r, 6 + layer : 7 + layer, 0:hidden]
        cdf = 0.5 * (1.0 + lax.erf(z * 0.7071067811865476))
        slope = cdf + z * (jnp.exp(-0.5 * z * z) * 0.3989422804014327)
        h = (z * cdf).astype(BF)
        h_st[r] = h
        slope_st[r] = slope.astype(BF)
        fetch_contract(layer, r)
        arrive(("contract", layer, r))
        acc[...] += dot_nn(h, wf[r, 1])

    def feed_close(layer):
        for source, target in zip(feed_st, feed_out[layer]):
            pending["feed"].append(store(source, target))

    def fetch_keys(r):
        fetch(("keys", r), r, [(KEY_VALUE, 0, middle, wk.at[r], ("ckv",))])

    def keys_unit(r):
        fetch_keys(r)
        arrive(("keys", r))
        chunk = 2 * padded
        for m in range(items // 2):
            rows = slice(m * chunk, (m + 1) * chunk)
            kc_st[r, rows] = dot_nt(pf[rows], wk[r, 0:width]).astype(BF)
            vc_st[r, rows] = (
                dot_nt(pf[rows], wk[r, width:middle]) + bias[r, 5:6, 0:width]
            ).astype(BF)

    def fetch_cross(r):
        wanted = [
            (JOIN_IN, 3 * width, 4 * width, wc.at[r, pl.ds(0, width)], ("cq",)),
            (CROSS_OUT, 0, width, wc.at[r, pl.ds(width, width)], ("co",)),
        ]
        fetch(("cross", r), r, wanted)

    def cross_unit(r):
        fetch_cross(r)
        arrive(("cross", r))
        q = (dot_nt(ub[...], wc[r, 0:width]) + bias[r, 4:5, 0:width]).astype(BF)
        qc_st[r] = q
        q_s[...] = q.astype(F32)
        for group in groups(items, 4):
            spans = [pl.ds(i * slots, slots) for i in group]
            keys = [pl.ds(i * padded, padded) for i in group]
            probs, mixed = items_forward(
                [
                    (q_s[rows], kc_st[r, part], vc_st[r, part], patches)
                    for rows, part in zip(spans, keys)
                ],
                masks,
            )
            for n, i in enumerate(group):
                pc_st[r, i] = probs[n]
                a_s[spans[n]] = mixed[n]
        ab = a_s[...].astype(BF)
        ac_st[r] = ab
        acc[...] += dot_nn(ab, wc[r, width:middle])

    def near_start(*arrays):
        for a in arrays:
            near[a].advance()

    move("s1p e1 k1")
    near_start(TEXT_IN, TEXT_OUT)
    bias[0] = jnp.zeros(bias.shape[1:], F32)
    bias[0, 0:2, 0:width] = bias_in[0][...].astype(F32)
    bias[0, 2:6, 0:width] = bias_in[1][...].astype(F32)
    bias[0, 6:7] = bias_in[2][...].astype(F32).reshape(1, hidden)
    bias[0, 7:8] = bias_in[3][...].astype(F32).reshape(1, hidden)
    bias_near.advance()
    bias_far.advance()
    near_start(KEY_VALUE)
    fetch_self(0, 0)
    fetch_keys(0)
    norm_rows(vecs, vecs_in[0:3], vecs_in[3:6])
    u[...] = x[...].astype(F32)
    ub[...] = x[...]
    open_layer(0)
    move("s1p s1o e1")
    self_unit(0, 0)
    move("s1p s2p")
    bias_near.need()
    fetch_self(0, 1)
    self_unit(0, 1)
    move("k1 s1p s1v e1 e2")
    bias_far.need()
    bias_last.advance()
    near_start(EXPAND_ONE, CONTRACT_ONE)
    pf_copy.wait()
    spread_patches(pf_raw, pf_wide, pf, items, padded)
    store(pf, pf_out)
    move("s2p ckv")
    keys_unit(0)
    move("k1 k2")
    fetch_keys(1)
    keys_unit(1)
    bias_last.need()
    move("s2o s1o e1")
    near_start(JOIN_IN, JOIN_OUT)
    fetch_self(0, 2)
    self_unit(0, 2)
    move("e2")
    fetch_feed(0, 0)
    fetch_feed(0, 1)
    self_unit(0, 3)
    self_close(0)
    move("s2v k1")
    close_layer(0)
    open_layer(1)
    move("s2p e2")
    feed_unit(0, 0)
    move("e1")
    feed_unit(0, 1)
    move("s2p ckv")
    fetch_keys(2)
    keys_unit(2)
    move("cq co k2")
    fetch_keys(3)
    fetch_feed(0, 2, True)
    fetch_feed(0, 3, True)
    keys_unit(3)
    for source, target in zip(cross_st[1:3], cross_out[1:3]):
        store(source, target)
    move("e2 k1")
    near_start(CROSS_OUT, EXPAND_TWO, CONTRACT_TWO)
    feed_unit(0, 2)
    fetch_contract(0, 3)
    fetch_self(1, 0)
    fetch_self(1, 1)
    feed_unit(0, 3)
    move("k2")
    feed_close(0)
    close_layer(1, text_out)
    open_layer(2)
    settle("self")
    move("s2p s2o")
    self_unit(1, 0)
    move("s2v")
    self_unit(1, 1)
    fetch_self(1, 2)
    fetch_cross(0)
    fetch_cross(1)
    self_unit(1, 2)
    move("k2")
    fetch_self(1, 3)
    self_unit(1, 3)
    self_close(1)
    move("cq")
    close_layer(2)
    open_layer(3)
    cross_unit(0)
    fetch_feed(1, 0)
    fetch_feed(1, 1)
    cross_unit(1)
    move("co")
    fetch_cross(2)
    cross_unit(2)
    fetch_cross(3)
    cross_unit(3)
    for n in (0, 3, 4):
        store(cross_st[n], cross_out[n])
    close_layer(3)
    open_layer(4)
    settle("feed")
    move("e2")
    feed_unit(1, 0)
    fetch_feed(1, 2, True)
    feed_unit(1, 1)
    move("k2")
    fetch_feed(1, 3, True)
    fetch_contract(1, 2)
    feed_unit(1, 2)
    fetch_contract(1, 3)
    feed_unit(1, 3)
    feed_close(1)
    close_layer(4, join_out)

    for copy in stores:
        if copy is not None:
            copy.wait()
    for flow in flows.values():
        flow.close()
    for direct in near + [bias_near, bias_far, bias_last]:
        direct.close()


def forward_all(links, own, biases, vecs, lengths, x, patch_rows, width):
    patches, items, features = patch_rows.shape
    rows, model = x.shape
    slots, padded = rows // items, -(-patches // 16) * 16
    hidden = own[EXPAND_ONE].shape[1]
    heads = width // HEAD_DIM
    anywhere = pl.BlockSpec(memory_space=ANY)
    vmem = pl.BlockSpec(memory_space=pltpu.VMEM)
    sizes = (links.tensor, links.dp, items, slots, patches, padded, width)
    mid = ((4, rows, width), BF)
    key = ((4, items * padded, width), BF)
    probs = ((4, items, slots, heads * slots), BF)
    cross_probs = ((4, items, padded, heads * slots), BF)
    feed = ((4, rows, hidden), BF)
    pf = ((items * padded, features), BF)
    self_kept = [mid] * 4 + [probs]
    cross_kept = [mid, key, key, mid, cross_probs]
    kept = self_kept * 2 + cross_kept + [feed] * 4
    outputs = [((3,) + a.shape, BF) for a in own]
    outputs += [((rows, model), BF)] * 2 + [((5, rows, model), F32), pf] + kept
    remotes = 13 * (2 + links.bits) + ARRAYS + 3
    outs = pl.pallas_call(
        functools.partial(forward_kernel, sizes),
        in_specs=[anywhere] * ARRAYS
        + [vmem] * 10
        + [pl.BlockSpec(memory_space=pltpu.SMEM), vmem, anywhere],
        out_specs=[anywhere] * ARRAYS + [vmem] * 2 + [anywhere] * (2 + len(kept)),
        out_shape=[jax.ShapeDtypeStruct(shape, dtype) for shape, dtype in outputs],
        scratch_shapes=[
            pltpu.VMEM((4, 4 * width, model), BF),
            pltpu.VMEM((4, 2, model, hidden), BF),
            pltpu.VMEM((4, 2 * width, model), BF),
            pltpu.VMEM((4, 2 * width, features), BF),
            pltpu.VMEM((rows, model), F32),
            pltpu.VMEM((rows, model), F32),
            pltpu.VMEM((rows, model), BF),
            pltpu.VMEM((5, rows, model), F32),
            pltpu.VMEM(patch_rows.shape, BF),
            pltpu.VMEM((features // 128, items * padded, 128), F32),
            pltpu.VMEM(*pf),
            pltpu.VMEM((5, 3, model), F32),
        ]
        + [pltpu.VMEM(*item) for item in self_kept + cross_kept + [feed] * 2]
        + [pltpu.VMEM((rows, width), F32)] * 4
        + [
            pltpu.VMEM((4, 8, model), F32),
            pltpu.SemaphoreType.DMA((remotes,)),
            pltpu.SemaphoreType.DMA((remotes,)),
            pltpu.SemaphoreType.DMA((64,)),
            pltpu.SemaphoreType.DMA((32,)),
            pltpu.SemaphoreType.DMA,
        ],
        compiler_params=pltpu.CompilerParams(
            collective_id=1, has_side_effects=True, vmem_limit_bytes=60 * 1024 * 1024
        ),
        name="forward_and_gather",
    )(*own, *biases, *vecs, lengths, x, patch_rows)
    n = ARRAYS
    got, (text_out, join_out, e, pf), kept = outs[:n], outs[n : n + 4], outs[n + 4 :]
    return got, text_out, join_out, e, pf, kept


(
    GRAD_CONTRACT_TWO,
    GRAD_EXPAND_TWO,
    GRAD_CROSS,
    GRAD_TWO,
    GRAD_CONTRACT_ONE,
    GRAD_EXPAND_ONE,
    GRAD_ONE,
) = range(7)


def backward_kernel(sizes, *refs):
    n_tensor, n_dp, items, slots, patches, padded, width, chunk, counts = sizes
    refs = list(refs)

    def take(n):
        got, refs[:n] = refs[:n], []
        return got

    own, got = take(ARRAYS), take(ARRAYS)
    e_in, pf_in, x, text_out, text_cot, join_cot = take(6)
    vecs_in = take(6)
    self_in = [take(5), take(5)]
    cross_in = take(5)
    feed_in = [take(2), take(2)]
    keeps, sends, outs = take(7), take(7), take(7)
    small_out, grad_text, dpf = take(3)
    wbuf, wk, stage_buf, e_s, ub, ub_t, dob, acc, pacc, pf, vecs = take(11)
    q_b, k_b, v_b, a_b, p_b = self_buf = take(5)
    qc_b, kc_b, vc_b, ac_b, pc_b = cross_buf = take(5)
    h_b, slope_b = take(2)
    q_s, k_s, v_s, da_s, dq_s, dk_s, dv_s = take(7)
    dkv_s, small_keep, small_send = take(3)
    fetch_sem, store_sem, e_sem, pf_sem = take(4)
    model = x.shape[1]
    hidden = own[EXPAND_ONE].shape[1]
    side = pf.shape[1] - model

    sums = Sums(
        n_tensor,
        n_dp,
        counts,
        chunk,
        sends,
        keeps,
        outs,
        (small_send, small_keep, small_out),
        refs,
    )

    norm_rows(vecs, vecs_in[0:3], vecs_in[3:6])
    pf_copy = pltpu.make_async_copy(pf_in, pf, pf_sem)
    e_copies = [
        pltpu.make_async_copy(e_in.at[n], e_s.at[n], e_sem.at[n]) for n in range(5)
    ]
    for n in (4, 3, 2, 1, 0):
        e_copies[n].start()
    pf_copy.start()

    units = []
    for layer in (1, 0):
        expand, contract = ((EXPAND_ONE, CONTRACT_ONE), (EXPAND_TWO, CONTRACT_TWO))[layer]
        for r in range(4):
            units.append(("contract", layer, r, [(feed_in[layer][0].at[r], h_b)]))
        for r in range(4):
            units.append(
                (
                    "expand",
                    layer,
                    r,
                    [
                        (contract, 0, hidden, wbuf, hidden),
                        (expand, 0, model, wbuf, 0),
                        (feed_in[layer][1].at[r], slope_b),
                    ],
                )
            )
        for r in range(4):
            if layer == 1:
                units.append(
                    (
                        "cross",
                        0,
                        r,
                        [
                            (CROSS_OUT, 0, width, wbuf, width),
                            (JOIN_IN, 3 * width, width, wbuf, 0),
                            (KEY_VALUE, 0, 2 * width, wk, 0),
                        ]
                        + [(cross_in[n].at[r], cross_buf[n]) for n in (3, 0, 1, 2, 4)],
                    )
                )
        for r in range(4):
            first, last = ((TEXT_IN, TEXT_OUT), (JOIN_IN, JOIN_OUT))[layer]
            units.append(
                (
                    "self",
                    layer,
                    r,
                    [(last, 0, width, wbuf, 3 * width), (first, 0, 3 * width, wbuf, 0)]
                    + [(self_in[layer][n].at[r], self_buf[n]) for n in (4, 0, 1, 2, 3)],
                )
            )
    position = {unit[:3]: n for n, unit in enumerate(units)}

    def fetches(n):
        _, _, r, wanted = units[n]
        parity = n % 2
        copies = []
        for i, item in enumerate(wanted):
            if len(item) == 5:
                a, low, count, target, row = item
                source = (own[a] if r == 0 else got[a].at[r - 1]).at[pl.ds(low, count)]
                target = target.at[parity, pl.ds(row, count)]
            else:
                source, target = item
                target = target.at[parity]
            copies.append(pltpu.make_async_copy(source, target, fetch_sem.at[parity, i]))
        return copies

    def begin(n):
        if n + 1 < len(units):
            for copy in fetches(n + 1):
                copy.start()
        for copy in fetches(n):
            copy.wait()
        return n % 2

    stores = {}

    def room(r):
        j = r % 2
        if stores.get(j) is not None:
            stores[j].wait()
            stores[j] = None
        return j

    def put(array, r):
        j = r % 2
        target = (keeps, sends)[j][array]
        rows = target.shape[1]
        stores[j] = pltpu.make_async_copy(
            stage_buf.at[j, pl.ds(0, rows)], target.at[r // 2], store_sem.at[j]
        )
        stores[j].start()

    def settle():
        for j in (0, 1):
            room(j)

    def small_row(r, row, value):
        target = (small_keep, small_send)[r % 2]
        n = 8 * (r // 2) + row
        target[n : n + 1, 0 : value.shape[1]] = value

    def open_layer(n, dy):
        e_copies[n].wait()
        de, partial = norm_backward(e_s[n], vecs[n, 1:2], dy)
        for target in (small_keep, small_send):
            target[16 + 3 * n : 19 + 3 * n] = partial
        dob[...] = de.astype(BF)
        acc[...] = de

    def input_rows(n):
        rows = norm_forward(e_s[n], vecs[n, 1:2], vecs[n, 2:3])
        ub[...] = rows.astype(BF)
        ub_t[...] = rows.T.astype(BF)

    def contract_unit(layer, r):
        b = begin(position["contract", layer, r])
        j = room(r)
        stage_buf[j, 0:hidden] = dot_tn(h_b[b], dob[...]).astype(BF)
        put((GRAD_CONTRACT_ONE, GRAD_CONTRACT_TWO)[layer], r)

    def expand_unit(layer, r):
        b = begin(position["expand", layer, r])
        dh = dot_nt(dob[...], wbuf[b, hidden : 2 * hidden])
        dz = (dh * slope_b[b].astype(F32)).astype(BF)
        j = room(r)
        stage_buf[j, 0:model] = dot_nn(ub_t[...], dz).astype(BF)
        put((GRAD_EXPAND_ONE, GRAD_EXPAND_TWO)[layer], r)
        small_row(r, 6 + layer, jnp.sum(dz.astype(F32), axis=0, keepdims=True))
        acc[...] += dot_nt(dz, wbuf[b, 0:model])

    masks = head_masks(width)

    def self_unit(layer, r):
        b = begin(position["self", layer, r])
        da_s[...] = dot_nt(dob[...], wbuf[b, 3 * width : 4 * width])
        j = room(r)
        stage_buf[j, 3 * width : 4 * width] = dot_tn(a_b[b], dob[...]).astype(BF)
        q_s[...], k_s[...], v_s[...] = (
            q_b[b].astype(F32),
            k_b[b].astype(F32),
            v_b[b].astype(F32),
        )
        for group in groups(items, 8):
            spans = [pl.ds(i * slots, slots) for i in group]
            dq, dk, dv = items_backward(
                [
                    (
                        q_s[rows],
                        k_s[rows].astype(BF),
                        v_s[rows].astype(BF),
                        da_s[rows],
                        p_b[b, i],
                    )
                    for i, rows in zip(group, spans)
                ],
                masks,
            )
            for n, rows in enumerate(spans):
                dq_s[rows], dk_s[rows], dv_s[rows] = dq[n], dk[n], dv[n]
        xb = ub[...]
        total = acc[...]
        for c, part in enumerate((dq_s, dk_s, dv_s)):
            pb = part[...].astype(BF)
            stage_buf[j, c * width : (c + 1) * width] = dot_tn(pb, xb).astype(BF)
            total = total + dot_nn(pb, wbuf[b, c * width : (c + 1) * width])
            if c != 1:
                small_row(
                    r, 2 * layer + c // 2, jnp.sum(pb.astype(F32), axis=0, keepdims=True)
                )
        acc[...] = total
        put((GRAD_ONE, GRAD_TWO)[layer], r)

    def cross_unit(r):
        b = begin(position["cross", 0, r])
        da_s[...] = dot_nt(dob[...], wbuf[b, width : 2 * width])
        j = room(r)
        stage_buf[j, width : 2 * width] = dot_tn(ac_b[b], dob[...]).astype(BF)
        q_s[...] = qc_b[b].astype(F32)
        vsum = jnp.zeros((1, width), F32)
        for group in groups(items, 4):
            spans = [pl.ds(i * slots, slots) for i in group]
            keys = [pl.ds(i * padded, padded) for i in group]
            dq, dk, dv = items_backward(
                [
                    (q_s[rows], kc_b[b, part], vc_b[b, part], da_s[rows], pc_b[b, i])
                    for i, rows, part in zip(group, spans, keys)
                ],
                masks,
            )
            for n, part in enumerate(keys):
                dq_s[spans[n]] = dq[n]
                dkv_s[0, part] = dk[n].astype(BF)
                dvb = dv[n].astype(BF)
                dkv_s[1, part] = dvb
                vsum = vsum + jnp.sum(dvb.astype(F32), axis=0, keepdims=True)
        ticks(1)
        dqb = dq_s[...].astype(BF)
        stage_buf[j, 0:width] = dot_tn(dqb, ub[...]).astype(BF)
        acc[...] += dot_nn(dqb, wbuf[b, 0:width])
        small_row(r, 4, jnp.sum(dqb.astype(F32), axis=0, keepdims=True))
        small_row(r, 5, vsum)
        tails = []
        for c in range(2):
            grad = dot_tn(dkv_s[c], pf[...]).astype(BF)
            stage_buf[j, (2 + c) * width : (3 + c) * width] = grad[:, 0:model]
            tails.append(grad[:, model:])
        back = dot_nn(dkv_s[0], wk[b, 0:width]) + dot_nn(dkv_s[1], wk[b, width : 2 * width])
        for n in range(pacc.shape[0]):
            lanes = back[:, n * 128 : (n + 1) * 128]
            if r == 0:
                pacc[n] = lanes
            else:
                pacc[n] += lanes
        tail = jnp.concatenate(tails, axis=0)
        count = tail.shape[0] // (model // side)
        for c in range(model // side):
            stage_buf[j, 4 * width : 4 * width + count, c * side : (c + 1) * side] = tail[
                c * count : (c + 1) * count
            ]
        extra = stage_buf.shape[1] - 4 * width - count
        if extra > 0:
            stage_buf[j, 4 * width + count :] = jnp.zeros((extra, model), BF)
        put(GRAD_CROSS, r)

    small_keep[...] = jnp.zeros_like(small_keep)
    small_send[...] = jnp.zeros_like(small_send)
    for copy in fetches(0):
        copy.start()
    open_layer(4, join_cot[...].astype(F32))
    sums.greet()
    clock = [0]

    def ticks(count):
        for _ in range(count):
            sums.tick(clock[0])
            clock[0] += 1

    def collected(n):
        e_copies[n].wait()
        e_copies[n] = Done()

    for r in range(4):
        contract_unit(1, r)
    settle()
    ticks(1)
    collected(3)
    input_rows(3)
    ticks(1)
    for r in range(4):
        expand_unit(1, r)
        if r == 3:
            settle()
        ticks((1, 1, 1, 0)[r])
    open_layer(3, acc[...])
    collected(2)
    input_rows(2)
    pf_copy.wait()
    for r in range(4):
        cross_unit(r)
        if r == 3:
            settle()
        ticks(1)
    open_layer(2, acc[...])
    ub[...] = text_out[...]
    for r in range(4):
        self_unit(1, r)
        if r == 3:
            settle()
        ticks((1, 2, 1, 2)[r])
    open_layer(1, acc[...] + text_cot[...].astype(F32))
    for r in range(4):
        contract_unit(0, r)
    settle()
    ticks(1)
    collected(0)
    input_rows(0)
    for r in range(4):
        expand_unit(0, r)
        if r == 3:
            settle()
        ticks(1)
    open_layer(0, acc[...])
    ub[...] = x[...]
    for r in range(4):
        self_unit(0, r)
        if r == 3:
            settle()
        ticks((1, 2, 1, 2)[r])
    grad_text[...] = acc[...].astype(BF)

    def gather_patches(n, carry):
        for c in range(pacc.shape[0]):
            dpf[n, :, c * 128 : (c + 1) * 128] = pacc[
                c, pl.ds(n, items, stride=padded)
            ].astype(BF)
        return carry

    lax.fori_loop(0, patches, gather_patches, 0)
    sums.finish(clock[0])


class Done:
    def wait(self):
        pass


def backward_all(links, own, got, e, pf, x, text_out, cots, vecs, kept, patches, items, width):
    rows, model = x.shape
    slots, padded = rows // items, pf.shape[0] // items
    hidden = own[EXPAND_ONE].shape[1]
    heads = width // HEAD_DIM
    chunk = links.chunk
    anywhere = pl.BlockSpec(memory_space=ANY)
    vmem = pl.BlockSpec(memory_space=pltpu.VMEM)
    cross_rows = 2 * width + 2 * width * pf.shape[1] // model
    extents = [hidden, model, cross_rows, 4 * width, hidden, model, 4 * width]
    extents = [-(-extent // chunk) * chunk for extent in extents]
    counts = tuple(extent // chunk for extent in extents)
    sizes = (links.tensor, links.dp, items, slots, patches, padded, width, chunk, counts)
    pairs = [((2, extent, model), BF) for extent in extents]
    totals = [((extent, model), BF) for extent in extents]
    units, small = 8, 32
    outputs = pairs * 2 + totals
    outputs += [
        ((small - units, model), F32),
        ((rows, model), BF),
        ((patches, items, pf.shape[1]), BF),
    ]
    f32_rows = pltpu.VMEM((rows, width), F32)
    outs = pl.pallas_call(
        functools.partial(backward_kernel, sizes),
        in_specs=[anywhere] * (2 * ARRAYS + 2) + [vmem] * 10 + [anywhere] * len(kept),
        out_specs=[anywhere] * 21 + [vmem] * 3,
        out_shape=[jax.ShapeDtypeStruct(shape, dtype) for shape, dtype in outputs],
        scratch_shapes=[
            pltpu.VMEM((2, 2 * hidden, model), BF),
            pltpu.VMEM((2, 2 * width, pf.shape[1]), BF),
            pltpu.VMEM((2, max(extents), model), BF),
            pltpu.VMEM((5, rows, model), F32),
            pltpu.VMEM((rows, model), BF),
            pltpu.VMEM((model, rows), BF),
            pltpu.VMEM((rows, model), BF),
            pltpu.VMEM((rows, model), F32),
            pltpu.VMEM((pf.shape[1] // 128, pf.shape[0], 128), F32),
            pltpu.VMEM(pf.shape, BF),
            pltpu.VMEM((5, 3, model), F32),
        ]
        + [pltpu.VMEM((2, rows, width), BF)] * 4
        + [pltpu.VMEM((2, items, slots, heads * slots), BF)]
        + [pltpu.VMEM((2, rows, width), BF)]
        + [pltpu.VMEM((2, pf.shape[0], width), BF)] * 2
        + [pltpu.VMEM((2, rows, width), BF)]
        + [pltpu.VMEM((2, items, padded, heads * slots), BF)]
        + [pltpu.VMEM((2, rows, hidden), BF)] * 2
        + [f32_rows] * 7
        + [
            pltpu.VMEM((2, pf.shape[0], width), BF),
            pltpu.VMEM((small, model), F32),
            pltpu.VMEM((small, model), F32),
            pltpu.SemaphoreType.DMA((2, 8)),
            pltpu.SemaphoreType.DMA((2,)),
            pltpu.SemaphoreType.DMA((5,)),
            pltpu.SemaphoreType.DMA,
        ]
        + Sums.scratch(links.dp, chunk, model, small, units),
        compiler_params=pltpu.CompilerParams(
            collective_id=0, has_side_effects=True, vmem_limit_bytes=60 * 1024 * 1024
        ),
        name="backward_and_sums",
    )(*own, *got, e, pf, x, text_out, *cots, *vecs, *kept)
    return outs[14:21], outs[21], outs[22], outs[23]


def finish_kernel(width, *refs):
    refs = list(refs)

    def take(n):
        got, refs[:n] = refs[:n], []
        return got

    totals, passed, (small,) = take(7), take(4), take(1)
    passed_out = take(4)
    text_in, text_out, expand_one, contract_one, join_in = take(5)
    join_out, cross_out, key_value, expand_two, contract_two = take(5)
    text_bias, join_bias, hidden_one, hidden_two = take(4)
    text_shared, join_shared = take(3), take(3)
    half, full, keys = take(3)
    bounced = take(4)
    load_sem, store_sem = take(2)
    model = full.shape[2]
    side = keys.shape[1] - model
    count = 2 * width * side // model

    loads, stores = [], []
    for n in range(7):
        rows = totals[n].shape[0]
        loads.append(
            pltpu.make_async_copy(totals[n], half.at[n, pl.ds(0, rows)], load_sem.at[n])
        )
        loads[n].start()
    for n in range(4):
        loads.append(pltpu.make_async_copy(passed[n], bounced[n], load_sem.at[7 + n]))
        loads[7 + n].start()

    def store(source, target):
        copy = pltpu.make_async_copy(source, target, store_sem.at[len(stores)])
        copy.start()
        stores.append(copy)

    text_bias[...] = small[0:2, 0:width]
    join_bias[...] = small[2:6, 0:width]
    hidden_one[...] = small[6]
    hidden_two[...] = small[7]
    for n in range(5):
        for c in range(3):
            row = 8 + 3 * n + c
            target, m = (text_shared[c], n) if n < 2 else (join_shared[c], n - 2)
            target[m : m + 1] = small[row : row + 1]

    def widen(n):
        loads[n].wait()
        rows = totals[n].shape[0]
        full[n, 0:rows] = half[n, 0:rows].astype(F32)

    def send(n, lo, rows, target):
        store(full.at[n, pl.ds(lo, rows)], target)

    for n, target in (
        (GRAD_CONTRACT_TWO, contract_two),
        (GRAD_EXPAND_TWO, expand_two),
        (GRAD_CONTRACT_ONE, contract_one),
        (GRAD_EXPAND_ONE, expand_one),
    ):
        widen(n)
        send(n, 0, target.shape[0], target)
    widen(GRAD_CROSS)
    send(GRAD_CROSS, 0, width, join_in.at[pl.ds(3 * width, width)])
    send(GRAD_CROSS, width, width, cross_out)
    keys[:, 0:model] = full[GRAD_CROSS, 2 * width : 4 * width]
    for c in range(model // side):
        keys[c * count : (c + 1) * count, model:] = full[
            GRAD_CROSS, 4 * width : 4 * width + count, c * side : (c + 1) * side
        ]
    store(keys, key_value)
    widen(GRAD_TWO)
    send(GRAD_TWO, 0, 3 * width, join_in.at[pl.ds(0, 3 * width)])
    send(GRAD_TWO, 3 * width, width, join_out)
    widen(GRAD_ONE)
    send(GRAD_ONE, 0, 3 * width, text_in)
    send(GRAD_ONE, 3 * width, width, text_out)
    for n in range(4):
        loads[7 + n].wait()
        store(bounced[n], passed_out[n])
    for copy in stores:
        copy.wait()


def finish_all(totals, passed, small, width, hidden, features):
    model = totals[0].shape[1]
    anywhere = pl.BlockSpec(memory_space=ANY)
    vmem = pl.BlockSpec(memory_space=pltpu.VMEM)
    big = [
        (3 * width, model),
        (width, model),
        (model, hidden),
        (hidden, model),
        (4 * width, model),
        (width, model),
        (width, model),
        (2 * width, features),
        (model, hidden),
        (hidden, model),
    ]
    little = [(2, width), (4, width), (hidden,), (hidden,)]
    little += [(2, model)] * 3 + [(3, model)] * 3
    most = max(total.shape[0] for total in totals)
    return pl.pallas_call(
        functools.partial(finish_kernel, width),
        in_specs=[anywhere] * 11 + [vmem],
        out_specs=[anywhere] * (4 + len(big)) + [vmem] * len(little),
        out_shape=[jax.ShapeDtypeStruct(a.shape, a.dtype) for a in passed]
        + [jax.ShapeDtypeStruct(shape, F32) for shape in big + little],
        scratch_shapes=[
            pltpu.VMEM((7, most, model), BF),
            pltpu.VMEM((7, most, model), F32),
            pltpu.VMEM((2 * width, features), F32),
        ]
        + [pltpu.VMEM(a.shape, a.dtype) for a in passed]
        + [
            pltpu.SemaphoreType.DMA((11,)),
            pltpu.SemaphoreType.DMA((16,)),
        ],
        compiler_params=pltpu.CompilerParams(vmem_limit_bytes=60 * 1024 * 1024),
        name="finish",
    )(*totals, *passed, small)


class Links:
    def __init__(self, mesh):
        self.tensor = mesh.shape["tensor"]
        self.dp = mesh.shape["dp"]
        self.bits = self.dp.bit_length() - 1
        self.chunk = 128


def turned(array):
    array = jnp.swapaxes(array, 1, 2)
    return array.reshape(-1, array.shape[2])


def turned_back(rows, units):
    return jnp.swapaxes(rows.reshape(-1, units, rows.shape[1]), 1, 2)


def per_device(
    links,
    text_rows,
    patch_features,
    lengths,
    text_cotangent,
    join_cotangent,
    text_project_in,
    text_project_bias,
    text_project_out,
    text_expand,
    text_expand_bias,
    text_contract,
    text_out_bias,
    text_norm_gain,
    text_norm_shift,
    join_project_in,
    join_project_bias,
    join_project_out,
    cross_project_out,
    cross_key_value,
    join_expand,
    join_expand_bias,
    join_contract,
    join_out_bias,
    join_norm_gain,
    join_norm_shift,
):
    items, slots, model = text_rows.shape
    patches, patch_width = patch_features.shape[1:]
    width = text_project_in.shape[2]
    hidden = text_expand.shape[1]

    own = [
        turned(text_project_in),
        text_project_out,
        text_expand,
        text_contract,
        turned(join_project_in),
        join_project_out,
        turned(cross_key_value),
        cross_project_out,
        join_expand,
        join_contract,
    ]
    biases = (text_project_bias, join_project_bias, text_expand_bias, join_expand_bias)
    vecs = (text_out_bias, text_norm_gain, text_norm_shift)
    vecs += (join_out_bias, join_norm_gain, join_norm_shift)
    x = text_rows.reshape(items * slots, model)
    text_cot = text_cotangent.reshape(items * slots, model)
    join_cot = join_cotangent.reshape(items * slots, model)
    patch_rows = jnp.swapaxes(patch_features, 0, 1)

    got, text_out, join_out, e, pf, kept = forward_all(
        links, own, biases, vecs, lengths, x, patch_rows, width
    )
    totals, small, grad_text, grad_patches = backward_all(
        links, own, got, e, pf, x, text_out, (text_cot, join_cot), vecs, kept, patches, items, width
    )
    outs = finish_all(
        totals, (text_out, join_out, grad_text, grad_patches), small, width, hidden, patch_width
    )
    text_out, join_out, grad_text, grad_patches = outs[:4]
    text_in, text_project, expand_one, contract_one, join_in = outs[4:9]
    join_project, cross_project, key_value, expand_two, contract_two = outs[9:14]
    text_bias, join_bias, hidden_one, hidden_two = outs[14:18]

    return (
        text_out.reshape(text_rows.shape),
        join_out.reshape(text_rows.shape),
        grad_text.reshape(text_rows.shape),
        jnp.swapaxes(grad_patches, 0, 1),
        turned_back(text_in, width),
        text_bias,
        text_project,
        expand_one,
        hidden_one,
        contract_one,
        *outs[18:21],
        turned_back(join_in, width),
        join_bias,
        join_project,
        cross_project,
        turned_back(key_value, width),
        expand_two,
        hidden_two,
        contract_two,
        *outs[21:24],
    )


def solution(mesh):
    rows = P(("dp", "tensor"), None, None)
    last = P(None, None, "tensor")
    second = P(None, "tensor")
    first = P("tensor", None)
    line = P("tensor")
    full = P()
    in_specs = (
        (rows, rows, P(("dp", "tensor")), rows, rows)
        + (last, second, first, second, line, first, full, full, full)
        + (last, second, first, first, last, second, line, first, full, full, full)
    )
    out_specs = (
        (rows, rows, rows, rows)
        + (last, second, first, second, line, first, full, full, full)
        + (last, second, first, first, last, second, line, first, full, full, full)
    )
    return jax.shard_map(
        functools.partial(per_device, Links(mesh)),
        mesh=mesh,
        in_specs=in_specs,
        out_specs=out_specs,
        check_vma=False,
    )
```

```python
import functools

import jax
import jax.numpy as jnp
from jax import lax
from jax.experimental import pallas as pl
from jax.experimental.pallas import tpu as pltpu
from jax.sharding import PartitionSpec as P

HEAD_DIM = 64
BF = jnp.bfloat16
F32 = jnp.float32
ANY = pl.ANY


def dot_nn(a, b):
    return lax.dot_general(a, b, (((1,), (0,)), ((), ())), preferred_element_type=F32)


def dot_nt(a, b):
    return lax.dot_general(a, b, (((1,), (1,)), ((), ())), preferred_element_type=F32)


def dot_tn(a, b):
    return lax.dot_general(a, b, (((0,), (0,)), ((), ())), preferred_element_type=F32)


def norm_forward(e, gain, shift):
    center = e - jnp.mean(e, axis=-1, keepdims=True)
    variance = jnp.mean(center * center, axis=-1, keepdims=True)
    return center * lax.rsqrt(variance + 1e-12) * gain + shift


def norm_backward(e, gain, dy):
    center = e - jnp.mean(e, axis=-1, keepdims=True)
    variance = jnp.mean(center * center, axis=-1, keepdims=True)
    rstd = lax.rsqrt(variance + 1e-12)
    normed = center * rstd
    scaled = dy * gain
    de = rstd * (
        scaled
        - jnp.mean(scaled, axis=-1, keepdims=True)
        - normed * jnp.mean(scaled * normed, axis=-1, keepdims=True)
    )
    sums = jnp.concatenate(
        [
            jnp.sum(de, axis=0, keepdims=True),
            jnp.sum(dy * normed, axis=0, keepdims=True),
            jnp.sum(dy, axis=0, keepdims=True),
        ],
        axis=0,
    )
    return de, sums


def head_masks(width):
    lane = lax.broadcasted_iota(jnp.int32, (1, width), 1)
    return [
        ((lane >= h * HEAD_DIM) & (lane < (h + 1) * HEAD_DIM)).astype(F32)
        for h in range(width // HEAD_DIM)
    ]


def groups(count, most):
    return [range(i, min(i + most, count)) for i in range(0, count, most)]


def stack_heads(rows, masks):
    return jnp.concatenate([rows * mask for mask in masks], axis=0).astype(BF)


def merge_heads(stacked, masks):
    count = stacked.shape[0] // len(masks)
    total = stacked[:count] * masks[0]
    for h in range(1, len(masks)):
        total = total + stacked[h * count : (h + 1) * count] * masks[h]
    return total


def items_forward(operands, masks):
    stacked = [stack_heads(q, masks) for q, _, _, _ in operands]
    scores = [dot_nt(k, qs) for qs, (_, k, _, _) in zip(stacked, operands)]
    row = lax.broadcasted_iota(jnp.int32, scores[0].shape, 0)
    scores = [
        jnp.where(row < length, s * HEAD_DIM ** (-0.5), -1e30)
        for s, (_, _, _, length) in zip(scores, operands)
    ]
    most = [jnp.max(s, axis=0, keepdims=True) for s in scores]
    weights = [jnp.exp(s - m) for s, m in zip(scores, most)]
    totals = [jnp.sum(w, axis=0, keepdims=True) for w in weights]
    probs = [(w / t).astype(BF) for w, t in zip(weights, totals)]
    mixed = [dot_tn(p, v) for p, (_, _, v, _) in zip(probs, operands)]
    return probs, [merge_heads(m, masks) for m in mixed]


def items_backward(operands, masks):
    qs = [stack_heads(q, masks) for q, _, _, _, _ in operands]
    das = [stack_heads(da, masks) for _, _, _, da, _ in operands]
    dp = [dot_nt(v, g) for g, (_, _, v, _, _) in zip(das, operands)]
    dv = [dot_nn(probs, g) for g, (_, _, _, _, probs) in zip(das, operands)]
    p = [probs.astype(F32) for _, _, _, _, probs in operands]
    inner = [jnp.sum(a * b, axis=0, keepdims=True) for a, b in zip(p, dp)]
    ds = [(a * (b - c)).astype(BF) for a, b, c in zip(p, dp, inner)]
    scaling = HEAD_DIM ** (-0.5)
    dk = [dot_nn(s, g) * scaling for s, g in zip(ds, qs)]
    dq = [dot_tn(s, k) for s, (_, k, _, _, _) in zip(ds, operands)]
    return [merge_heads(part, masks) * scaling for part in dq], dk, dv


def pair(index, width):
    return index + width - 2 * width * ((index // width) % 2)


def rest(m, n):
    return m % n if isinstance(m, int) else lax.rem(m, n)


def when(condition, act):
    if isinstance(condition, bool):
        if condition:
            act()
    else:
        pl.when(condition)(act)


def halvings(n_dp, chunk):
    return min(n_dp, chunk // 16).bit_length() - 1


class Sums:
    def __init__(self, n_tensor, n_dp, counts, chunk, sends, keeps, outs, small, scratch):
        self.n_dp, self.bits = n_dp, n_dp.bit_length() - 1
        self.counts, self.chunk = counts, chunk
        self.cuts = halvings(n_dp, chunk)
        self.sends, self.keeps, self.outs = sends, keeps, outs
        self.small_send, self.small_keep, self.small_out = small
        scratch = list(scratch)
        bits = self.bits
        self.core_in, self.kept, self.far_out, self.far_in, self.own, self.whole = scratch[:6]
        self.parts, self.halves = scratch[6 : 6 + bits], scratch[6 + bits : 6 + 2 * bits]
        self.gathered, self.tiny_sum, self.tiny_core, self.tiny_far, self.tiny_dp = scratch[
            6 + 2 * bits : 11 + 2 * bits
        ]
        self.send_sem, self.recv_sem, self.kept_sem, self.out_sem = scratch[
            11 + 2 * bits : 15 + 2 * bits
        ]
        self.tiny_send, self.tiny_recv = scratch[15 + 2 * bits :]
        t, d = lax.axis_index("tensor"), lax.axis_index("dp")
        self.dp_bits = [(d // (1 << b)) % 2 for b in range(bits)]
        self.peers = [{"tensor": pair(t, 1)}, {"tensor": lax.rem(t + 2, n_tensor)}]
        self.peers += [{"dp": pair(d, 1 << b)} for b in range(bits)]
        self.total = sum(counts)
        self.stages = 2 + bits + self.cuts
        self.slots, self.depth = self.core_in.shape[0], self.gathered.shape[0]

    def greet(self):
        barrier = pltpu.get_barrier_semaphore()
        for peer in self.peers:
            pl.semaphore_signal(
                barrier, inc=1, device_id=peer, device_id_type=pl.DeviceIdType.MESH
            )
        pl.semaphore_wait(barrier, len(self.peers))

    def remote(self, source, target, stage, slot, peer):
        return pltpu.make_async_remote_copy(
            src_ref=source,
            dst_ref=target,
            send_sem=self.send_sem.at[stage, slot],
            recv_sem=self.recv_sem.at[stage, slot],
            device_id=self.peers[peer],
            device_id_type=pl.DeviceIdType.MESH,
        )

    def region(self, b):
        b = min(b, self.cuts - 1)
        size = self.chunk >> (b + 1)
        start = 0
        for i in range(b + 1):
            start = start + self.dp_bits[i] * (self.chunk >> (i + 1))
        return pl.ds(pl.multiple_of(start, size), size)

    def half(self, b, mine):
        if b >= self.cuts:
            return pl.ds(0, self.chunk >> self.cuts)
        size = self.chunk >> (b + 1)
        which = self.dp_bits[b] if mine else 1 - self.dp_bits[b]
        return pl.ds(pl.multiple_of(which * size, size), size)

    def halved(self, b):
        return self.whole if b == 0 else self.parts[b - 1]

    def copy_of(self, stage, m):
        slot, two = rest(m, self.slots), rest(m, 2)
        if stage == 0:
            source = self.sends[0].at[:, pl.ds(0, self.chunk)]
            return self.remote(source, self.core_in.at[slot], 0, slot, 0)
        if stage == 1:
            ring = rest(m, self.far_in.shape[0])
            return self.remote(self.far_out.at[slot], self.far_in.at[ring], 1, ring, 1)
        if stage < 2 + self.bits:
            b = stage - 2
            source = self.halved(b).at[two, self.half(b, False)]
            return self.remote(source, self.halves[b].at[slot], stage, slot, 2 + b)
        b = 1 + self.bits + self.cuts - stage
        held = self.gathered.at[rest(m, self.depth), self.region(b)]
        return self.remote(held, held, stage, slot, 2 + b)

    def kept_copy(self, a, start, m):
        two = rest(m, 2)
        source = self.keeps[a].at[:, pl.ds(start, self.chunk)]
        return pltpu.make_async_copy(source, self.kept.at[two], self.kept_sem.at[two])

    def out_copy(self, a, start, m):
        ring = rest(m, self.depth)
        target = self.outs[a].at[pl.ds(start, self.chunk)]
        return pltpu.make_async_copy(self.gathered.at[ring], target, self.out_sem.at[ring])

    def each_array(self, m, act):
        base = 0
        for a, count in enumerate(self.counts):
            if isinstance(m, int):
                start = (m - base) * self.chunk
                inside = base <= m < base + count
            else:
                start = pl.multiple_of((m - base) * self.chunk, self.chunk)
                inside = (m >= base) & (m < base + count)
            when(inside, functools.partial(act, a, start))
            base += count

    def process(self, step, m):
        if step == 2:
            return
        stage = step if step < 2 else step - 1
        slot, two, ring = rest(m, self.slots), rest(m, 2), rest(m, self.depth)
        stages, bits = self.stages, self.bits
        if stage == 0:

            def begin(a, start):
                source = self.sends[a].at[:, pl.ds(start, self.chunk)]
                self.remote(source, self.core_in.at[slot], 0, slot, 0).start()
                self.kept_copy(a, start, m).start()

            self.each_array(m, begin)
            return
        if stage <= stages:
            self.copy_of(stage - 1, m).wait()
        if stage == 1:
            self.kept_copy(0, 0, m).wait()
            self.far_out[slot] = self.kept[two, 1] + self.core_in[slot, 1]
            self.own[slot] = self.kept[two, 0] + self.core_in[slot, 0]
        elif stage == 2:
            self.whole[two] = self.own[slot] + self.far_in[rest(m, self.far_in.shape[0])]
        elif stage <= 2 + bits:
            b = stage - 3
            summed = self.halved(b)[two, self.half(b, True)] + self.halves[b][slot]
            if b < bits - 1:
                self.parts[b][two] = summed
            else:
                self.gathered[ring, self.region(b)] = summed
        elif stage == stages:
            self.each_array(m, lambda a, start: self.out_copy(a, start, m).start())
        elif stage == stages + 1:
            self.out_copy(0, 0, m).wait()
        if stage < stages:
            self.copy_of(stage, m).start()

    def tiny(self, stage):
        count = self.tiny_far.shape[0]
        if stage == 0:
            source, target = self.small_send, self.tiny_core
        elif stage == 1:
            first = self.small_keep.shape[0] - count
            source, target = self.tiny_sum.at[0, pl.ds(first, count)], self.tiny_far
        else:
            source = self.tiny_sum.at[stage - 1, pl.ds(0, count)]
            target = self.tiny_dp.at[stage - 2]
        return pltpu.make_async_remote_copy(
            src_ref=source,
            dst_ref=target,
            send_sem=self.tiny_send.at[stage],
            recv_sem=self.tiny_recv.at[stage],
            device_id=self.peers[stage],
            device_id_type=pl.DeviceIdType.MESH,
        )

    def tiny_step(self, stage):
        bits = self.bits
        count = self.tiny_far.shape[0]
        units = self.small_keep.shape[0] - count
        if stage > 0:
            self.tiny(stage - 1).wait()
        if stage == 1:
            self.tiny_sum[0] = self.small_keep[...] + self.tiny_core[...]
        elif stage == 2:
            self.tiny_sum[1, 0:units] = self.tiny_sum[0, 0:units] + self.tiny_far[0:units]
            self.tiny_sum[1, units:count] = (
                self.tiny_sum[0, 2 * units :] + self.tiny_far[units:]
            )
        elif stage > 2:
            summed = self.tiny_sum[stage - 2, 0:count] + self.tiny_dp[stage - 3]
            if stage == 2 + bits:
                self.small_out[...] = summed
            else:
                self.tiny_sum[stage - 1, 0:count] = summed
        if stage < 2 + bits:
            self.tiny(stage).start()

    def tick(self, k):
        for step in range(self.stages + 3):
            m = k - step
            inside = (m >= 0) & (m < self.total)
            when(inside, functools.partial(self.process, step, m))

    def finish(self, first):
        def step(k, carry):
            self.tick(k)
            for stage in range(3 + self.bits):
                when(k == first + stage, functools.partial(self.tiny_step, stage))
            return carry

        lax.fori_loop(first, self.total + self.stages + 3, step, 0)

    @staticmethod
    def scratch(n_dp, chunk, model, small, units):
        bits, cuts = n_dp.bit_length() - 1, halvings(n_dp, chunk)
        slots, far, depth, stages = 4, 6, 8, 2 + bits + cuts
        sizes = [chunk >> min(b + 1, cuts) for b in range(bits)]
        return (
            [
                pltpu.VMEM((slots, 2, chunk, model), BF),
                pltpu.VMEM((2, 2, chunk, model), BF),
                pltpu.VMEM((slots, chunk, model), BF),
                pltpu.VMEM((far, chunk, model), BF),
                pltpu.VMEM((slots, chunk, model), BF),
                pltpu.VMEM((2, chunk, model), BF),
            ]
            + [pltpu.VMEM((2, size, model), BF) for size in sizes]
            + [pltpu.VMEM((slots, size, model), BF) for size in sizes]
            + [
                pltpu.VMEM((depth, chunk, model), BF),
                pltpu.VMEM((1 + bits, small, model), F32),
                pltpu.VMEM((small, model), F32),
                pltpu.VMEM((small - units, model), F32),
                pltpu.VMEM((bits, small - units, model), F32),
                pltpu.SemaphoreType.DMA((stages, far)),
                pltpu.SemaphoreType.DMA((stages, far)),
                pltpu.SemaphoreType.DMA((2,)),
                pltpu.SemaphoreType.DMA((depth,)),
                pltpu.SemaphoreType.DMA((2 + bits,)),
                pltpu.SemaphoreType.DMA((2 + bits,)),
            ]
        )


class Flow:
    def __init__(self, net, a, lo, hi, spread):
        rows = hi - lo
        own, got = net.own[a], net.got[a]
        here = pl.ds(lo, rows)
        self.copies = []
        self.started = self.waited = 0
        if spread and rows % (16 * net.n_dp) == 0:

            def region(count):
                size, start = rows, lo
                for i in range(count):
                    size //= 2
                    start = start + net.dp_bits[i] * size
                return pl.ds(pl.multiple_of(start, 16), size)

            part = region(net.bits)
            self.add(net, own.at[part], got.at[1, part], net.far_peer)
            for b in reversed(range(net.bits)):
                part = region(b + 1)
                self.add(net, got.at[1, part], got.at[1, part], net.dp_peers[b])
        else:
            self.add(net, own.at[here], got.at[1, here], net.far_peer)
        self.add(net, got.at[1, here], got.at[2, here], net.core_peer)

    def add(self, net, source, target, peer):
        self.copies.append(net.remote(source, target, peer))

    def advance(self):
        if self.started < len(self.copies):
            if self.started > 0:
                self.await_copy(self.started - 1)
            self.copies[self.started].start()
            self.started += 1

    def await_copy(self, n):
        while self.started <= n:
            self.advance()
        while self.waited <= n:
            self.copies[self.waited].wait_recv()
            self.waited += 1

    def need(self, r):
        self.await_copy(len(self.copies) - (2 if r == 2 else 1))

    def close(self):
        self.need(3)
        for copy in self.copies:
            copy.wait_send()


class Direct:
    def __init__(self, copy):
        self.copy, self.state = copy, 0

    def advance(self):
        if self.state == 0:
            self.copy.start()
            self.state = 1

    def need(self):
        self.advance()
        if self.state == 1:
            self.copy.wait_recv()
            self.state = 2

    def close(self):
        self.need()
        self.copy.wait_send()


class Net:
    def __init__(self, n_tensor, n_dp, own, got, send_sem, recv_sem):
        self.n_dp, self.bits = n_dp, n_dp.bit_length() - 1
        self.own, self.got = own, got
        self.send_sem, self.recv_sem = send_sem, recv_sem
        self.count = 0
        t, d = lax.axis_index("tensor"), lax.axis_index("dp")
        self.core_peer = {"tensor": pair(t, 1)}
        self.far_peer = {"tensor": lax.rem(t + 2, n_tensor)}
        self.dp_peers = [{"dp": pair(d, 1 << b)} for b in range(self.bits)]
        self.dp_bits = [(d // (1 << b)) % 2 for b in range(self.bits)]
        peers = [self.core_peer, self.far_peer] + self.dp_peers
        barrier = pltpu.get_barrier_semaphore()
        for peer in peers:
            pl.semaphore_signal(
                barrier, inc=1, device_id=peer, device_id_type=pl.DeviceIdType.MESH
            )
        pl.semaphore_wait(barrier, len(peers))

    def remote(self, source, target, peer):
        n = self.count
        self.count += 1
        return pltpu.make_async_remote_copy(
            src_ref=source,
            dst_ref=target,
            send_sem=self.send_sem.at[n],
            recv_sem=self.recv_sem.at[n],
            device_id=peer,
            device_id_type=pl.DeviceIdType.MESH,
        )


TEXT_IN, TEXT_OUT, EXPAND_ONE, CONTRACT_ONE, JOIN_IN = range(5)
JOIN_OUT, KEY_VALUE, CROSS_OUT, EXPAND_TWO, CONTRACT_TWO = range(5, 10)
ARRAYS = 10


def spread_patches(source, wide, target, items, padded):
    patches = source.shape[0]
    least = patches // 8 * 8
    groups, _, lanes = wide.shape
    for i in range(items):
        rows = pl.ds(i * padded + least, padded - least)
        wide[:, rows] = jnp.zeros((groups, padded - least, lanes), F32)

    def step(n, carry):
        for c in range(groups):
            wide[c, pl.ds(n, items, stride=padded)] = source[
                n, :, c * lanes : (c + 1) * lanes
            ].astype(F32)
        return carry

    lax.fori_loop(0, patches, step, 0)
    for c in range(groups):
        target[:, c * lanes : (c + 1) * lanes] = wide[c].astype(BF)


def norm_rows(vecs, text, join):
    for c in range(3):
        for n in range(2):
            vecs[n, c : c + 1] = text[c][...].astype(F32)[n : n + 1]
        for n in range(3):
            vecs[2 + n, c : c + 1] = join[c][...].astype(F32)[n : n + 1]


def forward_kernel(sizes, *refs):
    n_tensor, n_dp, items, slots, patches, padded, width = sizes
    refs = list(refs)

    def take(n):
        got, refs[:n] = refs[:n], []
        return got

    own = take(ARRAYS)
    bias_in, vecs_in = take(4), take(6)
    lengths, x, pf_in = take(3)
    got = take(ARRAYS)
    text_out, join_out, e_out, pf_out = take(4)
    self_out = [take(5), take(5)]
    cross_out = take(5)
    feed_out = [take(2), take(2)]
    ws, wf, wc, wk, acc, u, ub, e_s = take(8)
    pf_raw, pf_wide, pf, vecs = take(4)
    q_st, k_st, v_st, a_st, p_st = self_st = take(5)
    cross_st = take(5)
    qc_st, kc_st, vc_st, ac_st, pc_st = cross_st
    h_st, slope_st = feed_st = take(2)
    q_s, k_s, v_s, a_s, bias = take(5)
    send_sem, recv_sem, fetch_sem, store_sem, pf_sem = take(5)
    model = x.shape[1]
    hidden = own[EXPAND_ONE].shape[1]

    pf_copy = pltpu.make_async_copy(pf_in, pf_raw, pf_sem)
    pf_copy.start()
    net = Net(n_tensor, n_dp, own, got, send_sem, recv_sem)
    middle = 2 * width
    flows = {
        "s1p": Flow(net, TEXT_IN, 0, middle, True),
        "s1v": Flow(net, TEXT_IN, middle, 3 * width, False),
        "s1o": Flow(net, TEXT_OUT, 0, width, False),
        "e1": Flow(net, EXPAND_ONE, 0, model, True),
        "k1": Flow(net, CONTRACT_ONE, 0, hidden, True),
        "s2p": Flow(net, JOIN_IN, 0, middle, True),
        "s2v": Flow(net, JOIN_IN, middle, 3 * width, False),
        "s2o": Flow(net, JOIN_OUT, 0, width, False),
        "ckv": Flow(net, KEY_VALUE, 0, middle, False),
        "cq": Flow(net, JOIN_IN, 3 * width, 4 * width, False),
        "co": Flow(net, CROSS_OUT, 0, width, False),
        "e2": Flow(net, EXPAND_TWO, 0, model, True),
        "k2": Flow(net, CONTRACT_TWO, 0, hidden, True),
    }
    near = [Direct(net.remote(own[a], got[a].at[0], net.core_peer)) for a in range(ARRAYS)]
    bias_near = Direct(net.remote(bias.at[0], bias.at[1], net.core_peer))
    bias_far = Direct(net.remote(bias.at[0], bias.at[2], net.far_peer))
    bias_last = Direct(net.remote(bias.at[2], bias.at[3], net.core_peer))

    def move(names):
        for name in names.split():
            flows[name].advance()

    fetches = {}

    fetch_count = [0]

    def fetch(key, r, wanted):
        if key in fetches:
            return
        fetches[key] = []
        for a, lo, hi, target, names in wanted:
            if r == 1:
                near[a].need()
            elif r > 1:
                for name in names:
                    flows[name].need(r)
            source = own[a] if r == 0 else got[a].at[r - 1]
            copy = pltpu.make_async_copy(
                source.at[pl.ds(lo, hi - lo)], target, fetch_sem.at[fetch_count[0]]
            )
            fetch_count[0] += 1
            copy.start()
            fetches[key].append(copy)

    def arrive(key):
        for copy in fetches[key]:
            copy.wait()

    stores = []

    def store(source, target):
        copy = pltpu.make_async_copy(source, target, store_sem.at[len(stores)])
        copy.start()
        stores.append(copy)
        return len(stores) - 1

    masks = head_masks(width)
    pending = {"self": [], "feed": []}

    def settle(kind):
        for n in pending[kind]:
            stores[n].wait()
            stores[n] = None
        pending[kind] = []

    def close_layer(n, target=None):
        e = acc[...]
        e_s[n] = e
        store(e_s.at[n], e_out.at[n])
        y = norm_forward(e, vecs[n, 1:2], vecs[n, 2:3])
        if target is not None:
            yb = y.astype(BF)
            target[...] = yb
            ub[...] = yb
            u[...] = yb.astype(F32)
        else:
            u[...] = y
            ub[...] = y.astype(BF)

    def open_layer(n):
        acc[...] = u[...] + vecs[n, 0:1]

    def fetch_self(layer, r):
        first = pl.ds(0, 3 * width)
        last = pl.ds(3 * width, width)
        if layer == 0:
            wanted = [
                (TEXT_IN, 0, 3 * width, ws.at[r, first], ("s1p", "s1v")),
                (TEXT_OUT, 0, width, ws.at[r, last], ("s1o",)),
            ]
        else:
            wanted = [
                (JOIN_IN, 0, 3 * width, ws.at[r, first], ("s2p", "s2v")),
                (JOIN_OUT, 0, width, ws.at[r, last], ("s2o",)),
            ]
        fetch(("self", layer, r), r, wanted)

    def self_unit(layer, r):
        fetch_self(layer, r)
        arrive(("self", layer, r))
        xb = ub[...]
        q = (
            dot_nt(xb, ws[r, 0:width]) + bias[r, 2 * layer : 2 * layer + 1, 0:width]
        ).astype(BF)
        k = dot_nt(xb, ws[r, width : 2 * width]).astype(BF)
        v = (
            dot_nt(xb, ws[r, 2 * width : 3 * width])
            + bias[r, 2 * layer + 1 : 2 * layer + 2, 0:width]
        ).astype(BF)
        q_st[r], k_st[r], v_st[r] = q, k, v
        q_s[...], k_s[...], v_s[...] = q.astype(F32), k.astype(F32), v.astype(F32)
        for group in groups(items, 8):
            spans = [pl.ds(i * slots, slots) for i in group]
            probs, mixed = items_forward(
                [
                    (q_s[rows], k_s[rows].astype(BF), v_s[rows].astype(BF), lengths[i])
                    for i, rows in zip(group, spans)
                ],
                masks,
            )
            for n, i in enumerate(group):
                p_st[r, i] = probs[n]
                a_s[spans[n]] = mixed[n]
        ab = a_s[...].astype(BF)
        a_st[r] = ab
        acc[...] += dot_nn(ab, ws[r, 3 * width : 4 * width])

    def self_close(layer):
        for source, target in zip(self_st, self_out[layer]):
            pending["self"].append(store(source, target))

    def fetch_feed(layer, r, late=False):
        a = (EXPAND_ONE, EXPAND_TWO)[layer]
        fetch(("expand", layer, r), r, [(a, 0, model, wf.at[r, 0], (("e1", "e2")[layer],))])
        if not late:
            fetch_contract(layer, r)

    def fetch_contract(layer, r):
        b = (CONTRACT_ONE, CONTRACT_TWO)[layer]
        name = ("k1", "k2")[layer]
        fetch(("contract", layer, r), r, [(b, 0, hidden, wf.at[r, 1], (name,))])

    def feed_unit(layer, r):
        fetch_feed(layer, r, True)
        arrive(("expand", layer, r))
        z = dot_nn(ub[...], wf[r, 0]) + bias[r, 6 + layer : 7 + layer, 0:hidden]
        cdf = 0.5 * (1.0 + lax.erf(z * 0.7071067811865476))
        slope = cdf + z * (jnp.exp(-0.5 * z * z) * 0.3989422804014327)
        h = (z * cdf).astype(BF)
        h_st[r] = h
        slope_st[r] = slope.astype(BF)
        fetch_contract(layer, r)
        arrive(("contract", layer, r))
        acc[...] += dot_nn(h, wf[r, 1])

    def feed_close(layer):
        for source, target in zip(feed_st, feed_out[layer]):
            pending["feed"].append(store(source, target))

    def fetch_keys(r):
        fetch(("keys", r), r, [(KEY_VALUE, 0, middle, wk.at[r], ("ckv",))])

    def keys_unit(r):
        fetch_keys(r)
        arrive(("keys", r))
        chunk = 2 * padded
        for m in range(items // 2):
            rows = slice(m * chunk, (m + 1) * chunk)
            kc_st[r, rows] = dot_nt(pf[rows], wk[r, 0:width]).astype(BF)
            vc_st[r, rows] = (
                dot_nt(pf[rows], wk[r, width:middle]) + bias[r, 5:6, 0:width]
            ).astype(BF)

    def fetch_cross(r):
        wanted = [
            (JOIN_IN, 3 * width, 4 * width, wc.at[r, pl.ds(0, width)], ("cq",)),
            (CROSS_OUT, 0, width, wc.at[r, pl.ds(width, width)], ("co",)),
        ]
        fetch(("cross", r), r, wanted)

    def cross_unit(r):
        fetch_cross(r)
        arrive(("cross", r))
        q = (dot_nt(ub[...], wc[r, 0:width]) + bias[r, 4:5, 0:width]).astype(BF)
        qc_st[r] = q
        q_s[...] = q.astype(F32)
        for group in groups(items, 4):
            spans = [pl.ds(i * slots, slots) for i in group]
            keys = [pl.ds(i * padded, padded) for i in group]
            probs, mixed = items_forward(
                [
                    (q_s[rows], kc_st[r, part], vc_st[r, part], patches)
                    for rows, part in zip(spans, keys)
                ],
                masks,
            )
            for n, i in enumerate(group):
                pc_st[r, i] = probs[n]
                a_s[spans[n]] = mixed[n]
        ab = a_s[...].astype(BF)
        ac_st[r] = ab
        acc[...] += dot_nn(ab, wc[r, width:middle])

    def near_start(*arrays):
        for a in arrays:
            near[a].advance()

    move("s1p e1 k1")
    near_start(TEXT_IN, TEXT_OUT)
    bias[0] = jnp.zeros(bias.shape[1:], F32)
    bias[0, 0:2, 0:width] = bias_in[0][...].astype(F32)
    bias[0, 2:6, 0:width] = bias_in[1][...].astype(F32)
    bias[0, 6:7] = bias_in[2][...].astype(F32).reshape(1, hidden)
    bias[0, 7:8] = bias_in[3][...].astype(F32).reshape(1, hidden)
    bias_near.advance()
    bias_far.advance()
    near_start(KEY_VALUE)
    fetch_self(0, 0)
    fetch_keys(0)
    norm_rows(vecs, vecs_in[0:3], vecs_in[3:6])
    u[...] = x[...].astype(F32)
    ub[...] = x[...]
    open_layer(0)
    move("s1p s1o e1")
    self_unit(0, 0)
    move("s1p s2p")
    bias_near.need()
    fetch_self(0, 1)
    self_unit(0, 1)
    move("k1 s1p s1v e1 e2")
    bias_far.need()
    bias_last.advance()
    near_start(EXPAND_ONE, CONTRACT_ONE)
    pf_copy.wait()
    spread_patches(pf_raw, pf_wide, pf, items, padded)
    store(pf, pf_out)
    move("s2p ckv")
    keys_unit(0)
    move("k1 k2")
    fetch_keys(1)
    keys_unit(1)
    bias_last.need()
    move("s2o s1o e1")
    near_start(JOIN_IN, JOIN_OUT)
    fetch_self(0, 2)
    self_unit(0, 2)
    move("e2")
    fetch_feed(0, 0)
    fetch_feed(0, 1)
    self_unit(0, 3)
    self_close(0)
    move("s2v k1")
    close_layer(0)
    open_layer(1)
    move("s2p e2")
    feed_unit(0, 0)
    move("e1")
    feed_unit(0, 1)
    move("s2p ckv")
    fetch_keys(2)
    keys_unit(2)
    move("cq co k2")
    fetch_keys(3)
    fetch_feed(0, 2, True)
    fetch_feed(0, 3, True)
    keys_unit(3)
    for source, target in zip(cross_st[1:3], cross_out[1:3]):
        store(source, target)
    move("e2 k1")
    near_start(CROSS_OUT, EXPAND_TWO, CONTRACT_TWO)
    feed_unit(0, 2)
    fetch_contract(0, 3)
    fetch_self(1, 0)
    fetch_self(1, 1)
    feed_unit(0, 3)
    move("k2")
    feed_close(0)
    close_layer(1, text_out)
    open_layer(2)
    settle("self")
    move("s2p s2o")
    self_unit(1, 0)
    move("s2v")
    self_unit(1, 1)
    fetch_self(1, 2)
    fetch_cross(0)
    fetch_cross(1)
    self_unit(1, 2)
    move("k2")
    fetch_self(1, 3)
    self_unit(1, 3)
    self_close(1)
    move("cq")
    close_layer(2)
    open_layer(3)
    cross_unit(0)
    fetch_feed(1, 0)
    fetch_feed(1, 1)
    cross_unit(1)
    move("co")
    fetch_cross(2)
    cross_unit(2)
    fetch_cross(3)
    cross_unit(3)
    for n in (0, 3, 4):
        store(cross_st[n], cross_out[n])
    close_layer(3)
    open_layer(4)
    settle("feed")
    move("e2")
    feed_unit(1, 0)
    fetch_feed(1, 2, True)
    feed_unit(1, 1)
    move("k2")
    fetch_feed(1, 3, True)
    fetch_contract(1, 2)
    feed_unit(1, 2)
    fetch_contract(1, 3)
    feed_unit(1, 3)
    feed_close(1)
    close_layer(4, join_out)

    for copy in stores:
        if copy is not None:
            copy.wait()
    for flow in flows.values():
        flow.close()
    for direct in near + [bias_near, bias_far, bias_last]:
        direct.close()


def forward_all(links, own, biases, vecs, lengths, x, patch_rows, width):
    patches, items, features = patch_rows.shape
    rows, model = x.shape
    slots, padded = rows // items, -(-patches // 16) * 16
    hidden = own[EXPAND_ONE].shape[1]
    heads = width // HEAD_DIM
    anywhere = pl.BlockSpec(memory_space=ANY)
    vmem = pl.BlockSpec(memory_space=pltpu.VMEM)
    sizes = (links.tensor, links.dp, items, slots, patches, padded, width)
    mid = ((4, rows, width), BF)
    key = ((4, items * padded, width), BF)
    probs = ((4, items, slots, heads * slots), BF)
    cross_probs = ((4, items, padded, heads * slots), BF)
    feed = ((4, rows, hidden), BF)
    pf = ((items * padded, features), BF)
    self_kept = [mid] * 4 + [probs]
    cross_kept = [mid, key, key, mid, cross_probs]
    kept = self_kept * 2 + cross_kept + [feed] * 4
    outputs = [((3,) + a.shape, BF) for a in own]
    outputs += [((rows, model), BF)] * 2 + [((5, rows, model), F32), pf] + kept
    remotes = 13 * (2 + links.bits) + ARRAYS + 3
    outs = pl.pallas_call(
        functools.partial(forward_kernel, sizes),
        in_specs=[anywhere] * ARRAYS
        + [vmem] * 10
        + [pl.BlockSpec(memory_space=pltpu.SMEM), vmem, anywhere],
        out_specs=[anywhere] * ARRAYS + [vmem] * 2 + [anywhere] * (2 + len(kept)),
        out_shape=[jax.ShapeDtypeStruct(shape, dtype) for shape, dtype in outputs],
        scratch_shapes=[
            pltpu.VMEM((4, 4 * width, model), BF),
            pltpu.VMEM((4, 2, model, hidden), BF),
            pltpu.VMEM((4, 2 * width, model), BF),
            pltpu.VMEM((4, 2 * width, features), BF),
            pltpu.VMEM((rows, model), F32),
            pltpu.VMEM((rows, model), F32),
            pltpu.VMEM((rows, model), BF),
            pltpu.VMEM((5, rows, model), F32),
            pltpu.VMEM(patch_rows.shape, BF),
            pltpu.VMEM((features // 128, items * padded, 128), F32),
            pltpu.VMEM(*pf),
            pltpu.VMEM((5, 3, model), F32),
        ]
        + [pltpu.VMEM(*item) for item in self_kept + cross_kept + [feed] * 2]
        + [pltpu.VMEM((rows, width), F32)] * 4
        + [
            pltpu.VMEM((4, 8, model), F32),
            pltpu.SemaphoreType.DMA((remotes,)),
            pltpu.SemaphoreType.DMA((remotes,)),
            pltpu.SemaphoreType.DMA((64,)),
            pltpu.SemaphoreType.DMA((32,)),
            pltpu.SemaphoreType.DMA,
        ],
        compiler_params=pltpu.CompilerParams(
            collective_id=1, has_side_effects=True, vmem_limit_bytes=60 * 1024 * 1024
        ),
        name="forward_and_gather",
    )(*own, *biases, *vecs, lengths, x, patch_rows)
    n = ARRAYS
    got, (text_out, join_out, e, pf), kept = outs[:n], outs[n : n + 4], outs[n + 4 :]
    return got, text_out, join_out, e, pf, kept


(
    GRAD_CONTRACT_TWO,
    GRAD_EXPAND_TWO,
    GRAD_CROSS,
    GRAD_TWO,
    GRAD_CONTRACT_ONE,
    GRAD_EXPAND_ONE,
    GRAD_ONE,
) = range(7)


def backward_kernel(sizes, *refs):
    n_tensor, n_dp, items, slots, patches, padded, width, chunk, counts = sizes
    refs = list(refs)

    def take(n):
        got, refs[:n] = refs[:n], []
        return got

    own, got = take(ARRAYS), take(ARRAYS)
    e_in, pf_in, x, text_out, text_cot, join_cot = take(6)
    vecs_in = take(6)
    self_in = [take(5), take(5)]
    cross_in = take(5)
    feed_in = [take(2), take(2)]
    keeps, sends, outs = take(7), take(7), take(7)
    small_out, grad_text, dpf = take(3)
    wbuf, wk, stage_buf, e_s, ub, ub_t, dob, acc, pacc, pf, vecs = take(11)
    q_b, k_b, v_b, a_b, p_b = self_buf = take(5)
    qc_b, kc_b, vc_b, ac_b, pc_b = cross_buf = take(5)
    h_b, slope_b = take(2)
    q_s, k_s, v_s, da_s, dq_s, dk_s, dv_s = take(7)
    dkv_s, small_keep, small_send = take(3)
    fetch_sem, store_sem, e_sem, pf_sem, h_sem = take(5)
    model = x.shape[1]
    hidden = own[EXPAND_ONE].shape[1]
    side = pf.shape[1] - model

    sums = Sums(
        n_tensor,
        n_dp,
        counts,
        chunk,
        sends,
        keeps,
        outs,
        (small_send, small_keep, small_out),
        refs,
    )

    norm_rows(vecs, vecs_in[0:3], vecs_in[3:6])
    pf_copy = pltpu.make_async_copy(pf_in, pf, pf_sem)
    e_copies = [
        pltpu.make_async_copy(e_in.at[n], e_s.at[n], e_sem.at[n]) for n in range(5)
    ]
    for n in (4, 3, 2, 1, 0):
        e_copies[n].start()
    h_copies = [
        [
            pltpu.make_async_copy(feed_in[layer][0].at[r], h_b.at[r], h_sem.at[r])
            for r in range(4)
        ]
        for layer in range(2)
    ]
    for copy in h_copies[1]:
        copy.start()
    pf_copy.start()

    units = []
    for layer in (1, 0):
        expand, contract = ((EXPAND_ONE, CONTRACT_ONE), (EXPAND_TWO, CONTRACT_TWO))[layer]
        for r in range(4):
            units.append(
                (
                    "expand",
                    layer,
                    r,
                    [
                        (contract, 0, hidden, wbuf, hidden),
                        (expand, 0, model, wbuf, 0),
                        (feed_in[layer][1].at[r], slope_b),
                    ],
                )
            )
        for r in range(4):
            if layer == 1:
                units.append(
                    (
                        "cross",
                        0,
                        r,
                        [
                            (CROSS_OUT, 0, width, wbuf, width),
                            (JOIN_IN, 3 * width, width, wbuf, 0),
                            (KEY_VALUE, 0, 2 * width, wk, 0),
                        ]
                        + [(cross_in[n].at[r], cross_buf[n]) for n in (3, 0, 1, 2, 4)],
                    )
                )
        for r in range(4):
            first, last = ((TEXT_IN, TEXT_OUT), (JOIN_IN, JOIN_OUT))[layer]
            units.append(
                (
                    "self",
                    layer,
                    r,
                    [(last, 0, width, wbuf, 3 * width), (first, 0, 3 * width, wbuf, 0)]
                    + [(self_in[layer][n].at[r], self_buf[n]) for n in (4, 0, 1, 2, 3)],
                )
            )
    position = {unit[:3]: n for n, unit in enumerate(units)}

    def fetches(n):
        _, _, r, wanted = units[n]
        parity = n % 2
        copies = []
        for i, item in enumerate(wanted):
            if len(item) == 5:
                a, low, count, target, row = item
                source = (own[a] if r == 0 else got[a].at[r - 1]).at[pl.ds(low, count)]
                target = target.at[parity, pl.ds(row, count)]
            else:
                source, target = item
                target = target.at[parity]
            copies.append(pltpu.make_async_copy(source, target, fetch_sem.at[parity, i]))
        return copies

    def begin(n):
        if n + 1 < len(units):
            for copy in fetches(n + 1):
                copy.start()
        for copy in fetches(n):
            copy.wait()
        return n % 2

    stores = {}

    def room(r):
        j = r % 2
        if stores.get(j) is not None:
            stores[j].wait()
            stores[j] = None
        return j

    def put(array, r, lo=0, hi=None):
        j = r % 2
        target = (keeps, sends)[j][array]
        rows = (target.shape[1] if hi is None else hi) - lo
        stores[j] = pltpu.make_async_copy(
            stage_buf.at[j, pl.ds(0, rows)],
            target.at[r // 2, pl.ds(lo, rows)],
            store_sem.at[j],
        )
        stores[j].start()

    def settle():
        for j in (0, 1):
            room(j)

    def small_row(r, row, value):
        target = (small_keep, small_send)[r % 2]
        n = 8 * (r // 2) + row
        target[n : n + 1, 0 : value.shape[1]] = value

    def open_layer(n, dy):
        e_copies[n].wait()
        de, partial = norm_backward(e_s[n], vecs[n, 1:2], dy)
        for target in (small_keep, small_send):
            target[16 + 3 * n : 19 + 3 * n] = partial
        dob[...] = de.astype(BF)
        acc[...] = de

    def input_rows(n):
        rows = norm_forward(e_s[n], vecs[n, 1:2], vecs[n, 2:3])
        ub[...] = rows.astype(BF)
        ub_t[...] = rows.T.astype(BF)

    def contract_unit(layer, r, lo, hi):
        if lo == 0:
            h_copies[layer][r].wait()
        j = room(r)
        stage_buf[j, 0 : hi - lo] = dot_tn(h_b[r, :, lo:hi], dob[...]).astype(BF)
        put((GRAD_CONTRACT_ONE, GRAD_CONTRACT_TWO)[layer], r, lo, hi)

    def expand_unit(layer, r):
        b = begin(position["expand", layer, r])
        dh = dot_nt(dob[...], wbuf[b, hidden : 2 * hidden])
        dz = (dh * slope_b[b].astype(F32)).astype(BF)
        j = room(r)
        stage_buf[j, 0:model] = dot_nn(ub_t[...], dz).astype(BF)
        put((GRAD_EXPAND_ONE, GRAD_EXPAND_TWO)[layer], r)
        small_row(r, 6 + layer, jnp.sum(dz.astype(F32), axis=0, keepdims=True))
        acc[...] += dot_nt(dz, wbuf[b, 0:model])

    masks = head_masks(width)

    def self_unit(layer, r):
        b = begin(position["self", layer, r])
        da_s[...] = dot_nt(dob[...], wbuf[b, 3 * width : 4 * width])
        j = room(r)
        stage_buf[j, 3 * width : 4 * width] = dot_tn(a_b[b], dob[...]).astype(BF)
        q_s[...], k_s[...], v_s[...] = (
            q_b[b].astype(F32),
            k_b[b].astype(F32),
            v_b[b].astype(F32),
        )
        for group in groups(items, 8):
            spans = [pl.ds(i * slots, slots) for i in group]
            dq, dk, dv = items_backward(
                [
                    (
                        q_s[rows],
                        k_s[rows].astype(BF),
                        v_s[rows].astype(BF),
                        da_s[rows],
                        p_b[b, i],
                    )
                    for i, rows in zip(group, spans)
                ],
                masks,
            )
            for n, rows in enumerate(spans):
                dq_s[rows], dk_s[rows], dv_s[rows] = dq[n], dk[n], dv[n]
        xb = ub[...]
        total = acc[...]
        for c, part in enumerate((dq_s, dk_s, dv_s)):
            pb = part[...].astype(BF)
            stage_buf[j, c * width : (c + 1) * width] = dot_tn(pb, xb).astype(BF)
            total = total + dot_nn(pb, wbuf[b, c * width : (c + 1) * width])
            if c != 1:
                small_row(
                    r, 2 * layer + c // 2, jnp.sum(pb.astype(F32), axis=0, keepdims=True)
                )
        acc[...] = total
        put((GRAD_ONE, GRAD_TWO)[layer], r)

    def cross_unit(r):
        b = begin(position["cross", 0, r])
        da_s[...] = dot_nt(dob[...], wbuf[b, width : 2 * width])
        j = room(r)
        stage_buf[j, width : 2 * width] = dot_tn(ac_b[b], dob[...]).astype(BF)
        q_s[...] = qc_b[b].astype(F32)
        vsum = jnp.zeros((1, width), F32)
        for group in groups(items, 4):
            spans = [pl.ds(i * slots, slots) for i in group]
            keys = [pl.ds(i * padded, padded) for i in group]
            dq, dk, dv = items_backward(
                [
                    (q_s[rows], kc_b[b, part], vc_b[b, part], da_s[rows], pc_b[b, i])
                    for i, rows, part in zip(group, spans, keys)
                ],
                masks,
            )
            for n, part in enumerate(keys):
                dq_s[spans[n]] = dq[n]
                dkv_s[0, part] = dk[n].astype(BF)
                dvb = dv[n].astype(BF)
                dkv_s[1, part] = dvb
                vsum = vsum + jnp.sum(dvb.astype(F32), axis=0, keepdims=True)
        ticks(1)
        dqb = dq_s[...].astype(BF)
        stage_buf[j, 0:width] = dot_tn(dqb, ub[...]).astype(BF)
        acc[...] += dot_nn(dqb, wbuf[b, 0:width])
        small_row(r, 4, jnp.sum(dqb.astype(F32), axis=0, keepdims=True))
        small_row(r, 5, vsum)
        tails = []
        for c in range(2):
            grad = dot_tn(dkv_s[c], pf[...]).astype(BF)
            stage_buf[j, (2 + c) * width : (3 + c) * width] = grad[:, 0:model]
            tails.append(grad[:, model:])
        back = dot_nn(dkv_s[0], wk[b, 0:width]) + dot_nn(dkv_s[1], wk[b, width : 2 * width])
        for n in range(pacc.shape[0]):
            lanes = back[:, n * 128 : (n + 1) * 128]
            if r == 0:
                pacc[n] = lanes
            else:
                pacc[n] += lanes
        tail = jnp.concatenate(tails, axis=0)
        count = tail.shape[0] // (model // side)
        for c in range(model // side):
            stage_buf[j, 4 * width : 4 * width + count, c * side : (c + 1) * side] = tail[
                c * count : (c + 1) * count
            ]
        extra = stage_buf.shape[1] - 4 * width - count
        if extra > 0:
            stage_buf[j, 4 * width + count :] = jnp.zeros((extra, model), BF)
        put(GRAD_CROSS, r)

    small_keep[...] = jnp.zeros_like(small_keep)
    small_send[...] = jnp.zeros_like(small_send)
    for copy in fetches(0):
        copy.start()
    open_layer(4, join_cot[...].astype(F32))
    sums.greet()
    clock = [0]

    def ticks(count):
        for _ in range(count):
            sums.tick(clock[0])
            clock[0] += 1

    def collected(n):
        e_copies[n].wait()
        e_copies[n] = Done()

    first = 2 * chunk
    for r in range(4):
        contract_unit(1, r, 0, first)
    settle()
    ticks(1)
    collected(3)
    input_rows(3)
    ticks(1)
    for r in range(4):
        contract_unit(1, r, first, hidden)
    settle()
    ticks(1)
    for r in range(4):
        expand_unit(1, r)
        if r == 3:
            settle()
        ticks((1, 0, 1, 0)[r])
    open_layer(3, acc[...])
    collected(2)
    input_rows(2)
    pf_copy.wait()
    for r in range(4):
        cross_unit(r)
        if r == 3:
            settle()
        ticks(1)
    open_layer(2, acc[...])
    ub[...] = text_out[...]
    for copy in h_copies[0]:
        copy.start()
    for r in range(4):
        self_unit(1, r)
        if r == 3:
            settle()
        ticks((1, 2, 1, 2)[r])
    open_layer(1, acc[...] + text_cot[...].astype(F32))
    for r in range(4):
        contract_unit(0, r, 0, hidden)
    settle()
    ticks(1)
    collected(0)
    input_rows(0)
    for r in range(4):
        expand_unit(0, r)
        if r == 3:
            settle()
        ticks(1)
    open_layer(0, acc[...])
    ub[...] = x[...]
    for r in range(4):
        self_unit(0, r)
        if r == 3:
            settle()
        ticks((1, 2, 1, 2)[r])
    grad_text[...] = acc[...].astype(BF)

    def gather_patches(n, carry):
        for c in range(pacc.shape[0]):
            dpf[n, :, c * 128 : (c + 1) * 128] = pacc[
                c, pl.ds(n, items, stride=padded)
            ].astype(BF)
        return carry

    lax.fori_loop(0, patches, gather_patches, 0)
    sums.finish(clock[0])


class Done:
    def wait(self):
        pass


def backward_all(links, own, got, e, pf, x, text_out, cots, vecs, kept, patches, items, width):
    rows, model = x.shape
    slots, padded = rows // items, pf.shape[0] // items
    hidden = own[EXPAND_ONE].shape[1]
    heads = width // HEAD_DIM
    chunk = links.chunk
    anywhere = pl.BlockSpec(memory_space=ANY)
    vmem = pl.BlockSpec(memory_space=pltpu.VMEM)
    cross_rows = 2 * width + 2 * width * pf.shape[1] // model
    extents = [hidden, model, cross_rows, 4 * width, hidden, model, 4 * width]
    extents = [-(-extent // chunk) * chunk for extent in extents]
    counts = tuple(extent // chunk for extent in extents)
    sizes = (links.tensor, links.dp, items, slots, patches, padded, width, chunk, counts)
    pairs = [((2, extent, model), BF) for extent in extents]
    totals = [((extent, model), BF) for extent in extents]
    units, small = 8, 32
    outputs = pairs * 2 + totals
    outputs += [
        ((small - units, model), F32),
        ((rows, model), BF),
        ((patches, items, pf.shape[1]), BF),
    ]
    f32_rows = pltpu.VMEM((rows, width), F32)
    outs = pl.pallas_call(
        functools.partial(backward_kernel, sizes),
        in_specs=[anywhere] * (2 * ARRAYS + 2) + [vmem] * 10 + [anywhere] * len(kept),
        out_specs=[anywhere] * 21 + [vmem] * 3,
        out_shape=[jax.ShapeDtypeStruct(shape, dtype) for shape, dtype in outputs],
        scratch_shapes=[
            pltpu.VMEM((2, 2 * hidden, model), BF),
            pltpu.VMEM((2, 2 * width, pf.shape[1]), BF),
            pltpu.VMEM((2, max(extents), model), BF),
            pltpu.VMEM((5, rows, model), F32),
            pltpu.VMEM((rows, model), BF),
            pltpu.VMEM((model, rows), BF),
            pltpu.VMEM((rows, model), BF),
            pltpu.VMEM((rows, model), F32),
            pltpu.VMEM((pf.shape[1] // 128, pf.shape[0], 128), F32),
            pltpu.VMEM(pf.shape, BF),
            pltpu.VMEM((5, 3, model), F32),
        ]
        + [pltpu.VMEM((2, rows, width), BF)] * 4
        + [pltpu.VMEM((2, items, slots, heads * slots), BF)]
        + [pltpu.VMEM((2, rows, width), BF)]
        + [pltpu.VMEM((2, pf.shape[0], width), BF)] * 2
        + [pltpu.VMEM((2, rows, width), BF)]
        + [pltpu.VMEM((2, items, padded, heads * slots), BF)]
        + [pltpu.VMEM((4, rows, hidden), BF), pltpu.VMEM((2, rows, hidden), BF)]
        + [f32_rows] * 7
        + [
            pltpu.VMEM((2, pf.shape[0], width), BF),
            pltpu.VMEM((small, model), F32),
            pltpu.VMEM((small, model), F32),
            pltpu.SemaphoreType.DMA((2, 8)),
            pltpu.SemaphoreType.DMA((2,)),
            pltpu.SemaphoreType.DMA((5,)),
            pltpu.SemaphoreType.DMA,
            pltpu.SemaphoreType.DMA((4,)),
        ]
        + Sums.scratch(links.dp, chunk, model, small, units),
        compiler_params=pltpu.CompilerParams(
            collective_id=0, has_side_effects=True, vmem_limit_bytes=60 * 1024 * 1024
        ),
        name="backward_and_sums",
    )(*own, *got, e, pf, x, text_out, *cots, *vecs, *kept)
    return outs[14:21], outs[21], outs[22], outs[23]


def finish_kernel(width, *refs):
    refs = list(refs)

    def take(n):
        got, refs[:n] = refs[:n], []
        return got

    totals, passed, (small,) = take(7), take(4), take(1)
    passed_out = take(4)
    text_in, text_out, expand_one, contract_one, join_in = take(5)
    join_out, cross_out, key_value, expand_two, contract_two = take(5)
    text_bias, join_bias, hidden_one, hidden_two = take(4)
    text_shared, join_shared = take(3), take(3)
    half, full, keys = take(3)
    bounced = take(4)
    load_sem, store_sem = take(2)
    model = full.shape[2]
    side = keys.shape[1] - model
    count = 2 * width * side // model

    loads, stores = [], []
    for n in range(7):
        rows = totals[n].shape[0]
        loads.append(
            pltpu.make_async_copy(totals[n], half.at[n, pl.ds(0, rows)], load_sem.at[n])
        )
        loads[n].start()
    for n in range(4):
        loads.append(pltpu.make_async_copy(passed[n], bounced[n], load_sem.at[7 + n]))
        loads[7 + n].start()

    def store(source, target):
        copy = pltpu.make_async_copy(source, target, store_sem.at[len(stores)])
        copy.start()
        stores.append(copy)

    text_bias[...] = small[0:2, 0:width]
    join_bias[...] = small[2:6, 0:width]
    hidden_one[...] = small[6]
    hidden_two[...] = small[7]
    for n in range(5):
        for c in range(3):
            row = 8 + 3 * n + c
            target, m = (text_shared[c], n) if n < 2 else (join_shared[c], n - 2)
            target[m : m + 1] = small[row : row + 1]

    def widen(n):
        loads[n].wait()
        rows = totals[n].shape[0]
        full[n, 0:rows] = half[n, 0:rows].astype(F32)

    def send(n, lo, rows, target):
        store(full.at[n, pl.ds(lo, rows)], target)

    for n, target in (
        (GRAD_CONTRACT_TWO, contract_two),
        (GRAD_EXPAND_TWO, expand_two),
        (GRAD_CONTRACT_ONE, contract_one),
        (GRAD_EXPAND_ONE, expand_one),
    ):
        widen(n)
        send(n, 0, target.shape[0], target)
    widen(GRAD_CROSS)
    send(GRAD_CROSS, 0, width, join_in.at[pl.ds(3 * width, width)])
    send(GRAD_CROSS, width, width, cross_out)
    keys[:, 0:model] = full[GRAD_CROSS, 2 * width : 4 * width]
    for c in range(model // side):
        keys[c * count : (c + 1) * count, model:] = full[
            GRAD_CROSS, 4 * width : 4 * width + count, c * side : (c + 1) * side
        ]
    store(keys, key_value)
    widen(GRAD_TWO)
    send(GRAD_TWO, 0, 3 * width, join_in.at[pl.ds(0, 3 * width)])
    send(GRAD_TWO, 3 * width, width, join_out)
    widen(GRAD_ONE)
    send(GRAD_ONE, 0, 3 * width, text_in)
    send(GRAD_ONE, 3 * width, width, text_out)
    for n in range(4):
        loads[7 + n].wait()
        store(bounced[n], passed_out[n])
    for copy in stores:
        copy.wait()


def finish_all(totals, passed, small, width, hidden, features):
    model = totals[0].shape[1]
    anywhere = pl.BlockSpec(memory_space=ANY)
    vmem = pl.BlockSpec(memory_space=pltpu.VMEM)
    big = [
        (3 * width, model),
        (width, model),
        (model, hidden),
        (hidden, model),
        (4 * width, model),
        (width, model),
        (width, model),
        (2 * width, features),
        (model, hidden),
        (hidden, model),
    ]
    little = [(2, width), (4, width), (hidden,), (hidden,)]
    little += [(2, model)] * 3 + [(3, model)] * 3
    most = max(total.shape[0] for total in totals)
    return pl.pallas_call(
        functools.partial(finish_kernel, width),
        in_specs=[anywhere] * 11 + [vmem],
        out_specs=[anywhere] * (4 + len(big)) + [vmem] * len(little),
        out_shape=[jax.ShapeDtypeStruct(a.shape, a.dtype) for a in passed]
        + [jax.ShapeDtypeStruct(shape, F32) for shape in big + little],
        scratch_shapes=[
            pltpu.VMEM((7, most, model), BF),
            pltpu.VMEM((7, most, model), F32),
            pltpu.VMEM((2 * width, features), F32),
        ]
        + [pltpu.VMEM(a.shape, a.dtype) for a in passed]
        + [
            pltpu.SemaphoreType.DMA((11,)),
            pltpu.SemaphoreType.DMA((16,)),
        ],
        compiler_params=pltpu.CompilerParams(vmem_limit_bytes=60 * 1024 * 1024),
        name="finish",
    )(*totals, *passed, small)


class Links:
    def __init__(self, mesh):
        self.tensor = mesh.shape["tensor"]
        self.dp = mesh.shape["dp"]
        self.bits = self.dp.bit_length() - 1
        self.chunk = 128


def turned(array):
    array = jnp.swapaxes(array, 1, 2)
    return array.reshape(-1, array.shape[2])


def turned_back(rows, units):
    return jnp.swapaxes(rows.reshape(-1, units, rows.shape[1]), 1, 2)


def per_device(
    links,
    text_rows,
    patch_features,
    lengths,
    text_cotangent,
    join_cotangent,
    text_project_in,
    text_project_bias,
    text_project_out,
    text_expand,
    text_expand_bias,
    text_contract,
    text_out_bias,
    text_norm_gain,
    text_norm_shift,
    join_project_in,
    join_project_bias,
    join_project_out,
    cross_project_out,
    cross_key_value,
    join_expand,
    join_expand_bias,
    join_contract,
    join_out_bias,
    join_norm_gain,
    join_norm_shift,
):
    items, slots, model = text_rows.shape
    patches, patch_width = patch_features.shape[1:]
    width = text_project_in.shape[2]
    hidden = text_expand.shape[1]

    own = [
        turned(text_project_in),
        text_project_out,
        text_expand,
        text_contract,
        turned(join_project_in),
        join_project_out,
        turned(cross_key_value),
        cross_project_out,
        join_expand,
        join_contract,
    ]
    biases = (text_project_bias, join_project_bias, text_expand_bias, join_expand_bias)
    vecs = (text_out_bias, text_norm_gain, text_norm_shift)
    vecs += (join_out_bias, join_norm_gain, join_norm_shift)
    x = text_rows.reshape(items * slots, model)
    text_cot = text_cotangent.reshape(items * slots, model)
    join_cot = join_cotangent.reshape(items * slots, model)
    patch_rows = jnp.swapaxes(patch_features, 0, 1)

    got, text_out, join_out, e, pf, kept = forward_all(
        links, own, biases, vecs, lengths, x, patch_rows, width
    )
    totals, small, grad_text, grad_patches = backward_all(
        links, own, got, e, pf, x, text_out, (text_cot, join_cot), vecs, kept, patches, items, width
    )
    outs = finish_all(
        totals, (text_out, join_out, grad_text, grad_patches), small, width, hidden, patch_width
    )
    text_out, join_out, grad_text, grad_patches = outs[:4]
    text_in, text_project, expand_one, contract_one, join_in = outs[4:9]
    join_project, cross_project, key_value, expand_two, contract_two = outs[9:14]
    text_bias, join_bias, hidden_one, hidden_two = outs[14:18]

    return (
        text_out.reshape(text_rows.shape),
        join_out.reshape(text_rows.shape),
        grad_text.reshape(text_rows.shape),
        jnp.swapaxes(grad_patches, 0, 1),
        turned_back(text_in, width),
        text_bias,
        text_project,
        expand_one,
        hidden_one,
        contract_one,
        *outs[18:21],
        turned_back(join_in, width),
        join_bias,
        join_project,
        cross_project,
        turned_back(key_value, width),
        expand_two,
        hidden_two,
        contract_two,
        *outs[21:24],
    )


def solution(mesh):
    rows = P(("dp", "tensor"), None, None)
    last = P(None, None, "tensor")
    second = P(None, "tensor")
    first = P("tensor", None)
    line = P("tensor")
    full = P()
    in_specs = (
        (rows, rows, P(("dp", "tensor")), rows, rows)
        + (last, second, first, second, line, first, full, full, full)
        + (last, second, first, first, last, second, line, first, full, full, full)
    )
    out_specs = (
        (rows, rows, rows, rows)
        + (last, second, first, second, line, first, full, full, full)
        + (last, second, first, first, last, second, line, first, full, full, full)
    )
    return jax.shard_map(
        functools.partial(per_device, Links(mesh)),
        mesh=mesh,
        in_specs=in_specs,
        out_specs=out_specs,
        check_vma=False,
    )
```
